32 devices in a mesh: dp: 4 (over y, core), seq: 2 (over x), tensor: 4 (over z).
Axes of the slice: x: 2, y: 2, z: 4, core: 2. Of those that a mesh axis runs over, the one named last changes fastest.
Arguments:
- residual_in: bfloat16 [16, 2048, 1024], P('dp', 'seq'), may hold values from -6 to 6
- grad_out: float32 [16, 2048, 1024], P('dp', 'seq')
- segment_lengths: int32 [16, 3], P('dp'), may hold values from 300 to 1000, as said below
- attention_in: float32 [3, 1024, 1024], P(None, ('dp', 'seq'), 'tensor'), may hold values from -0.125 to 0.125
- attention_out: float32 [1024, 1024], P('tensor', ('dp', 'seq')), may hold values from -0.5 to 0.5
- expand: float32 [2, 1024, 4096], P(None, ('dp', 'seq'), 'tensor'), may hold values from -0.1875 to 0.1875
- contract: float32 [4096, 1024], P('tensor', ('dp', 'seq')), may hold values from -0.09375 to 0.09375
- gains: float32 [2, 1024], P(None, ('dp', 'seq'))
- mean_attention_in: float32 [3, 1024, 1024], P(None, ('dp', 'seq'), 'tensor'), may hold values from -0.00014647543 to 0.00014647543
- mean_attention_out: float32 [1024, 1024], P('tensor', ('dp', 'seq')), may hold values from -0.00014647543 to 0.00014647543
- mean_expand: float32 [2, 1024, 4096], P(None, ('dp', 'seq'), 'tensor'), may hold values from -0.00014647543 to 0.00014647543
- mean_contract: float32 [4096, 1024], P('tensor', ('dp', 'seq')), may hold values from -0.00014647543 to 0.00014647543
- mean_gains: float32 [2, 1024], P(None, ('dp', 'seq')), may hold values from -0.0005859017 to 0.0005859017
- square_attention_in: float32 [3, 1024, 1024], P(None, ('dp', 'seq'), 'tensor'), may hold values from 2.9798684e-11 to 4.7677895e-10
- square_attention_out: float32 [1024, 1024], P('tensor', ('dp', 'seq')), may hold values from 2.9798684e-11 to 4.7677895e-10
- square_expand: float32 [2, 1024, 4096], P(None, ('dp', 'seq'), 'tensor'), may hold values from 5.959737e-12 to 9.535579e-11
- square_contract: float32 [4096, 1024], P('tensor', ('dp', 'seq')), may hold values from 2.9798684e-11 to 4.7677895e-10
- square_gains: float32 [2, 1024], P(None, ('dp', 'seq')), may hold values from 2.9798684e-11 to 4.7677895e-10
Outputs:
- residual_out: bfloat16 [16, 2048, 1024], P('dp', 'seq')
- grad_in: float32 [16, 2048, 1024], P('dp', 'seq')
- grad_norm: float32 [], replicated
- new_mean_attention_in: float32 [3, 1024, 1024], P(None, ('dp', 'seq'), 'tensor')
- new_mean_attention_out: float32 [1024, 1024], P('tensor', ('dp', 'seq'))
- new_mean_expand: float32 [2, 1024, 4096], P(None, ('dp', 'seq'), 'tensor')
- new_mean_contract: float32 [4096, 1024], P('tensor', ('dp', 'seq'))
- new_mean_gains: float32 [2, 1024], P(None, ('dp', 'seq'))
- new_square_attention_in: float32 [3, 1024, 1024], P(None, ('dp', 'seq'), 'tensor')
- new_square_attention_out: float32 [1024, 1024], P('tensor', ('dp', 'seq'))
- new_square_expand: float32 [2, 1024, 4096], P(None, ('dp', 'seq'), 'tensor')
- new_square_contract: float32 [4096, 1024], P('tensor', ('dp', 'seq'))
- new_square_gains: float32 [2, 1024], P(None, ('dp', 'seq'))
- new_attention_in: float32 [3, 1024, 1024], P(None, ('dp', 'seq'), 'tensor')
- new_attention_out: float32 [1024, 1024], P('tensor', ('dp', 'seq'))
- new_expand: float32 [2, 1024, 4096], P(None, ('dp', 'seq'), 'tensor')
- new_contract: float32 [4096, 1024], P('tensor', ('dp', 'seq'))
- new_gains: float32 [2, 1024], P(None, ('dp', 'seq'))
The draws below stay inside these ranges and needn't reach their ends.
Inputs may be any that keep to these rules, and one draw needn't show every extreme that they name: `segment_lengths`: each row holds 3 segments whose lengths sum to 2048; in every row one of them has exactly 1000 tokens.
All inputs are finite; a program needn't handle non-finite values.
Results may differ from the reference program's by a relative error of at most 0.029.
Values may be sent and summed in bfloat16 or wider, within the bound.
No kernel may reach another device: no remote copies, remote signals or barrier semaphores. Data moves between devices by JAX's collectives and lax.ppermute only.
A program may use at most 512 MiB of HBM per device.

```python
import math
import jax
import jax.numpy as jnp
from jax import lax

D = 1024
H = 16
HD = 64
FF = 4096
LENGTH = 2048
SEG_LO = 300
SEG_HI = 1000
STEP = 10
ROWS = 16
NPARAM = 16779264


def draw_segment_lengths(key, part):
    key = jax.random.fold_in(key, 11)
    first_key, second_key = jax.random.split(key)
    spare = LENGTH - SEG_HI - 2 * SEG_LO
    extra = jax.random.randint(first_key, (ROWS,), 0, spare + 1)
    middle = (SEG_LO + extra).astype(jnp.int32)
    latter = (LENGTH - SEG_HI - middle).astype(jnp.int32)
    table = jnp.stack([jnp.full((ROWS,), SEG_HI, jnp.int32), middle, latter], axis=1)
    orders = jax.vmap(lambda k: jax.random.permutation(k, 3))(jax.random.split(second_key, ROWS))
    return jnp.take_along_axis(table, orders.astype(jnp.int32), axis=1)


def draw_grad_out(key, part):
    key = jax.random.fold_in(key, 12)
    ramp = jnp.arange(D, dtype=jnp.float32) / (D - 1)
    return jax.random.normal(key, (ROWS, LENGTH, D), jnp.float32) * (1.0 + 2.0 * ramp)


def draw_gains(key, part):
    key = jax.random.fold_in(key, 13)
    ramp = 1.0 + 2.0 * jnp.arange(D, dtype=jnp.float32) / (D - 1)
    spread = jnp.exp(0.12 * jnp.clip(jax.random.normal(key, (2, D), jnp.float32), -2.5, 2.5))
    return ramp[None, :] * spread


def block_levels(stream_key, shape, shards, low, largest):
    factor_of, own = 1.0, jax.random.fold_in(stream_key, 6)
    for axis_at, parts in shards:
        steps = jnp.exp(jax.random.uniform(jax.random.fold_in(own, axis_at), (parts,), jnp.float32, low / len(shards), largest / len(shards)))
        factor_of = factor_of * jnp.repeat(steps, shape[axis_at] // parts).reshape([-1 if axis == axis_at else 1 for axis in range(len(shape))])
    return factor_of


def bell_draw(key, shape, deviation, limit, shards=(), held_as=jnp.bfloat16):
    level = block_levels(key, shape, shards, -0.22, 0.18) if shards else 1.0
    entries = jax.random.normal(key, shape, jnp.float32) * deviation * level
    return jnp.minimum(jnp.maximum(entries, -limit), limit).astype(held_as)


def setup_inputs(seed: int = 0) -> dict:
    splits = jax.random.split(jax.random.key(seed), 19)
    return {
        "residual_in": bell_draw(splits[0], (ROWS, LENGTH, D), 1.0, 6.0, ((0, 4), (1, 2))),
        "grad_out": draw_grad_out(jax.random.fold_in(splits[18], 71), 0),
        "segment_lengths": draw_segment_lengths(jax.random.fold_in(splits[18], 71), 0),
        "attention_in": bell_draw(splits[3], (3, D, H * HD), (2 * D) ** -0.5, 0.125, ((1, 8), (2, 4)), jnp.float32),
        "attention_out": bell_draw(splits[4], (H * HD, D), (H * HD // 8) ** -0.5, 0.5, ((0, 4), (1, 8)), jnp.float32),
        "expand": bell_draw(splits[5], (2, D, FF), D ** -0.5, 0.1875, ((1, 8), (2, 4)), jnp.float32),
        "contract": bell_draw(splits[6], (FF, D), FF ** -0.5, 0.09375, ((0, 4), (1, 8)), jnp.float32),
        "gains": draw_gains(jax.random.fold_in(splits[18], 71), 0),
        "mean_attention_in": bell_draw(splits[8], (3, D, H * HD), (0.111 / NPARAM ** 0.5), 0.00014647543, ((1, 8), (2, 4)), jnp.float32),
        "mean_attention_out": bell_draw(splits[9], (H * HD, D), (0.111 / NPARAM ** 0.5), 0.00014647543, ((0, 4), (1, 8)), jnp.float32),
        "mean_expand": bell_draw(splits[10], (2, D, FF), (0.111 / NPARAM ** 0.5), 0.00014647543, ((1, 8), (2, 4)), jnp.float32),
        "mean_contract": bell_draw(splits[11], (FF, D), (0.111 / NPARAM ** 0.5), 0.00014647543, ((0, 4), (1, 8)), jnp.float32),
        "mean_gains": bell_draw(splits[12], (2, D), (0.444 / NPARAM ** 0.5), 0.0005859017, ((1, 8),), jnp.float32),
        "square_attention_in": jnp.clip(jnp.exp(math.log(4.767789496540331e-10) - 2.7725887 * jax.random.uniform(splits[13], (3, D, H * HD), jnp.float32) ** block_levels(splits[13], (3, D, H * HD), ((1, 8), (2, 4)), -0.2, 0.2)), 2.979868435337707e-11, 4.767789496540331e-10),
        "square_attention_out": jnp.clip(jnp.exp(math.log(4.767789496540331e-10) - 2.7725887 * jax.random.uniform(splits[14], (H * HD, D), jnp.float32) ** block_levels(splits[14], (H * HD, D), ((0, 4), (1, 8)), -0.2, 0.2)), 2.979868435337707e-11, 4.767789496540331e-10),
        "square_expand": jnp.clip(jnp.exp(math.log(9.535579270636418e-11) - 2.7725887 * jax.random.uniform(splits[15], (2, D, FF), jnp.float32) ** block_levels(splits[15], (2, D, FF), ((1, 8), (2, 4)), -0.2, 0.2)), 5.9597370441477615e-12, 9.535579270636418e-11),
        "square_contract": jnp.clip(jnp.exp(math.log(4.767789496540331e-10) - 2.7725887 * jax.random.uniform(splits[16], (FF, D), jnp.float32) ** block_levels(splits[16], (FF, D), ((0, 4), (1, 8)), -0.2, 0.2)), 2.979868435337707e-11, 4.767789496540331e-10),
        "square_gains": jnp.clip(jnp.exp(math.log(4.767789496540331e-10) - 2.7725887 * jax.random.uniform(splits[17], (2, D), jnp.float32) ** block_levels(splits[17], (2, D), ((1, 8),), -0.2, 0.2)), 2.979868435337707e-11, 4.767789496540331e-10),
    }


@jax.custom_vjp
def low(v):
    return lax.optimization_barrier(v.astype(jnp.bfloat16)).astype(jnp.float32)

@jax.custom_vjp
def low_back(v):
    return v

def low_keep(v):
    return (low(v), None)

def low_pass(kept, grad):
    return (grad,)

def back_keep(v):
    return (v, None)

def back_low(kept, grad):
    return (low(grad),)
low.defvjp(low_keep, low_pass)
low_back.defvjp(back_keep, back_low)
NORM_EPS = 1e-05
NEG = -1e+30
CLIP = 1.0
RATE = 0.04
GAIN_RATE = 1.0
BETA_ONE = 0.9
BETA_TWO = 0.999
ADAM_EPS = 1e-08
DECAY = 0.1
HIGH = lax.Precision.HIGHEST

def rms_norm(values, gain):
    return values * lax.rsqrt(lax.optimization_barrier(jnp.mean(values * values, axis=-1, keepdims=True)) + NORM_EPS) * gain

def segment_info(lens, first, count):
    ends = jnp.cumsum(lens, axis=-1)
    starts = ends - lens
    places = first + jnp.arange(count, dtype=jnp.int32)
    segment = lax.optimization_barrier(jnp.sum((places[None, :, None] >= ends[:, None, :]).astype(jnp.int32), axis=-1))
    picked = segment[:, :, None] == jnp.arange(lens.shape[-1], dtype=jnp.int32)[None, None, :]
    begin = lax.optimization_barrier(jnp.sum(jnp.where(picked, starts[:, None, :], 0), axis=-1))
    return (segment, (places[None, :] - begin).astype(jnp.float32))

def rope_tables(places, size):
    half = size // 2
    freq = jnp.exp(jnp.arange(half, dtype=jnp.float32) * (-2.0 * jnp.log(10000.0) / size))
    angle = places[..., None] * freq
    doubled = jnp.concatenate([angle, angle], axis=-1)
    return (jnp.cos(doubled), jnp.sin(doubled))

def rotate_half(values):
    half = values.shape[-1] // 2
    return jnp.concatenate([-values[..., half:], values[..., :half]], axis=-1)

def one_row(row_in, lens, weights):
    w_attend, w_output, w_expand, w_contract, gain_pair = weights
    segment, places = segment_info(lens[None, :], 0, LENGTH)
    segment = segment[0]
    cosine, sine = rope_tables(places[0], HD)
    cosine = cosine[:, None, :]
    sine = sine[:, None, :]

    def split_heads(values):
        return values.reshape(LENGTH, H, HD)

    def turn(values):
        return values * cosine + rotate_half(values) * sine
    normed_one = low(rms_norm(row_in, gain_pair[0]))
    query = low(turn(split_heads(low_back(jnp.dot(normed_one, w_attend[0], precision=HIGH)))))
    keys = low(turn(split_heads(low_back(jnp.dot(normed_one, w_attend[1], precision=HIGH)))))
    values = low(split_heads(low_back(jnp.dot(normed_one, w_attend[2], precision=HIGH))))
    width = min(512, LENGTH)

    def attend(pair):
        query_block, segment_block = pair
        scores = jnp.einsum('qhe,khe->hqk', query_block, keys, precision=HIGH) * HD ** (-0.5)
        scores = low_back(scores)
        alive = segment_block[:, None] == segment[None, :]
        scores = jnp.where(alive[None], scores, NEG)
        probs = jax.nn.softmax(scores, axis=-1)
        return jnp.einsum('hqk,khe->qhe', low(probs), values, precision=HIGH)
    attended = lax.map(jax.checkpoint(attend), (query.reshape(LENGTH // width, width, H, HD), segment.reshape(LENGTH // width, width)))
    attended = low(low_back(attended.reshape(LENGTH, H * HD)))
    hidden = row_in + low_back(jnp.dot(attended, w_output, precision=HIGH))
    normed_two = low(rms_norm(hidden, gain_pair[1]))
    gate = low_back(jnp.dot(normed_two, w_expand[0], precision=HIGH))
    upper = low_back(jnp.dot(normed_two, w_expand[1], precision=HIGH))
    middle = low(jax.nn.silu(gate) * upper)
    return hidden + low_back(jnp.dot(middle, w_contract, precision=HIGH))

def reference(residual_in, grad_out, segment_lengths, attention_in, attention_out, expand, contract, gains, mean_attention_in, mean_attention_out, mean_expand, mean_contract, mean_gains, square_attention_in, square_attention_out, square_expand, square_contract, square_gains):
    masters = (attention_in, attention_out, expand, contract, gains)

    def layer(whole_in, weights):
        rounded = tuple((low(weight) for weight in weights))

        def row(pair):
            return one_row(pair[0], pair[1], rounded)
        return lax.map(jax.checkpoint(row), (whole_in, segment_lengths))
    output, pull = jax.vjp(layer, residual_in.astype(jnp.float32), masters)
    input_grad, grads = pull(grad_out)
    total = sum((jnp.sum(grad * grad) for grad in grads))
    norm = jnp.sqrt(total)
    factor = jnp.minimum(1.0, CLIP / norm)
    firsts = (mean_attention_in, mean_attention_out, mean_expand, mean_contract, mean_gains)
    seconds = (square_attention_in, square_attention_out, square_expand, square_contract, square_gains)
    new_means = []
    new_squares = []
    new_weights = []
    for member in range(5):
        clipped = grads[member] * factor
        moment = BETA_ONE * firsts[member] + (1.0 - BETA_ONE) * clipped
        square = BETA_TWO * seconds[member] + (1.0 - BETA_TWO) * clipped * clipped
        update = moment / (1.0 - BETA_ONE ** STEP) / (jnp.sqrt(square / (1.0 - BETA_TWO ** STEP)) + ADAM_EPS)
        shrink = DECAY if member < 4 else 0.0
        speed = RATE if member < 4 else GAIN_RATE
        new_means.append(moment)
        new_squares.append(square)
        new_weights.append(masters[member] - speed * (update + shrink * masters[member]))
    return (output.astype(jnp.bfloat16), input_grad, norm, new_means[0], new_means[1], new_means[2], new_means[3], new_means[4], new_squares[0], new_squares[1], new_squares[2], new_squares[3], new_squares[4], new_weights[0], new_weights[1], new_weights[2], new_weights[3], new_weights[4])
```

```python
import jax
import jax.numpy as jnp
import numpy as np
from jax import lax
from jax.experimental import pallas as pl
from jax.experimental.pallas import tpu as pltpu
from jax.sharding import PartitionSpec as P

HD = 64
STEP = 10

NORM_EPS = 1e-05
NEG = -1e30
CLIP = 1.0
RATE = 0.04
GAIN_RATE = 1.0
BETA_ONE = 0.9
BETA_TWO = 0.999
ADAM_EPS = 1e-08
DECAY = 0.1

SCALE = HD ** (-0.5)
PAIR = 2 * HD
TILE = 256
VMEM = 60 * 1024 * 1024
F32 = jnp.float32
BF16 = jnp.bfloat16

NN = (((1,), (0,)), ((), ()))
NT = (((1,), (1,)), ((), ()))
TN = (((0,), (0,)), ((), ()))


def mm(left, right, dims=NN):
    return lax.dot_general(left, right, dims, preferred_element_type=F32)


def call(body, name, flops, moved, **rest):
    params = pltpu.CompilerParams(vmem_limit_bytes=VMEM)
    cost = pl.CostEstimate(flops=int(flops), bytes_accessed=int(moved), transcendentals=0)
    return pl.pallas_call(body, name=name, compiler_params=params, cost_estimate=cost, **rest)


def whole(shape):
    return pl.BlockSpec(shape, lambda *at: (0,) * len(shape), pipeline_mode=pl.Buffered(1))


def out(shape, kind=BF16):
    return jax.ShapeDtypeStruct(shape, kind)


def exchange(block, step):
    axis, bit = step
    return lax.ppermute(block, axis, [(i ^ bit, i) for i in range(lax.axis_size(axis))])


def exchange_steps():
    steps = []
    for axis in ("seq", "dp"):
        bits = [1 << k for k in range(lax.axis_size(axis).bit_length() - 1)]
        if axis == "dp":
            bits = bits[1:] + bits[:1]
        steps += [(axis, bit) for bit in bits]
    return steps


def owner_masks(steps):
    span = lax.axis_size("seq")
    masks = [0]
    for axis, bit in steps:
        masks += [m ^ (bit if axis == "seq" else bit * span) for m in masks]
    return np.array(masks, np.int32)


def reorder(values, masks, bits):
    order = [int(np.where(masks == mask ^ bits)[0][0]) for mask in masks]
    size = values.shape[1] // len(order)
    return jnp.concatenate([values[:, at * size : (at + 1) * size] for at in order], axis=1)


def gather_pieces(piece, steps):
    held = piece
    for step in steps[:-1]:
        held = jnp.concatenate([held, exchange(held, step)], axis=1)
    return held, exchange(held, steps[-1])


def add(left, right):
    return (left.astype(F32) + right.astype(F32)).astype(BF16)


def scatter_pieces(kept, sent, steps):
    held = add(kept, exchange(sent, steps[-1]))
    for step in reversed(steps[:-1]):
        half = held.shape[1] // 2
        held = add(held[:, :half], exchange(held[:, half:], step))
    return held


def swap_halves(values):
    lane = lax.broadcasted_iota(jnp.int32, values.shape, 1)
    size = values.shape[1]
    ahead = pltpu.roll(values, size - HD // 2, 1)
    behind = pltpu.roll(values, HD // 2, 1)
    return jnp.where(lane % HD < HD // 2, ahead, behind)


def half_sign(shape):
    lane = lax.broadcasted_iota(jnp.int32, shape, 1)
    return jnp.where(lane % HD < HD // 2, -1.0, 1.0)


def turn(values, cosine, sine):
    return values * cosine + swap_halves(values) * (sine * half_sign(values.shape))


def unturn(values, cosine, sine):
    return values * cosine - swap_halves(values * sine) * half_sign(values.shape)


def stack_pair(values):
    lane = lax.broadcasted_iota(jnp.int32, values.shape, 1)
    low = jnp.where(lane < HD, values, 0.0)
    high = jnp.where(lane >= HD, values, 0.0)
    return jnp.concatenate([low, high], axis=0).astype(BF16)


def unstack_pair(turned):
    count = turned.shape[1] // 2
    row = lax.broadcasted_iota(jnp.int32, (PAIR, count), 0)
    return jnp.where(row < HD, turned[:, :count], turned[:, count:]).T


def project_kernel(own, part, x_ref, g_ref, cos_ref, sin_ref, wa_ref, wb_ref, a_ref, at_ref, q_ref, k_ref, v_ref):
    values = x_ref[...].astype(F32)
    rate = lax.rsqrt(jnp.mean(values * values, axis=-1, keepdims=True) + NORM_EPS)
    normed = values * rate * g_ref[...]
    a_ref[...] = normed.astype(BF16)
    at_ref[...] = normed.T.astype(BF16)
    half = wa_ref.shape[1]
    low, high = a_ref[:, :half], a_ref[:, half:]
    cosine, sine = cos_ref[...], sin_ref[...]

    def product(z, m):
        cols = slice(m * part, (m + 1) * part)
        return mm(low, wa_ref[z, :, cols]) + mm(high, wb_ref[z, :, cols])

    def turned(ref, z, m):
        mixed = product(z, m)
        for at in range(0, part, PAIR):
            ref[:, z * part + at : z * part + at + PAIR] = turn(
                mixed[:, at : at + PAIR], cosine, sine
            ).astype(BF16)

    for z in range(wa_ref.shape[0]):
        turned(k_ref, z, 1)
        v_ref[:, z * part : (z + 1) * part] = product(z, 2).astype(BF16)

    @pl.when(pl.program_id(0) < own)
    def _():
        for z in range(wa_ref.shape[0]):
            turned(q_ref, z, 0)


def project(x_full, gain, cosine, sine, wa, wb, block):
    tokens, width = x_full.shape
    groups, half, cols = wa.shape
    part = cols // 4
    heads = groups * part
    own = block // TILE
    mine = lambda i: (jnp.minimum(i, own - 1), 0)
    return call(
        lambda *refs: project_kernel(own, part, *refs),
        "project",
        2 * (2 * tokens + block) * width * heads,
        2 * (tokens * width * 3 + 4 * width * heads),
        grid=(tokens // TILE,),
        in_specs=[
            pl.BlockSpec((TILE, width), lambda i: (i, 0)),
            whole((1, width)),
            pl.BlockSpec((TILE, PAIR), lambda i: (i, 0)),
            pl.BlockSpec((TILE, PAIR), lambda i: (i, 0)),
            whole(wa.shape),
            whole(wb.shape),
        ],
        out_specs=[
            pl.BlockSpec((TILE, width), lambda i: (i, 0)),
            pl.BlockSpec((width, TILE), lambda i: (0, i)),
            pl.BlockSpec((TILE, heads), mine),
            pl.BlockSpec((TILE, heads), lambda i: (i, 0)),
            pl.BlockSpec((TILE, heads), lambda i: (i, 0)),
        ],
        out_shape=[
            out((tokens, width)),
            out((width, tokens)),
            out((block, heads)),
            out((tokens, heads)),
            out((tokens, heads)),
        ],
    )(x_full, gain, cosine, sine, wa, wb)


def attend_kernel(count, reach, q_ref, k_ref, v_ref, qs_ref, ks_ref, o_ref, lse_ref, acc, top, total):
    at = pl.program_id(1)
    first, last, shift = reach[2 * at], reach[2 * at + 1], reach[2 * count]
    stacked = stack_pair(q_ref[...].astype(F32) * SCALE)
    segment = jnp.concatenate([qs_ref[0], qs_ref[0]], axis=1)
    acc[...] = jnp.zeros_like(acc)
    top[...] = jnp.full_like(top, NEG)
    total[...] = jnp.zeros_like(total)

    def step(tile, carry):
        place = tile ^ shift
        rows = pl.ds(pl.multiple_of(place * TILE, TILE), TILE)
        scores = mm(k_ref[rows, :], stacked, NT)
        scores = jnp.where(ks_ref[rows, :] == segment, scores, NEG)
        before = top[...]
        now = jnp.maximum(before, jnp.max(scores, axis=0, keepdims=True))
        probs = jnp.exp(scores - now)
        factor = jnp.exp(before - now)
        total[...] = total[...] * factor + jnp.sum(probs, axis=0, keepdims=True)
        acc[...] = acc[...] * factor + mm(v_ref[rows, :], probs.astype(BF16), TN)
        top[...] = now
        return carry

    lax.fori_loop(first, last, step, 0)
    o_ref[...] = unstack_pair(acc[...] / total[...]).astype(BF16)
    lse_ref[0, 0] = top[...] + jnp.log(total[...])


def attend(reach, query, keys, values, query_segment, key_segment):
    block, heads = query.shape
    tokens = keys.shape[0]
    pairs, count = heads // PAIR, block // TILE
    return call(
        lambda *refs: attend_kernel(count, *refs),
        "attend",
        4 * block * tokens * heads,
        2 * (2 * block * heads + 2 * tokens * heads),
        grid_spec=pltpu.PrefetchScalarGridSpec(
            num_scalar_prefetch=1,
            grid=(pairs, count),
            in_specs=[
                pl.BlockSpec((TILE, PAIR), lambda h, i, r: (i, h)),
                pl.BlockSpec((tokens, PAIR), lambda h, i, r: (0, h)),
                pl.BlockSpec((tokens, PAIR), lambda h, i, r: (0, h)),
                pl.BlockSpec((1, 1, TILE), lambda h, i, r: (i, 0, 0)),
                pl.BlockSpec((tokens, 1), lambda h, i, r: (0, 0)),
            ],
            out_specs=[
                pl.BlockSpec((TILE, PAIR), lambda h, i, r: (i, h)),
                pl.BlockSpec((1, 1, 1, 2 * TILE), lambda h, i, r: (h, i, 0, 0)),
            ],
            scratch_shapes=[
                pltpu.VMEM((PAIR, 2 * TILE), F32),
                pltpu.VMEM((1, 2 * TILE), F32),
                pltpu.VMEM((1, 2 * TILE), F32),
            ],
        ),
        out_shape=[out((block, heads)), out((pairs, count, 1, 2 * TILE), F32)],
    )(reach, query, keys, values, query_segment, key_segment)


def lift_kernel(part, o_ref, x_ref, g_ref, wa_ref, wb_ref, h_ref, a_ref, at_ref):
    half = wa_ref.shape[1]
    low = x_ref[:, :half].astype(F32)
    high = x_ref[:, half:].astype(F32)
    for z in range(wa_ref.shape[0]):
        attended = o_ref[:, z * part : (z + 1) * part]
        low += mm(attended, wa_ref[z, :, 3 * part :], NT)
        high += mm(attended, wb_ref[z, :, 3 * part :], NT)
    h_ref[:, :half] = low
    h_ref[:, half:] = high
    values = h_ref[...]
    rate = lax.rsqrt(jnp.mean(values * values, axis=-1, keepdims=True) + NORM_EPS)
    normed = values * rate * g_ref[...]
    a_ref[...] = normed.astype(BF16)
    at_ref[...] = normed.T.astype(BF16)


def lift(attended, x_full, gain, wa, wb):
    block, heads = attended.shape
    width = x_full.shape[1]
    return call(
        lambda *refs: lift_kernel(wa.shape[2] // 4, *refs),
        "lift",
        2 * block * width * heads,
        block * width * 14 + 2 * wa.size + 2 * wb.size,
        grid=(block // TILE,),
        in_specs=[
            pl.BlockSpec((TILE, heads), lambda i: (i, 0)),
            pl.BlockSpec((TILE, width), lambda i: (i, 0)),
            whole((1, width)),
            whole(wa.shape),
            whole(wb.shape),
        ],
        out_specs=[
            pl.BlockSpec((TILE, width), lambda i: (i, 0)),
            pl.BlockSpec((TILE, width), lambda i: (i, 0)),
            pl.BlockSpec((width, TILE), lambda i: (0, i)),
        ],
        out_shape=[out((block, width), F32), out((block, width)), out((width, block))],
    )(attended, x_full, gain, wa, wb)


def feed_kernel(first, *refs):
    a_ref, at_ref, e_ref, et_ref, wa_ref, wb_ref = refs[:6]
    rest = refs[6:]
    if not first:
        b_in, d_in = rest[:2]
        rest = rest[2:]
    b_ref, d_ref, ga_ref, gb_ref, mid, dgate, dup = rest
    block = a_ref.shape[0]
    half = wa_ref.shape[1]

    @pl.when(pl.program_id(0) == 0)
    def _():
        b_ref[...] = jnp.zeros_like(b_ref) if first else b_in[...]
        d_ref[...] = jnp.zeros_like(d_ref) if first else d_in[...]

    def tokens(i, carry):
        rows = pl.ds(pl.multiple_of(i * TILE, TILE), TILE)
        gate = mm(a_ref[rows, :half], wa_ref[0]) + mm(a_ref[rows, half:], wb_ref[0])
        upper = mm(a_ref[rows, :half], wa_ref[1]) + mm(a_ref[rows, half:], wb_ref[1])
        grad = mm(e_ref[rows, :half], wa_ref[2]) + mm(e_ref[rows, half:], wb_ref[2])
        sigma = jax.nn.sigmoid(gate)
        active = gate * sigma
        middle = (active * upper).astype(BF16)
        gate_grad = (grad * upper * (sigma * (1.0 + gate * (1.0 - sigma)))).astype(BF16)
        up_grad = (grad * active).astype(BF16)
        mid[rows, :] = middle
        dgate[rows, :] = gate_grad
        dup[rows, :] = up_grad
        b_ref[rows, :half] += mm(middle, wa_ref[2], NT)
        b_ref[rows, half:] += mm(middle, wb_ref[2], NT)
        d_ref[rows, :half] += mm(gate_grad, wa_ref[0], NT) + mm(up_grad, wa_ref[1], NT)
        d_ref[rows, half:] += mm(gate_grad, wb_ref[0], NT) + mm(up_grad, wb_ref[1], NT)
        return carry

    lax.fori_loop(0, block // TILE, tokens, 0)

    def features(i, carry):
        rows = pl.ds(pl.multiple_of(i * TILE, TILE), TILE)
        for ref, base in ((ga_ref, 0), (gb_ref, half)):
            source = pl.ds(pl.multiple_of(base + i * TILE, TILE), TILE)
            ref[0, rows, :] = mm(at_ref[source, :], dgate[...]).astype(BF16)
            ref[1, rows, :] = mm(at_ref[source, :], dup[...]).astype(BF16)
            ref[2, rows, :] = mm(et_ref[source, :], mid[...]).astype(BF16)
        return carry

    lax.fori_loop(0, half // TILE, features, 0)


def feed(normed, turned, cotangent, cotangent_turned, wa, wb, sums):
    block, width = normed.shape
    kinds, half, hidden = wa.shape
    cut = min(512, hidden)
    first = sums is None
    in_specs = [
        whole((block, width)),
        whole((width, block)),
        whole((block, width)),
        whole((width, block)),
        pl.BlockSpec((kinds, half, cut), lambda j: (0, 0, j)),
        pl.BlockSpec((kinds, half, cut), lambda j: (0, 0, j)),
    ]
    args = [normed, turned, cotangent, cotangent_turned, wa, wb]
    aliases = {}
    if not first:
        in_specs += [whole((block, width))] * 2
        args += list(sums)
        aliases = {6: 0, 7: 1}
    branch, grad, ga, gb = call(
        lambda *refs: feed_kernel(first, *refs),
        "feed",
        18 * block * width * hidden,
        8 * block * width + 16 * block * width + 4 * (wa.size + wb.size),
        grid=(hidden // cut,),
        in_specs=in_specs,
        out_specs=[
            whole((block, width)),
            whole((block, width)),
            pl.BlockSpec((kinds, half, cut), lambda j: (0, 0, j)),
            pl.BlockSpec((kinds, half, cut), lambda j: (0, 0, j)),
        ],
        out_shape=[out((block, width), F32), out((block, width), F32), out(wa.shape), out(wb.shape)],
        scratch_shapes=[pltpu.VMEM((block, cut), BF16)] * 3,
        input_output_aliases=aliases,
    )(*args)
    return (branch, grad), ga, gb


def back_kernel(part, h_ref, b_ref, d_ref, e_ref, f_ref, g_ref, place_ref, wa_ref, wb_ref, y_ref, dh_ref, ct_ref, do_ref, gg_ref):
    half = wa_ref.shape[1]
    hidden = h_ref[...]
    grad = d_ref[...].astype(BF16).astype(F32)
    branch = b_ref[...].astype(BF16).astype(F32)
    y_ref[...] = mm((hidden + branch).astype(BF16), place_ref[...], NT).astype(BF16)
    rate = lax.rsqrt(jnp.mean(hidden * hidden, axis=-1, keepdims=True) + NORM_EPS)
    scaled = grad * g_ref[...]
    dot = jnp.mean(hidden * scaled, axis=-1, keepdims=True)
    cotangent = e_ref[...].astype(F32) + f_ref[...].astype(F32)
    result = cotangent + rate * scaled - hidden * (rate * rate * rate * dot)
    dh_ref[...] = result
    rounded = result.astype(BF16)
    ct_ref[...] = result.T.astype(BF16)
    for z in range(wa_ref.shape[0]):
        do_ref[:, z * part : (z + 1) * part] = (
            mm(rounded[:, :half], wa_ref[z, :, 3 * part :]) + mm(rounded[:, half:], wb_ref[z, :, 3 * part :])
        ).astype(BF16)

    @pl.when(pl.program_id(0) == 0)
    def _():
        gg_ref[...] = jnp.zeros_like(gg_ref)

    gg_ref[...] += jnp.sum(grad * hidden * rate, axis=0, keepdims=True)


def back(hidden, branch, grad, high, low, gain, place, wa, wb):
    block, width = hidden.shape
    part = wa.shape[2] // 4
    heads = wa.shape[0] * part
    rows = lambda i: (i, 0)
    return call(
        lambda *refs: back_kernel(part, *refs),
        "back",
        2 * block * width * (heads + width),
        block * width * 26 + 2 * wa.size + 2 * wb.size,
        grid=(block // TILE,),
        in_specs=[pl.BlockSpec((TILE, width), rows)] * 5
        + [whole((1, width)), whole(place.shape), whole(wa.shape), whole(wb.shape)],
        out_specs=[
            pl.BlockSpec((TILE, width), rows),
            pl.BlockSpec((TILE, width), rows),
            pl.BlockSpec((width, TILE), lambda i: (0, i)),
            pl.BlockSpec((TILE, heads), rows),
            pl.BlockSpec((1, width), lambda i: (0, 0)),
        ],
        out_shape=[
            out((block, width)),
            out((block, width), F32),
            out((width, block)),
            out((block, heads)),
            out((1, width), F32),
        ],
    )(hidden, branch, grad, high, low, gain, place, wa, wb)


def unattend_kernel(
    count, reach, q_ref, g_ref, o_ref, k_ref, v_ref, lse_ref, qs_ref, ks_ref, cq_ref, sq_ref, ck_ref, sk_ref,
    dq_ref, dk_ref, dv_ref, dq_acc, dk_acc, dv_acc,
):
    at = pl.program_id(1)
    first, last, shift = reach[2 * at], reach[2 * at + 1], reach[2 * count]
    stacked = stack_pair(q_ref[...].astype(F32) * SCALE)
    grads = g_ref[...].astype(F32)
    stacked_grads = stack_pair(grads)
    product = (grads * o_ref[...].astype(F32)).T
    delta = jnp.concatenate(
        [jnp.sum(product[:HD], axis=0, keepdims=True), jnp.sum(product[HD:], axis=0, keepdims=True)], axis=1
    )
    segment = jnp.concatenate([qs_ref[0], qs_ref[0]], axis=1)
    lse = lse_ref[0, 0]
    dq_acc[...] = jnp.zeros_like(dq_acc)

    @pl.when(at == 0)
    def _():
        dk_acc[...] = jnp.zeros_like(dk_acc)
        dv_acc[...] = jnp.zeros_like(dv_acc)

    def step(tile, carry):
        place = tile ^ shift
        rows = pl.ds(pl.multiple_of(place * TILE, TILE), TILE)
        keys = k_ref[rows, :]
        scores = mm(keys, stacked, NT)
        probs = jnp.exp(jnp.where(ks_ref[rows, :] == segment, scores, NEG) - lse)
        prob_grads = mm(v_ref[rows, :], stacked_grads, NT)
        score_grads = (probs * (prob_grads - delta)).astype(BF16)
        dv_acc[rows, :] += mm(probs.astype(BF16), stacked_grads)
        dk_acc[rows, :] += mm(score_grads, stacked)
        dq_acc[...] += mm(keys, score_grads, TN)
        return carry

    lax.fori_loop(first, last, step, 0)
    dq_ref[...] = unturn(unstack_pair(dq_acc[...]) * SCALE, cq_ref[...], sq_ref[...]).astype(BF16)

    @pl.when(at == count - 1)
    def _():
        dk_ref[...] = unturn(dk_acc[...], ck_ref[...], sk_ref[...]).astype(BF16)
        dv_ref[...] = dv_acc[...].astype(BF16)


def unattend(reach, query, grads, attended, keys, values, lse, query_segment, key_segment, cosine, sine):
    block, heads = query.shape
    tokens = keys.shape[0]
    pairs, count = heads // PAIR, block // TILE
    tile = pl.BlockSpec((TILE, PAIR), lambda h, i, r: (i, h))
    full = pl.BlockSpec((tokens, PAIR), lambda h, i, r: (0, h))
    table = pl.BlockSpec((TILE, PAIR), lambda h, i, r: (i, 0))
    tables = pl.BlockSpec((tokens, PAIR), lambda h, i, r: (0, 0))
    return call(
        lambda *refs: unattend_kernel(count, *refs),
        "unattend",
        10 * block * tokens * heads,
        2 * (4 * block * heads + 4 * tokens * heads),
        grid_spec=pltpu.PrefetchScalarGridSpec(
            num_scalar_prefetch=1,
            grid=(pairs, count),
            in_specs=[
                tile,
                tile,
                tile,
                full,
                full,
                pl.BlockSpec((1, 1, 1, 2 * TILE), lambda h, i, r: (h, i, 0, 0)),
                pl.BlockSpec((1, 1, TILE), lambda h, i, r: (i, 0, 0)),
                pl.BlockSpec((tokens, 1), lambda h, i, r: (0, 0)),
                table,
                table,
                tables,
                tables,
            ],
            out_specs=[tile, full, full],
            scratch_shapes=[
                pltpu.VMEM((PAIR, 2 * TILE), F32),
                pltpu.VMEM((tokens, PAIR), F32),
                pltpu.VMEM((tokens, PAIR), F32),
            ],
        ),
        out_shape=[out((block, heads)), out((tokens, heads)), out((tokens, heads))],
    )(reach, query, grads, attended, keys, values, lse, query_segment, key_segment, cosine, sine, cosine, sine)


def unproject_kernel(own, part, dq_ref, dk_ref, dv_ref, x_ref, wa_ref, wb_ref, da_ref, gg_ref, acc):
    half = wa_ref.shape[1]
    groups = wa_ref.shape[0]

    def product(ref, m, w_ref):
        total = 0.0
        for z in range(groups):
            total += mm(ref[:, z * part : (z + 1) * part], w_ref[z, :, m * part : (m + 1) * part], NT)
        return total

    acc[:, :half] = product(dk_ref, 1, wa_ref) + product(dv_ref, 2, wa_ref)
    acc[:, half:] = product(dk_ref, 1, wb_ref) + product(dv_ref, 2, wb_ref)

    @pl.when(pl.program_id(0) < own)
    def _():
        acc[:, :half] += product(dq_ref, 0, wa_ref)
        acc[:, half:] += product(dq_ref, 0, wb_ref)

    @pl.when(pl.program_id(0) == 0)
    def _():
        gg_ref[...] = jnp.zeros_like(gg_ref)

    grad = acc[...]
    da_ref[...] = grad.astype(BF16)
    values = x_ref[...].astype(F32)
    rate = lax.rsqrt(jnp.mean(values * values, axis=-1, keepdims=True) + NORM_EPS)
    gg_ref[...] += jnp.sum(grad * values * rate, axis=0, keepdims=True)


def unproject(dq, dk, dv, x_full, wa, wb):
    tokens, width = x_full.shape
    block, heads = dq.shape
    own = block // TILE
    rows = lambda i: (i, 0)
    return call(
        lambda *refs: unproject_kernel(own, wa.shape[2] // 4, *refs),
        "unproject",
        2 * (2 * tokens + block) * width * heads,
        2 * (tokens * width * 4 + wa.size + wb.size),
        grid=(tokens // TILE,),
        in_specs=[
            pl.BlockSpec((TILE, heads), lambda i: (jnp.minimum(i, own - 1), 0)),
            pl.BlockSpec((TILE, heads), rows),
            pl.BlockSpec((TILE, heads), rows),
            pl.BlockSpec((TILE, width), rows),
            whole(wa.shape),
            whole(wb.shape),
        ],
        out_specs=[pl.BlockSpec((TILE, width), rows), pl.BlockSpec((1, width), lambda i: (0, 0))],
        out_shape=[out((tokens, width)), out((1, width), F32)],
        scratch_shapes=[pltpu.VMEM((TILE, width), F32)],
    )(dq, dk, dv, x_full, wa, wb)


def weigh_kernel(at_ref, ct_ref, dq_ref, dk_ref, dv_ref, o_ref, ga_ref, gb_ref):
    block = dq_ref.shape[0]
    part = dq_ref.shape[1]
    half = ga_ref.shape[1]

    def features(i, carry):
        rows = pl.ds(pl.multiple_of(i * TILE, TILE), TILE)
        for ref, base in ((ga_ref, 0), (gb_ref, half)):
            source = pl.ds(pl.multiple_of(base + i * TILE, TILE), TILE)
            ref[0, rows, :part] = mm(at_ref[source, :block], dq_ref[...]).astype(BF16)
            ref[0, rows, part : 2 * part] = mm(at_ref[source, :], dk_ref[...]).astype(BF16)
            ref[0, rows, 2 * part : 3 * part] = mm(at_ref[source, :], dv_ref[...]).astype(BF16)
            ref[0, rows, 3 * part :] = mm(ct_ref[source, :], o_ref[...]).astype(BF16)
        return carry

    lax.fori_loop(0, half // TILE, features, 0)


def weigh(turned, cotangent_turned, dq, dk, dv, attended, shape):
    width, tokens = turned.shape
    block = dq.shape[0]
    groups, half, cols = shape
    part = cols // 4
    column = lambda z: (0, z)
    return call(
        weigh_kernel,
        "weigh",
        2 * (2 * tokens + 2 * block) * width * groups * part,
        2 * (width * tokens * 3 + 2 * groups * half * cols),
        grid=(groups,),
        in_specs=[
            whole(turned.shape),
            whole(cotangent_turned.shape),
            pl.BlockSpec((block, part), column),
            pl.BlockSpec((tokens, part), column),
            pl.BlockSpec((tokens, part), column),
            pl.BlockSpec((block, part), column),
        ],
        out_specs=[pl.BlockSpec((1, half, cols), lambda z: (z, 0, 0))] * 2,
        out_shape=[out(shape), out(shape)],
    )(turned, cotangent_turned, dq, dk, dv, attended)


def finish_kernel(others, x_ref, dh_ref, g_ref, place_ref, *refs):
    grad = refs[0][...].astype(F32)
    for k in range(others):
        grad += refs[1 + k][...].astype(F32)
    y_ref = refs[1 + others]
    values = x_ref[...].astype(F32)
    rate = lax.rsqrt(jnp.mean(values * values, axis=-1, keepdims=True) + NORM_EPS)
    scaled = grad * g_ref[...]
    dot = jnp.mean(values * scaled, axis=-1, keepdims=True)
    result = dh_ref[...] + rate * scaled - values * (rate * rate * rate * dot)
    y_ref[...] = mm(result.astype(BF16), place_ref[...], NT).astype(BF16)


def finish(x_full, hidden_grad, gain, place, parts):
    block, width = hidden_grad.shape
    rows = lambda i: (i, 0)
    return call(
        lambda *refs: finish_kernel(len(parts) - 1, *refs),
        "finish",
        2 * block * width * width,
        block * width * (10 + 2 * len(parts)),
        grid=(block // TILE,),
        in_specs=[
            pl.BlockSpec((TILE, width), rows),
            pl.BlockSpec((TILE, width), rows),
            whole((1, width)),
            whole(place.shape),
        ]
        + [pl.BlockSpec((TILE, width), rows)] * len(parts),
        out_specs=pl.BlockSpec((TILE, width), rows),
        out_shape=out((block, width)),
    )(x_full, hidden_grad, gain, place, *parts)


def on_device(
    residual_in,
    grad_out,
    segment_lengths,
    attention_in,
    attention_out,
    expand,
    contract,
    gains,
    mean_attention_in,
    mean_attention_out,
    mean_expand,
    mean_contract,
    mean_gains,
    square_attention_in,
    square_attention_out,
    square_expand,
    square_contract,
    square_gains,
):
    span, copies = lax.axis_size("seq"), lax.axis_size("tensor")
    place, lane = lax.axis_index("seq"), lax.axis_index("tensor")
    rows, block, width = residual_in.shape
    tokens = span * block
    fold = copies // rows
    row = lane // fold
    piece = attention_in.shape[1]
    part = attention_in.shape[2]
    steps = exchange_steps()
    masks = owner_masks(steps)
    own = lax.axis_index("dp") * span + place

    attention_piece = jnp.concatenate(
        [attention_in[0], attention_in[1], attention_in[2], attention_out.T], axis=1
    ).astype(BF16)
    feed_piece = jnp.stack([expand[0], expand[1], contract.T]).astype(BF16)
    x_own = lax.dynamic_index_in_dim(residual_in, row, 0, keepdims=False)
    cotangent = lax.dynamic_index_in_dim(grad_out, row, 0, keepdims=False)
    attention_all = lax.all_gather(attention_piece, "tensor", axis=0)
    attention_a, attention_b = gather_pieces(attention_all, steps)
    x_parts = [x_own] + [exchange(x_own, ("seq", k)) for k in range(1, span)]
    full_gains = lax.all_gather(gains.astype(BF16), ("dp", "seq"), axis=1, tiled=True)
    feed_all = lax.all_gather(feed_piece, "tensor", axis=0)
    feeds = [gather_pieces(feed_all[z], steps) for z in range(copies)]

    owners = own ^ jnp.asarray(masks)
    columns = (owners[:, None] * piece + jnp.arange(piece, dtype=jnp.int32)[None, :]).reshape(width)
    placing = (jnp.arange(width, dtype=jnp.int32)[:, None] == columns[None, :]).astype(BF16)
    gain = mm(full_gains, placing)
    gain_one, gain_two = gain[:1], gain[1:]
    x_full = mm(jnp.concatenate(x_parts, axis=0), placing).astype(BF16)
    high = cotangent.astype(BF16)
    low = (cotangent - high.astype(F32)).astype(BF16)
    cotangent_turned = mm(placing, high, (((0,), (1,)), ((), ()))).astype(BF16)
    high = mm(high, placing).astype(BF16)
    low = mm(low, placing).astype(BF16)

    lens = lax.dynamic_index_in_dim(segment_lengths, row, 0, keepdims=False)
    ends = jnp.cumsum(lens)
    starts = ends - lens
    blocks = place ^ jnp.arange(span, dtype=jnp.int32)
    places = (blocks[:, None] * block + jnp.arange(block, dtype=jnp.int32)[None, :]).reshape(tokens)
    segment = jnp.sum((places[:, None] >= ends[None, :]).astype(jnp.int32), axis=-1)
    picked = segment[:, None] == jnp.arange(lens.shape[0], dtype=jnp.int32)[None, :]
    begin = jnp.sum(jnp.where(picked, starts[None, :], 0), axis=-1)
    finish_at = jnp.sum(jnp.where(picked, ends[None, :], 0), axis=-1)
    freq = jnp.exp(jnp.arange(HD // 2, dtype=F32) * (-2.0 * jnp.log(10000.0) / HD))
    angle = (places - begin).astype(F32)[:, None] * freq
    cosine = jnp.tile(jnp.cos(angle), (1, PAIR // (HD // 2)))
    sine = jnp.tile(jnp.sin(angle), (1, PAIR // (HD // 2)))
    count = block // TILE
    firsts = begin[:block].reshape(count, TILE)[:, 0] // TILE
    lasts = (finish_at[:block].reshape(count, TILE)[:, -1] + TILE - 1) // TILE
    reach = jnp.concatenate(
        [jnp.stack([firsts, lasts], axis=1).reshape(-1), (place * (block // TILE))[None]]
    ).astype(jnp.int32)
    query_segment = segment[:block].reshape(count, 1, TILE)
    key_segment = segment[:, None]

    normed_one, turned_one, query, keys, values = project(
        x_full, gain_one, cosine, sine, attention_a, attention_b, block
    )
    attended, lse = attend(reach, query, keys, values, query_segment, key_segment)
    hidden, normed_two, turned_two = lift(attended, x_full, gain_two, attention_a, attention_b)

    sums = None
    feed_shards = []
    for z in range(copies):
        sums, grad_a, grad_b = feed(normed_two, turned_two, high, cotangent_turned, *feeds[z], sums)
        feed_shards.append(scatter_pieces(grad_a, grad_b, steps))
    branch, normed_two_grad = sums
    result, hidden_grad, hidden_grad_turned, output_grad, grad_gain_two = back(
        hidden, branch, normed_two_grad, high, low, gain_two, placing, attention_a, attention_b
    )
    residual_out = lax.all_gather(result, "tensor", axis=0)[::fold]

    dq, dk, dv = unattend(
        reach, query, output_grad, attended, keys, values, lse, query_segment, key_segment, cosine, sine
    )
    normed_one_grad, grad_gain_one = unproject(dq, dk, dv, x_full, attention_a, attention_b)
    parts = [normed_one_grad[:block]] + [
        exchange(reorder(normed_one_grad[k * block : (k + 1) * block], masks, k), ("seq", k))
        for k in range(1, span)
    ]
    grad_a, grad_b = weigh(turned_one, hidden_grad_turned, dq, dk, dv, attended, attention_a.shape)
    attention_shard = scatter_pieces(grad_a, grad_b, steps)
    back_in = finish(x_full, hidden_grad, gain_one, placing, parts)
    grad_in = lax.all_gather(back_in, "tensor", axis=0)[::fold].astype(F32)

    share = 1.0 / fold
    attention_shard = lax.psum_scatter(attention_shard, "tensor", scatter_dimension=0).astype(F32) * share
    feed_shard = lax.psum_scatter(jnp.stack(feed_shards), "tensor", scatter_dimension=0).astype(F32) * share
    gain_grads = lax.dot_general(
        jnp.concatenate([grad_gain_one, grad_gain_two]), placing.astype(F32), NT, precision=lax.Precision.HIGHEST
    )
    gain_grads = lax.psum(gain_grads * share, ("dp", "seq", "tensor"))
    gain_shard = lax.dynamic_slice_in_dim(gain_grads, own * piece, piece, 1)

    local = jnp.sum(attention_shard * attention_shard) + jnp.sum(feed_shard * feed_shard)
    norm = jnp.sqrt(lax.psum(local, ("dp", "seq", "tensor")) + jnp.sum(gain_grads * gain_grads))
    factor = jnp.minimum(1.0, CLIP / norm)
    shards = (
        jnp.stack([attention_shard[:, k * part : (k + 1) * part] for k in range(3)]),
        attention_shard[:, 3 * part :].T,
        feed_shard[:2],
        feed_shard[2].T,
        gain_shard,
    )
    masters = (attention_in, attention_out, expand, contract, gains)
    firsts = (mean_attention_in, mean_attention_out, mean_expand, mean_contract, mean_gains)
    seconds = (
        square_attention_in,
        square_attention_out,
        square_expand,
        square_contract,
        square_gains,
    )
    new_means = []
    new_squares = []
    new_weights = []
    for member in range(5):
        clipped = shards[member] * factor
        moment = BETA_ONE * firsts[member] + (1.0 - BETA_ONE) * clipped
        square = BETA_TWO * seconds[member] + (1.0 - BETA_TWO) * clipped * clipped
        update = (
            moment / (1.0 - BETA_ONE**STEP) / (jnp.sqrt(square / (1.0 - BETA_TWO**STEP)) + ADAM_EPS)
        )
        shrink = DECAY if member < 4 else 0.0
        speed = RATE if member < 4 else GAIN_RATE
        new_means.append(moment)
        new_squares.append(square)
        new_weights.append(masters[member] - speed * (update + shrink * masters[member]))
    return (residual_out, grad_in, norm, *new_means, *new_squares, *new_weights)


def solution(mesh):
    tokens = P("dp", "seq", None)
    weights = (
        P(None, ("dp", "seq"), "tensor"),
        P("tensor", ("dp", "seq")),
        P(None, ("dp", "seq"), "tensor"),
        P("tensor", ("dp", "seq")),
        P(None, ("dp", "seq")),
    )
    return jax.shard_map(
        on_device,
        mesh=mesh,
        in_specs=(tokens, tokens, P("dp", None)) + weights * 3,
        out_specs=(tokens, tokens, P()) + weights * 3,
        check_vma=False,
    )
```

```python
import jax
import jax.numpy as jnp
from jax import lax
from jax.experimental import pallas as pl
from jax.experimental.pallas import tpu as pltpu
from jax.sharding import PartitionSpec as P

HD = 64
STEP = 10

NORM_EPS = 1e-05
NEG = -1e30
CLIP = 1.0
RATE = 0.04
GAIN_RATE = 1.0
BETA_ONE = 0.9
BETA_TWO = 0.999
ADAM_EPS = 1e-08
DECAY = 0.1

SCALE = HD ** (-0.5)
PAIR = 2 * HD
TILE = 256
VMEM = 60 * 1024 * 1024
F32 = jnp.float32
BF16 = jnp.bfloat16

NN = (((1,), (0,)), ((), ()))
NT = (((1,), (1,)), ((), ()))
TN = (((0,), (0,)), ((), ()))


def mm(left, right, dims=NN):
    return lax.dot_general(left, right, dims, preferred_element_type=F32)


def call(body, name, flops, args, grid, in_specs, out_specs, out_shape, scratch=(), prefetch=0, after=()):
    count, extra = len(args), len(after)
    moved = sum(a.size * a.dtype.itemsize for a in args) + sum(o.size * o.dtype.itemsize for o in out_shape)
    return pl.pallas_call(
        lambda *refs: body(*refs[:count], *refs[count + extra :]),
        name=name,
        grid_spec=pltpu.PrefetchScalarGridSpec(
            num_scalar_prefetch=prefetch,
            grid=grid,
            in_specs=list(in_specs) + [pl.BlockSpec(memory_space=pl.ANY)] * extra,
            out_specs=out_specs,
            scratch_shapes=list(scratch),
        ),
        out_shape=out_shape,
        compiler_params=pltpu.CompilerParams(vmem_limit_bytes=VMEM),
        cost_estimate=pl.CostEstimate(flops=int(flops) // 64, bytes_accessed=int(moved) // 64, transcendentals=0),
    )(*args, *after)


def whole(shape):
    return pl.BlockSpec(shape, lambda *at: (0,) * len(shape), pipeline_mode=pl.Buffered(1))


def scalar():
    return pl.BlockSpec(memory_space=pltpu.SMEM)


def out(shape, kind=BF16):
    return jax.ShapeDtypeStruct(shape, kind)


def exchange(block, step):
    axis, bit = step
    return lax.ppermute(block, axis, [(i ^ bit, i) for i in range(lax.axis_size(axis))])


def axis_steps():
    bits = lambda axis: [(axis, 1 << k) for k in range(lax.axis_size(axis).bit_length() - 1)]
    across = bits("dp")
    return bits("seq"), across[1:], across[0]


def owner_masks():
    span = lax.axis_size("seq")
    along, across, last = axis_steps()
    masks = [0]
    for axis, bit in along + across + [last]:
        masks += [m ^ (bit if axis == "seq" else bit * span) for m in masks]
    return masks


def gather_owners(array, axes):
    whole_array = lax.all_gather(array, axes, axis=0)
    return whole_array.reshape(lax.axis_size(axes[0]), -1, *array.shape)


def add(left, right):
    return (left.astype(F32) + right.astype(F32)).astype(BF16)


def scatter_start(kept, sent):
    return kept, exchange(sent, axis_steps()[2])


def scatter_rest(along_first):
    along, across, last = axis_steps()
    return list(reversed(across)) + list(reversed(along)) if not along_first else list(reversed(along)) + list(reversed(across))


def halve(held, step):
    axis = held.ndim - 3 if step[0] == "seq" else held.ndim - 4
    half = held.shape[axis] // 2
    kept = lax.slice_in_dim(held, 0, half, axis=axis)
    sent = lax.slice_in_dim(held, half, 2 * half, axis=axis)
    return kept, exchange(sent, step)


def scatter_tensor(held):
    size, here = lax.axis_size("tensor"), lax.axis_index("tensor")
    total = lax.dynamic_index_in_dim(held, here, 0, keepdims=False).astype(F32)
    for k in range(1, size):
        sent = lax.dynamic_index_in_dim(held, lax.rem(here + k, size), 0, keepdims=False)
        total += lax.ppermute(sent, "tensor", [(i, (i + k) % size) for i in range(size)]).astype(F32)
    return total


def row_block(own, mask, piece):
    return pl.ds(pl.multiple_of((own ^ mask) * piece, piece), piece)


def store_turned(own, masks, ref, values, scratch):
    scratch[...] = values.T.astype(BF16)
    piece = scratch.shape[0] // len(masks)
    for j, mask in enumerate(masks):
        ref[j * piece : (j + 1) * piece, :] = scratch[row_block(own, mask, piece), :]


def swap_halves(values):
    lane = lax.broadcasted_iota(jnp.int32, values.shape, 1)
    size = values.shape[1]
    ahead = pltpu.roll(values, size - HD // 2, 1)
    behind = pltpu.roll(values, HD // 2, 1)
    return jnp.where(lane % HD < HD // 2, ahead, behind)


def half_sign(shape):
    lane = lax.broadcasted_iota(jnp.int32, shape, 1)
    return jnp.where(lane % HD < HD // 2, -1.0, 1.0)


def turn(values, cosine, sine):
    return values * cosine + swap_halves(values) * (sine * half_sign(values.shape))


def unturn(values, cosine, sine):
    return values * cosine - swap_halves(values * sine) * half_sign(values.shape)


def pair_lanes(values, head):
    lane = lax.broadcasted_iota(jnp.int32, values.shape, 1)
    return jnp.where((lane < HD) == (head == 0), values, 0.0)


def stack_pair(values):
    return jnp.concatenate([pair_lanes(values, 0), pair_lanes(values, 1)], axis=0).astype(BF16)


def norm_rate(values):
    return lax.rsqrt(jnp.mean(values * values, axis=-1, keepdims=True) + NORM_EPS)


def inward_spec(weights):
    groups, owners, piece, cols = weights.shape
    return pl.BlockSpec((groups, owners, piece, cols // 4 * 3), lambda *at: (0, 0, 0, 0), pipeline_mode=pl.Buffered(1))


def outward_spec(weights):
    groups, owners, piece, cols = weights.shape
    return pl.BlockSpec((groups, owners, piece, cols // 4), lambda *at: (0, 0, 0, 3), pipeline_mode=pl.Buffered(1))


def outward(w_ref, w_all):
    groups, owners, piece, part = w_ref.shape
    for z in range(groups):
        w_all[:, z * part : (z + 1) * part] = w_ref[z].reshape(owners * piece, part)


def project(own, masks, x_full, gain, cosine, sine, weights, block):
    tokens, width = x_full.shape
    groups, owners, piece, cols = weights.shape
    part = cols // 4
    heads = groups * part
    mine = block // TILE

    def body(own_ref, x_ref, g_ref, cos_ref, sin_ref, w_ref, at_ref, q_ref, k_ref, v_ref, a_one, turned):
        own = own_ref[0]

        values = x_ref[...].astype(F32)
        normed = values * norm_rate(values) * g_ref[...]
        a_one[...] = normed.astype(BF16)
        store_turned(own, masks, at_ref, normed, turned)
        cosine, sine = cos_ref[...], sin_ref[...]

        def product(z, m):
            return mm(a_one[...], w_ref[z, :, :, m * part : (m + 1) * part].reshape(width, part))

        def rotated(ref, m):
            for z in range(groups):
                mixed = product(z, m)
                for lane in range(0, part, PAIR):
                    ref[:, z * part + lane : z * part + lane + PAIR] = turn(
                        mixed[:, lane : lane + PAIR], cosine, sine
                    ).astype(BF16)

        rotated(k_ref, 1)
        for z in range(groups):
            v_ref[:, z * part : (z + 1) * part] = product(z, 2).astype(BF16)

        @pl.when(pl.program_id(0) < mine)
        def _():
            rotated(q_ref, 0)

    rows = lambda i: (i, 0)
    return call(
        body,
        "project",
        2 * (2 * tokens + block) * width * heads,
        (own, x_full, gain, cosine, sine, weights),
        (tokens // TILE,),
        [
            scalar(),
            pl.BlockSpec((TILE, width), rows),
            whole((1, width)),
            pl.BlockSpec((TILE, PAIR), rows),
            pl.BlockSpec((TILE, PAIR), rows),
            inward_spec(weights),
        ],
        [
            pl.BlockSpec((width, TILE), lambda i: (0, i)),
            pl.BlockSpec((TILE, heads), lambda i: (jnp.minimum(i, mine - 1), 0)),
            pl.BlockSpec((TILE, heads), rows),
            pl.BlockSpec((TILE, heads), rows),
        ],
        [out((width, tokens)), out((block, heads)), out((tokens, heads)), out((tokens, heads))],
        [pltpu.VMEM((TILE, width), BF16), pltpu.VMEM((width, TILE), BF16)],
    )


def attend(reach, query, keys, values, query_marks, key_marks):
    block, heads = query.shape
    tokens = keys.shape[0]
    wide = 2 * PAIR
    count = block // TILE

    def body(reach, q_ref, k_ref, v_ref, qm_ref, km_ref, o_ref, lse_ref, turned, acc, top, total):
        at = pl.program_id(1)
        first, last, shift = reach[2 * at], reach[2 * at + 1], reach[2 * count]

        @pl.when(at == 0)
        def _():
            for tile in range(tokens // TILE):
                rows = slice(tile * TILE, (tile + 1) * TILE)
                turned[:, rows] = v_ref[rows, :].astype(F32).T.astype(BF16)

        marks = jnp.concatenate([qm_ref[...], qm_ref[...]], axis=0)
        stacked = [
            jnp.concatenate([stack_pair(q_ref[:, p * PAIR : (p + 1) * PAIR].astype(F32) * SCALE), marks], axis=1)
            for p in range(2)
        ]
        acc[...] = jnp.zeros_like(acc)
        top[...] = jnp.full_like(top, NEG)
        total[...] = jnp.zeros_like(total)

        def step(tile, carry):
            rows = pl.ds(pl.multiple_of((tile ^ shift) * TILE, TILE), TILE)
            for p in range(2):
                lanes = slice(p * PAIR, (p + 1) * PAIR)
                scores = mm(jnp.concatenate([k_ref[rows, lanes], km_ref[rows, :]], axis=1), stacked[p], NT)
                before = top[p : p + 1]
                now = jnp.maximum(before, jnp.max(scores, axis=0, keepdims=True))
                probs = jnp.exp(scores - now)
                factor = jnp.exp(before - now)
                total[p : p + 1] = total[p : p + 1] * factor + jnp.sum(probs, axis=0, keepdims=True)
                top[p : p + 1] = now
                probs = probs.astype(BF16)
                for h in range(2):
                    part = slice(p * PAIR + h * HD, p * PAIR + (h + 1) * HD)
                    cols = slice(h * TILE, (h + 1) * TILE)
                    acc[part, :] = acc[part, :] * factor[:, cols] + mm(turned[part, rows], probs[:, cols])
            return carry

        lax.fori_loop(first, last, step, 0)
        for p in range(2):
            rate = 1.0 / total[p : p + 1]
            for h in range(2):
                part = slice(p * PAIR + h * HD, p * PAIR + (h + 1) * HD)
                acc[part, :] = acc[part, :] * rate[:, h * TILE : (h + 1) * TILE]
        o_ref[...] = acc[...].T.astype(BF16)
        lse_ref[0, 0] = top[...] + jnp.log(total[...])

    return call(
        body,
        "attend",
        4 * block * tokens * heads,
        (reach, query, keys, values, query_marks, key_marks),
        (heads // wide, count),
        [
            pl.BlockSpec((TILE, wide), lambda h, i, r: (i, h)),
            pl.BlockSpec((tokens, wide), lambda h, i, r: (0, h)),
            pl.BlockSpec((tokens, wide), lambda h, i, r: (0, h)),
            pl.BlockSpec((TILE, PAIR), lambda h, i, r: (i, 0)),
            pl.BlockSpec((tokens, PAIR), lambda h, i, r: (0, 0)),
        ],
        [
            pl.BlockSpec((TILE, wide), lambda h, i, r: (i, h)),
            pl.BlockSpec((1, 1, 2, 2 * TILE), lambda h, i, r: (h, i, 0, 0)),
        ],
        [out((block, heads)), out((heads // wide, count, 2, 2 * TILE), F32)],
        [
            pltpu.VMEM((wide, tokens), BF16),
            pltpu.VMEM((wide, TILE), F32),
            pltpu.VMEM((2, 2 * TILE), F32),
            pltpu.VMEM((2, 2 * TILE), F32),
        ],
        prefetch=1,
    )


def lift(own, masks, attended, x_full, cotangent, gain, weights):
    block, heads = attended.shape
    width = x_full.shape[1]

    def body(own_ref, o_ref, x_ref, c_ref, g_ref, w_ref, h_ref, a_ref, at_ref, e_ref, et_ref, w_all, turned):
        own = own_ref[0]

        @pl.when(pl.program_id(0) == 0)
        def _():
            outward(w_ref, w_all)

        values = x_ref[...].astype(F32) + mm(o_ref[...], w_all[...], NT)
        h_ref[...] = values
        normed = values * norm_rate(values) * g_ref[...]
        a_ref[...] = normed.astype(BF16)
        store_turned(own, masks, at_ref, normed, turned)
        cotangent = c_ref[...]
        e_ref[...] = cotangent.astype(BF16)
        store_turned(own, masks, et_ref, cotangent, turned)

    rows = lambda i: (i, 0)
    wide = pl.BlockSpec((TILE, width), rows)
    tall = pl.BlockSpec((width, TILE), lambda i: (0, i))
    return call(
        body,
        "lift",
        2 * block * width * heads,
        (own, attended, x_full, cotangent, gain, weights),
        (block // TILE,),
        [scalar(), pl.BlockSpec((TILE, heads), rows), wide, wide, whole((1, width)), outward_spec(weights)],
        [wide, wide, tall, wide, tall],
        [out((block, width), F32), out((block, width)), out((width, block)), out((block, width)), out((width, block))],
        [pltpu.VMEM((width, heads), BF16), pltpu.VMEM((width, TILE), BF16)],
    )


def feed(normed, turned, cotangent, cotangent_turned, weights, after=()):
    block, width = normed.shape
    groups, owners, kinds, piece, hidden = weights.shape
    half = width // 2
    cut = min(512, hidden)
    tile = min(512, block)

    def body(a_ref, at_ref, e_ref, et_ref, w_ref, b_ref, d_ref, ga_ref, gb_ref, mid, dgate, dup):
        @pl.when((pl.program_id(0) == 0) & (pl.program_id(1) == 0))
        def _():
            b_ref[...] = jnp.zeros_like(b_ref)
            d_ref[...] = jnp.zeros_like(d_ref)

        def weight(m):
            return w_ref[0, :, m].reshape(width, cut)

        def tokens(i, carry):
            rows = pl.ds(pl.multiple_of(i * tile, tile), tile)
            gate = mm(a_ref[rows, :], weight(0))
            upper = mm(a_ref[rows, :], weight(1))
            grad = mm(e_ref[rows, :], weight(2))
            sigma = jax.nn.sigmoid(gate)
            active = gate * sigma
            mid[rows, :] = (active * upper).astype(BF16)
            dgate[rows, :] = (grad * upper * (sigma * (1.0 + gate * (1.0 - sigma)))).astype(BF16)
            dup[rows, :] = (grad * active).astype(BF16)
            b_ref[rows, :] += mm(mid[rows, :], weight(2), NT)
            d_ref[rows, :] += mm(dgate[rows, :], weight(0), NT) + mm(dup[rows, :], weight(1), NT)
            return carry

        lax.fori_loop(0, block // tile, tokens, 0)
        for ref, rows in ((ga_ref, slice(0, half)), (gb_ref, slice(half, width))):
            ref[0, 0] = mm(at_ref[rows, :], dgate[...]).astype(BF16)
            ref[0, 1] = mm(at_ref[rows, :], dup[...]).astype(BF16)
            ref[0, 2] = mm(et_ref[rows, :], mid[...]).astype(BF16)

    place = lambda z, j: (z, 0, 0, j)
    shape = (groups, kinds, half, hidden)
    return call(
        body,
        "feed",
        18 * block * width * hidden * groups,
        (normed, turned, cotangent, cotangent_turned, weights),
        (groups, hidden // cut),
        [
            whole((block, width)),
            whole((width, block)),
            whole((block, width)),
            whole((width, block)),
            pl.BlockSpec((1, owners, kinds, piece, cut), lambda z, j: (z, 0, 0, 0, j)),
        ],
        [
            whole((block, width)),
            whole((block, width)),
            pl.BlockSpec((1, kinds, half, cut), place),
            pl.BlockSpec((1, kinds, half, cut), place),
        ],
        [out((block, width), F32), out((block, width), F32), out(shape), out(shape)],
        [pltpu.VMEM((block, cut), BF16)] * 3,
        after=after,
    )


def back(own, masks, hidden, branches, grads, cotangent, gain, weights, after=()):
    block, width = hidden.shape
    groups, owners, piece, cols = weights.shape
    heads = groups * cols // 4

    def body(
        own_ref, h_ref, b0_ref, b1_ref, d0_ref, d1_ref, c_ref, g_ref, w_ref,
        y_ref, dh_ref, ct_ref, do_ref, gg_ref, w_all, turned,
    ):
        own = own_ref[0]

        @pl.when(pl.program_id(0) == 0)
        def _():
            outward(w_ref, w_all)
            gg_ref[...] = jnp.zeros_like(gg_ref)

        hidden = h_ref[...]
        grad = d0_ref[...] + d1_ref[...]
        y_ref[...] = (hidden + (b0_ref[...] + b1_ref[...])).astype(BF16)
        rate = norm_rate(hidden)
        scaled = grad * g_ref[...]
        dot = jnp.mean(hidden * scaled, axis=-1, keepdims=True)
        result = c_ref[...] + rate * scaled - hidden * (rate * rate * rate * dot)
        dh_ref[...] = result
        store_turned(own, masks, ct_ref, result, turned)
        do_ref[...] = mm(result.astype(BF16), w_all[...]).astype(BF16)
        gg_ref[...] += jnp.sum(grad * hidden * rate, axis=0, keepdims=True)

    rows = lambda i: (i, 0)
    wide = pl.BlockSpec((TILE, width), rows)
    return call(
        body,
        "back",
        2 * block * width * heads,
        (own, hidden, *branches, *grads, cotangent, gain, weights),
        (block // TILE,),
        [scalar()] + [wide] * 6 + [whole((1, width)), outward_spec(weights)],
        [
            wide,
            wide,
            pl.BlockSpec((width, TILE), lambda i: (0, i)),
            pl.BlockSpec((TILE, heads), rows),
            pl.BlockSpec((1, width), lambda i: (0, 0)),
        ],
        [
            out((block, width)),
            out((block, width), F32),
            out((width, block)),
            out((block, heads)),
            out((1, width), F32),
        ],
        [pltpu.VMEM((width, heads), BF16), pltpu.VMEM((width, TILE), BF16)],
        after=after,
    )


def unattend(side, reach, query, grads, attended, keys, values, lse, query_marks, key_marks, cosine, sine, after=()):
    block, heads = query.shape
    tokens = keys.shape[0]
    wide = 2 * PAIR
    count = block // TILE
    sets = heads // wide // 2

    def body(
        reach, q_ref, g_ref, o_ref, k_ref, v_ref, lse_ref, qm_ref, km_ref, cq_ref, sq_ref, ck_ref, sk_ref,
        dq_ref, dk_ref, dv_ref, dq_acc, dk_acc, dv_acc, lse_all, delta_all,
    ):
        at = pl.program_id(1)
        first, last, shift = reach[2 * at], reach[2 * at + 1], reach[2 * count]
        marks = jnp.concatenate([qm_ref[...], qm_ref[...]], axis=0)
        queries = q_ref[...].astype(F32) * SCALE
        grads = g_ref[...].astype(F32)
        product = grads * o_ref[...].astype(F32)
        query_turned = queries.T.astype(BF16)
        grad_turned = grads.T.astype(BF16)
        stacked, stacked_grads = [], []
        for p in range(2):
            lanes = slice(p * PAIR, (p + 1) * PAIR)
            stacked.append(jnp.concatenate([stack_pair(queries[:, lanes]), marks], axis=1))
            stacked_grads.append(stack_pair(grads[:, lanes]))
            lse_all[p] = jnp.broadcast_to(lse_ref[0, 0, p : p + 1, :], (PAIR, 2 * TILE)).T
            for h in range(2):
                delta = jnp.sum(pair_lanes(product[:, lanes], h), axis=1, keepdims=True)
                delta_all[p, h * TILE : (h + 1) * TILE, :] = jnp.broadcast_to(delta, (TILE, PAIR))
        dq_acc[...] = jnp.zeros_like(dq_acc)

        @pl.when(at == 0)
        def _():
            dk_acc[...] = jnp.zeros_like(dk_acc)
            dv_acc[...] = jnp.zeros_like(dv_acc)

        def step(tile, carry):
            rows = pl.ds(pl.multiple_of((tile ^ shift) * TILE, TILE), TILE)
            for p in range(2):
                lanes = slice(p * PAIR, (p + 1) * PAIR)
                keys = k_ref[rows, lanes]
                scores = mm(stacked[p], jnp.concatenate([keys, km_ref[rows, :]], axis=1), NT)
                probs = jnp.exp(scores - jnp.concatenate([lse_all[p]] * (TILE // PAIR), axis=1))
                prob_grads = mm(stacked_grads[p], v_ref[rows, lanes], NT)
                score_grads = probs * (prob_grads - jnp.concatenate([delta_all[p]] * (TILE // PAIR), axis=1))
                score_grads = score_grads.astype(BF16)
                probs = probs.astype(BF16)
                for h in range(2):
                    part = slice(p * PAIR + h * HD, p * PAIR + (h + 1) * HD)
                    these = slice(h * TILE, (h + 1) * TILE)
                    dv_acc[part, rows] += mm(grad_turned[part], probs[these])
                    dk_acc[part, rows] += mm(query_turned[part], score_grads[these])
                dq_acc[p] += mm(score_grads, keys)
            return carry

        lax.fori_loop(first, last, step, 0)
        for p in range(2):
            lanes = slice(p * PAIR, (p + 1) * PAIR)
            grad = pair_lanes(dq_acc[p, :TILE], 0) + pair_lanes(dq_acc[p, TILE:], 1)
            dq_ref[:, lanes] = unturn(grad * SCALE, cq_ref[...], sq_ref[...]).astype(BF16)

        @pl.when(at == count - 1)
        def _():
            for tile in range(tokens // TILE):
                rows = slice(tile * TILE, (tile + 1) * TILE)
                dv_ref[rows, :] = dv_acc[:, rows].T.astype(BF16)
                grad = dk_acc[:, rows].T
                for lane in (0, PAIR):
                    dk_ref[rows, lane : lane + PAIR] = unturn(
                        grad[:, lane : lane + PAIR], ck_ref[rows, :], sk_ref[rows, :]
                    ).astype(BF16)

    base = side * sets
    tile = pl.BlockSpec((TILE, wide), lambda h, i, r: (i, base + h))
    full = pl.BlockSpec((tokens, wide), lambda h, i, r: (0, base + h))
    table = pl.BlockSpec((TILE, PAIR), lambda h, i, r: (i, 0))
    tables = pl.BlockSpec((tokens, PAIR), lambda h, i, r: (0, 0))
    return call(
        body,
        "unattend",
        5 * block * tokens * heads,
        (reach, query, grads, attended, keys, values, lse, query_marks, key_marks, cosine, sine, cosine, sine),
        (sets, count),
        [
            tile,
            tile,
            tile,
            full,
            full,
            pl.BlockSpec((1, 1, 2, 2 * TILE), lambda h, i, r: (base + h, i, 0, 0)),
            table,
            tables,
            table,
            table,
            tables,
            tables,
        ],
        [
            pl.BlockSpec((TILE, wide), lambda h, i, r: (i, h)),
            pl.BlockSpec((tokens, wide), lambda h, i, r: (0, h)),
            pl.BlockSpec((tokens, wide), lambda h, i, r: (0, h)),
        ],
        [out((block, heads // 2)), out((tokens, heads // 2)), out((tokens, heads // 2))],
        [
            pltpu.VMEM((2, 2 * TILE, PAIR), F32),
            pltpu.VMEM((wide, tokens), F32),
            pltpu.VMEM((wide, tokens), F32),
            pltpu.VMEM((2, 2 * TILE, PAIR), F32),
            pltpu.VMEM((2, 2 * TILE, PAIR), F32),
        ],
        prefetch=1,
        after=after,
    )


def unproject(grads, x_full, first, block, weights, after=()):
    width = x_full.shape[1]
    groups, owners, piece, cols = weights.shape
    part = cols // 4
    kinds = len(grads)
    side = grads[0][0].shape[1]
    base = first // TILE

    def body(x_ref, *refs):
        g_refs, refs = refs[: 2 * kinds], refs[2 * kinds :]
        w_ref, da_ref, gg_ref, w_all = refs

        @pl.when(pl.program_id(0) == 0)
        def _():
            gg_ref[...] = jnp.zeros_like(gg_ref)
            for m in range(kinds):
                column = (3 - kinds + m) * part
                for z in range(groups):
                    w_all[m, :, z * part : (z + 1) * part] = w_ref[z, :, :, column : column + part].reshape(width, part)

        grad = mm(g_refs[0][...], w_all[0, :, :side], NT)
        for at in range(1, 2 * kinds):
            lanes = slice((at % 2) * side, (at % 2 + 1) * side)
            grad += mm(g_refs[at][...], w_all[at // 2, :, lanes], NT)
        da_ref[...] = grad.astype(BF16)
        values = x_ref[...].astype(F32)
        gg_ref[...] += jnp.sum(grad * values * norm_rate(values), axis=0, keepdims=True)

    def place(array):
        return (lambda i: (i, 0)) if array.shape[0] == block else (lambda i: (base + i, 0))

    flat = [array for pair in grads for array in pair]
    return call(
        body,
        "unproject",
        4 * kinds * block * width * side,
        (x_full, *flat, weights),
        (block // TILE,),
        [pl.BlockSpec((TILE, width), lambda i: (base + i, 0))]
        + [pl.BlockSpec((TILE, side), place(array)) for array in flat]
        + [inward_spec(weights)],
        [pl.BlockSpec((TILE, width), lambda i: (i, 0)), pl.BlockSpec((1, width), lambda i: (0, 0))],
        [out((block, width)), out((1, width), F32)],
        [pltpu.VMEM((kinds, width, 2 * side), BF16)],
        after=after,
    )


def weigh(turned, cotangent_turned, dq, dk, dv, attended, base, groups, part, after=()):
    width, tokens = turned.shape
    block = dq.shape[0]
    half = width // 2

    def body(at_ref, ct_ref, dq_ref, dk_ref, dv_ref, o_ref, ga_ref, gb_ref):
        for ref, rows in ((ga_ref, slice(0, half)), (gb_ref, slice(half, width))):
            ref[0, :, :part] = mm(at_ref[rows, :block], dq_ref[...]).astype(BF16)
            ref[0, :, part : 2 * part] = mm(at_ref[rows, :], dk_ref[...]).astype(BF16)
            ref[0, :, 2 * part : 3 * part] = mm(at_ref[rows, :], dv_ref[...]).astype(BF16)
            ref[0, :, 3 * part :] = mm(ct_ref[rows, :], o_ref[...]).astype(BF16)

    column = lambda z: (0, z)
    shape = (groups, half, 4 * part)
    return call(
        body,
        "weigh",
        4 * (tokens + block) * width * groups * part,
        (turned, cotangent_turned, dq, dk, dv, attended),
        (groups,),
        [
            whole(turned.shape),
            whole(cotangent_turned.shape),
            pl.BlockSpec((block, part), column),
            pl.BlockSpec((tokens, part), column),
            pl.BlockSpec((tokens, part), column),
            pl.BlockSpec((block, part), lambda z: (0, base + z)),
        ],
        [pl.BlockSpec((1, half, 4 * part), lambda z: (z, 0, 0))] * 2,
        [out(shape), out(shape)],
        after=after,
    )


def finish(x_full, hidden_grad, gain, parts, after=()):
    block, width = hidden_grad.shape

    def body(x_ref, dh_ref, g_ref, *refs):
        grad = refs[0][...].astype(F32)
        for ref in refs[1:-1]:
            grad += ref[...].astype(F32)
        values = x_ref[...].astype(F32)
        rate = norm_rate(values)
        scaled = grad * g_ref[...]
        dot = jnp.mean(values * scaled, axis=-1, keepdims=True)
        refs[-1][...] = (dh_ref[...] + rate * scaled - values * (rate * rate * rate * dot)).astype(BF16)

    wide = pl.BlockSpec((TILE, width), lambda i: (i, 0))
    return call(
        body,
        "finish",
        16 * block * width,
        (x_full, hidden_grad, gain, *parts),
        (block // TILE,),
        [wide, wide, whole((1, width))] + [wide] * len(parts),
        [wide],
        [out((block, width))],
        after=after,
    )[0]


def on_device(
    residual_in,
    grad_out,
    segment_lengths,
    attention_in,
    attention_out,
    expand,
    contract,
    gains,
    mean_attention_in,
    mean_attention_out,
    mean_expand,
    mean_contract,
    mean_gains,
    square_attention_in,
    square_attention_out,
    square_expand,
    square_contract,
    square_gains,
):
    span, copies = lax.axis_size("seq"), lax.axis_size("tensor")
    place, lane = lax.axis_index("seq"), lax.axis_index("tensor")
    rows, block, width = residual_in.shape
    tokens = span * block
    fold = copies // rows
    row = lane // fold
    piece = attention_in.shape[1]
    part = attention_in.shape[2]
    masks = owner_masks()
    index = lax.axis_index("dp") * span + place
    own = index.astype(jnp.int32)[None]
    near = copies // 2

    attention_piece = jnp.concatenate(
        [attention_in[0], attention_in[1], attention_in[2], attention_out.T], axis=1
    ).astype(BF16)
    feed_piece = jnp.stack([expand[0], expand[1], contract.T]).astype(BF16)
    x_own = lax.dynamic_index_in_dim(residual_in, row, 0, keepdims=False)
    cotangent = lax.dynamic_index_in_dim(grad_out, row, 0, keepdims=False)
    x_parts = [x_own] + [exchange(x_own, ("seq", k)) for k in range(1, span)]
    everywhere = ("tensor", "dp", "seq")
    weights = gather_owners(attention_piece, everywhere)
    full_gains = lax.all_gather(gains.astype(BF16), ("dp", "seq"), axis=1, tiled=True).astype(F32)
    gain_one, gain_two = full_gains[:1], full_gains[1:]
    cut = feed_piece.shape[2] // 2
    feeds = [gather_owners(feed_piece[:, :, at * cut : (at + 1) * cut], everywhere) for at in range(2)]

    x_full = jnp.concatenate(x_parts, axis=0)
    lens = lax.dynamic_index_in_dim(segment_lengths, row, 0, keepdims=False)
    ends = jnp.cumsum(lens)
    starts = ends - lens
    blocks = place ^ jnp.arange(span, dtype=jnp.int32)
    places = (blocks[:, None] * block + jnp.arange(block, dtype=jnp.int32)[None, :]).reshape(tokens)
    segment = jnp.sum((places[:, None] >= ends[None, :]).astype(jnp.int32), axis=-1)
    picked = segment[:, None] == jnp.arange(lens.shape[0], dtype=jnp.int32)[None, :]
    begin = jnp.sum(jnp.where(picked, starts[None, :], 0), axis=-1)
    finish_at = jnp.sum(jnp.where(picked, ends[None, :], 0), axis=-1)
    freq = jnp.exp(jnp.arange(HD // 2, dtype=F32) * (-2.0 * jnp.log(10000.0) / HD))
    angle = (places - begin).astype(F32)[:, None] * freq
    cosine = jnp.tile(jnp.cos(angle), (1, PAIR // (HD // 2)))
    sine = jnp.tile(jnp.sin(angle), (1, PAIR // (HD // 2)))
    count = block // TILE
    firsts = begin[:block].reshape(count, TILE)[:, 0] // TILE
    lasts = (finish_at[:block].reshape(count, TILE)[:, -1] + TILE - 1) // TILE
    reach = jnp.concatenate(
        [jnp.stack([firsts, lasts], axis=1).reshape(-1), (place * (block // TILE))[None]]
    ).astype(jnp.int32)
    lanes = jnp.arange(PAIR, dtype=jnp.int32)[None, :]
    key_marks = jnp.where(segment[:, None] == lanes, NEG, 0.0).astype(BF16)
    query_marks = ((segment[:block, None] != lanes) & (lanes < lens.shape[0])).astype(BF16)

    turned_one, query, keys, values = project(own, masks, x_full, gain_one, cosine, sine, weights, block)
    attended, lse = attend(reach, query, keys, values, query_marks, key_marks)
    hidden, normed_two, turned_two, rounded, rounded_turned = lift(
        own, masks, attended, x_full, cotangent, gain_two, weights
    )

    def spread(array):
        return array.reshape(*array.shape[:-2], -1, span, piece, array.shape[-1])

    orders = (scatter_rest(False), scatter_rest(True))
    branch_a, grad_a, kept_a, sent_a = feed(normed_two, turned_two, rounded, rounded_turned, feeds[0])
    flight_a = scatter_start(kept_a, sent_a)
    branch_b, grad_b, kept_b, sent_b = feed(normed_two, turned_two, rounded, rounded_turned, feeds[1], after=[branch_a])
    flight_b = scatter_start(kept_b, sent_b)
    held_a = spread(add(*flight_a))
    flight_a = halve(held_a, orders[0][0])
    result, hidden_grad, hidden_grad_turned, output_grad, grad_gain_two = back(
        own, masks, hidden, (branch_a, branch_b), (grad_a, grad_b), cotangent, gain_two, weights, after=[held_a]
    )
    residual_out = lax.all_gather(result, "tensor", axis=0)
    flight_b, output_grad = lax.optimization_barrier((flight_b, output_grad))
    held_b = spread(add(*flight_b))
    flight_b = halve(held_b, orders[1][0])
    sides = []
    common = (reach, query, output_grad, attended, keys, values, lse, query_marks, key_marks, cosine, sine)
    sides.append(unattend(0, *common, after=[held_b]))
    flight_a, flight_b, sides[0] = lax.optimization_barrier((flight_a, flight_b, sides[0]))
    for step in orders[0][1:]:
        held_a = add(*flight_a)
        flight_a = halve(held_a, step)
    for step in orders[1][1:]:
        held_b = add(*flight_b)
        flight_b = halve(held_b, step)
    sides.append(unattend(1, *common, after=[held_a, held_b, sides[0][0]]))
    flight_a, flight_b, sides[1] = lax.optimization_barrier((flight_a, flight_b, sides[1]))
    shard_a, shard_b = add(*flight_a), add(*flight_b)
    dqs, dks, dvs = zip(*sides)

    parts, gain_parts = [], []
    for k in range(1, span):
        grad, gain_part = unproject([dks, dvs], x_full, k * block, block, weights, after=[shard_a, shard_b])
        parts.append(exchange(grad, ("seq", k)))
        gain_parts.append(gain_part)
    feed_shard = scatter_tensor(
        jnp.concatenate([shard_a, shard_b], axis=-1).reshape(copies, -1, piece, feed_piece.shape[2])
    )

    flights = []
    for side in range(2):
        kept, sent = weigh(
            turned_one, hidden_grad_turned, *sides[side], attended, side * near, near, part, after=[gain_parts[-1]]
        )
        flights.append(scatter_start(kept, sent))
    own_grad, gain_part = unproject(
        [dqs, dks, dvs], x_full, 0, block, weights, after=[flights[1][0], feed_shard]
    )
    gain_parts.append(gain_part)
    helds = [spread(add(*flight)) for flight in flights]
    flights = [halve(held, order[0]) for held, order in zip(helds, orders)]
    back_in = finish(x_full, hidden_grad, gain_one, [own_grad] + parts, after=helds)
    grad_in = lax.all_gather(back_in, "tensor", axis=0)
    for at in range(1, len(orders[0])):
        flights = [halve(add(*flight), order[at]) for flight, order in zip(flights, orders)]
    attention_shard = scatter_tensor(
        jnp.concatenate([add(*flight) for flight in flights]).reshape(copies, piece, 4 * part)
    )
    if fold > 1:
        residual_out, grad_in = residual_out[::fold], grad_in[::fold]
    grad_in = grad_in.astype(F32)

    share = 1.0 / fold
    attention_shard, feed_shard = attention_shard * share, feed_shard * share
    gain_grads = jnp.concatenate([sum(gain_parts), grad_gain_two]) * share
    gain_grads = lax.psum(gain_grads, ("dp", "seq", "tensor"))
    gain_shard = lax.dynamic_slice_in_dim(gain_grads, index * piece, piece, 1)

    local = jnp.sum(attention_shard * attention_shard) + jnp.sum(feed_shard * feed_shard)
    norm = jnp.sqrt(lax.psum(local, ("dp", "seq", "tensor")) + jnp.sum(gain_grads * gain_grads))
    factor = jnp.minimum(1.0, CLIP / norm)
    shards = (
        jnp.stack([attention_shard[:, k * part : (k + 1) * part] for k in range(3)]),
        attention_shard[:, 3 * part :].T,
        feed_shard[:2],
        feed_shard[2].T,
        gain_shard,
    )
    masters = (attention_in, attention_out, expand, contract, gains)
    firsts = (mean_attention_in, mean_attention_out, mean_expand, mean_contract, mean_gains)
    seconds = (
        square_attention_in,
        square_attention_out,
        square_expand,
        square_contract,
        square_gains,
    )
    new_means = []
    new_squares = []
    new_weights = []
    for member in range(5):
        clipped = shards[member] * factor
        moment = BETA_ONE * firsts[member] + (1.0 - BETA_ONE) * clipped
        square = BETA_TWO * seconds[member] + (1.0 - BETA_TWO) * clipped * clipped
        update = (
            moment / (1.0 - BETA_ONE**STEP) / (jnp.sqrt(square / (1.0 - BETA_TWO**STEP)) + ADAM_EPS)
        )
        shrink = DECAY if member < 4 else 0.0
        speed = RATE if member < 4 else GAIN_RATE
        new_means.append(moment)
        new_squares.append(square)
        new_weights.append(masters[member] - speed * (update + shrink * masters[member]))
    return (residual_out, grad_in, norm, *new_means, *new_squares, *new_weights)


def solution(mesh):
    tokens = P("dp", "seq", None)
    weights = (
        P(None, ("dp", "seq"), "tensor"),
        P("tensor", ("dp", "seq")),
        P(None, ("dp", "seq"), "tensor"),
        P("tensor", ("dp", "seq")),
        P(None, ("dp", "seq")),
    )
    return jax.shard_map(
        on_device,
        mesh=mesh,
        in_specs=(tokens, tokens, P("dp", None)) + weights * 3,
        out_specs=(tokens, tokens, P()) + weights * 3,
        check_vma=False,
    )
```

```python
import jax
import jax.numpy as jnp
from jax import lax
from jax.experimental import pallas as pl
from jax.experimental.pallas import tpu as pltpu
from jax.sharding import Mesh
from jax.sharding import PartitionSpec as P

HD = 64
STEP = 10

NORM_EPS = 1e-05
NEG = -1e30
CLIP = 1.0
RATE = 0.04
GAIN_RATE = 1.0
BETA_ONE = 0.9
BETA_TWO = 0.999
ADAM_EPS = 1e-08
DECAY = 0.1

SCALE = HD ** (-0.5)
PAIR = 2 * HD
TILE = 256
VMEM = 60 * 1024 * 1024
F32 = jnp.float32
BF16 = jnp.bfloat16

NN = (((1,), (0,)), ((), ()))
NT = (((1,), (1,)), ((), ()))
TN = (((0,), (0,)), ((), ()))


def mm(left, right, dims=NN):
    return lax.dot_general(left, right, dims, preferred_element_type=F32)


def call(body, name, flops, args, grid, in_specs, out_specs, out_shape, scratch=(), prefetch=0, after=(), aliases={}):
    count, extra = len(args), len(after)
    moved = sum(a.size * a.dtype.itemsize for a in args) + sum(o.size * o.dtype.itemsize for o in out_shape)
    return pl.pallas_call(
        lambda *refs: body(*refs[:count], *refs[count + extra :]),
        name=name,
        grid_spec=pltpu.PrefetchScalarGridSpec(
            num_scalar_prefetch=prefetch,
            grid=grid,
            in_specs=list(in_specs) + [pl.BlockSpec(memory_space=pl.ANY)] * extra,
            out_specs=out_specs,
            scratch_shapes=list(scratch),
        ),
        out_shape=out_shape,
        input_output_aliases=dict(aliases),
        compiler_params=pltpu.CompilerParams(vmem_limit_bytes=VMEM),
        cost_estimate=pl.CostEstimate(flops=int(flops) // 64, bytes_accessed=int(moved) // 64, transcendentals=0),
    )(*args, *after)


def whole(shape):
    return pl.BlockSpec(shape, lambda *at: (0,) * len(shape), pipeline_mode=pl.Buffered(1))


def scalar():
    return pl.BlockSpec(memory_space=pltpu.SMEM)


def out(shape, kind=BF16):
    return jax.ShapeDtypeStruct(shape, kind)


def exchange(block, step):
    axis, bit = step
    return lax.ppermute(block, axis, [(i ^ bit, i) for i in range(lax.axis_size(axis))])


def axis_steps():
    bits = lambda axis: [(axis, 1 << k) for k in range(lax.axis_size(axis).bit_length() - 1)]
    return bits("seq"), bits("dp"), ("core", 1)


def owner_masks():
    span = lax.axis_size("seq")
    weight = {"seq": 1, "core": span, "dp": 2 * span}
    along, across, last = axis_steps()
    masks = [0]
    for axis, bit in along + across + [last]:
        masks += [m ^ bit * weight[axis] for m in masks]
    return masks


def gather_owners(array):
    near = lax.all_gather(array, ("tensor", "dp", "seq"), axis=0)
    return near.reshape(lax.axis_size("tensor"), lax.axis_size("dp"), lax.axis_size("seq"), *array.shape)


def gather_small(array):
    along, across, last = axis_steps()
    for step in along + [last] + across:
        other = exchange(array, step)
        pair, swapped = jnp.concatenate([array, other], axis=1), jnp.concatenate([other, array], axis=1)
        array = jnp.where(lax.axis_index(step[0]) & step[1], swapped, pair)
    return array


def sum_everywhere(array):
    for axis in ("core", "seq", "dp", "tensor"):
        for k in range(lax.axis_size(axis).bit_length() - 1):
            array = array + exchange(array, (axis, 1 << k))
    return array


def add(left, right):
    return (left.astype(F32) + right.astype(F32)).astype(BF16)


def scatter_start(kept, sent):
    return kept, exchange(sent, axis_steps()[2])


def scatter_rest(along_first):
    along, across, last = axis_steps()
    return list(reversed(across)) + list(reversed(along)) if not along_first else list(reversed(along)) + list(reversed(across))


def halve(held, step):
    axis = held.ndim - 3 if step[0] == "seq" else held.ndim - 4
    half = held.shape[axis] // 2
    kept = lax.slice_in_dim(held, 0, half, axis=axis)
    sent = lax.slice_in_dim(held, half, 2 * half, axis=axis)
    return kept, exchange(sent, step)


def tensor_sends(held, distances):
    size, here = lax.axis_size("tensor"), lax.axis_index("tensor")
    return [
        lax.ppermute(
            lax.dynamic_index_in_dim(held, lax.rem(here + k, size), 0, keepdims=False),
            "tensor",
            [(i, (i + k) % size) for i in range(size)],
        )
        for k in distances
    ]


def tensor_sum(held, received):
    own = lax.dynamic_index_in_dim(held, lax.axis_index("tensor"), 0, keepdims=False).astype(F32)
    return sum([array.astype(F32) for array in received], own)


def row_block(own, mask, piece):
    return pl.ds(pl.multiple_of((own ^ mask) * piece, piece), piece)


def store_turned(own, masks, ref, values, scratch):
    scratch[...] = values.T.astype(BF16)
    piece = scratch.shape[0] // len(masks)
    for j, mask in enumerate(masks):
        ref[j * piece : (j + 1) * piece, :] = scratch[row_block(own, mask, piece), :]


def swap_halves(values):
    lane = lax.broadcasted_iota(jnp.int32, values.shape, 1)
    size = values.shape[1]
    ahead = pltpu.roll(values, size - HD // 2, 1)
    behind = pltpu.roll(values, HD // 2, 1)
    return jnp.where(lane % HD < HD // 2, ahead, behind)


def half_sign(shape):
    lane = lax.broadcasted_iota(jnp.int32, shape, 1)
    return jnp.where(lane % HD < HD // 2, -1.0, 1.0)


def turn(values, cosine, sine):
    return values * cosine + swap_halves(values) * (sine * half_sign(values.shape))


def unturn(values, cosine, sine):
    return values * cosine - swap_halves(values * sine) * half_sign(values.shape)


def pair_lanes(values, head):
    lane = lax.broadcasted_iota(jnp.int32, values.shape, 1)
    return jnp.where((lane < HD) == (head == 0), values, 0.0)


def stack_pair(values):
    return jnp.concatenate([pair_lanes(values, 0), pair_lanes(values, 1)], axis=0).astype(BF16)


def norm_rate(values):
    return lax.rsqrt(jnp.mean(values * values, axis=-1, keepdims=True) + NORM_EPS)


def weight_specs(weights, first, count):
    *lead, cols = weights[0].shape
    part = cols // 4
    block = (*lead, count * part)
    return [pl.BlockSpec(block, lambda *at: (0,) * len(lead) + (first // count,), pipeline_mode=pl.Buffered(1))] * 2


def lay(core, store, near, far, pick):
    for flip, ref in ((0, near), (1, far)):
        for y in range(ref.shape[1]):
            rows = pick(ref, y)
            run = rows.shape[0] * rows.shape[1]
            store(pl.ds(pl.multiple_of((2 * y + (core ^ flip)) * run, run), run), rows.reshape(run, rows.shape[2]))


def lay_projections(core, w_all, near, far):
    part = near.shape[4] // w_all.shape[0]
    for m in range(w_all.shape[0]):
        cols = slice(m * part, (m + 1) * part)
        for z in range(near.shape[0]):

            def store(rows, value):
                w_all[m, rows, z * part : (z + 1) * part] = value

            lay(core, store, near, far, lambda ref, y: ref[z, y, :, :, cols])


def project(own, masks, x_full, gain, cosine, sine, weights, block):
    tokens, width = x_full.shape
    heads = weights[0].shape[0] * weights[0].shape[4] // 4
    mine = block // TILE

    def body(own_ref, x_ref, g_ref, cos_ref, sin_ref, wn_ref, wf_ref, at_ref, q_ref, k_ref, v_ref, w_all, a_one, turned):
        own = own_ref[0]

        @pl.when(pl.program_id(0) == 0)
        def _():
            lay_projections(own_ref[1], w_all, wn_ref, wf_ref)

        values = x_ref[...].astype(F32)
        normed = values * norm_rate(values) * g_ref[...]
        a_one[...] = normed.astype(BF16)
        store_turned(own, masks, at_ref, normed, turned)
        cosine, sine = cos_ref[...], sin_ref[...]

        def rotated(ref, m):
            for at in range(0, heads, 2 * PAIR):
                mixed = mm(a_one[...], w_all[m, :, at : at + 2 * PAIR])
                for lane in (0, PAIR):
                    ref[:, at + lane : at + lane + PAIR] = turn(mixed[:, lane : lane + PAIR], cosine, sine).astype(BF16)

        rotated(k_ref, 1)
        v_ref[...] = mm(a_one[...], w_all[2]).astype(BF16)

        @pl.when(pl.program_id(0) < mine)
        def _():
            rotated(q_ref, 0)

    rows = lambda i: (i, 0)
    return call(
        body,
        "project",
        2 * (2 * tokens + block) * width * heads,
        (own, x_full, gain, cosine, sine, *weights),
        (tokens // TILE,),
        [
            scalar(),
            pl.BlockSpec((TILE, width), rows),
            whole((1, width)),
            pl.BlockSpec((TILE, PAIR), rows),
            pl.BlockSpec((TILE, PAIR), rows),
            *weight_specs(weights, 0, 3),
        ],
        [
            pl.BlockSpec((width, TILE), lambda i: (0, i)),
            pl.BlockSpec((TILE, heads), lambda i: (jnp.minimum(i, mine - 1), 0)),
            pl.BlockSpec((TILE, heads), rows),
            pl.BlockSpec((TILE, heads), rows),
        ],
        [out((width, tokens)), out((block, heads)), out((tokens, heads)), out((tokens, heads))],
        [pltpu.VMEM((3, width, heads), BF16), pltpu.VMEM((TILE, width), BF16), pltpu.VMEM((width, TILE), BF16)],
    )


def attend(side, reach, query, keys, values, query_marks, key_marks, before):
    block, heads = query.shape
    tokens = keys.shape[0]
    wide = 2 * PAIR
    count = block // TILE
    sets = heads // wide // 2
    base = side * sets

    def body(reach, q_ref, k_ref, v_ref, qm_ref, km_ref, o_ref, lse_ref, turned, acc, top, total):
        at = pl.program_id(1)
        first, last, shift = reach[2 * at], reach[2 * at + 1], reach[2 * count]

        @pl.when(at == 0)
        def _():
            for tile in range(tokens // TILE):
                rows = slice(tile * TILE, (tile + 1) * TILE)
                turned[:, rows] = v_ref[rows, :].astype(F32).T.astype(BF16)

        marks = jnp.concatenate([qm_ref[...], qm_ref[...]], axis=0)
        stacked = [
            jnp.concatenate([stack_pair(q_ref[:, p * PAIR : (p + 1) * PAIR].astype(F32) * SCALE), marks], axis=1)
            for p in range(2)
        ]
        acc[...] = jnp.zeros_like(acc)
        top[...] = jnp.full_like(top, NEG)
        total[...] = jnp.zeros_like(total)

        def step(tile, carry):
            rows = pl.ds(pl.multiple_of((tile ^ shift) * TILE, TILE), TILE)
            for p in range(2):
                lanes = slice(p * PAIR, (p + 1) * PAIR)
                scores = mm(jnp.concatenate([k_ref[rows, lanes], km_ref[rows, :]], axis=1), stacked[p], NT)
                before = top[p : p + 1]
                now = jnp.maximum(before, jnp.max(scores, axis=0, keepdims=True))
                probs = jnp.exp(scores - now)
                factor = jnp.exp(before - now)
                total[p : p + 1] = total[p : p + 1] * factor + jnp.sum(probs, axis=0, keepdims=True)
                top[p : p + 1] = now
                probs = probs.astype(BF16)
                for h in range(2):
                    part = slice(p * PAIR + h * HD, p * PAIR + (h + 1) * HD)
                    cols = slice(h * TILE, (h + 1) * TILE)
                    acc[part, :] = acc[part, :] * factor[:, cols] + mm(turned[part, rows], probs[:, cols])
            return carry

        lax.fori_loop(first, last, step, 0)
        for p in range(2):
            rate = 1.0 / total[p : p + 1]
            for h in range(2):
                part = slice(p * PAIR + h * HD, p * PAIR + (h + 1) * HD)
                acc[part, :] = acc[part, :] * rate[:, h * TILE : (h + 1) * TILE]
        o_ref[...] = acc[...].T.astype(BF16)
        lse_ref[0, 0] = top[...] + jnp.log(total[...])

    return call(
        body,
        "attend",
        4 * block * tokens * heads,
        (reach, query, keys, values, query_marks, key_marks),
        (sets, count),
        [
            pl.BlockSpec((TILE, wide), lambda h, i, r: (i, base + h)),
            pl.BlockSpec((tokens, wide), lambda h, i, r: (0, base + h)),
            pl.BlockSpec((tokens, wide), lambda h, i, r: (0, base + h)),
            pl.BlockSpec((TILE, PAIR), lambda h, i, r: (i, 0)),
            pl.BlockSpec((tokens, PAIR), lambda h, i, r: (0, 0)),
        ],
        [
            pl.BlockSpec((TILE, wide), lambda h, i, r: (i, base + h)),
            pl.BlockSpec((1, 1, 2, 2 * TILE), lambda h, i, r: (base + h, i, 0, 0)),
        ],
        [out((block, heads)), out((heads // wide, count, 2, 2 * TILE), F32)],
        [
            pltpu.VMEM((wide, tokens), BF16),
            pltpu.VMEM((wide, TILE), F32),
            pltpu.VMEM((2, 2 * TILE), F32),
            pltpu.VMEM((2, 2 * TILE), F32),
        ],
        prefetch=1,
        after=before or (),
        aliases={6: 0, 7: 1} if before else {},
    )


def lift(own, masks, attended, x_full, cotangent, gain, weights):
    block, heads = attended.shape
    width = x_full.shape[1]

    def body(own_ref, o_ref, x_ref, c_ref, g_ref, wn_ref, wf_ref, h_ref, a_ref, at_ref, e_ref, et_ref, w_all, turned):
        own = own_ref[0]

        @pl.when(pl.program_id(0) == 0)
        def _():
            lay_projections(own_ref[1], w_all, wn_ref, wf_ref)

        values = x_ref[...].astype(F32) + mm(o_ref[...], w_all[0], NT)
        h_ref[...] = values
        normed = values * norm_rate(values) * g_ref[...]
        a_ref[...] = normed.astype(BF16)
        store_turned(own, masks, at_ref, normed, turned)
        cotangent = c_ref[...]
        e_ref[...] = cotangent.astype(BF16)
        store_turned(own, masks, et_ref, cotangent, turned)

    rows = lambda i: (i, 0)
    wide = pl.BlockSpec((TILE, width), rows)
    tall = pl.BlockSpec((width, TILE), lambda i: (0, i))
    return call(
        body,
        "lift",
        2 * block * width * heads,
        (own, attended, x_full, cotangent, gain, *weights),
        (block // TILE,),
        [scalar(), pl.BlockSpec((TILE, heads), rows), wide, wide, whole((1, width)), *weight_specs(weights, 3, 1)],
        [wide, wide, tall, wide, tall],
        [out((block, width), F32), out((block, width)), out((width, block)), out((block, width)), out((width, block))],
        [pltpu.VMEM((1, width, heads), BF16), pltpu.VMEM((width, TILE), BF16)],
    )


def feed(own, normed, turned, cotangent, cotangent_turned, weights, after=()):
    block, width = normed.shape
    groups, across, along, kinds, piece, hidden = weights[0].shape
    half = width // 2
    cut = min(512, hidden)
    tile = min(512, block)

    def body(
            own_ref, a_ref, at_ref, e_ref, et_ref, wn_ref, wf_ref, b_ref, d_ref, ga_ref, gb_ref, w_all, mid, dgate, dup
        ):
        @pl.when((pl.program_id(0) == 0) & (pl.program_id(1) == 0))
        def _():
            b_ref[...] = jnp.zeros_like(b_ref)
            d_ref[...] = jnp.zeros_like(d_ref)

        for m in range(kinds):

            def store(rows, value):
                w_all[m, rows, :] = value

            lay(own_ref[1], store, wn_ref, wf_ref, lambda ref, y: ref[0, y, :, m])

        def tokens(i, carry):
            rows = pl.ds(pl.multiple_of(i * tile, tile), tile)
            gate = mm(a_ref[rows, :], w_all[0])
            upper = mm(a_ref[rows, :], w_all[1])
            grad = mm(e_ref[rows, :], w_all[2])
            sigma = jax.nn.sigmoid(gate)
            active = gate * sigma
            mid[rows, :] = (active * upper).astype(BF16)
            dgate[rows, :] = (grad * upper * (sigma * (1.0 + gate * (1.0 - sigma)))).astype(BF16)
            dup[rows, :] = (grad * active).astype(BF16)
            b_ref[rows, :] += mm(mid[rows, :], w_all[2], NT)
            d_ref[rows, :] += mm(dgate[rows, :], w_all[0], NT) + mm(dup[rows, :], w_all[1], NT)
            return carry

        lax.fori_loop(0, block // tile, tokens, 0)
        for ref, rows in ((ga_ref, slice(0, half)), (gb_ref, slice(half, width))):
            ref[0, 0] = mm(at_ref[rows, :], dgate[...]).astype(BF16)
            ref[0, 1] = mm(at_ref[rows, :], dup[...]).astype(BF16)
            ref[0, 2] = mm(et_ref[rows, :], mid[...]).astype(BF16)

    place = lambda z, j: (z, 0, 0, j)
    shape = (groups, kinds, half, hidden)
    return call(
        body,
        "feed",
        18 * block * width * hidden * groups,
        (own, normed, turned, cotangent, cotangent_turned, *weights),
        (groups, hidden // cut),
        [
            scalar(),
            whole((block, width)),
            whole((width, block)),
            whole((block, width)),
            whole((width, block)),
            *[pl.BlockSpec((1, across, along, kinds, piece, cut), lambda z, j: (z, 0, 0, 0, 0, j))] * 2,
        ],
        [
            whole((block, width)),
            whole((block, width)),
            pl.BlockSpec((1, kinds, half, cut), place),
            pl.BlockSpec((1, kinds, half, cut), place),
        ],
        [out((block, width), F32), out((block, width), F32), out(shape), out(shape)],
        [pltpu.VMEM((kinds, width, cut), BF16)] + [pltpu.VMEM((block, cut), BF16)] * 3,
        after=after,
    )


def back(own, masks, hidden, branches, grads, cotangent, gain, weights, after=()):
    block, width = hidden.shape
    heads = weights[0].shape[0] * weights[0].shape[4] // 4

    def body(
        own_ref, h_ref, b0_ref, b1_ref, d0_ref, d1_ref, c_ref, g_ref, wn_ref, wf_ref,
        y_ref, dh_ref, ct_ref, do_ref, gg_ref, w_all, turned,
    ):
        own = own_ref[0]

        @pl.when(pl.program_id(0) == 0)
        def _():
            lay_projections(own_ref[1], w_all, wn_ref, wf_ref)
            gg_ref[...] = jnp.zeros_like(gg_ref)

        hidden = h_ref[...]
        grad = d0_ref[...] + d1_ref[...]
        y_ref[...] = (hidden + (b0_ref[...] + b1_ref[...])).astype(BF16)
        rate = norm_rate(hidden)
        scaled = grad * g_ref[...]
        dot = jnp.mean(hidden * scaled, axis=-1, keepdims=True)
        result = c_ref[...] + rate * scaled - hidden * (rate * rate * rate * dot)
        dh_ref[...] = result
        store_turned(own, masks, ct_ref, result, turned)
        do_ref[...] = mm(result.astype(BF16), w_all[0]).astype(BF16)
        gg_ref[...] += jnp.sum(grad * hidden * rate, axis=0, keepdims=True)

    rows = lambda i: (i, 0)
    wide = pl.BlockSpec((TILE, width), rows)
    return call(
        body,
        "back",
        2 * block * width * heads,
        (own, hidden, *branches, *grads, cotangent, gain, *weights),
        (block // TILE,),
        [scalar()] + [wide] * 6 + [whole((1, width)), *weight_specs(weights, 3, 1)],
        [
            wide,
            wide,
            pl.BlockSpec((width, TILE), lambda i: (0, i)),
            pl.BlockSpec((TILE, heads), rows),
            pl.BlockSpec((1, width), lambda i: (0, 0)),
        ],
        [
            out((block, width)),
            out((block, width), F32),
            out((width, block)),
            out((block, heads)),
            out((1, width), F32),
        ],
        [pltpu.VMEM((1, width, heads), BF16), pltpu.VMEM((width, TILE), BF16)],
        after=after,
    )


def unattend(k, reach, query, grads, attended, keys, values, lse, query_marks, key_marks, cosine, sine, partial, after=()):
    block, heads = query.shape
    wide = 2 * PAIR
    count = block // TILE
    first_block, last_block = partial is None, k == 0

    def body(reach, q_ref, g_ref, o_ref, k_ref, v_ref, lse_ref, qm_ref, km_ref, *refs):
        if last_block:
            cq_ref, sq_ref, *refs = refs
        ck_ref, sk_ref, *refs = refs
        if not first_block:
            part_ref, *refs = refs
        dq_ref, dk_ref, dv_ref, dq_acc, dk_acc, dv_acc, lse_all, delta_all = refs
        at = pl.program_id(1)
        first, last = reach[2 * at], reach[2 * at + 1]

        @pl.when(at == 0)
        def _():
            dk_acc[...] = jnp.zeros_like(dk_acc)
            dv_acc[...] = jnp.zeros_like(dv_acc)

        dq_acc[...] = jnp.zeros_like(dq_acc)

        @pl.when(first < last)
        def _():
            marks = jnp.concatenate([qm_ref[...], qm_ref[...]], axis=0)
            queries = q_ref[...].astype(F32) * SCALE
            grads = g_ref[...].astype(F32)
            product = grads * o_ref[...].astype(F32)
            query_turned = queries.T.astype(BF16)
            grad_turned = grads.T.astype(BF16)
            stacked, stacked_grads = [], []
            for p in range(2):
                lanes = slice(p * PAIR, (p + 1) * PAIR)
                stacked.append(jnp.concatenate([stack_pair(queries[:, lanes]), marks], axis=1))
                stacked_grads.append(stack_pair(grads[:, lanes]))
                lse_all[p] = jnp.broadcast_to(lse_ref[0, 0, p : p + 1, :], (PAIR, 2 * TILE)).T
                for h in range(2):
                    delta = jnp.sum(pair_lanes(product[:, lanes], h), axis=1, keepdims=True)
                    delta_all[p, h * TILE : (h + 1) * TILE, :] = jnp.broadcast_to(delta, (TILE, PAIR))

            def step(tile, carry):
                rows = pl.ds(pl.multiple_of(tile * TILE, TILE), TILE)
                for p in range(2):
                    lanes = slice(p * PAIR, (p + 1) * PAIR)
                    keys = k_ref[rows, lanes]
                    scores = mm(stacked[p], jnp.concatenate([keys, km_ref[rows, :]], axis=1), NT)
                    probs = jnp.exp(scores - jnp.concatenate([lse_all[p]] * (TILE // PAIR), axis=1))
                    prob_grads = mm(stacked_grads[p], v_ref[rows, lanes], NT)
                    score_grads = probs * (prob_grads - jnp.concatenate([delta_all[p]] * (TILE // PAIR), axis=1))
                    score_grads = score_grads.astype(BF16)
                    probs = probs.astype(BF16)
                    for h in range(2):
                        part = slice(p * PAIR + h * HD, p * PAIR + (h + 1) * HD)
                        these = slice(h * TILE, (h + 1) * TILE)
                        dv_acc[part, rows] += mm(grad_turned[part], probs[these])
                        dk_acc[part, rows] += mm(query_turned[part], score_grads[these])
                    dq_acc[p] += mm(score_grads, keys)
                return carry

            lax.fori_loop(first, last, step, 0)

        for p in range(2):
            lanes = slice(p * PAIR, (p + 1) * PAIR)
            grad = (pair_lanes(dq_acc[p, :TILE], 0) + pair_lanes(dq_acc[p, TILE:], 1)) * SCALE
            if not first_block:
                grad += part_ref[:, lanes]
            if last_block:
                grad = unturn(grad, cq_ref[...], sq_ref[...])
            dq_ref[:, lanes] = grad.astype(dq_ref.dtype)

        @pl.when(at == count - 1)
        def _():
            for tile in range(count):
                rows = slice(tile * TILE, (tile + 1) * TILE)
                dv_ref[rows, :] = dv_acc[:, rows].T.astype(BF16)
                grad = dk_acc[:, rows].T
                for lane in (0, PAIR):
                    dk_ref[rows, lane : lane + PAIR] = unturn(
                        grad[:, lane : lane + PAIR], ck_ref[rows, :], sk_ref[rows, :]
                    ).astype(BF16)

    tile = pl.BlockSpec((TILE, wide), lambda h, i, r: (i, h))
    full = pl.BlockSpec((block, wide), lambda h, i, r: (k, h))
    table = pl.BlockSpec((TILE, PAIR), lambda h, i, r: (i, 0))
    tables = pl.BlockSpec((block, PAIR), lambda h, i, r: (k, 0))
    done = pl.BlockSpec((block, wide), lambda h, i, r: (0, h))
    args = [reach, query, grads, attended, keys, values, lse, query_marks, key_marks]
    specs = [tile, tile, tile, full, full]
    specs += [pl.BlockSpec((1, 1, 2, 2 * TILE), lambda h, i, r: (h, i, 0, 0)), table, tables]
    if last_block:
        args += [cosine, sine]
        specs += [table, table]
    args += [cosine, sine]
    specs += [tables, tables]
    if not first_block:
        args.append(partial)
        specs.append(tile)
    return call(
        body,
        "unattend",
        5 * block * block * heads,
        args,
        (heads // wide, count),
        specs,
        [tile, done, done],
        [out((block, heads), BF16 if last_block else F32), out((block, heads)), out((block, heads))],
        [
            pltpu.VMEM((2, 2 * TILE, PAIR), F32),
            pltpu.VMEM((wide, block), F32),
            pltpu.VMEM((wide, block), F32),
            pltpu.VMEM((2, 2 * TILE, PAIR), F32),
            pltpu.VMEM((2, 2 * TILE, PAIR), F32),
        ],
        prefetch=1,
        after=after,
    )


def unproject(own, grads, x_full, k, weights, after=()):
    block, heads = grads[0].shape
    width = x_full.shape[1]
    kinds = len(grads)
    base = k * block // TILE

    def body(own_ref, x_ref, *refs):
        g_refs, (wn_ref, wf_ref, da_ref, gg_ref, w_all) = refs[:kinds], refs[kinds:]

        @pl.when(pl.program_id(0) == 0)
        def _():
            gg_ref[...] = jnp.zeros_like(gg_ref)
            lay_projections(own_ref[0], w_all, wn_ref, wf_ref)

        grad = mm(g_refs[0][...], w_all[3 - kinds], NT)
        for at in range(1, kinds):
            grad += mm(g_refs[at][...], w_all[3 - kinds + at], NT)
        da_ref[...] = grad.astype(BF16)
        values = x_ref[...].astype(F32)
        gg_ref[...] += jnp.sum(grad * values * norm_rate(values), axis=0, keepdims=True)

    rows = lambda i: (i, 0)
    return call(
        body,
        "unproject",
        2 * kinds * block * width * heads,
        (own[1:], x_full, *grads, *weights),
        (block // TILE,),
        [scalar(), pl.BlockSpec((TILE, width), lambda i: (base + i, 0))]
        + [pl.BlockSpec((TILE, heads), rows)] * kinds
        + weight_specs(weights, 0, 3),
        [pl.BlockSpec((TILE, width), rows), pl.BlockSpec((1, width), lambda i: (0, 0))],
        [out((block, width)), out((1, width), F32)],
        [pltpu.VMEM((3, width, heads), BF16)],
        after=after,
    )


def weigh(turned, cotangent_turned, dq, dks, dvs, attended, base, groups, part, after=()):
    width, tokens = turned.shape
    block = dq.shape[0]
    half = width // 2
    span = len(dks)

    def body(at_ref, ct_ref, dq_ref, o_ref, *refs):
        dk_refs, dv_refs, (ga_ref, gb_ref) = refs[:span], refs[span : 2 * span], refs[2 * span :]
        for ref, rows in ((ga_ref, slice(0, half)), (gb_ref, slice(half, width))):

            def total(refs):
                return sum(mm(at_ref[rows, k * block : (k + 1) * block], refs[k][...]) for k in range(span))

            ref[0, :, :part] = mm(at_ref[rows, :block], dq_ref[...]).astype(BF16)
            ref[0, :, part : 2 * part] = total(dk_refs).astype(BF16)
            ref[0, :, 2 * part : 3 * part] = total(dv_refs).astype(BF16)
            ref[0, :, 3 * part :] = mm(ct_ref[rows, :], o_ref[...]).astype(BF16)

    column = pl.BlockSpec((block, part), lambda z: (0, base + z))
    shape = (groups, half, 4 * part)
    return call(
        body,
        "weigh",
        4 * (tokens + block) * width * groups * part,
        (turned, cotangent_turned, dq, attended, *dks, *dvs),
        (groups,),
        [whole(turned.shape), whole(cotangent_turned.shape)] + [column] * (2 + 2 * span),
        [pl.BlockSpec((1, half, 4 * part), lambda z: (z, 0, 0))] * 2,
        [out(shape), out(shape)],
        after=after,
    )


def deliver(array, kind, after=()):
    rows, width = array.shape

    def body(x_ref, y_ref):
        y_ref[...] = x_ref[...].astype(kind)

    spec = pl.BlockSpec((2 * TILE, width), lambda i: (i, 0))
    return call(
        body, "deliver", rows * width, (array,), (rows // (2 * TILE),), [spec], [spec], [out(array.shape, kind)], after=after
    )[0]


def finish(x_full, hidden_grad, gain, parts, after=()):
    block, width = hidden_grad.shape

    def body(x_ref, dh_ref, g_ref, *refs):
        grad = refs[0][...].astype(F32)
        for ref in refs[1:-1]:
            grad += ref[...].astype(F32)
        values = x_ref[...].astype(F32)
        rate = norm_rate(values)
        scaled = grad * g_ref[...]
        dot = jnp.mean(values * scaled, axis=-1, keepdims=True)
        refs[-1][...] = (dh_ref[...] + rate * scaled - values * (rate * rate * rate * dot)).astype(BF16)

    wide = pl.BlockSpec((TILE, width), lambda i: (i, 0))
    return call(
        body,
        "finish",
        16 * block * width,
        (x_full, hidden_grad, gain, *parts),
        (block // TILE,),
        [wide, wide, whole((1, width))] + [wide] * len(parts),
        [wide],
        [out((block, width))],
        after=after,
    )[0]


def on_device(
    residual_in,
    grad_out,
    segment_lengths,
    attention_in,
    attention_out,
    expand,
    contract,
    gains,
    mean_attention_in,
    mean_attention_out,
    mean_expand,
    mean_contract,
    mean_gains,
    square_attention_in,
    square_attention_out,
    square_expand,
    square_contract,
    square_gains,
):
    span, copies = lax.axis_size("seq"), lax.axis_size("tensor")
    place, lane = lax.axis_index("seq"), lax.axis_index("tensor")
    rows, block, width = residual_in.shape
    tokens = span * block
    fold = copies // rows
    row = lane // fold
    piece = attention_in.shape[1]
    part = attention_in.shape[2]
    masks = owner_masks()
    core = lax.axis_index("core")
    index = (lax.axis_index("dp") * 2 + core) * span + place
    own = jnp.stack([index, core]).astype(jnp.int32)
    near = copies // 2

    attention_piece = jnp.concatenate(
        [attention_in[0], attention_in[1], attention_in[2], attention_out.T], axis=1
    ).astype(BF16)
    feed_piece = jnp.stack([expand[0], expand[1], contract.T]).astype(BF16)
    x_own = lax.dynamic_index_in_dim(residual_in, row, 0, keepdims=False)
    cotangent = lax.dynamic_index_in_dim(grad_out, row, 0, keepdims=False)
    x_parts = [x_own] + [exchange(x_own, ("seq", k)) for k in range(1, span)]
    near_weights = gather_owners(attention_piece)
    full_gains = gather_small(gains.astype(BF16).astype(F32))
    near_weights, feed_piece, x_parts, full_gains = lax.optimization_barrier(
        (near_weights, feed_piece, x_parts, full_gains)
    )
    weights = (near_weights, exchange(near_weights, ("core", 1)))
    gain_one, gain_two = full_gains[:1], full_gains[1:]
    cut = feed_piece.shape[2] // 2
    feeds = [gather_owners(feed_piece[:, :, at * cut : (at + 1) * cut]) for at in range(2)]

    x_full = jnp.concatenate(x_parts, axis=0)
    lens = lax.dynamic_index_in_dim(segment_lengths, row, 0, keepdims=False)
    ends = jnp.cumsum(lens)
    starts = ends - lens
    blocks = place ^ jnp.arange(span, dtype=jnp.int32)
    places = (blocks[:, None] * block + jnp.arange(block, dtype=jnp.int32)[None, :]).reshape(tokens)
    segment = jnp.sum((places[:, None] >= ends[None, :]).astype(jnp.int32), axis=-1)
    picked = segment[:, None] == jnp.arange(lens.shape[0], dtype=jnp.int32)[None, :]
    begin = jnp.sum(jnp.where(picked, starts[None, :], 0), axis=-1)
    finish_at = jnp.sum(jnp.where(picked, ends[None, :], 0), axis=-1)
    freq = jnp.exp(jnp.arange(HD // 2, dtype=F32) * (-2.0 * jnp.log(10000.0) / HD))
    angle = (places - begin).astype(F32)[:, None] * freq
    cosine = jnp.tile(jnp.cos(angle), (1, PAIR // (HD // 2)))
    sine = jnp.tile(jnp.sin(angle), (1, PAIR // (HD // 2)))
    count = block // TILE
    firsts = begin[:block].reshape(count, TILE)[:, 0] // TILE
    lasts = (finish_at[:block].reshape(count, TILE)[:, -1] + TILE - 1) // TILE
    reach = jnp.concatenate(
        [jnp.stack([firsts, lasts], axis=1).reshape(-1), (place * (block // TILE))[None]]
    ).astype(jnp.int32)
    tiles = block // TILE

    def within(k):
        start = (place ^ k) * tiles
        ends = jnp.stack([jnp.clip(firsts - start, 0, tiles), jnp.clip(lasts - start, 0, tiles)], axis=1)
        return ends.reshape(-1).astype(jnp.int32)

    lanes = jnp.arange(PAIR, dtype=jnp.int32)[None, :]
    key_marks = jnp.where(segment[:, None] == lanes, NEG, 0.0).astype(BF16)
    query_marks = ((segment[:block, None] != lanes) & (lanes < lens.shape[0])).astype(BF16)

    turned_one, query, keys, values = project(own, masks, x_full, gain_one, cosine, sine, weights, block)
    halves = None
    for side in range(2):
        halves = attend(side, reach, query, keys, values, query_marks, key_marks, halves)
        near_feed, *halves = lax.optimization_barrier((feeds[side], *halves))
        feeds[side] = (near_feed, exchange(near_feed, ("core", 1)))
    attended, lse = halves
    hidden, normed_two, turned_two, rounded, rounded_turned = lift(
        own, masks, attended, x_full, cotangent, gain_two, weights
    )

    def spread(array):
        return array.reshape(*array.shape[:-2], -1, span, piece, array.shape[-1])

    orders = (scatter_rest(False), scatter_rest(True))
    branch_a, grad_a, kept_a, sent_a = feed(own, normed_two, turned_two, rounded, rounded_turned, feeds[0])
    flight_a = scatter_start(kept_a, sent_a)
    branch_b, grad_b, kept_b, sent_b = feed(own, normed_two, turned_two, rounded, rounded_turned, feeds[1], after=[branch_a])
    flight_b = scatter_start(kept_b, sent_b)
    held_a = spread(add(*flight_a))
    flight_a = halve(held_a, orders[0][0])
    result, hidden_grad, hidden_grad_turned, output_grad, grad_gain_two = back(
        own, masks, hidden, (branch_a, branch_b), (grad_a, grad_b), cotangent, gain_two, weights, after=[held_a]
    )
    residual_out = lax.all_gather(result, "tensor", axis=0)
    flight_b, output_grad = lax.optimization_barrier((flight_b, output_grad))
    held_b = spread(add(*flight_b))
    flight_b = halve(held_b, orders[1][0])
    common = (query, output_grad, attended, keys, values, lse, query_marks, key_marks, cosine, sine)
    grad = None
    dks, dvs, parts, gain_parts = {}, {}, [], []
    for k in range(1, span):
        grad, dks[k], dvs[k] = unattend(k, within(k), *common, grad, after=[held_b])
        part_grad, gain_part = unproject(own, [dks[k], dvs[k]], x_full, k, weights)
        parts.append(exchange(part_grad, ("seq", k)))
        gain_parts.append(gain_part)
    flight_a, flight_b, grad = lax.optimization_barrier((flight_a, flight_b, grad))
    for step in orders[0][1:]:
        held_a = add(*flight_a)
        flight_a = halve(held_a, step)
    for step in orders[1][1:]:
        held_b = add(*flight_b)
        flight_b = halve(held_b, step)
    dq, dks[0], dvs[0] = unattend(0, within(0), *common, grad, after=[held_a, held_b, gain_parts[-1]])
    flight_a, flight_b, dq = lax.optimization_barrier((flight_a, flight_b, dq))
    shard_a, shard_b = add(*flight_a), add(*flight_b)
    feed_sums = jnp.concatenate([shard_a, shard_b], axis=-1).reshape(copies, -1, piece, feed_piece.shape[2])
    distances = list(range(1, copies))
    third = -(-len(distances) // 3)
    received = [tensor_sends(feed_sums, distances[:third])]

    dks, dvs = [dks[k] for k in range(span)], [dvs[k] for k in range(span)]
    flights = []
    for side in range(2):
        after = [feed_sums, *parts] if side == 0 else received[0]
        kept, sent = weigh(
            turned_one, hidden_grad_turned, dq, dks, dvs, attended, side * near, near, part, after=after
        )
        flights.append(scatter_start(kept, sent))
        kept, feed_sums = lax.optimization_barrier((kept, feed_sums))
        flights[side] = (kept, flights[side][1])
        received.append(tensor_sends(feed_sums, distances[third * (side + 1) : third * (side + 2)]))
    own_grad, gain_part = unproject(own, [dq, dks[0], dvs[0]], x_full, 0, weights, after=[flights[1][0], *received[1]])
    gain_parts.append(gain_part)
    helds = [spread(add(*flight)) for flight in flights]
    flights = [halve(held, order[0]) for held, order in zip(helds, orders)]
    back_in = finish(x_full, hidden_grad, gain_one, [own_grad] + parts, after=[*helds, *received[2]])
    grad_in = lax.all_gather(back_in, "tensor", axis=0)
    for at in range(1, len(orders[0])):
        flights = [halve(add(*flight), order[at]) for flight, order in zip(flights, orders)]
    feed_shard = tensor_sum(feed_sums, received[0] + received[1] + received[2])
    attention_sums = jnp.concatenate([add(*flight) for flight in flights]).reshape(copies, piece, 4 * part)
    attention_shard = tensor_sum(attention_sums, tensor_sends(attention_sums, distances))
    if fold > 1:
        residual_out, grad_in = residual_out[::fold], grad_in[::fold]
    residual_out = deliver(residual_out.reshape(-1, width), BF16, after=[back_in])
    grad_in = deliver(grad_in.reshape(-1, width), F32, after=[residual_out])
    residual_out, grad_in = residual_out.reshape(rows, block, width), grad_in.reshape(rows, block, width)

    share = 1.0 / fold
    attention_shard, feed_shard = attention_shard * share, feed_shard * share
    gain_grads = jnp.concatenate([sum(gain_parts), grad_gain_two]) * share
    gain_grads = sum_everywhere(gain_grads)
    gain_shard = lax.dynamic_slice_in_dim(gain_grads, index * piece, piece, 1)

    local = jnp.sum(attention_shard * attention_shard) + jnp.sum(feed_shard * feed_shard)
    norm = jnp.sqrt(sum_everywhere(jnp.full((8, 128), local))[0, 0] + jnp.sum(gain_grads * gain_grads))
    factor = jnp.minimum(1.0, CLIP / norm)
    shards = (
        jnp.stack([attention_shard[:, k * part : (k + 1) * part] for k in range(3)]),
        attention_shard[:, 3 * part :].T,
        feed_shard[:2],
        feed_shard[2].T,
        gain_shard,
    )
    masters = (attention_in, attention_out, expand, contract, gains)
    firsts = (mean_attention_in, mean_attention_out, mean_expand, mean_contract, mean_gains)
    seconds = (
        square_attention_in,
        square_attention_out,
        square_expand,
        square_contract,
        square_gains,
    )
    new_means = []
    new_squares = []
    new_weights = []
    for member in range(5):
        clipped = shards[member] * factor
        moment = BETA_ONE * firsts[member] + (1.0 - BETA_ONE) * clipped
        square = BETA_TWO * seconds[member] + (1.0 - BETA_TWO) * clipped * clipped
        update = (
            moment / (1.0 - BETA_ONE**STEP) / (jnp.sqrt(square / (1.0 - BETA_TWO**STEP)) + ADAM_EPS)
        )
        shrink = DECAY if member < 4 else 0.0
        speed = RATE if member < 4 else GAIN_RATE
        new_means.append(moment)
        new_squares.append(square)
        new_weights.append(masters[member] - speed * (update + shrink * masters[member]))
    return (residual_out, grad_in, norm, *new_means, *new_squares, *new_weights)


def solution(mesh):
    devices = mesh.devices
    dp, *others = devices.shape
    split = Mesh(devices.reshape(dp // 2, 2, *others), ("dp", "core", "seq", "tensor"))
    rows = ("dp", "core")
    shards = ("dp", "core", "seq")
    tokens = P(rows, "seq", None)
    weights = (P(None, shards, "tensor"), P("tensor", shards), P(None, shards, "tensor"), P("tensor", shards), P(None, shards))
    return jax.shard_map(
        on_device,
        mesh=split,
        in_specs=(tokens, tokens, P(rows, None)) + weights * 3,
        out_specs=(tokens, tokens, P()) + weights * 3,
        check_vma=False,
    )
```

```python
import jax
import jax.numpy as jnp
from jax import lax
from jax.experimental import pallas as pl
from jax.experimental.pallas import tpu as pltpu
from jax.sharding import PartitionSpec as P

HD = 64
STEP = 10

NORM_EPS = 1e-05
NEG = -1e30
CLIP = 1.0
RATE = 0.04
GAIN_RATE = 1.0
BETA_ONE = 0.9
BETA_TWO = 0.999
ADAM_EPS = 1e-08
DECAY = 0.1

SCALE = HD ** (-0.5)
PAIR = 2 * HD
TILE = 256
VMEM = 60 * 1024 * 1024
F32 = jnp.float32
BF16 = jnp.bfloat16

NN = (((1,), (0,)), ((), ()))
NT = (((1,), (1,)), ((), ()))
TN = (((0,), (0,)), ((), ()))


def mm(left, right, dims=NN):
    return lax.dot_general(left, right, dims, preferred_element_type=F32)


def call(body, name, flops, args, grid, in_specs, out_specs, out_shape, scratch=(), prefetch=0, after=()):
    count, extra = len(args), len(after)
    moved = sum(a.size * a.dtype.itemsize for a in args) + sum(o.size * o.dtype.itemsize for o in out_shape)
    return pl.pallas_call(
        lambda *refs: body(*refs[:count], *refs[count + extra :]),
        name=name,
        grid_spec=pltpu.PrefetchScalarGridSpec(
            num_scalar_prefetch=prefetch,
            grid=grid,
            in_specs=list(in_specs) + [pl.BlockSpec(memory_space=pl.ANY)] * extra,
            out_specs=out_specs,
            scratch_shapes=list(scratch),
        ),
        out_shape=out_shape,
        compiler_params=pltpu.CompilerParams(vmem_limit_bytes=VMEM),
        cost_estimate=pl.CostEstimate(flops=int(flops) // 64, bytes_accessed=int(moved) // 64, transcendentals=0),
    )(*args, *after)


def whole(shape):
    return pl.BlockSpec(shape, lambda *at: (0,) * len(shape), pipeline_mode=pl.Buffered(1))


def scalar():
    return pl.BlockSpec(memory_space=pltpu.SMEM)


def out(shape, kind=BF16):
    return jax.ShapeDtypeStruct(shape, kind)


def exchange(block, step):
    axis, bit = step
    return lax.ppermute(block, axis, [(i ^ bit, i) for i in range(lax.axis_size(axis))])


def axis_steps():
    bits = lambda axis: [(axis, 1 << k) for k in range(lax.axis_size(axis).bit_length() - 1)]
    across = bits("dp")
    return bits("seq"), across[1:], across[0]


def owner_masks():
    span = lax.axis_size("seq")
    along, across, last = axis_steps()
    masks = [0]
    for axis, bit in along + across + [last]:
        masks += [m ^ (bit if axis == "seq" else bit * span) for m in masks]
    return masks


def gather_owners(array, axes):
    whole_array = lax.all_gather(array, axes, axis=0)
    return whole_array.reshape(lax.axis_size(axes[0]), -1, *array.shape)


def gather_small(array):
    along, across, last = axis_steps()
    for step in along + [last] + across:
        other = exchange(array, step)
        pair, swapped = jnp.concatenate([array, other], axis=1), jnp.concatenate([other, array], axis=1)
        array = jnp.where(lax.axis_index(step[0]) & step[1], swapped, pair)
    return array


def sum_everywhere(array):
    for axis in ("dp", "seq", "tensor"):
        for k in range(lax.axis_size(axis).bit_length() - 1):
            array = array + exchange(array, (axis, 1 << k))
    return array


def scatter_order(along_first):
    along, across, _ = axis_steps()
    ordered = [list(reversed(along)), list(reversed(across))]
    return ordered[0] + ordered[1] if along_first else ordered[1] + ordered[0]


def tensor_sends(held, distances):
    size, here = lax.axis_size("tensor"), lax.axis_index("tensor")
    return [
        lax.ppermute(
            lax.dynamic_index_in_dim(held, lax.rem(here + k, size), 0, keepdims=False),
            "tensor",
            [(i, (i + k) % size) for i in range(size)],
        )
        for k in distances
    ]


def tensor_sum(held, received):
    own = lax.dynamic_index_in_dim(held, lax.axis_index("tensor"), 0, keepdims=False).astype(F32)
    return sum([array.astype(F32) for array in received], own)


def row_block(own, mask, piece):
    return pl.ds(pl.multiple_of((own ^ mask) * piece, piece), piece)


def store_turned(own, masks, ref, values, scratch):
    scratch[...] = values.T.astype(BF16)
    piece = scratch.shape[0] // len(masks)
    for j, mask in enumerate(masks):
        ref[j * piece : (j + 1) * piece, :] = scratch[row_block(own, mask, piece), :]


def swap_halves(values):
    lane = lax.broadcasted_iota(jnp.int32, values.shape, 1)
    size = values.shape[1]
    ahead = pltpu.roll(values, size - HD // 2, 1)
    behind = pltpu.roll(values, HD // 2, 1)
    return jnp.where(lane % HD < HD // 2, ahead, behind)


def half_sign(shape):
    lane = lax.broadcasted_iota(jnp.int32, shape, 1)
    return jnp.where(lane % HD < HD // 2, -1.0, 1.0)


def turn(values, cosine, sine):
    return values * cosine + swap_halves(values) * (sine * half_sign(values.shape))


def unturn(values, cosine, sine):
    return values * cosine - swap_halves(values * sine) * half_sign(values.shape)


def pair_lanes(values, head):
    lane = lax.broadcasted_iota(jnp.int32, values.shape, 1)
    return jnp.where((lane < HD) == (head == 0), values, 0.0)


def stack_pair(values):
    return jnp.concatenate([pair_lanes(values, 0), pair_lanes(values, 1)], axis=0).astype(BF16)


def norm_rate(values):
    return lax.rsqrt(jnp.mean(values * values, axis=-1, keepdims=True) + NORM_EPS)


def inward_spec(weights):
    groups, owners, piece, cols = weights.shape
    return pl.BlockSpec((groups, owners, piece, cols // 4 * 3), lambda *at: (0, 0, 0, 0), pipeline_mode=pl.Buffered(1))


def outward_spec(weights):
    groups, owners, piece, cols = weights.shape
    return pl.BlockSpec((groups, owners, piece, cols // 4), lambda *at: (0, 0, 0, 3), pipeline_mode=pl.Buffered(1))


def outward(w_ref, w_all):
    groups, owners, piece, part = w_ref.shape
    for z in range(groups):
        w_all[:, z * part : (z + 1) * part] = w_ref[z].reshape(owners * piece, part)


def project(own, masks, x_full, gain, cosine, sine, weights, block):
    tokens, width = x_full.shape
    groups, owners, piece, cols = weights.shape
    part = cols // 4
    heads = groups * part
    mine = block // TILE

    def body(own_ref, x_ref, g_ref, cos_ref, sin_ref, w_ref, at_ref, q_ref, k_ref, v_ref, a_one, turned):
        own = own_ref[0]

        values = x_ref[...].astype(F32)
        normed = values * norm_rate(values) * g_ref[...]
        a_one[...] = normed.astype(BF16)
        store_turned(own, masks, at_ref, normed, turned)
        cosine, sine = cos_ref[...], sin_ref[...]

        def product(z, m):
            return mm(a_one[...], w_ref[z, :, :, m * part : (m + 1) * part].reshape(width, part))

        def rotated(ref, m):
            for z in range(groups):
                mixed = product(z, m)
                for lane in range(0, part, PAIR):
                    ref[:, z * part + lane : z * part + lane + PAIR] = turn(
                        mixed[:, lane : lane + PAIR], cosine, sine
                    ).astype(BF16)

        rotated(k_ref, 1)
        for z in range(groups):
            v_ref[:, z * part : (z + 1) * part] = product(z, 2).astype(BF16)

        @pl.when(pl.program_id(0) < mine)
        def _():
            rotated(q_ref, 0)

    rows = lambda i: (i, 0)
    return call(
        body,
        "project",
        2 * (2 * tokens + block) * width * heads,
        (own, x_full, gain, cosine, sine, weights),
        (tokens // TILE,),
        [
            scalar(),
            pl.BlockSpec((TILE, width), rows),
            whole((1, width)),
            pl.BlockSpec((TILE, PAIR), rows),
            pl.BlockSpec((TILE, PAIR), rows),
            inward_spec(weights),
        ],
        [
            pl.BlockSpec((width, TILE), lambda i: (0, i)),
            pl.BlockSpec((TILE, heads), lambda i: (jnp.minimum(i, mine - 1), 0)),
            pl.BlockSpec((TILE, heads), rows),
            pl.BlockSpec((TILE, heads), rows),
        ],
        [out((width, tokens)), out((block, heads)), out((tokens, heads)), out((tokens, heads))],
        [pltpu.VMEM((TILE, width), BF16), pltpu.VMEM((width, TILE), BF16)],
    )


def attend(reach, query, keys, values, query_marks, key_marks):
    block, heads = query.shape
    tokens = keys.shape[0]
    wide = 2 * PAIR
    count = block // TILE

    def body(reach, q_ref, k_ref, v_ref, qm_ref, km_ref, o_ref, lse_ref, turned, acc, top, total):
        at = pl.program_id(1)
        first, last, shift = reach[2 * at], reach[2 * at + 1], reach[2 * count]

        @pl.when(at == 0)
        def _():
            for tile in range(tokens // TILE):
                rows = slice(tile * TILE, (tile + 1) * TILE)
                turned[:, rows] = v_ref[rows, :].astype(F32).T.astype(BF16)

        marks = jnp.concatenate([qm_ref[...], qm_ref[...]], axis=0)
        stacked = [
            jnp.concatenate([stack_pair(q_ref[:, p * PAIR : (p + 1) * PAIR].astype(F32) * SCALE), marks], axis=1)
            for p in range(2)
        ]
        acc[...] = jnp.zeros_like(acc)
        top[...] = jnp.full_like(top, NEG)
        total[...] = jnp.zeros_like(total)

        def step(tile, carry):
            rows = pl.ds(pl.multiple_of((tile ^ shift) * TILE, TILE), TILE)
            for p in range(2):
                lanes = slice(p * PAIR, (p + 1) * PAIR)
                scores = mm(jnp.concatenate([k_ref[rows, lanes], km_ref[rows, :]], axis=1), stacked[p], NT)
                before = top[p : p + 1]
                now = jnp.maximum(before, jnp.max(scores, axis=0, keepdims=True))
                probs = jnp.exp(scores - now)
                factor = jnp.exp(before - now)
                total[p : p + 1] = total[p : p + 1] * factor + jnp.sum(probs, axis=0, keepdims=True)
                top[p : p + 1] = now
                probs = probs.astype(BF16)
                for h in range(2):
                    part = slice(p * PAIR + h * HD, p * PAIR + (h + 1) * HD)
                    cols = slice(h * TILE, (h + 1) * TILE)
                    acc[part, :] = acc[part, :] * factor[:, cols] + mm(turned[part, rows], probs[:, cols])
            return carry

        lax.fori_loop(first, last, step, 0)
        for p in range(2):
            rate = 1.0 / total[p : p + 1]
            for h in range(2):
                part = slice(p * PAIR + h * HD, p * PAIR + (h + 1) * HD)
                acc[part, :] = acc[part, :] * rate[:, h * TILE : (h + 1) * TILE]
        o_ref[...] = acc[...].T.astype(BF16)
        lse_ref[0, 0] = top[...] + jnp.log(total[...])

    return call(
        body,
        "attend",
        4 * block * tokens * heads,
        (reach, query, keys, values, query_marks, key_marks),
        (heads // wide, count),
        [
            pl.BlockSpec((TILE, wide), lambda h, i, r: (i, h)),
            pl.BlockSpec((tokens, wide), lambda h, i, r: (0, h)),
            pl.BlockSpec((tokens, wide), lambda h, i, r: (0, h)),
            pl.BlockSpec((TILE, PAIR), lambda h, i, r: (i, 0)),
            pl.BlockSpec((tokens, PAIR), lambda h, i, r: (0, 0)),
        ],
        [
            pl.BlockSpec((TILE, wide), lambda h, i, r: (i, h)),
            pl.BlockSpec((1, 1, 2, 2 * TILE), lambda h, i, r: (h, i, 0, 0)),
        ],
        [out((block, heads)), out((heads // wide, count, 2, 2 * TILE), F32)],
        [
            pltpu.VMEM((wide, tokens), BF16),
            pltpu.VMEM((wide, TILE), F32),
            pltpu.VMEM((2, 2 * TILE), F32),
            pltpu.VMEM((2, 2 * TILE), F32),
        ],
        prefetch=1,
    )


def lift(own, masks, attended, x_full, cotangent, gain, weights):
    block, heads = attended.shape
    width = x_full.shape[1]

    def body(own_ref, o_ref, x_ref, c_ref, g_ref, w_ref, h_ref, a_ref, at_ref, e_ref, et_ref, w_all, turned):
        own = own_ref[0]

        @pl.when(pl.program_id(0) == 0)
        def _():
            outward(w_ref, w_all)

        values = x_ref[...].astype(F32) + mm(o_ref[...], w_all[...], NT)
        h_ref[...] = values
        normed = values * norm_rate(values) * g_ref[...]
        a_ref[...] = normed.astype(BF16)
        store_turned(own, masks, at_ref, normed, turned)
        cotangent = c_ref[...]
        e_ref[...] = cotangent.astype(BF16)
        store_turned(own, masks, et_ref, cotangent, turned)

    rows = lambda i: (i, 0)
    wide = pl.BlockSpec((TILE, width), rows)
    tall = pl.BlockSpec((width, TILE), lambda i: (0, i))
    return call(
        body,
        "lift",
        2 * block * width * heads,
        (own, attended, x_full, cotangent, gain, weights),
        (block // TILE,),
        [scalar(), pl.BlockSpec((TILE, heads), rows), wide, wide, whole((1, width)), outward_spec(weights)],
        [wide, wide, tall, wide, tall],
        [out((block, width), F32), out((block, width)), out((width, block)), out((block, width)), out((width, block))],
        [pltpu.VMEM((width, heads), BF16), pltpu.VMEM((width, TILE), BF16)],
    )


def feed(normed, turned, cotangent, cotangent_turned, weights, after=()):
    block, width = normed.shape
    groups, owners, kinds, piece, hidden = weights.shape
    half = width // 2
    cut = min(512, hidden)
    tile = min(512, block)

    def body(a_ref, at_ref, e_ref, et_ref, w_ref, b_ref, d_ref, ga_ref, gb_ref, mid, dgate, dup):
        @pl.when((pl.program_id(0) == 0) & (pl.program_id(1) == 0))
        def _():
            b_ref[...] = jnp.zeros_like(b_ref)
            d_ref[...] = jnp.zeros_like(d_ref)

        def weight(m):
            return w_ref[0, :, m].reshape(width, cut)

        def tokens(i, carry):
            rows = pl.ds(pl.multiple_of(i * tile, tile), tile)
            gate = mm(a_ref[rows, :], weight(0))
            upper = mm(a_ref[rows, :], weight(1))
            grad = mm(e_ref[rows, :], weight(2))
            sigma = jax.nn.sigmoid(gate)
            active = gate * sigma
            mid[rows, :] = (active * upper).astype(BF16)
            dgate[rows, :] = (grad * upper * (sigma * (1.0 + gate * (1.0 - sigma)))).astype(BF16)
            dup[rows, :] = (grad * active).astype(BF16)
            b_ref[rows, :] += mm(mid[rows, :], weight(2), NT)
            d_ref[rows, :] += mm(dgate[rows, :], weight(0), NT) + mm(dup[rows, :], weight(1), NT)
            return carry

        lax.fori_loop(0, block // tile, tokens, 0)
        for ref, rows in ((ga_ref, slice(0, half)), (gb_ref, slice(half, width))):
            ref[0, 0] = mm(at_ref[rows, :], dgate[...]).astype(BF16)
            ref[0, 1] = mm(at_ref[rows, :], dup[...]).astype(BF16)
            ref[0, 2] = mm(et_ref[rows, :], mid[...]).astype(BF16)

    place = lambda z, j: (z, 0, 0, j)
    shape = (groups, kinds, half, hidden)
    return call(
        body,
        "feed",
        18 * block * width * hidden * groups,
        (normed, turned, cotangent, cotangent_turned, weights),
        (groups, hidden // cut),
        [
            whole((block, width)),
            whole((width, block)),
            whole((block, width)),
            whole((width, block)),
            pl.BlockSpec((1, owners, kinds, piece, cut), lambda z, j: (z, 0, 0, 0, j)),
        ],
        [
            whole((block, width)),
            whole((block, width)),
            pl.BlockSpec((1, kinds, half, cut), place),
            pl.BlockSpec((1, kinds, half, cut), place),
        ],
        [out((block, width), F32), out((block, width), F32), out(shape), out(shape)],
        [pltpu.VMEM((block, cut), BF16)] * 3,
        after=after,
    )


def back(own, masks, hidden, branches, grads, cotangent, gain, weights, after=()):
    block, width = hidden.shape
    groups, owners, piece, cols = weights.shape
    heads = groups * cols // 4

    def body(
        own_ref, h_ref, b0_ref, b1_ref, d0_ref, d1_ref, c_ref, g_ref, w_ref,
        y_ref, dh_ref, ct_ref, do_ref, gg_ref, w_all, turned,
    ):
        own = own_ref[0]

        @pl.when(pl.program_id(0) == 0)
        def _():
            outward(w_ref, w_all)
            gg_ref[...] = jnp.zeros_like(gg_ref)

        hidden = h_ref[...]
        grad = d0_ref[...] + d1_ref[...]
        y_ref[...] = (hidden + (b0_ref[...] + b1_ref[...])).astype(BF16)
        rate = norm_rate(hidden)
        scaled = grad * g_ref[...]
        dot = jnp.mean(hidden * scaled, axis=-1, keepdims=True)
        result = c_ref[...] + rate * scaled - hidden * (rate * rate * rate * dot)
        dh_ref[...] = result
        store_turned(own, masks, ct_ref, result, turned)
        do_ref[...] = mm(result.astype(BF16), w_all[...]).astype(BF16)
        gg_ref[...] += jnp.sum(grad * hidden * rate, axis=0, keepdims=True)

    rows = lambda i: (i, 0)
    wide = pl.BlockSpec((TILE, width), rows)
    return call(
        body,
        "back",
        2 * block * width * heads,
        (own, hidden, *branches, *grads, cotangent, gain, weights),
        (block // TILE,),
        [scalar()] + [wide] * 6 + [whole((1, width)), outward_spec(weights)],
        [
            wide,
            wide,
            pl.BlockSpec((width, TILE), lambda i: (0, i)),
            pl.BlockSpec((TILE, heads), rows),
            pl.BlockSpec((1, width), lambda i: (0, 0)),
        ],
        [
            out((block, width)),
            out((block, width), F32),
            out((width, block)),
            out((block, heads)),
            out((1, width), F32),
        ],
        [pltpu.VMEM((width, heads), BF16), pltpu.VMEM((width, TILE), BF16)],
        after=after,
    )


def unattend(side, reach, query, grads, attended, keys, values, lse, query_marks, key_marks, cosine, sine, after=()):
    block, heads = query.shape
    tokens = keys.shape[0]
    wide = 2 * PAIR
    count = block // TILE
    sets = heads // wide // 2

    def body(
        reach, q_ref, g_ref, o_ref, k_ref, v_ref, lse_ref, qm_ref, km_ref, cq_ref, sq_ref, ck_ref, sk_ref,
        dq_ref, dk_ref, dv_ref, keys_turned, dq_acc, dk_acc, dv_acc,
    ):
        at = pl.program_id(1)
        first, last, shift = reach[2 * at], reach[2 * at + 1], reach[2 * count]
        marks = jnp.concatenate([qm_ref[...], qm_ref[...]], axis=0)
        queries = q_ref[...].astype(F32) * SCALE
        grads = g_ref[...].astype(F32)
        product = (grads * o_ref[...].astype(F32)).T
        stacked, marked, stacked_grads, deltas = [], [], [], []
        for p in range(2):
            lanes = slice(p * PAIR, (p + 1) * PAIR)
            stacked.append(stack_pair(queries[:, lanes]))
            marked.append(jnp.concatenate([stacked[p], marks], axis=1))
            stacked_grads.append(stack_pair(grads[:, lanes]))
            sums = [
                jnp.sum(product[p * PAIR + h * HD : p * PAIR + (h + 1) * HD], axis=0, keepdims=True) for h in range(2)
            ]
            deltas.append(jnp.concatenate(sums, axis=1))
        dq_acc[...] = jnp.zeros_like(dq_acc)

        @pl.when(at == 0)
        def _():
            dk_acc[...] = jnp.zeros_like(dk_acc)
            dv_acc[...] = jnp.zeros_like(dv_acc)
            for tile in range(tokens // TILE):
                rows = slice(tile * TILE, (tile + 1) * TILE)
                keys_turned[:, rows] = k_ref[rows, :].astype(F32).T.astype(BF16)

        def step(tile, carry):
            rows = pl.ds(pl.multiple_of((tile ^ shift) * TILE, TILE), TILE)
            for p in range(2):
                lanes = slice(p * PAIR, (p + 1) * PAIR)
                scores = mm(jnp.concatenate([k_ref[rows, lanes], km_ref[rows, :]], axis=1), marked[p], NT)
                probs = jnp.exp(scores - lse_ref[0, 0, p : p + 1, :])
                prob_grads = mm(v_ref[rows, lanes], stacked_grads[p], NT)
                score_grads = (probs * (prob_grads - deltas[p])).astype(BF16)
                dv_acc[rows, lanes] += mm(probs.astype(BF16), stacked_grads[p])
                dk_acc[rows, lanes] += mm(score_grads, stacked[p])
                for h in range(2):
                    part = slice(p * PAIR + h * HD, p * PAIR + (h + 1) * HD)
                    dq_acc[part, :] += mm(keys_turned[part, rows], score_grads[:, h * TILE : (h + 1) * TILE])
            return carry

        lax.fori_loop(first, last, step, 0)
        grad = dq_acc[...].T * SCALE
        for lane in (0, PAIR):
            dq_ref[:, lane : lane + PAIR] = unturn(grad[:, lane : lane + PAIR], cq_ref[...], sq_ref[...]).astype(BF16)

        @pl.when(at == count - 1)
        def _():
            dv_ref[...] = dv_acc[...].astype(BF16)
            for lane in (0, PAIR):
                dk_ref[:, lane : lane + PAIR] = unturn(
                    dk_acc[:, lane : lane + PAIR], ck_ref[...], sk_ref[...]
                ).astype(BF16)

    base = side * sets
    tile = pl.BlockSpec((TILE, wide), lambda h, i, r: (i, base + h))
    full = pl.BlockSpec((tokens, wide), lambda h, i, r: (0, base + h))
    table = pl.BlockSpec((TILE, PAIR), lambda h, i, r: (i, 0))
    tables = pl.BlockSpec((tokens, PAIR), lambda h, i, r: (0, 0))
    return call(
        body,
        "unattend",
        5 * block * tokens * heads,
        (reach, query, grads, attended, keys, values, lse, query_marks, key_marks, cosine, sine, cosine, sine),
        (sets, count),
        [
            tile,
            tile,
            tile,
            full,
            full,
            pl.BlockSpec((1, 1, 2, 2 * TILE), lambda h, i, r: (base + h, i, 0, 0)),
            table,
            tables,
            table,
            table,
            tables,
            tables,
        ],
        [
            pl.BlockSpec((TILE, wide), lambda h, i, r: (i, h)),
            pl.BlockSpec((tokens, wide), lambda h, i, r: (0, h)),
            pl.BlockSpec((tokens, wide), lambda h, i, r: (0, h)),
        ],
        [out((block, heads // 2)), out((tokens, heads // 2)), out((tokens, heads // 2))],
        [
            pltpu.VMEM((wide, tokens), BF16),
            pltpu.VMEM((wide, TILE), F32),
            pltpu.VMEM((tokens, wide), F32),
            pltpu.VMEM((tokens, wide), F32),
        ],
        prefetch=1,
        after=after,
    )


def unproject(grads, x_full, first, block, weights, after=()):
    width = x_full.shape[1]
    groups, owners, piece, cols = weights.shape
    part = cols // 4
    kinds = len(grads)
    side = grads[0][0].shape[1]
    base = first // TILE

    def body(x_ref, *refs):
        g_refs, refs = refs[: 2 * kinds], refs[2 * kinds :]
        w_ref, da_ref, gg_ref, w_all = refs

        @pl.when(pl.program_id(0) == 0)
        def _():
            gg_ref[...] = jnp.zeros_like(gg_ref)
            for m in range(kinds):
                column = (3 - kinds + m) * part
                for z in range(groups):
                    w_all[m, :, z * part : (z + 1) * part] = w_ref[z, :, :, column : column + part].reshape(width, part)

        grad = mm(g_refs[0][...], w_all[0, :, :side], NT)
        for at in range(1, 2 * kinds):
            lanes = slice((at % 2) * side, (at % 2 + 1) * side)
            grad += mm(g_refs[at][...], w_all[at // 2, :, lanes], NT)
        da_ref[...] = grad.astype(BF16)
        values = x_ref[...].astype(F32)
        gg_ref[...] += jnp.sum(grad * values * norm_rate(values), axis=0, keepdims=True)

    def place(array):
        return (lambda i: (i, 0)) if array.shape[0] == block else (lambda i: (base + i, 0))

    flat = [array for pair in grads for array in pair]
    return call(
        body,
        "unproject",
        4 * kinds * block * width * side,
        (x_full, *flat, weights),
        (block // TILE,),
        [pl.BlockSpec((TILE, width), lambda i: (base + i, 0))]
        + [pl.BlockSpec((TILE, side), place(array)) for array in flat]
        + [inward_spec(weights)],
        [pl.BlockSpec((TILE, width), lambda i: (i, 0)), pl.BlockSpec((1, width), lambda i: (0, 0))],
        [out((block, width)), out((1, width), F32)],
        [pltpu.VMEM((kinds, width, 2 * side), BF16)],
        after=after,
    )


def weigh(turned, cotangent_turned, dq, dk, dv, attended, base, groups, part, after=()):
    width, tokens = turned.shape
    block = dq.shape[0]
    half = width // 2

    def body(at_ref, ct_ref, dq_ref, dk_ref, dv_ref, o_ref, ga_ref, gb_ref):
        for ref, rows in ((ga_ref, slice(0, half)), (gb_ref, slice(half, width))):
            ref[0, :, :part] = mm(at_ref[rows, :block], dq_ref[...]).astype(BF16)
            ref[0, :, part : 2 * part] = mm(at_ref[rows, :], dk_ref[...]).astype(BF16)
            ref[0, :, 2 * part : 3 * part] = mm(at_ref[rows, :], dv_ref[...]).astype(BF16)
            ref[0, :, 3 * part :] = mm(ct_ref[rows, :], o_ref[...]).astype(BF16)

    column = lambda z: (0, z)
    shape = (groups, half, 4 * part)
    return call(
        body,
        "weigh",
        4 * (tokens + block) * width * groups * part,
        (turned, cotangent_turned, dq, dk, dv, attended),
        (groups,),
        [
            whole(turned.shape),
            whole(cotangent_turned.shape),
            pl.BlockSpec((block, part), column),
            pl.BlockSpec((tokens, part), column),
            pl.BlockSpec((tokens, part), column),
            pl.BlockSpec((block, part), lambda z: (0, base + z)),
        ],
        [pl.BlockSpec((1, half, 4 * part), lambda z: (z, 0, 0))] * 2,
        [out(shape), out(shape)],
        after=after,
    )


def fold(kept, received, step, after=()):
    axis = None if step is None else 2 if step[0] == "seq" else 1
    shapes = [kept.shape]
    if axis is not None:
        half = kept.shape[axis] // 2
        shapes = [tuple(half if at == axis else n for at, n in enumerate(kept.shape))] * 2

    def body(kept_ref, received_ref, *refs):
        total = (kept_ref[...].astype(F32) + received_ref[...].astype(F32)).astype(BF16)
        if axis is None:
            refs[0][...] = total
        elif axis == 1:
            refs[0][...], refs[1][...] = total[:, :half], total[:, half:]
        else:
            refs[0][...], refs[1][...] = total[:, :, :half], total[:, :, half:]

    spec = lambda shape: pl.BlockSpec((1, *shape[1:]), lambda g: (g, 0, 0, 0, 0))
    return call(
        body,
        "fold",
        kept.size,
        (kept, received),
        (kept.shape[0],),
        [spec(kept.shape)] * 2,
        [spec(shape) for shape in shapes],
        [out(shape) for shape in shapes],
        after=after,
    )


def deliver(array, kind, after=()):
    rows, width = array.shape

    def body(x_ref, y_ref):
        y_ref[...] = x_ref[...].astype(kind)

    spec = pl.BlockSpec((2 * TILE, width), lambda i: (i, 0))
    return call(
        body, "deliver", rows * width, (array,), (rows // (2 * TILE),), [spec], [spec], [out(array.shape, kind)], after=after
    )[0]


def finish(x_full, hidden_grad, gain, parts, after=()):
    block, width = hidden_grad.shape

    def body(x_ref, dh_ref, g_ref, *refs):
        grad = sum([ref[...].astype(F32) for ref in refs[1:-1]], refs[0][...].astype(F32))
        values = x_ref[...].astype(F32)
        rate = norm_rate(values)
        scaled = grad * g_ref[...]
        dot = jnp.mean(values * scaled, axis=-1, keepdims=True)
        refs[-1][...] = (dh_ref[...] + rate * scaled - values * (rate * rate * rate * dot)).astype(BF16)

    wide = pl.BlockSpec((TILE, width), lambda i: (i, 0))
    return call(
        body,
        "finish",
        16 * block * width,
        (x_full, hidden_grad, gain, *parts),
        (block // TILE,),
        [wide, wide, whole((1, width))] + [wide] * len(parts),
        [wide],
        [out((block, width))],
        after=after,
    )[0]


def on_device(
    residual_in,
    grad_out,
    segment_lengths,
    attention_in,
    attention_out,
    expand,
    contract,
    gains,
    mean_attention_in,
    mean_attention_out,
    mean_expand,
    mean_contract,
    mean_gains,
    square_attention_in,
    square_attention_out,
    square_expand,
    square_contract,
    square_gains,
):
    span, copies = lax.axis_size("seq"), lax.axis_size("tensor")
    place, lane = lax.axis_index("seq"), lax.axis_index("tensor")
    rows, block, width = residual_in.shape
    tokens = span * block
    repeats = copies // rows
    row = lane // repeats
    piece = attention_in.shape[1]
    part = attention_in.shape[2]
    masks = owner_masks()
    index = lax.axis_index("dp") * span + place
    own = index.astype(jnp.int32)[None]
    near = copies // 2

    attention_piece = jnp.concatenate(
        [attention_in[0], attention_in[1], attention_in[2], attention_out.T], axis=1
    ).astype(BF16)
    feed_piece = jnp.stack([expand[0], expand[1], contract.T]).astype(BF16)
    x_own = lax.dynamic_index_in_dim(residual_in, row, 0, keepdims=False)
    cotangent = lax.dynamic_index_in_dim(grad_out, row, 0, keepdims=False)
    x_parts = [x_own] + [exchange(x_own, ("seq", k)) for k in range(1, span)]
    everywhere = ("tensor", "dp", "seq")
    full_gains = gather_small(gains.astype(BF16).astype(F32))
    gain_one, gain_two = full_gains[:1], full_gains[1:]
    weights = gather_owners(attention_piece, everywhere)
    cut = feed_piece.shape[2] // 2
    weights, feed_piece, x_parts, gain_one = lax.optimization_barrier((weights, feed_piece, x_parts, gain_one))
    feeds = [gather_owners(feed_piece[:, :, at * cut : (at + 1) * cut], everywhere) for at in range(2)]

    x_full = jnp.concatenate(x_parts, axis=0)
    lens = lax.dynamic_index_in_dim(segment_lengths, row, 0, keepdims=False)
    ends = jnp.cumsum(lens)
    starts = ends - lens
    blocks = place ^ jnp.arange(span, dtype=jnp.int32)
    places = (blocks[:, None] * block + jnp.arange(block, dtype=jnp.int32)[None, :]).reshape(tokens)
    segment = jnp.sum((places[:, None] >= ends[None, :]).astype(jnp.int32), axis=-1)
    picked = segment[:, None] == jnp.arange(lens.shape[0], dtype=jnp.int32)[None, :]
    begin = jnp.sum(jnp.where(picked, starts[None, :], 0), axis=-1)
    finish_at = jnp.sum(jnp.where(picked, ends[None, :], 0), axis=-1)
    freq = jnp.exp(jnp.arange(HD // 2, dtype=F32) * (-2.0 * jnp.log(10000.0) / HD))
    angle = (places - begin).astype(F32)[:, None] * freq
    cosine = jnp.tile(jnp.cos(angle), (1, PAIR // (HD // 2)))
    sine = jnp.tile(jnp.sin(angle), (1, PAIR // (HD // 2)))
    count = block // TILE
    firsts = begin[:block].reshape(count, TILE)[:, 0] // TILE
    lasts = (finish_at[:block].reshape(count, TILE)[:, -1] + TILE - 1) // TILE
    reach = jnp.concatenate(
        [jnp.stack([firsts, lasts], axis=1).reshape(-1), (place * (block // TILE))[None]]
    ).astype(jnp.int32)
    lanes = jnp.arange(PAIR, dtype=jnp.int32)[None, :]
    key_marks = jnp.where(segment[:, None] == lanes, NEG, 0.0).astype(BF16)
    query_marks = ((segment[:block, None] != lanes) & (lanes < lens.shape[0])).astype(BF16)

    turned_one, query, keys, values = project(own, masks, x_full, gain_one, cosine, sine, weights, block)
    attended, lse = attend(reach, query, keys, values, query_marks, key_marks)
    hidden, normed_two, turned_two, rounded, rounded_turned = lift(
        own, masks, attended, x_full, cotangent, gain_two, weights
    )

    def spread(array):
        half, columns = array.shape[-2:]
        return array.reshape(-1, half // (span * piece), span, piece, columns)

    last_step = axis_steps()[2]
    orders = (scatter_order(False), scatter_order(True))
    flights, branches, grads = [], [], []
    for side in range(2):
        branch, grad, kept, sent = feed(
            normed_two, turned_two, rounded, rounded_turned, feeds[side], after=branches[:side]
        )
        branches.append(branch)
        grads.append(grad)
        flights.append((spread(kept), spread(exchange(sent, last_step))))

    def move_on(at):
        for side in range(2):
            kept, sent = fold(*flights[side], orders[side][at])
            flights[side] = (kept, exchange(sent, orders[side][at]))
        return [kept for kept, _ in flights]

    result, hidden_grad, hidden_grad_turned, output_grad, grad_gain_two = back(
        own, masks, hidden, branches, grads, cotangent, gain_two, weights, after=move_on(0)
    )
    residual_out = lax.all_gather(result, "tensor", axis=0)
    common = (reach, query, output_grad, attended, keys, values, lse, query_marks, key_marks, cosine, sine)
    sides = [unattend(0, *common)]
    after = [sides[0][0]]
    for at in range(1, len(orders[0])):
        *tied, sides[0] = lax.optimization_barrier((*flights, sides[0]))
        flights = [tuple(flight) for flight in tied]
        after = move_on(at)
    sides.append(unattend(1, *common, after=after))
    *tied, sides[1] = lax.optimization_barrier((*flights, sides[1]))
    shards = [fold(*flight, None)[0] for flight in tied]
    feed_sums = jnp.concatenate([shard.reshape(copies, -1, piece, cut) for shard in shards], axis=-1)
    dqs, dks, dvs = zip(*sides)

    distances = list(range(1, copies))
    third = -(-len(distances) // 3)
    received = [tensor_sends(feed_sums, distances[at * third : (at + 1) * third]) for at in range(3)]
    parts, gain_parts = [], []
    for k in range(1, span):
        grad, gain_part = unproject([dks, dvs], x_full, k * block, block, weights, after=[feed_sums])
        parts.append(exchange(grad, ("seq", k)))
        gain_parts.append(gain_part)
    flights = []
    for side in range(2):
        kept, sent = weigh(
            turned_one, hidden_grad_turned, *sides[side], attended, side * near, near, part,
            after=received[0] + gain_parts if side == 0 else received[1],
        )
        flights.append((spread(kept), spread(exchange(sent, last_step))))
    own_grad, gain_part = unproject(
        [dqs, dks, dvs], x_full, 0, block, weights, after=[flights[1][0], *received[2], *parts]
    )
    gain_parts.append(gain_part)
    back_in = finish(x_full, hidden_grad, gain_one, [own_grad] + parts, after=move_on(0))
    grad_in = lax.all_gather(back_in, "tensor", axis=0)
    for at in range(1, len(orders[0])):
        move_on(at)
    attention_sums = jnp.concatenate([fold(*flight, None)[0] for flight in flights])
    attention_sums = attention_sums.reshape(copies, piece, 4 * part)
    attention_shard = tensor_sum(attention_sums, tensor_sends(attention_sums, distances))
    feed_shard = tensor_sum(feed_sums, received[0] + received[1] + received[2])
    if repeats > 1:
        residual_out, grad_in = residual_out[::repeats], grad_in[::repeats]
    residual_out = deliver(residual_out.reshape(-1, width), BF16, after=[back_in])
    grad_in = deliver(grad_in.reshape(-1, width), F32, after=[residual_out])
    residual_out, grad_in = residual_out.reshape(rows, block, width), grad_in.reshape(rows, block, width)

    share = 1.0 / repeats
    attention_shard, feed_shard = attention_shard * share, feed_shard * share
    gain_grads = jnp.concatenate([sum(gain_parts), grad_gain_two]) * share
    gain_grads = sum_everywhere(gain_grads)
    gain_shard = lax.dynamic_slice_in_dim(gain_grads, index * piece, piece, 1)

    local = jnp.sum(attention_shard * attention_shard) + jnp.sum(feed_shard * feed_shard)
    norm = jnp.sqrt(sum_everywhere(jnp.full((8, 128), local))[0, 0] + jnp.sum(gain_grads * gain_grads))
    factor = jnp.minimum(1.0, CLIP / norm)
    shards = (
        jnp.stack([attention_shard[:, k * part : (k + 1) * part] for k in range(3)]),
        attention_shard[:, 3 * part :].T,
        feed_shard[:2],
        feed_shard[2].T,
        gain_shard,
    )
    masters = (attention_in, attention_out, expand, contract, gains)
    firsts = (mean_attention_in, mean_attention_out, mean_expand, mean_contract, mean_gains)
    seconds = (
        square_attention_in,
        square_attention_out,
        square_expand,
        square_contract,
        square_gains,
    )
    new_means = []
    new_squares = []
    new_weights = []
    for member in range(5):
        clipped = shards[member] * factor
        moment = BETA_ONE * firsts[member] + (1.0 - BETA_ONE) * clipped
        square = BETA_TWO * seconds[member] + (1.0 - BETA_TWO) * clipped * clipped
        update = (
            moment / (1.0 - BETA_ONE**STEP) / (jnp.sqrt(square / (1.0 - BETA_TWO**STEP)) + ADAM_EPS)
        )
        shrink = DECAY if member < 4 else 0.0
        speed = RATE if member < 4 else GAIN_RATE
        new_means.append(moment)
        new_squares.append(square)
        new_weights.append(masters[member] - speed * (update + shrink * masters[member]))
    return (residual_out, grad_in, norm, *new_means, *new_squares, *new_weights)


def solution(mesh):
    tokens = P("dp", "seq", None)
    weights = (
        P(None, ("dp", "seq"), "tensor"),
        P("tensor", ("dp", "seq")),
        P(None, ("dp", "seq"), "tensor"),
        P("tensor", ("dp", "seq")),
        P(None, ("dp", "seq")),
    )
    return jax.shard_map(
        on_device,
        mesh=mesh,
        in_specs=(tokens, tokens, P("dp", None)) + weights * 3,
        out_specs=(tokens, tokens, P()) + weights * 3,
        check_vma=False,
    )
```

```python
import jax
import jax.numpy as jnp
from jax import lax
from jax.experimental import pallas as pl
from jax.experimental.pallas import tpu as pltpu
from jax.sharding import PartitionSpec as P

HD = 64
STEP = 10

NORM_EPS = 1e-05
NEG = -1e30
CLIP = 1.0
RATE = 0.04
GAIN_RATE = 1.0
BETA_ONE = 0.9
BETA_TWO = 0.999
ADAM_EPS = 1e-08
DECAY = 0.1

SCALE = HD ** (-0.5)
PAIR = 2 * HD
TILE = 256
VMEM = 60 * 1024 * 1024
FOLD = 1024 * 1024
F32 = jnp.float32
BF16 = jnp.bfloat16

NN = (((1,), (0,)), ((), ()))
NT = (((1,), (1,)), ((), ()))
TN = (((0,), (0,)), ((), ()))


def mm(left, right, dims=NN):
    return lax.dot_general(left, right, dims, preferred_element_type=F32)


def call(body, name, flops, args, grid, in_specs, out_specs, out_shape, scratch=(), prefetch=0, after=(), aliases={}):
    count, extra = len(args), len(after)
    moved = sum(a.size * a.dtype.itemsize for a in args) + sum(o.size * o.dtype.itemsize for o in out_shape)
    return pl.pallas_call(
        lambda *refs: body(*refs[:count], *refs[count + extra :]),
        name=name,
        grid_spec=pltpu.PrefetchScalarGridSpec(
            num_scalar_prefetch=prefetch,
            grid=grid,
            in_specs=list(in_specs) + [pl.BlockSpec(memory_space=pl.ANY)] * extra,
            out_specs=out_specs,
            scratch_shapes=list(scratch),
        ),
        out_shape=out_shape,
        input_output_aliases=dict(aliases),
        compiler_params=pltpu.CompilerParams(vmem_limit_bytes=VMEM),
        cost_estimate=pl.CostEstimate(flops=int(flops) >> 24, bytes_accessed=int(moved) >> 20, transcendentals=0),
    )(*args, *after)


def whole(shape):
    return pl.BlockSpec(shape, lambda *at: (0,) * len(shape), pipeline_mode=pl.Buffered(1))


def scalar():
    return pl.BlockSpec(memory_space=pltpu.SMEM)


def out(shape, kind=BF16):
    return jax.ShapeDtypeStruct(shape, kind)


def exchange(block, step):
    axis, bit = step
    return lax.ppermute(block, axis, [(i ^ bit, i) for i in range(lax.axis_size(axis))])


def axis_steps():
    bits = lambda axis: [(axis, 1 << k) for k in range(lax.axis_size(axis).bit_length() - 1)]
    across = bits("dp")
    return bits("seq"), across[1:], across[0]


def owner_masks():
    span = lax.axis_size("seq")
    along, across, last = axis_steps()
    masks = [0]
    for axis, bit in along + across + [last]:
        masks += [m ^ (bit if axis == "seq" else bit * span) for m in masks]
    return masks


def gather_owners(array, axes):
    whole_array = lax.all_gather(array, axes, axis=0)
    return whole_array.reshape(lax.axis_size(axes[0]), -1, *array.shape)


def gather_small(array):
    along, across, last = axis_steps()
    for step in along + [last] + across:
        other = exchange(array, step)
        pair, swapped = jnp.concatenate([array, other], axis=1), jnp.concatenate([other, array], axis=1)
        array = jnp.where(lax.axis_index(step[0]) & step[1], swapped, pair)
    return array


def sum_everywhere(array):
    for axis in ("dp", "seq", "tensor"):
        for k in range(lax.axis_size(axis).bit_length() - 1):
            array = array + exchange(array, (axis, 1 << k))
    return array


def scatter_order(along_first):
    along, across, _ = axis_steps()
    ordered = [list(reversed(along)), list(reversed(across))]
    return ordered[0] + ordered[1] if along_first else ordered[1] + ordered[0]


def tensor_sends(held, distances):
    size, here = lax.axis_size("tensor"), lax.axis_index("tensor")
    return [
        lax.ppermute(
            lax.dynamic_index_in_dim(held, lax.rem(here + k, size), 0, keepdims=False),
            "tensor",
            [(i, (i + k) % size) for i in range(size)],
        )
        for k in distances
    ]


def tensor_sum(held, received):
    own = lax.dynamic_index_in_dim(held, lax.axis_index("tensor"), 0, keepdims=False).astype(F32)
    return sum([array.astype(F32) for array in received], own)


def row_block(own, mask, piece):
    return pl.ds(pl.multiple_of((own ^ mask) * piece, piece), piece)


def store_turned(own, masks, ref, values, scratch):
    scratch[...] = values.T.astype(BF16)
    piece = scratch.shape[0] // len(masks)
    for j, mask in enumerate(masks):
        ref[j * piece : (j + 1) * piece, :] = scratch[row_block(own, mask, piece), :]


def swap_halves(values):
    lane = lax.broadcasted_iota(jnp.int32, values.shape, 1)
    size = values.shape[1]
    ahead = pltpu.roll(values, size - HD // 2, 1)
    behind = pltpu.roll(values, HD // 2, 1)
    return jnp.where(lane % HD < HD // 2, ahead, behind)


def half_sign(shape):
    lane = lax.broadcasted_iota(jnp.int32, shape, 1)
    return jnp.where(lane % HD < HD // 2, -1.0, 1.0)


def turn(values, cosine, sine):
    return values * cosine + swap_halves(values) * (sine * half_sign(values.shape))


def unturn(values, cosine, sine):
    return values * cosine - swap_halves(values * sine) * half_sign(values.shape)


def pair_lanes(values, head):
    lane = lax.broadcasted_iota(jnp.int32, values.shape, 1)
    return jnp.where((lane < HD) == (head == 0), values, 0.0)


def stack_pair(values):
    return jnp.concatenate([pair_lanes(values, 0), pair_lanes(values, 1)], axis=0).astype(BF16)


def norm_rate(values):
    return lax.rsqrt(jnp.mean(values * values, axis=-1, keepdims=True) + NORM_EPS)


def inward_spec(weights):
    groups, owners, piece, cols = weights.shape
    return pl.BlockSpec((groups, owners, piece, cols // 4 * 3), lambda *at: (0, 0, 0, 0), pipeline_mode=pl.Buffered(1))


def outward_spec(weights):
    groups, owners, piece, cols = weights.shape
    return pl.BlockSpec((groups, owners, piece, cols // 4), lambda *at: (0, 0, 0, 3), pipeline_mode=pl.Buffered(1))


def outward(w_ref, w_all):
    groups, owners, piece, part = w_ref.shape
    for z in range(groups):
        w_all[:, z * part : (z + 1) * part] = w_ref[z].reshape(owners * piece, part)


def project(own, masks, x_full, gain, cosine, sine, weights, block):
    tokens, width = x_full.shape
    groups, owners, piece, cols = weights.shape
    part = cols // 4
    heads = groups * part
    mine = block // TILE

    def body(own_ref, x_ref, g_ref, cos_ref, sin_ref, w_ref, at_ref, q_ref, k_ref, v_ref, a_one, turned):
        own = own_ref[0]

        values = x_ref[...].astype(F32)
        normed = values * norm_rate(values) * g_ref[...]
        a_one[...] = normed.astype(BF16)
        store_turned(own, masks, at_ref, normed, turned)
        cosine, sine = cos_ref[...], sin_ref[...]

        def product(z, m):
            return mm(a_one[...], w_ref[z, :, :, m * part : (m + 1) * part].reshape(width, part))

        def rotated(ref, m):
            for z in range(groups):
                mixed = product(z, m)
                for lane in range(0, part, PAIR):
                    ref[:, z * part + lane : z * part + lane + PAIR] = turn(
                        mixed[:, lane : lane + PAIR], cosine, sine
                    ).astype(BF16)

        rotated(k_ref, 1)
        for z in range(groups):
            v_ref[:, z * part : (z + 1) * part] = product(z, 2).astype(BF16)

        @pl.when(pl.program_id(0) < mine)
        def _():
            rotated(q_ref, 0)

    rows = lambda i: (i, 0)
    return call(
        body,
        "project",
        2 * (2 * tokens + block) * width * heads,
        (own, x_full, gain, cosine, sine, weights),
        (tokens // TILE,),
        [
            scalar(),
            pl.BlockSpec((TILE, width), rows),
            whole((1, width)),
            pl.BlockSpec((TILE, PAIR), rows),
            pl.BlockSpec((TILE, PAIR), rows),
            inward_spec(weights),
        ],
        [
            pl.BlockSpec((width, TILE), lambda i: (0, i)),
            pl.BlockSpec((TILE, heads), lambda i: (jnp.minimum(i, mine - 1), 0)),
            pl.BlockSpec((TILE, heads), rows),
            pl.BlockSpec((TILE, heads), rows),
        ],
        [out((width, tokens)), out((block, heads)), out((tokens, heads)), out((tokens, heads))],
        [pltpu.VMEM((TILE, width), BF16), pltpu.VMEM((width, TILE), BF16)],
    )


def attend(reach, query, keys, values, query_marks, key_marks):
    block, heads = query.shape
    tokens = keys.shape[0]
    wide = 2 * PAIR
    count = block // TILE

    def body(reach, q_ref, k_ref, v_ref, qm_ref, km_ref, o_ref, lse_ref, turned, acc, top, total, kept):
        at = pl.program_id(1)
        first, last, shift = reach[2 * at], reach[2 * at + 1], reach[2 * count]

        @pl.when(at == 0)
        def _():
            for tile in range(tokens // TILE):
                rows = slice(tile * TILE, (tile + 1) * TILE)
                turned[:, rows] = v_ref[rows, :].astype(F32).T.astype(BF16)

        marks = jnp.concatenate([qm_ref[...], qm_ref[...]], axis=0)
        stacked = [
            jnp.concatenate([stack_pair(q_ref[:, p * PAIR : (p + 1) * PAIR].astype(F32) * SCALE), marks], axis=1)
            for p in range(2)
        ]
        top[...] = jnp.full_like(top, NEG)
        acc[...] = jnp.zeros_like(acc)
        total[...] = jnp.zeros_like(total)

        def by_eight(values):
            return values.reshape(values.shape[0] // 8, 8, values.shape[1])

        def score(tile, carry):
            rows = pl.ds(pl.multiple_of((tile ^ shift) * TILE, TILE), TILE)
            for p in range(2):
                lanes = slice(p * PAIR, (p + 1) * PAIR)
                scores = mm(jnp.concatenate([k_ref[rows, lanes], km_ref[rows, :]], axis=1), stacked[p], NT)
                kept[p, rows, :] = scores
                top[p] = jnp.maximum(top[p], jnp.max(by_eight(scores), axis=0))
            return carry

        lax.fori_loop(first, last, score, 0)
        tops = [jnp.max(top[p], axis=0, keepdims=True) for p in range(2)]

        def step(tile, carry):
            rows = pl.ds(pl.multiple_of((tile ^ shift) * TILE, TILE), TILE)
            for p in range(2):
                probs = jnp.exp(kept[p, rows, :] - tops[p])
                total[p] += jnp.sum(by_eight(probs), axis=0)
                probs = probs.astype(BF16)
                for h in range(2):
                    part = slice(p * PAIR + h * HD, p * PAIR + (h + 1) * HD)
                    acc[part, :] += mm(turned[part, rows], probs[:, h * TILE : (h + 1) * TILE])
            return carry

        lax.fori_loop(first, last, step, 0)
        for p in range(2):
            sums = jnp.sum(total[p], axis=0, keepdims=True)
            rate = 1.0 / sums
            for h in range(2):
                part = slice(p * PAIR + h * HD, p * PAIR + (h + 1) * HD)
                acc[part, :] = acc[part, :] * rate[:, h * TILE : (h + 1) * TILE]
            lse_ref[0, 0, p : p + 1, :] = tops[p] + jnp.log(sums)
        o_ref[...] = acc[...].T.astype(BF16)

    return call(
        body,
        "attend",
        4 * block * tokens * heads,
        (reach, query, keys, values, query_marks, key_marks),
        (heads // wide, count),
        [
            pl.BlockSpec((TILE, wide), lambda h, i, r: (i, h)),
            pl.BlockSpec((tokens, wide), lambda h, i, r: (0, h)),
            pl.BlockSpec((tokens, wide), lambda h, i, r: (0, h)),
            pl.BlockSpec((TILE, PAIR), lambda h, i, r: (i, 0)),
            pl.BlockSpec((tokens, PAIR), lambda h, i, r: (0, 0)),
        ],
        [
            pl.BlockSpec((TILE, wide), lambda h, i, r: (i, h)),
            pl.BlockSpec((1, 1, 2, 2 * TILE), lambda h, i, r: (h, i, 0, 0)),
        ],
        [out((block, heads)), out((heads // wide, count, 2, 2 * TILE), F32)],
        [
            pltpu.VMEM((wide, tokens), BF16),
            pltpu.VMEM((wide, TILE), F32),
            pltpu.VMEM((2, 8, 2 * TILE), F32),
            pltpu.VMEM((2, 8, 2 * TILE), F32),
            pltpu.VMEM((2, tokens, 2 * TILE), F32),
        ],
        prefetch=1,
    )


def lift(own, masks, attended, x_full, cotangent, gain, weights):
    block, heads = attended.shape
    width = x_full.shape[1]

    def body(own_ref, o_ref, x_ref, c_ref, g_ref, w_ref, h_ref, a_ref, at_ref, e_ref, et_ref, w_all, turned):
        own = own_ref[0]

        @pl.when(pl.program_id(0) == 0)
        def _():
            outward(w_ref, w_all)

        values = x_ref[...].astype(F32) + mm(o_ref[...], w_all[...], NT)
        h_ref[...] = values
        normed = values * norm_rate(values) * g_ref[...]
        a_ref[...] = normed.astype(BF16)
        store_turned(own, masks, at_ref, normed, turned)
        cotangent = c_ref[...]
        e_ref[...] = cotangent.astype(BF16)
        store_turned(own, masks, et_ref, cotangent, turned)

    rows = lambda i: (i, 0)
    wide = pl.BlockSpec((TILE, width), rows)
    tall = pl.BlockSpec((width, TILE), lambda i: (0, i))
    return call(
        body,
        "lift",
        2 * block * width * heads,
        (own, attended, x_full, cotangent, gain, weights),
        (block // TILE,),
        [scalar(), pl.BlockSpec((TILE, heads), rows), wide, wide, whole((1, width)), outward_spec(weights)],
        [wide, wide, tall, wide, tall],
        [out((block, width), F32), out((block, width)), out((width, block)), out((block, width)), out((width, block))],
        [pltpu.VMEM((width, heads), BF16), pltpu.VMEM((width, TILE), BF16)],
    )


def feed(normed, turned, cotangent, cotangent_turned, weights, chunk, hidden, after=()):
    block, width = normed.shape
    groups, owners, kinds, piece, _ = weights.shape
    half = width // 2
    cut = min(512, hidden)
    tile = min(512, block)

    def body(a_ref, at_ref, e_ref, et_ref, w_ref, b_out, d_out, ga_ref, gb_ref, b_ref, d_ref, mid, dgate, dup):
        @pl.when((pl.program_id(0) == 0) & (pl.program_id(1) == 0))
        def _():
            b_ref[...] = jnp.zeros_like(b_ref)
            d_ref[...] = jnp.zeros_like(d_ref)

        def weight(m):
            return w_ref[0, :, m].reshape(width, cut)

        def tokens(i, carry):
            rows = pl.ds(pl.multiple_of(i * tile, tile), tile)
            gate = mm(a_ref[rows, :], weight(0))
            upper = mm(a_ref[rows, :], weight(1))
            grad = mm(e_ref[rows, :], weight(2))
            sigma = jax.nn.sigmoid(gate)
            active = gate * sigma
            mid[rows, :] = (active * upper).astype(BF16)
            dgate[rows, :] = (grad * upper * (sigma * (1.0 + gate * (1.0 - sigma)))).astype(BF16)
            dup[rows, :] = (grad * active).astype(BF16)
            b_ref[rows, :] += mm(mid[rows, :], weight(2), NT)
            d_ref[rows, :] += mm(dgate[rows, :], weight(0), NT) + mm(dup[rows, :], weight(1), NT)
            return carry

        lax.fori_loop(0, block // tile, tokens, 0)
        for ref, rows in ((ga_ref, slice(0, half)), (gb_ref, slice(half, width))):
            ref[0, 0] = mm(at_ref[rows, :], dgate[...]).astype(BF16)
            ref[0, 1] = mm(at_ref[rows, :], dup[...]).astype(BF16)
            ref[0, 2] = mm(et_ref[rows, :], mid[...]).astype(BF16)

        @pl.when((pl.program_id(0) == groups - 1) & (pl.program_id(1) == hidden // cut - 1))
        def _():
            b_out[...] = b_ref[...].astype(BF16)
            d_out[...] = d_ref[...].astype(BF16)

    place = lambda z, j: (z, 0, 0, j)
    shape = (groups, kinds, half, hidden)
    return call(
        body,
        "feed",
        18 * block * width * hidden * groups,
        (normed, turned, cotangent, cotangent_turned, weights),
        (groups, hidden // cut),
        [
            whole((block, width)),
            whole((width, block)),
            whole((block, width)),
            whole((width, block)),
            pl.BlockSpec((1, owners, kinds, piece, cut), lambda z, j: (z, 0, 0, 0, chunk * (hidden // cut) + j)),
        ],
        [
            whole((block, width)),
            whole((block, width)),
            pl.BlockSpec((1, kinds, half, cut), place),
            pl.BlockSpec((1, kinds, half, cut), place),
        ],
        [out((block, width)), out((block, width)), out(shape), out(shape)],
        [pltpu.VMEM((block, width), F32)] * 2 + [pltpu.VMEM((block, cut), BF16)] * 3,
        after=after,
    )


def back(own, masks, hidden, branches, grads, cotangent, gain, weights, after=()):
    block, width = hidden.shape
    groups, owners, piece, cols = weights.shape
    heads = groups * cols // 4

    count = len(branches)

    def body(own_ref, h_ref, c_ref, g_ref, w_ref, *refs):
        b_refs, d_refs, refs = refs[:count], refs[count : 2 * count], refs[2 * count :]
        y_ref, dh_ref, ct_ref, do_ref, gg_ref, w_all, turned = refs
        own = own_ref[0]

        @pl.when(pl.program_id(0) == 0)
        def _():
            outward(w_ref, w_all)
            gg_ref[...] = jnp.zeros_like(gg_ref)

        hidden = h_ref[...]
        grad = sum([ref[...].astype(F32) for ref in d_refs[1:]], d_refs[0][...].astype(F32))
        y_ref[...] = sum([ref[...].astype(F32) for ref in b_refs], hidden).astype(BF16)
        rate = norm_rate(hidden)
        scaled = grad * g_ref[...]
        dot = jnp.mean(hidden * scaled, axis=-1, keepdims=True)
        result = c_ref[...] + rate * scaled - hidden * (rate * rate * rate * dot)
        dh_ref[...] = result
        store_turned(own, masks, ct_ref, result, turned)
        do_ref[...] = mm(result.astype(BF16), w_all[...]).astype(BF16)
        gg_ref[...] += jnp.sum(grad * hidden * rate, axis=0, keepdims=True)

    rows = lambda i: (i, 0)
    wide = pl.BlockSpec((TILE, width), rows)
    return call(
        body,
        "back",
        2 * block * width * heads,
        (own, hidden, cotangent, gain, weights, *branches, *grads),
        (block // TILE,),
        [scalar(), wide, wide, whole((1, width)), outward_spec(weights)] + [wide] * (2 * count),
        [
            wide,
            wide,
            pl.BlockSpec((width, TILE), lambda i: (0, i)),
            pl.BlockSpec((TILE, heads), rows),
            pl.BlockSpec((1, width), lambda i: (0, 0)),
        ],
        [
            out((block, width)),
            out((block, width), F32),
            out((width, block)),
            out((block, heads)),
            out((1, width), F32),
        ],
        [pltpu.VMEM((width, heads), BF16), pltpu.VMEM((width, TILE), BF16)],
        after=after,
    )


def unattend(side, reach, query, grads, attended, keys, values, lse, query_marks, key_marks, cosine, sine, before, after=()):
    block, heads = query.shape
    tokens = keys.shape[0]
    wide = 2 * PAIR
    count = block // TILE

    def body(
        reach, q_ref, g_ref, o_ref, k_ref, v_ref, lse_ref, qm_ref, km_ref, cq_ref, sq_ref, ck_ref, sk_ref,
        dq_ref, dk_ref, dv_ref, keys_turned, dq_acc, dk_acc, dv_acc,
    ):
        at = pl.program_id(1)
        first, last, shift = reach[2 * at], reach[2 * at + 1], reach[2 * count]
        marks = jnp.concatenate([qm_ref[...], qm_ref[...]], axis=0)
        queries = q_ref[...].astype(F32) * SCALE
        grads = g_ref[...].astype(F32)
        product = (grads * o_ref[...].astype(F32)).T
        stacked, marked, stacked_grads, deltas = [], [], [], []
        for p in range(2):
            lanes = slice(p * PAIR, (p + 1) * PAIR)
            stacked.append(stack_pair(queries[:, lanes]))
            marked.append(jnp.concatenate([stacked[p], marks], axis=1))
            stacked_grads.append(stack_pair(grads[:, lanes]))
            sums = [
                jnp.sum(product[p * PAIR + h * HD : p * PAIR + (h + 1) * HD], axis=0, keepdims=True) for h in range(2)
            ]
            deltas.append(jnp.concatenate(sums, axis=1))
        dq_acc[...] = jnp.zeros_like(dq_acc)

        @pl.when(at == 0)
        def _():
            dk_acc[...] = jnp.zeros_like(dk_acc)
            dv_acc[...] = jnp.zeros_like(dv_acc)
            for tile in range(tokens // TILE):
                rows = slice(tile * TILE, (tile + 1) * TILE)
                keys_turned[:, rows] = k_ref[rows, :].astype(F32).T.astype(BF16)

        def step(tile, carry):
            rows = pl.ds(pl.multiple_of((tile ^ shift) * TILE, TILE), TILE)
            for p in range(2):
                lanes = slice(p * PAIR, (p + 1) * PAIR)
                scores = mm(jnp.concatenate([k_ref[rows, lanes], km_ref[rows, :]], axis=1), marked[p], NT)
                probs = jnp.exp(scores - lse_ref[0, 0, p : p + 1, :])
                prob_grads = mm(v_ref[rows, lanes], stacked_grads[p], NT)
                score_grads = (probs * (prob_grads - deltas[p])).astype(BF16)
                dv_acc[rows, lanes] += mm(probs.astype(BF16), stacked_grads[p])
                dk_acc[rows, lanes] += mm(score_grads, stacked[p])
                for h in range(2):
                    part = slice(p * PAIR + h * HD, p * PAIR + (h + 1) * HD)
                    dq_acc[part, :] += mm(keys_turned[part, rows], score_grads[:, h * TILE : (h + 1) * TILE])
            return carry

        lax.fori_loop(first, last, step, 0)
        grad = dq_acc[...].T * SCALE
        for lane in (0, PAIR):
            dq_ref[:, lane : lane + PAIR] = unturn(grad[:, lane : lane + PAIR], cq_ref[...], sq_ref[...]).astype(BF16)

        @pl.when(at == count - 1)
        def _():
            dv_ref[...] = dv_acc[...].astype(BF16)
            for lane in (0, PAIR):
                dk_ref[:, lane : lane + PAIR] = unturn(
                    dk_acc[:, lane : lane + PAIR], ck_ref[...], sk_ref[...]
                ).astype(BF16)

    tile = pl.BlockSpec((TILE, wide), lambda h, i, r: (i, side))
    full = pl.BlockSpec((tokens, wide), lambda h, i, r: (0, side))
    table = pl.BlockSpec((TILE, PAIR), lambda h, i, r: (i, 0))
    tables = pl.BlockSpec((tokens, PAIR), lambda h, i, r: (0, 0))
    return call(
        body,
        "unattend",
        10 * block * tokens * wide,
        (reach, query, grads, attended, keys, values, lse, query_marks, key_marks, cosine, sine, cosine, sine),
        (1, count),
        [
            tile,
            tile,
            tile,
            full,
            full,
            pl.BlockSpec((1, 1, 2, 2 * TILE), lambda h, i, r: (side, i, 0, 0)),
            table,
            tables,
            table,
            table,
            tables,
            tables,
        ],
        [
            tile,
            full,
            full,
        ],
        [out((block, heads)), out((tokens, heads)), out((tokens, heads))],
        [
            pltpu.VMEM((wide, tokens), BF16),
            pltpu.VMEM((wide, TILE), F32),
            pltpu.VMEM((tokens, wide), F32),
            pltpu.VMEM((tokens, wide), F32),
        ],
        prefetch=1,
        after=[*(before or ()), *after],
        aliases={13: 0, 14: 1, 15: 2} if before else {},
    )


def unproject(grads, x_full, k, block, weights, after=()):
    width = x_full.shape[1]
    heads = grads[0].shape[1]
    kinds = len(grads)
    groups, owners, piece, cols = weights.shape
    part = cols // 4
    base = k * block // TILE

    def body(x_ref, *refs):
        g_refs, (w_ref, da_ref, gg_ref, w_all) = refs[:kinds], refs[kinds:]

        @pl.when(pl.program_id(0) == 0)
        def _():
            gg_ref[...] = jnp.zeros_like(gg_ref)
            for m in range(kinds):
                column = (3 - kinds + m) * part
                for z in range(groups):
                    w_all[m, :, z * part : (z + 1) * part] = w_ref[z, :, :, column : column + part].reshape(width, part)

        grad = mm(g_refs[0][...], w_all[0], NT)
        for at in range(1, kinds):
            grad += mm(g_refs[at][...], w_all[at], NT)
        da_ref[...] = grad.astype(BF16)
        values = x_ref[...].astype(F32)
        gg_ref[...] += jnp.sum(grad * values * norm_rate(values), axis=0, keepdims=True)

    def place(array):
        return (lambda i: (i, 0)) if array.shape[0] == block else (lambda i: (base + i, 0))

    return call(
        body,
        "unproject",
        2 * kinds * block * width * heads,
        (x_full, *grads, weights),
        (block // TILE,),
        [pl.BlockSpec((TILE, width), lambda i: (base + i, 0))]
        + [pl.BlockSpec((TILE, heads), place(array)) for array in grads]
        + [inward_spec(weights)],
        [pl.BlockSpec((TILE, width), lambda i: (i, 0)), pl.BlockSpec((1, width), lambda i: (0, 0))],
        [out((block, width)), out((1, width), F32)],
        [pltpu.VMEM((kinds, width, heads), BF16)],
        after=after,
    )


def weigh(turned, cotangent_turned, dq, dk, dv, attended, groups, part, after=()):
    width, tokens = turned.shape
    block = dq.shape[0]
    half, near = width // 2, groups // 2

    def body(at_ref, ct_ref, dq_ref, dk_ref, dv_ref, o_ref, *refs):
        def write(targets):
            for ref, rows in zip(targets, (slice(0, half), slice(half, width))):
                ref[0, :, :part] = mm(at_ref[rows, :block], dq_ref[...]).astype(BF16)
                ref[0, :, part : 2 * part] = mm(at_ref[rows, :], dk_ref[...]).astype(BF16)
                ref[0, :, 2 * part : 3 * part] = mm(at_ref[rows, :], dv_ref[...]).astype(BF16)
                ref[0, :, 3 * part :] = mm(ct_ref[rows, :], o_ref[...]).astype(BF16)

        @pl.when(pl.program_id(0) < near)
        def _():
            write(refs[:2])

        @pl.when(pl.program_id(0) >= near)
        def _():
            write(refs[2:])

    column = lambda z: (0, z)
    shape = (near, half, 4 * part)
    block_shape = (1, half, 4 * part)
    return call(
        body,
        "weigh",
        4 * (tokens + block) * width * groups * part,
        (turned, cotangent_turned, dq, dk, dv, attended),
        (groups,),
        [
            whole(turned.shape),
            whole(cotangent_turned.shape),
            pl.BlockSpec((block, part), column),
            pl.BlockSpec((tokens, part), column),
            pl.BlockSpec((tokens, part), column),
            pl.BlockSpec((block, part), column),
        ],
        [pl.BlockSpec(block_shape, lambda z: (jnp.minimum(z, near - 1), 0, 0))] * 2
        + [pl.BlockSpec(block_shape, lambda z: (jnp.maximum(z - near, 0), 0, 0))] * 2,
        [out(shape)] * 4,
        after=after,
    )


def fold(kept, received, step, after=()):
    axis = None if step is None else 2 if step[0] == "seq" else 1
    shapes = [kept.shape]
    if axis is not None:
        half = kept.shape[axis] // 2
        shapes = [tuple(half if at == axis else n for at, n in enumerate(kept.shape))] * 2

    def body(kept_ref, received_ref, *refs):
        total = (kept_ref[...].astype(F32) + received_ref[...].astype(F32)).astype(BF16)
        if axis is None:
            refs[0][...] = total
        elif axis == 1:
            refs[0][...], refs[1][...] = total[:, :half], total[:, half:]
        else:
            refs[0][...], refs[1][...] = total[:, :, :half], total[:, :, half:]

    groups = kept.shape[0]
    run = next(n for n in range(groups, 0, -1) if groups % n == 0 and n * kept[0].size <= FOLD)
    spec = lambda shape: pl.BlockSpec((run, *shape[1:]), lambda g: (g, 0, 0, 0, 0))
    return call(
        body,
        "fold",
        kept.size,
        (kept, received),
        (groups // run,),
        [spec(kept.shape)] * 2,
        [spec(shape) for shape in shapes],
        [out(shape) for shape in shapes],
        after=after,
    )


def deliver(array, kind, after=()):
    rows, width = array.shape

    def body(x_ref, y_ref):
        y_ref[...] = x_ref[...].astype(kind)

    spec = pl.BlockSpec((2 * TILE, width), lambda i: (i, 0))
    return call(
        body, "deliver", rows * width, (array,), (rows // (2 * TILE),), [spec], [spec], [out(array.shape, kind)], after=after
    )[0]


def finish(x_full, hidden_grad, gain, parts, after=()):
    block, width = hidden_grad.shape

    def body(x_ref, dh_ref, g_ref, *refs):
        grad = sum([ref[...].astype(F32) for ref in refs[1:-1]], refs[0][...].astype(F32))
        values = x_ref[...].astype(F32)
        rate = norm_rate(values)
        scaled = grad * g_ref[...]
        dot = jnp.mean(values * scaled, axis=-1, keepdims=True)
        refs[-1][...] = (dh_ref[...] + rate * scaled - values * (rate * rate * rate * dot)).astype(BF16)

    wide = pl.BlockSpec((TILE, width), lambda i: (i, 0))
    return call(
        body,
        "finish",
        16 * block * width,
        (x_full, hidden_grad, gain, *parts),
        (block // TILE,),
        [wide, wide, whole((1, width))] + [wide] * len(parts),
        [wide],
        [out((block, width))],
        after=after,
    )[0]


def on_device(
    residual_in,
    grad_out,
    segment_lengths,
    attention_in,
    attention_out,
    expand,
    contract,
    gains,
    mean_attention_in,
    mean_attention_out,
    mean_expand,
    mean_contract,
    mean_gains,
    square_attention_in,
    square_attention_out,
    square_expand,
    square_contract,
    square_gains,
):
    span, copies = lax.axis_size("seq"), lax.axis_size("tensor")
    place, lane = lax.axis_index("seq"), lax.axis_index("tensor")
    rows, block, width = residual_in.shape
    tokens = span * block
    repeats = copies // rows
    row = lane // repeats
    piece = attention_in.shape[1]
    part = attention_in.shape[2]
    masks = owner_masks()
    index = lax.axis_index("dp") * span + place
    own = index.astype(jnp.int32)[None]
    near = copies // 2

    attention_piece = jnp.concatenate(
        [attention_in[0], attention_in[1], attention_in[2], attention_out.T], axis=1
    ).astype(BF16)
    feed_piece = jnp.stack([expand[0], expand[1], contract.T]).astype(BF16)
    x_own = lax.dynamic_index_in_dim(residual_in, row, 0, keepdims=False)
    cotangent = lax.dynamic_index_in_dim(grad_out, row, 0, keepdims=False)
    full_gains = gather_small(gains.astype(BF16).astype(F32))
    full_gains, x_own = lax.optimization_barrier((full_gains, x_own))
    x_parts = [x_own] + [exchange(x_own, ("seq", k)) for k in range(1, span)]
    everywhere = ("tensor", "dp", "seq")
    gain_one, gain_two = full_gains[:1], full_gains[1:]
    weights = gather_owners(attention_piece, everywhere)
    x_full = jnp.concatenate(x_parts, axis=0)
    weights, feed_piece, x_full, cotangent = lax.optimization_barrier((weights, feed_piece, x_full, cotangent))
    chunks = 4
    cut = feed_piece.shape[2] // chunks
    bounds = (0, 2 * cut, 3 * cut, 4 * cut)
    gathered = [gather_owners(feed_piece[:, :, low:high], everywhere) for low, high in zip(bounds, bounds[1:])]
    feeds = [(gathered[0], 0), (gathered[0], 1), (gathered[1], 0), (gathered[2], 0)]

    lens = lax.dynamic_index_in_dim(segment_lengths, row, 0, keepdims=False)
    ends = jnp.cumsum(lens)
    starts = ends - lens
    blocks = place ^ jnp.arange(span, dtype=jnp.int32)
    places = (blocks[:, None] * block + jnp.arange(block, dtype=jnp.int32)[None, :]).reshape(tokens)
    segment = jnp.sum((places[:, None] >= ends[None, :]).astype(jnp.int32), axis=-1)
    picked = segment[:, None] == jnp.arange(lens.shape[0], dtype=jnp.int32)[None, :]
    begin = jnp.sum(jnp.where(picked, starts[None, :], 0), axis=-1)
    finish_at = jnp.sum(jnp.where(picked, ends[None, :], 0), axis=-1)
    freq = jnp.exp(jnp.arange(HD // 2, dtype=F32) * (-2.0 * jnp.log(10000.0) / HD))
    angle = (places - begin).astype(F32)[:, None] * freq
    cosine = jnp.tile(jnp.cos(angle), (1, PAIR // (HD // 2)))
    sine = jnp.tile(jnp.sin(angle), (1, PAIR // (HD // 2)))
    count = block // TILE
    firsts = begin[:block].reshape(count, TILE)[:, 0] // TILE
    lasts = (finish_at[:block].reshape(count, TILE)[:, -1] + TILE - 1) // TILE
    reach = jnp.concatenate(
        [jnp.stack([firsts, lasts], axis=1).reshape(-1), (place * (block // TILE))[None]]
    ).astype(jnp.int32)
    lanes = jnp.arange(PAIR, dtype=jnp.int32)[None, :]
    key_marks = jnp.where(segment[:, None] == lanes, NEG, 0.0).astype(BF16)
    query_marks = ((segment[:block, None] != lanes) & (lanes < lens.shape[0])).astype(BF16)

    turned_one, query, keys, values = project(own, masks, x_full, gain_one, cosine, sine, weights, block)
    attended, lse = attend(reach, query, keys, values, query_marks, key_marks)
    hidden, normed_two, turned_two, rounded, rounded_turned = lift(
        own, masks, attended, x_full, cotangent, gain_two, weights
    )

    def spread(array):
        half, columns = array.shape[-2:]
        return array.reshape(-1, half // (span * piece), span, piece, columns)

    last_step = axis_steps()[2]
    orders = [scatter_order(bool(at % 2)) for at in range(chunks)]
    flights, places, branches, grads = [], [0] * chunks, [], []

    def tie(anchor, *which):
        *tied, anchor = lax.optimization_barrier((*[flights[at] for at in which], anchor))
        for at, flight in zip(which, tied):
            flights[at] = tuple(flight) if isinstance(flight, (tuple, list)) else flight

    def move_on(*which):
        for at in which:
            if places[at] < len(orders[at]):
                step = orders[at][places[at]]
                kept, sent = fold(*flights[at], step)
                flights[at] = (kept, exchange(sent, step))
                places[at] += 1
            elif isinstance(flights[at], tuple):
                flights[at] = fold(*flights[at], None)[0]
        return [flights[at][0] if isinstance(flights[at], tuple) else flights[at] for at in which]

    after = []
    for at in range(chunks):
        branch, grad, kept, sent = feed(normed_two, turned_two, rounded, rounded_turned, *feeds[at], cut, after=after)
        flights.append((spread(kept), spread(exchange(sent, last_step))))
        branches.append(branch)
        grads.append(grad)
        after = [branch]
        if 0 < at < chunks - 1:
            tie(branch, at - 1)
            after += move_on(at - 1)
    result, hidden_grad, hidden_grad_turned, output_grad, grad_gain_two = back(
        own, masks, hidden, branches, grads, cotangent, gain_two, weights
    )
    tie(output_grad, 2, 3)
    residual_out = lax.all_gather(result, "tensor", axis=0)
    common = (reach, query, output_grad, attended, keys, values, lse, query_marks, key_marks, cosine, sine)

    def finish_chunks(first):
        for at in (first, first + 1):
            while isinstance(flights[at], tuple):
                move_on(at)
        pair = [flights[at].reshape(copies, -1, piece, cut) for at in (first, first + 1)]
        sums = jnp.concatenate(pair, axis=-1)
        feed_sums.append(sums)
        received.append(tensor_sends(sums, distances))
        return [sums]

    distances = list(range(1, copies))
    feed_sums, received = [], []
    found = unattend(0, *common, None, after=move_on(2, 3))
    tie(found[0], 0, 1)
    found = unattend(1, *common, found, after=move_on(0, 1))
    tie(found[0], 0, 1, 2, 3)
    found = unattend(2, *common, found, after=finish_chunks(0) + move_on(2, 3))
    tie(found[0], 2, 3)
    found = unattend(3, *common, found, after=finish_chunks(2) + received[0])
    dq, dk, dv = found

    parts, gain_parts = [], []
    for k in range(1, span):
        grad, gain_part = unproject([dk, dv], x_full, k, block, weights, after=received[1])
        parts.append(exchange(grad, ("seq", k)))
        gain_parts.append(gain_part)
    chunks, places = 2, [0, 0]
    found = weigh(turned_one, hidden_grad_turned, dq, dk, dv, attended, copies, part, after=gain_parts)
    flights = [(spread(found[at]), spread(exchange(found[at + 1], last_step))) for at in (0, 2)]
    own_grad, gain_part = unproject(
        [dq, dk, dv], x_full, 0, block, weights, after=[found[0], *parts]
    )
    gain_parts.append(gain_part)
    back_in = finish(x_full, hidden_grad, gain_one, [own_grad] + parts, after=move_on(0, 1))
    grad_in = lax.all_gather(back_in, "tensor", axis=0)
    while isinstance(flights[1], tuple):
        move_on(0, 1)
    attention_sums = jnp.concatenate(flights)
    attention_sums = attention_sums.reshape(copies, piece, 4 * part)
    attention_shard = tensor_sum(attention_sums, tensor_sends(attention_sums, distances))
    feed_shard = jnp.concatenate([tensor_sum(*pair) for pair in zip(feed_sums, received)], axis=-1)
    if repeats > 1:
        residual_out, grad_in = residual_out[::repeats], grad_in[::repeats]
    residual_out = deliver(residual_out.reshape(-1, width), BF16, after=[back_in])
    grad_in = deliver(grad_in.reshape(-1, width), F32, after=[residual_out])
    residual_out, grad_in = residual_out.reshape(rows, block, width), grad_in.reshape(rows, block, width)

    share = 1.0 / repeats
    attention_shard, feed_shard = attention_shard * share, feed_shard * share
    gain_grads = jnp.concatenate([sum(gain_parts), grad_gain_two]) * share
    gain_grads = sum_everywhere(gain_grads)
    gain_shard = lax.dynamic_slice_in_dim(gain_grads, index * piece, piece, 1)

    local = jnp.sum(attention_shard * attention_shard) + jnp.sum(feed_shard * feed_shard)
    norm = jnp.sqrt(sum_everywhere(jnp.full((8, 128), local))[0, 0] + jnp.sum(gain_grads * gain_grads))
    factor = jnp.minimum(1.0, CLIP / norm)
    shards = (
        jnp.stack([attention_shard[:, k * part : (k + 1) * part] for k in range(3)]),
        attention_shard[:, 3 * part :].T,
        feed_shard[:2],
        feed_shard[2].T,
        gain_shard,
    )
    masters = (attention_in, attention_out, expand, contract, gains)
    firsts = (mean_attention_in, mean_attention_out, mean_expand, mean_contract, mean_gains)
    seconds = (
        square_attention_in,
        square_attention_out,
        square_expand,
        square_contract,
        square_gains,
    )
    new_means = []
    new_squares = []
    new_weights = []
    for member in range(5):
        clipped = shards[member] * factor
        moment = BETA_ONE * firsts[member] + (1.0 - BETA_ONE) * clipped
        square = BETA_TWO * seconds[member] + (1.0 - BETA_TWO) * clipped * clipped
        update = (
            moment / (1.0 - BETA_ONE**STEP) / (jnp.sqrt(square / (1.0 - BETA_TWO**STEP)) + ADAM_EPS)
        )
        shrink = DECAY if member < 4 else 0.0
        speed = RATE if member < 4 else GAIN_RATE
        new_means.append(moment)
        new_squares.append(square)
        new_weights.append(masters[member] - speed * (update + shrink * masters[member]))
    return (residual_out, grad_in, norm, *new_means, *new_squares, *new_weights)


def solution(mesh):
    tokens = P("dp", "seq", None)
    weights = (
        P(None, ("dp", "seq"), "tensor"),
        P("tensor", ("dp", "seq")),
        P(None, ("dp", "seq"), "tensor"),
        P("tensor", ("dp", "seq")),
        P(None, ("dp", "seq")),
    )
    return jax.shard_map(
        on_device,
        mesh=mesh,
        in_specs=(tokens, tokens, P("dp", None)) + weights * 3,
        out_specs=(tokens, tokens, P()) + weights * 3,
        check_vma=False,
    )
```

```python
import jax
import jax.numpy as jnp
from jax import lax
from jax.experimental import pallas as pl
from jax.experimental.pallas import tpu as pltpu
from jax.sharding import PartitionSpec as P

HD = 64
STEP = 10

NORM_EPS = 1e-05
NEG = -1e30
CLIP = 1.0
RATE = 0.04
GAIN_RATE = 1.0
BETA_ONE = 0.9
BETA_TWO = 0.999
ADAM_EPS = 1e-08
DECAY = 0.1

SCALE = HD ** (-0.5)
PAIR = 2 * HD
TILE = 256
VMEM = 60 * 1024 * 1024
FOLD = 1024 * 1024
F32 = jnp.float32
BF16 = jnp.bfloat16

NN = (((1,), (0,)), ((), ()))
NT = (((1,), (1,)), ((), ()))
TN = (((0,), (0,)), ((), ()))


def mm(left, right, dims=NN):
    return lax.dot_general(left, right, dims, preferred_element_type=F32)


def call(body, name, flops, args, grid, in_specs, out_specs, out_shape, scratch=(), prefetch=0, after=(), aliases={}):
    count, extra = len(args), len(after)
    moved = sum(a.size * a.dtype.itemsize for a in args) + sum(o.size * o.dtype.itemsize for o in out_shape)
    return pl.pallas_call(
        lambda *refs: body(*refs[:count], *refs[count + extra :]),
        name=name,
        grid_spec=pltpu.PrefetchScalarGridSpec(
            num_scalar_prefetch=prefetch,
            grid=grid,
            in_specs=list(in_specs) + [pl.BlockSpec(memory_space=pl.ANY)] * extra,
            out_specs=out_specs,
            scratch_shapes=list(scratch),
        ),
        out_shape=out_shape,
        input_output_aliases=dict(aliases),
        compiler_params=pltpu.CompilerParams(vmem_limit_bytes=VMEM),
        cost_estimate=pl.CostEstimate(flops=int(flops) >> 24, bytes_accessed=int(moved) >> 20, transcendentals=0),
    )(*args, *after)


def whole(shape):
    return pl.BlockSpec(shape, lambda *at: (0,) * len(shape), pipeline_mode=pl.Buffered(1))


def scalar():
    return pl.BlockSpec(memory_space=pltpu.SMEM)


def out(shape, kind=BF16):
    return jax.ShapeDtypeStruct(shape, kind)


def exchange(block, step):
    axis, bit = step
    return lax.ppermute(block, axis, [(i ^ bit, i) for i in range(lax.axis_size(axis))])


def axis_steps():
    bits = lambda axis: [(axis, 1 << k) for k in range(lax.axis_size(axis).bit_length() - 1)]
    across = bits("dp")
    return bits("seq"), across[1:], across[0]


def owner_masks():
    span = lax.axis_size("seq")
    along, across, last = axis_steps()
    masks = [0]
    for axis, bit in along + across + [last]:
        masks += [m ^ (bit if axis == "seq" else bit * span) for m in masks]
    return masks


def gather_owners(array, axes):
    whole_array = lax.all_gather(array, axes, axis=0)
    return whole_array.reshape(lax.axis_size(axes[0]), -1, *array.shape)


def gather_small(array):
    along, across, last = axis_steps()
    for step in along + [last] + across:
        other = exchange(array, step)
        pair, swapped = jnp.concatenate([array, other], axis=1), jnp.concatenate([other, array], axis=1)
        array = jnp.where(lax.axis_index(step[0]) & step[1], swapped, pair)
    return array


def sum_everywhere(array):
    for axis in ("dp", "seq", "tensor"):
        for k in range(lax.axis_size(axis).bit_length() - 1):
            array = array + exchange(array, (axis, 1 << k))
    return array


def scatter_order(along_first):
    along, across, _ = axis_steps()
    ordered = [list(reversed(along)), list(reversed(across))]
    return ordered[0] + ordered[1] if along_first else ordered[1] + ordered[0]


def tensor_sends(held, distances):
    size, here = lax.axis_size("tensor"), lax.axis_index("tensor")
    return [
        lax.ppermute(
            lax.dynamic_index_in_dim(held, lax.rem(here + k, size), 0, keepdims=False),
            "tensor",
            [(i, (i + k) % size) for i in range(size)],
        )
        for k in distances
    ]


def tensor_sum(held, received):
    own = lax.dynamic_index_in_dim(held, lax.axis_index("tensor"), 0, keepdims=False).astype(F32)
    return sum([array.astype(F32) for array in received], own)


def row_block(own, mask, piece):
    return pl.ds(pl.multiple_of((own ^ mask) * piece, piece), piece)


def store_turned(own, masks, ref, values, scratch):
    scratch[...] = values.T.astype(BF16)
    piece = scratch.shape[0] // len(masks)
    for j, mask in enumerate(masks):
        ref[j * piece : (j + 1) * piece, :] = scratch[row_block(own, mask, piece), :]


def swap_halves(values):
    lane = lax.broadcasted_iota(jnp.int32, values.shape, 1)
    size = values.shape[1]
    ahead = pltpu.roll(values, size - HD // 2, 1)
    behind = pltpu.roll(values, HD // 2, 1)
    return jnp.where(lane % HD < HD // 2, ahead, behind)


def half_sign(shape):
    lane = lax.broadcasted_iota(jnp.int32, shape, 1)
    return jnp.where(lane % HD < HD // 2, -1.0, 1.0)


def turn(values, cosine, sine):
    return values * cosine + swap_halves(values) * (sine * half_sign(values.shape))


def unturn(values, cosine, sine):
    return values * cosine - swap_halves(values * sine) * half_sign(values.shape)


def pair_lanes(values, head):
    lane = lax.broadcasted_iota(jnp.int32, values.shape, 1)
    return jnp.where((lane < HD) == (head == 0), values, 0.0)


def stack_pair(values):
    return jnp.concatenate([pair_lanes(values, 0), pair_lanes(values, 1)], axis=0).astype(BF16)


def norm_rate(values):
    return lax.rsqrt(jnp.mean(values * values, axis=-1, keepdims=True) + NORM_EPS)


def inward_spec(weights):
    groups, owners, piece, cols = weights.shape
    return pl.BlockSpec((groups, owners, piece, cols // 4 * 3), lambda *at: (0, 0, 0, 0), pipeline_mode=pl.Buffered(1))


def outward_spec(weights):
    groups, owners, piece, cols = weights.shape
    return pl.BlockSpec((groups, owners, piece, cols // 4), lambda *at: (0, 0, 0, 3), pipeline_mode=pl.Buffered(1))


def outward(w_ref, w_all):
    groups, owners, piece, part = w_ref.shape
    for z in range(groups):
        w_all[:, z * part : (z + 1) * part] = w_ref[z].reshape(owners * piece, part)


def project(own, masks, x_full, gain, cosine, sine, weights, block):
    tokens, width = x_full.shape
    groups, owners, piece, cols = weights.shape
    part = cols // 4
    heads = groups * part
    mine = block // TILE

    def body(own_ref, x_ref, g_ref, cos_ref, sin_ref, w_ref, at_ref, q_ref, k_ref, v_ref, a_one, turned):
        own = own_ref[0]

        values = x_ref[...].astype(F32)
        normed = values * norm_rate(values) * g_ref[...]
        a_one[...] = normed.astype(BF16)
        store_turned(own, masks, at_ref, normed, turned)
        cosine, sine = cos_ref[...], sin_ref[...]

        def product(z, m):
            return mm(a_one[...], w_ref[z, :, :, m * part : (m + 1) * part].reshape(width, part))

        def rotated(ref, m):
            for z in range(groups):
                mixed = product(z, m)
                for lane in range(0, part, PAIR):
                    ref[:, z * part + lane : z * part + lane + PAIR] = turn(
                        mixed[:, lane : lane + PAIR], cosine, sine
                    ).astype(BF16)

        rotated(k_ref, 1)
        for z in range(groups):
            v_ref[:, z * part : (z + 1) * part] = product(z, 2).astype(BF16)

        @pl.when(pl.program_id(0) < mine)
        def _():
            rotated(q_ref, 0)

    rows = lambda i: (i, 0)
    return call(
        body,
        "project",
        2 * (2 * tokens + block) * width * heads,
        (own, x_full, gain, cosine, sine, weights),
        (tokens // TILE,),
        [
            scalar(),
            pl.BlockSpec((TILE, width), rows),
            whole((1, width)),
            pl.BlockSpec((TILE, PAIR), rows),
            pl.BlockSpec((TILE, PAIR), rows),
            inward_spec(weights),
        ],
        [
            pl.BlockSpec((width, TILE), lambda i: (0, i)),
            pl.BlockSpec((TILE, heads), lambda i: (jnp.minimum(i, mine - 1), 0)),
            pl.BlockSpec((TILE, heads), rows),
            pl.BlockSpec((TILE, heads), rows),
        ],
        [out((width, tokens)), out((block, heads)), out((tokens, heads)), out((tokens, heads))],
        [pltpu.VMEM((TILE, width), BF16), pltpu.VMEM((width, TILE), BF16)],
    )


def attend(reach, query, keys, values, query_marks, key_marks):
    block, heads = query.shape
    tokens = keys.shape[0]
    wide = 2 * PAIR
    count = block // TILE

    def body(reach, q_ref, k_ref, v_ref, qm_ref, km_ref, o_ref, lse_ref, turned, acc, top, total, kept):
        at = pl.program_id(1)
        first, last, shift = reach[2 * at], reach[2 * at + 1], reach[2 * count]

        @pl.when(at == 0)
        def _():
            for tile in range(tokens // TILE):
                rows = slice(tile * TILE, (tile + 1) * TILE)
                turned[:, rows] = v_ref[rows, :].astype(F32).T.astype(BF16)

        marks = jnp.concatenate([qm_ref[...], qm_ref[...]], axis=0)
        stacked = [
            jnp.concatenate([stack_pair(q_ref[:, p * PAIR : (p + 1) * PAIR].astype(F32) * SCALE), marks], axis=1)
            for p in range(2)
        ]
        top[...] = jnp.full_like(top, NEG)
        acc[...] = jnp.zeros_like(acc)
        total[...] = jnp.zeros_like(total)

        def by_eight(values):
            return values.reshape(values.shape[0] // 8, 8, values.shape[1])

        def score(tile, carry):
            rows = pl.ds(pl.multiple_of((tile ^ shift) * TILE, TILE), TILE)
            for p in range(2):
                lanes = slice(p * PAIR, (p + 1) * PAIR)
                scores = mm(jnp.concatenate([k_ref[rows, lanes], km_ref[rows, :]], axis=1), stacked[p], NT)
                kept[p, rows, :] = scores
                top[p] = jnp.maximum(top[p], jnp.max(by_eight(scores), axis=0))
            return carry

        lax.fori_loop(first, last, score, 0)
        tops = [jnp.max(top[p], axis=0, keepdims=True) for p in range(2)]

        def step(tile, carry):
            rows = pl.ds(pl.multiple_of((tile ^ shift) * TILE, TILE), TILE)
            for p in range(2):
                probs = jnp.exp(kept[p, rows, :] - tops[p])
                total[p] += jnp.sum(by_eight(probs), axis=0)
                probs = probs.astype(BF16)
                for h in range(2):
                    part = slice(p * PAIR + h * HD, p * PAIR + (h + 1) * HD)
                    acc[part, :] += mm(turned[part, rows], probs[:, h * TILE : (h + 1) * TILE])
            return carry

        lax.fori_loop(first, last, step, 0)
        for p in range(2):
            sums = jnp.sum(total[p], axis=0, keepdims=True)
            rate = 1.0 / sums
            for h in range(2):
                part = slice(p * PAIR + h * HD, p * PAIR + (h + 1) * HD)
                acc[part, :] = acc[part, :] * rate[:, h * TILE : (h + 1) * TILE]
            lse_ref[0, 0, p : p + 1, :] = tops[p] + jnp.log(sums)
        o_ref[...] = acc[...].T.astype(BF16)

    return call(
        body,
        "attend",
        4 * block * tokens * heads,
        (reach, query, keys, values, query_marks, key_marks),
        (heads // wide, count),
        [
            pl.BlockSpec((TILE, wide), lambda h, i, r: (i, h)),
            pl.BlockSpec((tokens, wide), lambda h, i, r: (0, h)),
            pl.BlockSpec((tokens, wide), lambda h, i, r: (0, h)),
            pl.BlockSpec((TILE, PAIR), lambda h, i, r: (i, 0)),
            pl.BlockSpec((tokens, PAIR), lambda h, i, r: (0, 0)),
        ],
        [
            pl.BlockSpec((TILE, wide), lambda h, i, r: (i, h)),
            pl.BlockSpec((1, 1, 2, 2 * TILE), lambda h, i, r: (h, i, 0, 0)),
        ],
        [out((block, heads)), out((heads // wide, count, 2, 2 * TILE), F32)],
        [
            pltpu.VMEM((wide, tokens), BF16),
            pltpu.VMEM((wide, TILE), F32),
            pltpu.VMEM((2, 8, 2 * TILE), F32),
            pltpu.VMEM((2, 8, 2 * TILE), F32),
            pltpu.VMEM((2, tokens, 2 * TILE), F32),
        ],
        prefetch=1,
    )


def lift(own, masks, attended, x_full, cotangent, gain, weights):
    block, heads = attended.shape
    width = x_full.shape[1]

    def body(own_ref, o_ref, x_ref, c_ref, g_ref, w_ref, h_ref, a_ref, at_ref, e_ref, et_ref, w_all, turned):
        own = own_ref[0]

        @pl.when(pl.program_id(0) == 0)
        def _():
            outward(w_ref, w_all)

        values = x_ref[...].astype(F32) + mm(o_ref[...], w_all[...], NT)
        h_ref[...] = values
        normed = values * norm_rate(values) * g_ref[...]
        a_ref[...] = normed.astype(BF16)
        store_turned(own, masks, at_ref, normed, turned)
        cotangent = c_ref[...]
        e_ref[...] = cotangent.astype(BF16)
        store_turned(own, masks, et_ref, cotangent, turned)

    rows = lambda i: (i, 0)
    wide = pl.BlockSpec((TILE, width), rows)
    tall = pl.BlockSpec((width, TILE), lambda i: (0, i))
    return call(
        body,
        "lift",
        2 * block * width * heads,
        (own, attended, x_full, cotangent, gain, weights),
        (block // TILE,),
        [scalar(), pl.BlockSpec((TILE, heads), rows), wide, wide, whole((1, width)), outward_spec(weights)],
        [wide, wide, tall, wide, tall],
        [out((block, width), F32), out((block, width)), out((width, block)), out((block, width)), out((width, block))],
        [pltpu.VMEM((width, heads), BF16), pltpu.VMEM((width, TILE), BF16)],
    )


def feed(normed, turned, cotangent, cotangent_turned, weights, chunk, hidden, after=()):
    block, width = normed.shape
    groups, owners, kinds, piece, _ = weights.shape
    half = width // 2
    cut = min(512, hidden)
    tile = min(512, block)

    def body(a_ref, at_ref, e_ref, et_ref, w_ref, b_out, d_out, ga_ref, gb_ref, b_ref, d_ref, mid, dgate, dup):
        @pl.when((pl.program_id(0) == 0) & (pl.program_id(1) == 0))
        def _():
            b_ref[...] = jnp.zeros_like(b_ref)
            d_ref[...] = jnp.zeros_like(d_ref)

        def weight(m):
            return w_ref[0, :, m].reshape(width, cut)

        def tokens(i, carry):
            rows = pl.ds(pl.multiple_of(i * tile, tile), tile)
            gate = mm(a_ref[rows, :], weight(0))
            upper = mm(a_ref[rows, :], weight(1))
            grad = mm(e_ref[rows, :], weight(2))
            sigma = jax.nn.sigmoid(gate)
            active = gate * sigma
            mid[rows, :] = (active * upper).astype(BF16)
            dgate[rows, :] = (grad * upper * (sigma * (1.0 + gate * (1.0 - sigma)))).astype(BF16)
            dup[rows, :] = (grad * active).astype(BF16)
            b_ref[rows, :] += mm(mid[rows, :], weight(2), NT)
            d_ref[rows, :] += mm(dgate[rows, :], weight(0), NT) + mm(dup[rows, :], weight(1), NT)
            return carry

        lax.fori_loop(0, block // tile, tokens, 0)
        for ref, rows in ((ga_ref, slice(0, half)), (gb_ref, slice(half, width))):
            ref[0, 0] = mm(at_ref[rows, :], dgate[...]).astype(BF16)
            ref[0, 1] = mm(at_ref[rows, :], dup[...]).astype(BF16)
            ref[0, 2] = mm(et_ref[rows, :], mid[...]).astype(BF16)

        @pl.when((pl.program_id(0) == groups - 1) & (pl.program_id(1) == hidden // cut - 1))
        def _():
            b_out[...] = b_ref[...].astype(BF16)
            d_out[...] = d_ref[...].astype(BF16)

    place = lambda z, j: (z, 0, 0, j)
    shape = (groups, kinds, half, hidden)
    return call(
        body,
        "feed",
        18 * block * width * hidden * groups,
        (normed, turned, cotangent, cotangent_turned, weights),
        (groups, hidden // cut),
        [
            whole((block, width)),
            whole((width, block)),
            whole((block, width)),
            whole((width, block)),
            pl.BlockSpec((1, owners, kinds, piece, cut), lambda z, j: (z, 0, 0, 0, chunk * (hidden // cut) + j)),
        ],
        [
            whole((block, width)),
            whole((block, width)),
            pl.BlockSpec((1, kinds, half, cut), place),
            pl.BlockSpec((1, kinds, half, cut), place),
        ],
        [out((block, width)), out((block, width)), out(shape), out(shape)],
        [pltpu.VMEM((block, width), F32)] * 2 + [pltpu.VMEM((block, cut), BF16)] * 3,
        after=after,
    )


def back(own, masks, hidden, branches, grads, cotangent, gain, weights, after=()):
    block, width = hidden.shape
    groups, owners, piece, cols = weights.shape
    heads = groups * cols // 4

    count = len(branches)

    def body(own_ref, h_ref, c_ref, g_ref, w_ref, *refs):
        b_refs, d_refs, refs = refs[:count], refs[count : 2 * count], refs[2 * count :]
        y_ref, dh_ref, ct_ref, do_ref, gg_ref, w_all, turned = refs
        own = own_ref[0]

        @pl.when(pl.program_id(0) == 0)
        def _():
            outward(w_ref, w_all)
            gg_ref[...] = jnp.zeros_like(gg_ref)

        hidden = h_ref[...]
        grad = sum([ref[...].astype(F32) for ref in d_refs[1:]], d_refs[0][...].astype(F32))
        y_ref[...] = sum([ref[...].astype(F32) for ref in b_refs], hidden).astype(BF16)
        rate = norm_rate(hidden)
        scaled = grad * g_ref[...]
        dot = jnp.mean(hidden * scaled, axis=-1, keepdims=True)
        result = c_ref[...] + rate * scaled - hidden * (rate * rate * rate * dot)
        dh_ref[...] = result
        store_turned(own, masks, ct_ref, result, turned)
        do_ref[...] = mm(result.astype(BF16), w_all[...]).astype(BF16)
        gg_ref[...] += jnp.sum(grad * hidden * rate, axis=0, keepdims=True)

    rows = lambda i: (i, 0)
    wide = pl.BlockSpec((TILE, width), rows)
    return call(
        body,
        "back",
        2 * block * width * heads,
        (own, hidden, cotangent, gain, weights, *branches, *grads),
        (block // TILE,),
        [scalar(), wide, wide, whole((1, width)), outward_spec(weights)] + [wide] * (2 * count),
        [
            wide,
            wide,
            pl.BlockSpec((width, TILE), lambda i: (0, i)),
            pl.BlockSpec((TILE, heads), rows),
            pl.BlockSpec((1, width), lambda i: (0, 0)),
        ],
        [
            out((block, width)),
            out((block, width), F32),
            out((width, block)),
            out((block, heads)),
            out((1, width), F32),
        ],
        [pltpu.VMEM((width, heads), BF16), pltpu.VMEM((width, TILE), BF16)],
        after=after,
    )


def unattend(base, sets, reach, query, grads, attended, keys, values, lse, query_marks, key_marks, cosine, sine, before, after=()):
    block, heads = query.shape
    tokens = keys.shape[0]
    wide = 2 * PAIR
    count = block // TILE

    def body(
        reach, q_ref, g_ref, o_ref, k_ref, v_ref, lse_ref, qm_ref, km_ref, cq_ref, sq_ref, ck_ref, sk_ref,
        dq_ref, dk_ref, dv_ref, keys_turned, dq_acc, dk_acc, dv_acc,
    ):
        at = pl.program_id(1)
        first, last, shift = reach[2 * at], reach[2 * at + 1], reach[2 * count]
        marks = jnp.concatenate([qm_ref[...], qm_ref[...]], axis=0)
        queries = q_ref[...].astype(F32) * SCALE
        grads = g_ref[...].astype(F32)
        product = (grads * o_ref[...].astype(F32)).T
        stacked, marked, stacked_grads, deltas = [], [], [], []
        for p in range(2):
            lanes = slice(p * PAIR, (p + 1) * PAIR)
            stacked.append(stack_pair(queries[:, lanes]))
            marked.append(jnp.concatenate([stacked[p], marks], axis=1))
            stacked_grads.append(stack_pair(grads[:, lanes]))
            sums = [
                jnp.sum(product[p * PAIR + h * HD : p * PAIR + (h + 1) * HD], axis=0, keepdims=True) for h in range(2)
            ]
            deltas.append(jnp.concatenate(sums, axis=1))
        dq_acc[...] = jnp.zeros_like(dq_acc)

        @pl.when(at == 0)
        def _():
            dk_acc[...] = jnp.zeros_like(dk_acc)
            dv_acc[...] = jnp.zeros_like(dv_acc)
            for tile in range(tokens // TILE):
                rows = slice(tile * TILE, (tile + 1) * TILE)
                keys_turned[:, rows] = k_ref[rows, :].astype(F32).T.astype(BF16)

        def step(tile, carry):
            rows = pl.ds(pl.multiple_of((tile ^ shift) * TILE, TILE), TILE)
            for p in range(2):
                lanes = slice(p * PAIR, (p + 1) * PAIR)
                scores = mm(jnp.concatenate([k_ref[rows, lanes], km_ref[rows, :]], axis=1), marked[p], NT)
                probs = jnp.exp(scores - lse_ref[0, 0, p : p + 1, :])
                prob_grads = mm(v_ref[rows, lanes], stacked_grads[p], NT)
                score_grads = (probs * (prob_grads - deltas[p])).astype(BF16)
                dv_acc[rows, lanes] += mm(probs.astype(BF16), stacked_grads[p])
                dk_acc[rows, lanes] += mm(score_grads, stacked[p])
                for h in range(2):
                    part = slice(p * PAIR + h * HD, p * PAIR + (h + 1) * HD)
                    dq_acc[part, :] += mm(keys_turned[part, rows], score_grads[:, h * TILE : (h + 1) * TILE])
            return carry

        lax.fori_loop(first, last, step, 0)
        grad = dq_acc[...].T * SCALE
        for lane in (0, PAIR):
            dq_ref[:, lane : lane + PAIR] = unturn(grad[:, lane : lane + PAIR], cq_ref[...], sq_ref[...]).astype(BF16)

        @pl.when(at == count - 1)
        def _():
            dv_ref[...] = dv_acc[...].astype(BF16)
            for lane in (0, PAIR):
                dk_ref[:, lane : lane + PAIR] = unturn(
                    dk_acc[:, lane : lane + PAIR], ck_ref[...], sk_ref[...]
                ).astype(BF16)

    tile = pl.BlockSpec((TILE, wide), lambda h, i, r: (i, base + h))
    full = pl.BlockSpec((tokens, wide), lambda h, i, r: (0, base + h))
    table = pl.BlockSpec((TILE, PAIR), lambda h, i, r: (i, 0))
    tables = pl.BlockSpec((tokens, PAIR), lambda h, i, r: (0, 0))
    return call(
        body,
        "unattend",
        10 * block * tokens * wide * sets,
        (reach, query, grads, attended, keys, values, lse, query_marks, key_marks, cosine, sine, cosine, sine),
        (sets, count),
        [
            tile,
            tile,
            tile,
            full,
            full,
            pl.BlockSpec((1, 1, 2, 2 * TILE), lambda h, i, r: (base + h, i, 0, 0)),
            table,
            tables,
            table,
            table,
            tables,
            tables,
        ],
        [
            tile,
            full,
            full,
        ],
        [out((block, heads)), out((tokens, heads)), out((tokens, heads))],
        [
            pltpu.VMEM((wide, tokens), BF16),
            pltpu.VMEM((wide, TILE), F32),
            pltpu.VMEM((tokens, wide), F32),
            pltpu.VMEM((tokens, wide), F32),
        ],
        prefetch=1,
        after=[*(before or ()), *after],
        aliases={13: 0, 14: 1, 15: 2} if before else {},
    )


def unproject(grads, x_full, k, block, weights, after=()):
    width = x_full.shape[1]
    heads = grads[0].shape[1]
    kinds = len(grads)
    groups, owners, piece, cols = weights.shape
    part = cols // 4
    base = k * block // TILE

    def body(x_ref, *refs):
        g_refs, (w_ref, da_ref, gg_ref, w_all) = refs[:kinds], refs[kinds:]

        @pl.when(pl.program_id(0) == 0)
        def _():
            gg_ref[...] = jnp.zeros_like(gg_ref)
            for m in range(kinds):
                column = (3 - kinds + m) * part
                for z in range(groups):
                    w_all[m, :, z * part : (z + 1) * part] = w_ref[z, :, :, column : column + part].reshape(width, part)

        grad = mm(g_refs[0][...], w_all[0], NT)
        for at in range(1, kinds):
            grad += mm(g_refs[at][...], w_all[at], NT)
        da_ref[...] = grad.astype(BF16)
        values = x_ref[...].astype(F32)
        gg_ref[...] += jnp.sum(grad * values * norm_rate(values), axis=0, keepdims=True)

    def place(array):
        return (lambda i: (i, 0)) if array.shape[0] == block else (lambda i: (base + i, 0))

    return call(
        body,
        "unproject",
        2 * kinds * block * width * heads,
        (x_full, *grads, weights),
        (block // TILE,),
        [pl.BlockSpec((TILE, width), lambda i: (base + i, 0))]
        + [pl.BlockSpec((TILE, heads), place(array)) for array in grads]
        + [inward_spec(weights)],
        [pl.BlockSpec((TILE, width), lambda i: (i, 0)), pl.BlockSpec((1, width), lambda i: (0, 0))],
        [out((block, width)), out((1, width), F32)],
        [pltpu.VMEM((kinds, width, heads), BF16)],
        after=after,
    )


def weigh(turned, cotangent_turned, dq, dk, dv, attended, x_full, weights, after=()):
    width, tokens = turned.shape
    block, heads = dq.shape
    groups, owners, piece, cols = weights.shape
    part = cols // 4
    half, near = width // 2, groups // 2
    tiles = block // TILE

    def body(
        at_ref, ct_ref, dq_ref, dk_ref, dv_ref, o_ref, x_ref, dq_row, dk_row, dv_row, w_ref,
        ga_near, gb_near, ga_far, gb_far, da_ref, gg_ref, w_all,
    ):
        at = pl.program_id(0)

        def write(targets):
            for ref, rows in zip(targets, (slice(0, half), slice(half, width))):
                ref[0, :, :part] = mm(at_ref[rows, :block], dq_ref[...]).astype(BF16)
                ref[0, :, part : 2 * part] = mm(at_ref[rows, :], dk_ref[...]).astype(BF16)
                ref[0, :, 2 * part : 3 * part] = mm(at_ref[rows, :], dv_ref[...]).astype(BF16)
                ref[0, :, 3 * part :] = mm(ct_ref[rows, :], o_ref[...]).astype(BF16)

        @pl.when(at < near)
        def _():
            write((ga_near, gb_near))

        @pl.when((at >= near) & (at < groups))
        def _():
            write((ga_far, gb_far))

        @pl.when(at == 0)
        def _():
            gg_ref[...] = jnp.zeros_like(gg_ref)
            for m in range(3):
                for z in range(groups):
                    w_all[m, :, z * part : (z + 1) * part] = w_ref[z, :, :, m * part : (m + 1) * part].reshape(width, part)

        @pl.when(at < tiles)
        def _():
            grad = mm(dq_row[...], w_all[0], NT)
            grad += mm(dk_row[...], w_all[1], NT)
            grad += mm(dv_row[...], w_all[2], NT)
            da_ref[...] = grad.astype(BF16)
            values = x_ref[...].astype(F32)
            gg_ref[...] += jnp.sum(grad * values * norm_rate(values), axis=0, keepdims=True)

    column = lambda i: (0, jnp.minimum(i, groups - 1))
    row = lambda i: (jnp.minimum(i, tiles - 1), 0)
    shape = (near, half, cols)
    near_spec = pl.BlockSpec((1, half, cols), lambda i: (jnp.minimum(i, near - 1), 0, 0))
    far_spec = pl.BlockSpec((1, half, cols), lambda i: (jnp.clip(i - near, 0, near - 1), 0, 0))
    return call(
        body,
        "weigh",
        4 * (tokens + block) * width * heads + 6 * block * width * heads,
        (turned, cotangent_turned, dq, dk, dv, attended, x_full, dq, dk, dv, weights),
        (max(groups, tiles),),
        [
            whole(turned.shape),
            whole(cotangent_turned.shape),
            pl.BlockSpec((block, part), column),
            pl.BlockSpec((tokens, part), column),
            pl.BlockSpec((tokens, part), column),
            pl.BlockSpec((block, part), column),
            pl.BlockSpec((TILE, width), row),
            pl.BlockSpec((TILE, heads), row),
            pl.BlockSpec((TILE, heads), row),
            pl.BlockSpec((TILE, heads), row),
            inward_spec(weights),
        ],
        [near_spec, near_spec, far_spec, far_spec, pl.BlockSpec((TILE, width), row), pl.BlockSpec((1, width), lambda i: (0, 0))],
        [out(shape)] * 4 + [out((block, width)), out((1, width), F32)],
        [pltpu.VMEM((3, width, heads), BF16)],
        after=after,
    )


def fold(kept, received, step, after=()):
    axis = None if step is None else 2 if step[0] == "seq" else 1
    shapes = [kept.shape]
    if axis is not None:
        half = kept.shape[axis] // 2
        shapes = [tuple(half if at == axis else n for at, n in enumerate(kept.shape))] * 2

    def body(kept_ref, received_ref, *refs):
        total = (kept_ref[...].astype(F32) + received_ref[...].astype(F32)).astype(BF16)
        if axis is None:
            refs[0][...] = total
        elif axis == 1:
            refs[0][...], refs[1][...] = total[:, :half], total[:, half:]
        else:
            refs[0][...], refs[1][...] = total[:, :, :half], total[:, :, half:]

    groups = kept.shape[0]
    run = next(n for n in range(groups, 0, -1) if groups % n == 0 and n * kept[0].size <= FOLD)
    spec = lambda shape: pl.BlockSpec((run, *shape[1:]), lambda g: (g, 0, 0, 0, 0))
    return call(
        body,
        "fold",
        kept.size,
        (kept, received),
        (groups // run,),
        [spec(kept.shape)] * 2,
        [spec(shape) for shape in shapes],
        [out(shape) for shape in shapes],
        after=after,
    )


def deliver(array, kind, after=()):
    rows, width = array.shape

    def body(x_ref, y_ref):
        y_ref[...] = x_ref[...].astype(kind)

    spec = pl.BlockSpec((2 * TILE, width), lambda i: (i, 0))
    return call(
        body, "deliver", rows * width, (array,), (rows // (2 * TILE),), [spec], [spec], [out(array.shape, kind)], after=after
    )[0]


def finish(x_full, hidden_grad, gain, parts, first, count, after=()):
    width = hidden_grad.shape[1]

    def body(x_ref, dh_ref, g_ref, *refs):
        grad = sum([ref[...].astype(F32) for ref in refs[1:-1]], refs[0][...].astype(F32))
        values = x_ref[...].astype(F32)
        rate = norm_rate(values)
        scaled = grad * g_ref[...]
        dot = jnp.mean(values * scaled, axis=-1, keepdims=True)
        refs[-1][...] = (dh_ref[...] + rate * scaled - values * (rate * rate * rate * dot)).astype(BF16)

    wide = pl.BlockSpec((TILE, width), lambda i: (first // TILE + i, 0))
    return call(
        body,
        "finish",
        16 * count * width,
        (x_full, hidden_grad, gain, *parts),
        (count // TILE,),
        [wide, wide, whole((1, width))] + [wide] * len(parts),
        [pl.BlockSpec((TILE, width), lambda i: (i, 0))],
        [out((count, width))],
        after=after,
    )[0]


def widen(target, fitting, first, block, right, left, before, after=()):
    count, width = right.shape
    rows = fitting * block
    step = min(2 * TILE, count)

    def body(target, right_ref, left_ref, y_ref):
        @pl.when(target[1] == 0)
        def _():
            y_ref[...] = left_ref[...].astype(F32)

        @pl.when(target[1] != 0)
        def _():
            y_ref[...] = right_ref[...].astype(F32)

    spec = pl.BlockSpec((step, width), lambda i, t: (i, 0))
    place = pl.BlockSpec((step, width), lambda i, t: (t[0] * (block // step) + first // step + i, 0))
    before = [] if before is None else [before]
    return call(
        body,
        "widen",
        count * width,
        (target, right, left),
        (count // step,),
        [spec, spec],
        [place],
        [out((rows, width), F32)],
        prefetch=1,
        after=[*before, *after],
        aliases={3: 0} if before else {},
    )[0]


def on_device(
    residual_in,
    grad_out,
    segment_lengths,
    attention_in,
    attention_out,
    expand,
    contract,
    gains,
    mean_attention_in,
    mean_attention_out,
    mean_expand,
    mean_contract,
    mean_gains,
    square_attention_in,
    square_attention_out,
    square_expand,
    square_contract,
    square_gains,
):
    span, copies = lax.axis_size("seq"), lax.axis_size("tensor")
    place, lane = lax.axis_index("seq"), lax.axis_index("tensor")
    rows, block, width = residual_in.shape
    tokens = span * block
    repeats = copies // rows
    row = lane // repeats
    piece = attention_in.shape[1]
    part = attention_in.shape[2]
    masks = owner_masks()
    index = lax.axis_index("dp") * span + place
    own = index.astype(jnp.int32)[None]
    near = copies // 2

    attention_piece = jnp.concatenate(
        [attention_in[0], attention_in[1], attention_in[2], attention_out.T], axis=1
    ).astype(BF16)
    feed_piece = jnp.stack([expand[0], expand[1], contract.T]).astype(BF16)
    x_own = lax.dynamic_index_in_dim(residual_in, row, 0, keepdims=False)
    cotangent = lax.dynamic_index_in_dim(grad_out, row, 0, keepdims=False)
    full_gains = gather_small(gains.astype(BF16).astype(F32))
    full_gains, x_own = lax.optimization_barrier((full_gains, x_own))
    x_parts = [x_own] + [exchange(x_own, ("seq", k)) for k in range(1, span)]
    everywhere = ("tensor", "dp", "seq")
    gain_one, gain_two = full_gains[:1], full_gains[1:]
    weights = gather_owners(attention_piece, everywhere)
    x_full = jnp.concatenate(x_parts, axis=0)
    chunks = 2
    cut = feed_piece.shape[2] // chunks
    feed_pieces = [feed_piece[:, :, at * cut : (at + 1) * cut] for at in range(chunks)]
    weights, feed_pieces, x_full, cotangent = lax.optimization_barrier((weights, feed_pieces, x_full, cotangent))
    feeds = [gather_owners(chunk, everywhere) for chunk in feed_pieces]

    lens = lax.dynamic_index_in_dim(segment_lengths, row, 0, keepdims=False)
    ends = jnp.cumsum(lens)
    starts = ends - lens
    blocks = place ^ jnp.arange(span, dtype=jnp.int32)
    places = (blocks[:, None] * block + jnp.arange(block, dtype=jnp.int32)[None, :]).reshape(tokens)
    segment = jnp.sum((places[:, None] >= ends[None, :]).astype(jnp.int32), axis=-1)
    picked = segment[:, None] == jnp.arange(lens.shape[0], dtype=jnp.int32)[None, :]
    begin = jnp.sum(jnp.where(picked, starts[None, :], 0), axis=-1)
    finish_at = jnp.sum(jnp.where(picked, ends[None, :], 0), axis=-1)
    freq = jnp.exp(jnp.arange(HD // 2, dtype=F32) * (-2.0 * jnp.log(10000.0) / HD))
    angle = (places - begin).astype(F32)[:, None] * freq
    cosine = jnp.tile(jnp.cos(angle), (1, PAIR // (HD // 2)))
    sine = jnp.tile(jnp.sin(angle), (1, PAIR // (HD // 2)))
    count = block // TILE
    firsts = begin[:block].reshape(count, TILE)[:, 0] // TILE
    lasts = (finish_at[:block].reshape(count, TILE)[:, -1] + TILE - 1) // TILE
    reach = jnp.concatenate(
        [jnp.stack([firsts, lasts], axis=1).reshape(-1), (place * (block // TILE))[None]]
    ).astype(jnp.int32)
    lanes = jnp.arange(PAIR, dtype=jnp.int32)[None, :]
    key_marks = jnp.where(segment[:, None] == lanes, NEG, 0.0).astype(BF16)
    query_marks = ((segment[:block, None] != lanes) & (lanes < lens.shape[0])).astype(BF16)

    turned_one, query, keys, values = project(own, masks, x_full, gain_one, cosine, sine, weights, block)
    attended, lse = attend(reach, query, keys, values, query_marks, key_marks)
    hidden, normed_two, turned_two, rounded, rounded_turned = lift(
        own, masks, attended, x_full, cotangent, gain_two, weights
    )

    def spread(array):
        half, columns = array.shape[-2:]
        return array.reshape(-1, half // (span * piece), span, piece, columns)

    last_step = axis_steps()[2]
    orders = [scatter_order(bool(at % 2)) for at in range(chunks)]
    flights, places, branches, grads = [], [0] * chunks, [], []

    def tie(anchor, *which):
        *tied, anchor = lax.optimization_barrier((*[flights[at] for at in which], anchor))
        for at, flight in zip(which, tied):
            flights[at] = tuple(flight) if isinstance(flight, (tuple, list)) else flight

    def move_on(*which):
        for at in which:
            if places[at] < len(orders[at]):
                step = orders[at][places[at]]
                kept, sent = fold(*flights[at], step)
                flights[at] = (kept, exchange(sent, step))
                places[at] += 1
            elif isinstance(flights[at], tuple):
                flights[at] = fold(*flights[at], None)[0]
        return [flights[at][0] if isinstance(flights[at], tuple) else flights[at] for at in which]

    for at in range(chunks):
        branch, grad, kept, sent = feed(normed_two, turned_two, rounded, rounded_turned, feeds[at], 0, cut, after=branches)
        flights.append((spread(kept), spread(exchange(sent, last_step))))
        branches.append(branch)
        grads.append(grad)
    result, hidden_grad, hidden_grad_turned, output_grad, grad_gain_two = back(
        own, masks, hidden, branches, grads, cotangent, gain_two, weights
    )
    tie(output_grad, 0, 1)
    residual_out = lax.all_gather(result, "tensor", axis=0)
    common = (reach, query, output_grad, attended, keys, values, lse, query_marks, key_marks, cosine, sine)
    sets = query.shape[1] // (2 * PAIR)
    found = unattend(0, sets - 1, *common, None, after=move_on(0, 1))
    tie(found[0], 0, 1)
    after = []
    for _ in orders[0][1:]:
        after = move_on(0, 1)
    dq, dk, dv = unattend(sets - 1, 1, *common, found, after=after)
    tie(dq, 0, 1)
    move_on(0, 1)
    feed_sums = jnp.concatenate([flight.reshape(copies, -1, piece, cut) for flight in flights], axis=-1)
    distances = list(range(1, copies))

    parts, gain_parts = [], []
    for k in range(1, span):
        grad, gain_part = unproject([dk, dv], x_full, k, block, weights, after=[feed_sums])
        parts.append(exchange(grad, ("seq", k)))
        gain_parts.append(gain_part)
    received = tensor_sends(feed_sums, distances)
    places = [0, 0]
    *found, own_grad, gain_part = weigh(
        turned_one, hidden_grad_turned, dq, dk, dv, attended, x_full, weights, after=gain_parts
    )
    gain_parts.append(gain_part)
    flights = [(spread(found[at]), spread(exchange(found[at + 1], last_step))) for at in (0, 2)]
    steady = [*received, residual_out]
    shares = 1
    size = block // shares
    lines = []
    for at in range(shares):
        own_rows = finish(x_full, hidden_grad, gain_one, [own_grad] + parts, at * size, size, after=steady)
        lines.append([(own_rows, own_rows)])
    up = [(i, i + 1) for i in range(copies - 1)]
    down = [(i + 1, i) for i in range(copies - 1)]

    def hop(count):
        for _ in range(count):
            for line in lines:
                from_low, from_high = line[-1]
                line.append((lax.ppermute(from_low, "tensor", up), lax.ppermute(from_high, "tensor", down)))

    hop(2)
    tie(lines[-1][0][0], 0, 1)
    while isinstance(flights[1], tuple):
        move_on(0, 1)
    attention_sums = jnp.concatenate(flights)
    attention_sums = attention_sums.reshape(copies, piece, 4 * part)
    attention_sums, lines[0][2] = lax.optimization_barrier((attention_sums, lines[0][2]))
    hop(copies - 3)
    grad_in = None
    for distance in range(copies):
        source = lax.rem(lane - distance + copies, copies)
        target = jnp.stack([source // repeats, (source > lane).astype(jnp.int32)]).astype(jnp.int32)
        for at, line in enumerate(lines):
            from_low, from_high = line[distance][0], line[(copies - distance) % copies][1]
            grad_in = widen(target, rows, at * size, block, from_high, from_low, grad_in)
    attention_shard = tensor_sum(attention_sums, tensor_sends(attention_sums, distances))
    feed_shard = tensor_sum(feed_sums, received)
    residual_out = residual_out[::repeats] if repeats > 1 else residual_out
    residual_out = deliver(residual_out.reshape(-1, width), BF16, after=[lines[-1][0][0]])
    residual_out, grad_in = residual_out.reshape(rows, block, width), grad_in.reshape(rows, block, width)

    share = 1.0 / repeats
    attention_shard, feed_shard = attention_shard * share, feed_shard * share
    gain_grads = jnp.concatenate([sum(gain_parts), grad_gain_two]) * share
    gain_grads = sum_everywhere(gain_grads)
    gain_shard = lax.dynamic_slice_in_dim(gain_grads, index * piece, piece, 1)

    local = jnp.sum(attention_shard * attention_shard) + jnp.sum(feed_shard * feed_shard)
    norm = jnp.sqrt(sum_everywhere(jnp.full((8, 128), local))[0, 0] + jnp.sum(gain_grads * gain_grads))
    factor = jnp.minimum(1.0, CLIP / norm)
    shards = (
        jnp.stack([attention_shard[:, k * part : (k + 1) * part] for k in range(3)]),
        attention_shard[:, 3 * part :].T,
        feed_shard[:2],
        feed_shard[2].T,
        gain_shard,
    )
    masters = (attention_in, attention_out, expand, contract, gains)
    firsts = (mean_attention_in, mean_attention_out, mean_expand, mean_contract, mean_gains)
    seconds = (
        square_attention_in,
        square_attention_out,
        square_expand,
        square_contract,
        square_gains,
    )
    new_means = []
    new_squares = []
    new_weights = []
    for member in range(5):
        clipped = shards[member] * factor
        moment = BETA_ONE * firsts[member] + (1.0 - BETA_ONE) * clipped
        square = BETA_TWO * seconds[member] + (1.0 - BETA_TWO) * clipped * clipped
        update = (
            moment / (1.0 - BETA_ONE**STEP) / (jnp.sqrt(square / (1.0 - BETA_TWO**STEP)) + ADAM_EPS)
        )
        shrink = DECAY if member < 4 else 0.0
        speed = RATE if member < 4 else GAIN_RATE
        new_means.append(moment)
        new_squares.append(square)
        new_weights.append(masters[member] - speed * (update + shrink * masters[member]))
    return (residual_out, grad_in, norm, *new_means, *new_squares, *new_weights)


def solution(mesh):
    tokens = P("dp", "seq", None)
    weights = (
        P(None, ("dp", "seq"), "tensor"),
        P("tensor", ("dp", "seq")),
        P(None, ("dp", "seq"), "tensor"),
        P("tensor", ("dp", "seq")),
        P(None, ("dp", "seq")),
    )
    return jax.shard_map(
        on_device,
        mesh=mesh,
        in_specs=(tokens, tokens, P("dp", None)) + weights * 3,
        out_specs=(tokens, tokens, P()) + weights * 3,
        check_vma=False,
    )
```

```python
import jax
import jax.numpy as jnp
from jax import lax
from jax.experimental import pallas as pl
from jax.experimental.pallas import tpu as pltpu
from jax.sharding import PartitionSpec as P

HD = 64
STEP = 10

NORM_EPS = 1e-05
NEG = -1e30
CLIP = 1.0
RATE = 0.04
GAIN_RATE = 1.0
BETA_ONE = 0.9
BETA_TWO = 0.999
ADAM_EPS = 1e-08
DECAY = 0.1

SCALE = HD ** (-0.5)
PAIR = 2 * HD
TILE = 256
VMEM = 60 * 1024 * 1024
FOLD = 1024 * 1024
F32 = jnp.float32
BF16 = jnp.bfloat16

NN = (((1,), (0,)), ((), ()))
NT = (((1,), (1,)), ((), ()))
TN = (((0,), (0,)), ((), ()))


def mm(left, right, dims=NN):
    return lax.dot_general(left, right, dims, preferred_element_type=F32)


def call(body, name, flops, args, grid, in_specs, out_specs, out_shape, scratch=(), prefetch=0, after=(), aliases={}):
    count, extra = len(args), len(after)
    moved = sum(a.size * a.dtype.itemsize for a in args) + sum(o.size * o.dtype.itemsize for o in out_shape)
    return pl.pallas_call(
        lambda *refs: body(*refs[:count], *refs[count + extra :]),
        name=name,
        grid_spec=pltpu.PrefetchScalarGridSpec(
            num_scalar_prefetch=prefetch,
            grid=grid,
            in_specs=list(in_specs) + [pl.BlockSpec(memory_space=pl.ANY)] * extra,
            out_specs=out_specs,
            scratch_shapes=list(scratch),
        ),
        out_shape=out_shape,
        input_output_aliases=dict(aliases),
        compiler_params=pltpu.CompilerParams(vmem_limit_bytes=VMEM),
        cost_estimate=pl.CostEstimate(flops=int(flops) >> 24, bytes_accessed=int(moved) >> 20, transcendentals=0),
    )(*args, *after)


def whole(shape):
    return pl.BlockSpec(shape, lambda *at: (0,) * len(shape), pipeline_mode=pl.Buffered(1))


def scalar():
    return pl.BlockSpec(memory_space=pltpu.SMEM)


def out(shape, kind=BF16):
    return jax.ShapeDtypeStruct(shape, kind)


def exchange(block, step):
    axis, bit = step
    return lax.ppermute(block, axis, [(i ^ bit, i) for i in range(lax.axis_size(axis))])


def axis_steps():
    bits = lambda axis: [(axis, 1 << k) for k in range(lax.axis_size(axis).bit_length() - 1)]
    across = bits("dp")
    return bits("seq"), across[1:], across[0]


def owner_masks():
    span = lax.axis_size("seq")
    along, across, last = axis_steps()
    masks = [0]
    for axis, bit in along + across + [last]:
        masks += [m ^ (bit if axis == "seq" else bit * span) for m in masks]
    return masks


def gather_owners(array, axes):
    whole_array = lax.all_gather(array, axes, axis=0)
    return whole_array.reshape(lax.axis_size(axes[0]), -1, *array.shape)


def gather_small(array):
    along, across, last = axis_steps()
    for step in along + [last] + across:
        other = exchange(array, step)
        pair, swapped = jnp.concatenate([array, other], axis=1), jnp.concatenate([other, array], axis=1)
        array = jnp.where(lax.axis_index(step[0]) & step[1], swapped, pair)
    return array


def sum_over(array, axes):
    for axis in axes:
        for k in range(lax.axis_size(axis).bit_length() - 1):
            array = array + exchange(array, (axis, 1 << k))
    return array


def scatter_order(along_first):
    along, across, _ = axis_steps()
    ordered = [list(reversed(along)), list(reversed(across))]
    return ordered[0] + ordered[1] if along_first else ordered[1] + ordered[0]


def tensor_sends(held, distances):
    size, here = lax.axis_size("tensor"), lax.axis_index("tensor")
    return [
        lax.ppermute(
            lax.dynamic_index_in_dim(held, lax.rem(here + k, size), 0, keepdims=False),
            "tensor",
            [(i, (i + k) % size) for i in range(size)],
        )
        for k in distances
    ]


def tensor_sum(held, received):
    own = lax.dynamic_index_in_dim(held, lax.axis_index("tensor"), 0, keepdims=False).astype(F32)
    return sum([array.astype(F32) for array in received], own)


def row_block(own, mask, piece):
    return pl.ds(pl.multiple_of((own ^ mask) * piece, piece), piece)


def store_turned(own, masks, ref, values, scratch):
    scratch[...] = values.T.astype(BF16)
    piece = scratch.shape[0] // len(masks)
    for j, mask in enumerate(masks):
        ref[j * piece : (j + 1) * piece, :] = scratch[row_block(own, mask, piece), :]


def swap_halves(values):
    lane = lax.broadcasted_iota(jnp.int32, values.shape, 1)
    size = values.shape[1]
    ahead = pltpu.roll(values, size - HD // 2, 1)
    behind = pltpu.roll(values, HD // 2, 1)
    return jnp.where(lane % HD < HD // 2, ahead, behind)


def half_sign(shape):
    lane = lax.broadcasted_iota(jnp.int32, shape, 1)
    return jnp.where(lane % HD < HD // 2, -1.0, 1.0)


def turn(values, cosine, sine):
    return values * cosine + swap_halves(values) * (sine * half_sign(values.shape))


def unturn(values, cosine, sine):
    return values * cosine - swap_halves(values * sine) * half_sign(values.shape)


def pair_lanes(values, head):
    lane = lax.broadcasted_iota(jnp.int32, values.shape, 1)
    return jnp.where((lane < HD) == (head == 0), values, 0.0)


def stack_pair(values):
    return jnp.concatenate([pair_lanes(values, 0), pair_lanes(values, 1)], axis=0).astype(BF16)


def norm_rate(values):
    return lax.rsqrt(jnp.mean(values * values, axis=-1, keepdims=True) + NORM_EPS)


def inward_spec(weights):
    groups, owners, piece, cols = weights.shape
    return pl.BlockSpec((groups, owners, piece, cols // 4 * 3), lambda *at: (0, 0, 0, 0), pipeline_mode=pl.Buffered(1))


def outward_spec(weights):
    groups, owners, piece, cols = weights.shape
    return pl.BlockSpec((groups, owners, piece, cols // 4), lambda *at: (0, 0, 0, 3), pipeline_mode=pl.Buffered(1))


def outward(w_ref, w_all):
    groups, owners, piece, part = w_ref.shape
    for z in range(groups):
        w_all[:, z * part : (z + 1) * part] = w_ref[z].reshape(owners * piece, part)


def project(own, masks, x_full, gain, cosine, sine, weights, block):
    tokens, width = x_full.shape
    groups, owners, piece, cols = weights.shape
    part = cols // 4
    heads = groups * part
    mine = block // TILE

    def body(own_ref, x_ref, g_ref, cos_ref, sin_ref, w_ref, at_ref, q_ref, k_ref, v_ref, a_one, turned):
        own = own_ref[0]

        values = x_ref[...].astype(F32)
        normed = values * norm_rate(values) * g_ref[...]
        a_one[...] = normed.astype(BF16)
        store_turned(own, masks, at_ref, normed, turned)
        cosine, sine = cos_ref[...], sin_ref[...]

        def product(z, m):
            return mm(a_one[...], w_ref[z, :, :, m * part : (m + 1) * part].reshape(width, part))

        def rotated(ref, m):
            for z in range(groups):
                mixed = product(z, m)
                for lane in range(0, part, PAIR):
                    ref[:, z * part + lane : z * part + lane + PAIR] = turn(
                        mixed[:, lane : lane + PAIR], cosine, sine
                    ).astype(BF16)

        rotated(k_ref, 1)
        for z in range(groups):
            v_ref[:, z * part : (z + 1) * part] = product(z, 2).astype(BF16)

        @pl.when(pl.program_id(0) < mine)
        def _():
            rotated(q_ref, 0)

    rows = lambda i: (i, 0)
    return call(
        body,
        "project",
        2 * (2 * tokens + block) * width * heads,
        (own, x_full, gain, cosine, sine, weights),
        (tokens // TILE,),
        [
            scalar(),
            pl.BlockSpec((TILE, width), rows),
            whole((1, width)),
            pl.BlockSpec((TILE, PAIR), rows),
            pl.BlockSpec((TILE, PAIR), rows),
            inward_spec(weights),
        ],
        [
            pl.BlockSpec((width, TILE), lambda i: (0, i)),
            pl.BlockSpec((TILE, heads), lambda i: (jnp.minimum(i, mine - 1), 0)),
            pl.BlockSpec((TILE, heads), rows),
            pl.BlockSpec((TILE, heads), rows),
        ],
        [out((width, tokens)), out((block, heads)), out((tokens, heads)), out((tokens, heads))],
        [pltpu.VMEM((TILE, width), BF16), pltpu.VMEM((width, TILE), BF16)],
    )


def attend(reach, query, keys, values, query_marks, key_marks):
    block, heads = query.shape
    tokens = keys.shape[0]
    wide = 2 * PAIR
    count = block // TILE

    def body(reach, q_ref, k_ref, v_ref, qm_ref, km_ref, o_ref, lse_ref, turned, acc, top, total, kept):
        at = pl.program_id(1)
        first, last, shift = reach[2 * at], reach[2 * at + 1], reach[2 * count]

        @pl.when(at == 0)
        def _():
            for tile in range(tokens // TILE):
                rows = slice(tile * TILE, (tile + 1) * TILE)
                turned[:, rows] = v_ref[rows, :].astype(F32).T.astype(BF16)

        marks = jnp.concatenate([qm_ref[...], qm_ref[...]], axis=0)
        stacked = [
            jnp.concatenate([stack_pair(q_ref[:, p * PAIR : (p + 1) * PAIR].astype(F32) * SCALE), marks], axis=1)
            for p in range(2)
        ]
        top[...] = jnp.full_like(top, NEG)
        acc[...] = jnp.zeros_like(acc)
        total[...] = jnp.zeros_like(total)

        def by_eight(values):
            return values.reshape(values.shape[0] // 8, 8, values.shape[1])

        def score(tile, carry):
            rows = pl.ds(pl.multiple_of((tile ^ shift) * TILE, TILE), TILE)
            for p in range(2):
                lanes = slice(p * PAIR, (p + 1) * PAIR)
                scores = mm(jnp.concatenate([k_ref[rows, lanes], km_ref[rows, :]], axis=1), stacked[p], NT)
                kept[p, rows, :] = scores
                top[p] = jnp.maximum(top[p], jnp.max(by_eight(scores), axis=0))
            return carry

        lax.fori_loop(first, last, score, 0)
        tops = [jnp.max(top[p], axis=0, keepdims=True) for p in range(2)]

        def step(tile, carry):
            rows = pl.ds(pl.multiple_of((tile ^ shift) * TILE, TILE), TILE)
            for p in range(2):
                probs = jnp.exp(kept[p, rows, :] - tops[p])
                total[p] += jnp.sum(by_eight(probs), axis=0)
                probs = probs.astype(BF16)
                for h in range(2):
                    part = slice(p * PAIR + h * HD, p * PAIR + (h + 1) * HD)
                    acc[part, :] += mm(turned[part, rows], probs[:, h * TILE : (h + 1) * TILE])
            return carry

        lax.fori_loop(first, last, step, 0)
        for p in range(2):
            sums = jnp.sum(total[p], axis=0, keepdims=True)
            rate = 1.0 / sums
            for h in range(2):
                part = slice(p * PAIR + h * HD, p * PAIR + (h + 1) * HD)
                acc[part, :] = acc[part, :] * rate[:, h * TILE : (h + 1) * TILE]
            lse_ref[0, 0, p : p + 1, :] = tops[p] + jnp.log(sums)
        o_ref[...] = acc[...].T.astype(BF16)

    return call(
        body,
        "attend",
        4 * block * tokens * heads,
        (reach, query, keys, values, query_marks, key_marks),
        (heads // wide, count),
        [
            pl.BlockSpec((TILE, wide), lambda h, i, r: (i, h)),
            pl.BlockSpec((tokens, wide), lambda h, i, r: (0, h)),
            pl.BlockSpec((tokens, wide), lambda h, i, r: (0, h)),
            pl.BlockSpec((TILE, PAIR), lambda h, i, r: (i, 0)),
            pl.BlockSpec((tokens, PAIR), lambda h, i, r: (0, 0)),
        ],
        [
            pl.BlockSpec((TILE, wide), lambda h, i, r: (i, h)),
            pl.BlockSpec((1, 1, 2, 2 * TILE), lambda h, i, r: (h, i, 0, 0)),
        ],
        [out((block, heads)), out((heads // wide, count, 2, 2 * TILE), F32)],
        [
            pltpu.VMEM((wide, tokens), BF16),
            pltpu.VMEM((wide, TILE), F32),
            pltpu.VMEM((2, 8, 2 * TILE), F32),
            pltpu.VMEM((2, 8, 2 * TILE), F32),
            pltpu.VMEM((2, tokens, 2 * TILE), F32),
        ],
        prefetch=1,
    )


def lift(own, masks, attended, x_full, cotangent, gain, weights):
    block, heads = attended.shape
    width = x_full.shape[1]

    def body(own_ref, o_ref, x_ref, c_ref, g_ref, w_ref, h_ref, a_ref, at_ref, e_ref, et_ref, w_all, turned):
        own = own_ref[0]

        @pl.when(pl.program_id(0) == 0)
        def _():
            outward(w_ref, w_all)

        values = x_ref[...].astype(F32) + mm(o_ref[...], w_all[...], NT)
        h_ref[...] = values
        normed = values * norm_rate(values) * g_ref[...]
        a_ref[...] = normed.astype(BF16)
        store_turned(own, masks, at_ref, normed, turned)
        cotangent = c_ref[...]
        e_ref[...] = cotangent.astype(BF16)
        store_turned(own, masks, et_ref, cotangent, turned)

    rows = lambda i: (i, 0)
    wide = pl.BlockSpec((TILE, width), rows)
    tall = pl.BlockSpec((width, TILE), lambda i: (0, i))
    return call(
        body,
        "lift",
        2 * block * width * heads,
        (own, attended, x_full, cotangent, gain, weights),
        (block // TILE,),
        [scalar(), pl.BlockSpec((TILE, heads), rows), wide, wide, whole((1, width)), outward_spec(weights)],
        [wide, wide, tall, wide, tall],
        [out((block, width), F32), out((block, width)), out((width, block)), out((block, width)), out((width, block))],
        [pltpu.VMEM((width, heads), BF16), pltpu.VMEM((width, TILE), BF16)],
    )


def feed(normed, turned, cotangent, cotangent_turned, weights, chunk, hidden, after=()):
    block, width = normed.shape
    groups, owners, kinds, piece, _ = weights.shape
    half = width // 2
    cut = min(512, hidden)
    tile = min(512, block)

    def body(a_ref, at_ref, e_ref, et_ref, w_ref, b_out, d_out, ga_ref, gb_ref, b_ref, d_ref, mid, dgate, dup):
        @pl.when((pl.program_id(0) == 0) & (pl.program_id(1) == 0))
        def _():
            b_ref[...] = jnp.zeros_like(b_ref)
            d_ref[...] = jnp.zeros_like(d_ref)

        def weight(m):
            return w_ref[0, :, m].reshape(width, cut)

        def tokens(i, carry):
            rows = pl.ds(pl.multiple_of(i * tile, tile), tile)
            gate = mm(a_ref[rows, :], weight(0))
            upper = mm(a_ref[rows, :], weight(1))
            grad = mm(e_ref[rows, :], weight(2))
            sigma = jax.nn.sigmoid(gate)
            active = gate * sigma
            mid[rows, :] = (active * upper).astype(BF16)
            dgate[rows, :] = (grad * upper * (sigma * (1.0 + gate * (1.0 - sigma)))).astype(BF16)
            dup[rows, :] = (grad * active).astype(BF16)
            b_ref[rows, :] += mm(mid[rows, :], weight(2), NT)
            d_ref[rows, :] += mm(dgate[rows, :], weight(0), NT) + mm(dup[rows, :], weight(1), NT)
            return carry

        lax.fori_loop(0, block // tile, tokens, 0)
        for ref, rows in ((ga_ref, slice(0, half)), (gb_ref, slice(half, width))):
            ref[0, 0] = mm(at_ref[rows, :], dgate[...]).astype(BF16)
            ref[0, 1] = mm(at_ref[rows, :], dup[...]).astype(BF16)
            ref[0, 2] = mm(et_ref[rows, :], mid[...]).astype(BF16)

        @pl.when((pl.program_id(0) == groups - 1) & (pl.program_id(1) == hidden // cut - 1))
        def _():
            b_out[...] = b_ref[...].astype(BF16)
            d_out[...] = d_ref[...].astype(BF16)

    place = lambda z, j: (z, 0, 0, j)
    shape = (groups, kinds, half, hidden)
    return call(
        body,
        "feed",
        18 * block * width * hidden * groups,
        (normed, turned, cotangent, cotangent_turned, weights),
        (groups, hidden // cut),
        [
            whole((block, width)),
            whole((width, block)),
            whole((block, width)),
            whole((width, block)),
            pl.BlockSpec((1, owners, kinds, piece, cut), lambda z, j: (z, 0, 0, 0, chunk * (hidden // cut) + j)),
        ],
        [
            whole((block, width)),
            whole((block, width)),
            pl.BlockSpec((1, kinds, half, cut), place),
            pl.BlockSpec((1, kinds, half, cut), place),
        ],
        [out((block, width)), out((block, width)), out(shape), out(shape)],
        [pltpu.VMEM((block, width), F32)] * 2 + [pltpu.VMEM((block, cut), BF16)] * 3,
        after=after,
    )


def back(own, masks, hidden, branches, grads, cotangent, gain, weights, after=()):
    block, width = hidden.shape
    groups, owners, piece, cols = weights.shape
    heads = groups * cols // 4

    count = len(branches)

    def body(own_ref, h_ref, c_ref, g_ref, w_ref, *refs):
        b_refs, d_refs, refs = refs[:count], refs[count : 2 * count], refs[2 * count :]
        y_ref, dh_ref, ct_ref, do_ref, gg_ref, w_all, turned = refs
        own = own_ref[0]

        @pl.when(pl.program_id(0) == 0)
        def _():
            outward(w_ref, w_all)
            gg_ref[...] = jnp.zeros_like(gg_ref)

        hidden = h_ref[...]
        grad = sum([ref[...].astype(F32) for ref in d_refs[1:]], d_refs[0][...].astype(F32))
        y_ref[...] = sum([ref[...].astype(F32) for ref in b_refs], hidden).astype(BF16)
        rate = norm_rate(hidden)
        scaled = grad * g_ref[...]
        dot = jnp.mean(hidden * scaled, axis=-1, keepdims=True)
        result = c_ref[...] + rate * scaled - hidden * (rate * rate * rate * dot)
        dh_ref[...] = result
        store_turned(own, masks, ct_ref, result, turned)
        do_ref[...] = mm(result.astype(BF16), w_all[...]).astype(BF16)
        gg_ref[...] += jnp.sum(grad * hidden * rate, axis=0, keepdims=True)

    rows = lambda i: (i, 0)
    wide = pl.BlockSpec((TILE, width), rows)
    return call(
        body,
        "back",
        2 * block * width * heads,
        (own, hidden, cotangent, gain, weights, *branches, *grads),
        (block // TILE,),
        [scalar(), wide, wide, whole((1, width)), outward_spec(weights)] + [wide] * (2 * count),
        [
            wide,
            wide,
            pl.BlockSpec((width, TILE), lambda i: (0, i)),
            pl.BlockSpec((TILE, heads), rows),
            pl.BlockSpec((1, width), lambda i: (0, 0)),
        ],
        [
            out((block, width)),
            out((block, width), F32),
            out((width, block)),
            out((block, heads)),
            out((1, width), F32),
        ],
        [pltpu.VMEM((width, heads), BF16), pltpu.VMEM((width, TILE), BF16)],
        after=after,
    )


def unattend(base, sets, reach, query, grads, attended, keys, values, lse, query_marks, key_marks, cosine, sine, before, after=()):
    block, heads = query.shape
    tokens = keys.shape[0]
    wide = 2 * PAIR
    count = block // TILE

    def body(
        reach, q_ref, g_ref, o_ref, k_ref, v_ref, lse_ref, qm_ref, km_ref, cq_ref, sq_ref, ck_ref, sk_ref,
        dq_ref, dk_ref, dv_ref, keys_turned, dq_acc, dk_acc, dv_acc,
    ):
        at = pl.program_id(1)
        first, last, shift = reach[2 * at], reach[2 * at + 1], reach[2 * count]
        marks = jnp.concatenate([qm_ref[...], qm_ref[...]], axis=0)
        queries = q_ref[...].astype(F32) * SCALE
        grads = g_ref[...].astype(F32)
        product = (grads * o_ref[...].astype(F32)).T
        stacked, marked, stacked_grads, deltas = [], [], [], []
        for p in range(2):
            lanes = slice(p * PAIR, (p + 1) * PAIR)
            stacked.append(stack_pair(queries[:, lanes]))
            marked.append(jnp.concatenate([stacked[p], marks], axis=1))
            stacked_grads.append(stack_pair(grads[:, lanes]))
            sums = [
                jnp.sum(product[p * PAIR + h * HD : p * PAIR + (h + 1) * HD], axis=0, keepdims=True) for h in range(2)
            ]
            deltas.append(jnp.concatenate(sums, axis=1))
        dq_acc[...] = jnp.zeros_like(dq_acc)

        @pl.when(at == 0)
        def _():
            dk_acc[...] = jnp.zeros_like(dk_acc)
            dv_acc[...] = jnp.zeros_like(dv_acc)
            for tile in range(tokens // TILE):
                rows = slice(tile * TILE, (tile + 1) * TILE)
                keys_turned[:, rows] = k_ref[rows, :].astype(F32).T.astype(BF16)

        def step(tile, carry):
            rows = pl.ds(pl.multiple_of((tile ^ shift) * TILE, TILE), TILE)
            for p in range(2):
                lanes = slice(p * PAIR, (p + 1) * PAIR)
                scores = mm(jnp.concatenate([k_ref[rows, lanes], km_ref[rows, :]], axis=1), marked[p], NT)
                probs = jnp.exp(scores - lse_ref[0, 0, p : p + 1, :])
                prob_grads = mm(v_ref[rows, lanes], stacked_grads[p], NT)
                score_grads = (probs * (prob_grads - deltas[p])).astype(BF16)
                dv_acc[rows, lanes] += mm(probs.astype(BF16), stacked_grads[p])
                dk_acc[rows, lanes] += mm(score_grads, stacked[p])
                for h in range(2):
                    part = slice(p * PAIR + h * HD, p * PAIR + (h + 1) * HD)
                    dq_acc[part, :] += mm(keys_turned[part, rows], score_grads[:, h * TILE : (h + 1) * TILE])
            return carry

        lax.fori_loop(first, last, step, 0)
        grad = dq_acc[...].T * SCALE
        for lane in (0, PAIR):
            dq_ref[:, lane : lane + PAIR] = unturn(grad[:, lane : lane + PAIR], cq_ref[...], sq_ref[...]).astype(BF16)

        @pl.when(at == count - 1)
        def _():
            dv_ref[...] = dv_acc[...].astype(BF16)
            for lane in (0, PAIR):
                dk_ref[:, lane : lane + PAIR] = unturn(
                    dk_acc[:, lane : lane + PAIR], ck_ref[...], sk_ref[...]
                ).astype(BF16)

    tile = pl.BlockSpec((TILE, wide), lambda h, i, r: (i, base + h))
    full = pl.BlockSpec((tokens, wide), lambda h, i, r: (0, base + h))
    table = pl.BlockSpec((TILE, PAIR), lambda h, i, r: (i, 0))
    tables = pl.BlockSpec((tokens, PAIR), lambda h, i, r: (0, 0))
    return call(
        body,
        "unattend",
        10 * block * tokens * wide * sets,
        (reach, query, grads, attended, keys, values, lse, query_marks, key_marks, cosine, sine, cosine, sine),
        (sets, count),
        [
            tile,
            tile,
            tile,
            full,
            full,
            pl.BlockSpec((1, 1, 2, 2 * TILE), lambda h, i, r: (base + h, i, 0, 0)),
            table,
            tables,
            table,
            table,
            tables,
            tables,
        ],
        [
            tile,
            full,
            full,
        ],
        [out((block, heads)), out((tokens, heads)), out((tokens, heads))],
        [
            pltpu.VMEM((wide, tokens), BF16),
            pltpu.VMEM((wide, TILE), F32),
            pltpu.VMEM((tokens, wide), F32),
            pltpu.VMEM((tokens, wide), F32),
        ],
        prefetch=1,
        after=[*(before or ()), *after],
        aliases={13: 0, 14: 1, 15: 2} if before else {},
    )


def unproject(grads, x_full, k, block, weights, after=()):
    width = x_full.shape[1]
    heads = grads[0].shape[1]
    kinds = len(grads)
    groups, owners, piece, cols = weights.shape
    part = cols // 4
    base = k * block // TILE

    def body(x_ref, *refs):
        g_refs, (w_ref, da_ref, gg_ref, w_all) = refs[:kinds], refs[kinds:]

        @pl.when(pl.program_id(0) == 0)
        def _():
            gg_ref[...] = jnp.zeros_like(gg_ref)
            for m in range(kinds):
                column = (3 - kinds + m) * part
                for z in range(groups):
                    w_all[m, :, z * part : (z + 1) * part] = w_ref[z, :, :, column : column + part].reshape(width, part)

        grad = mm(g_refs[0][...], w_all[0], NT)
        for at in range(1, kinds):
            grad += mm(g_refs[at][...], w_all[at], NT)
        da_ref[...] = grad.astype(BF16)
        values = x_ref[...].astype(F32)
        gg_ref[...] += jnp.sum(grad * values * norm_rate(values), axis=0, keepdims=True)

    def place(array):
        return (lambda i: (i, 0)) if array.shape[0] == block else (lambda i: (base + i, 0))

    return call(
        body,
        "unproject",
        2 * kinds * block * width * heads,
        (x_full, *grads, weights),
        (block // TILE,),
        [pl.BlockSpec((TILE, width), lambda i: (base + i, 0))]
        + [pl.BlockSpec((TILE, heads), place(array)) for array in grads]
        + [inward_spec(weights)],
        [pl.BlockSpec((TILE, width), lambda i: (i, 0)), pl.BlockSpec((1, width), lambda i: (0, 0))],
        [out((block, width)), out((1, width), F32)],
        [pltpu.VMEM((kinds, width, heads), BF16)],
        after=after,
    )


def weigh(turned, cotangent_turned, dq, dk, dv, attended, x_full, weights, after=()):
    width, tokens = turned.shape
    block, heads = dq.shape
    groups, owners, piece, cols = weights.shape
    part = cols // 4
    half, near = width // 2, groups // 2
    tiles = block // TILE

    def body(
        at_ref, ct_ref, dq_ref, dk_ref, dv_ref, o_ref, x_ref, dq_row, dk_row, dv_row, w_ref,
        ga_near, gb_near, ga_far, gb_far, da_ref, gg_ref, w_all,
    ):
        at = pl.program_id(0)

        def write(targets):
            for ref, rows in zip(targets, (slice(0, half), slice(half, width))):
                ref[0, :, :part] = mm(at_ref[rows, :block], dq_ref[...]).astype(BF16)
                ref[0, :, part : 2 * part] = mm(at_ref[rows, :], dk_ref[...]).astype(BF16)
                ref[0, :, 2 * part : 3 * part] = mm(at_ref[rows, :], dv_ref[...]).astype(BF16)
                ref[0, :, 3 * part :] = mm(ct_ref[rows, :], o_ref[...]).astype(BF16)

        @pl.when(at < near)
        def _():
            write((ga_near, gb_near))

        @pl.when((at >= near) & (at < groups))
        def _():
            write((ga_far, gb_far))

        @pl.when(at == 0)
        def _():
            gg_ref[...] = jnp.zeros_like(gg_ref)
            for m in range(3):
                for z in range(groups):
                    w_all[m, :, z * part : (z + 1) * part] = w_ref[z, :, :, m * part : (m + 1) * part].reshape(width, part)

        @pl.when(at < tiles)
        def _():
            grad = mm(dq_row[...], w_all[0], NT)
            grad += mm(dk_row[...], w_all[1], NT)
            grad += mm(dv_row[...], w_all[2], NT)
            da_ref[...] = grad.astype(BF16)
            values = x_ref[...].astype(F32)
            gg_ref[...] += jnp.sum(grad * values * norm_rate(values), axis=0, keepdims=True)

    column = lambda i: (0, jnp.minimum(i, groups - 1))
    row = lambda i: (jnp.minimum(i, tiles - 1), 0)
    shape = (near, half, cols)
    near_spec = pl.BlockSpec((1, half, cols), lambda i: (jnp.minimum(i, near - 1), 0, 0))
    far_spec = pl.BlockSpec((1, half, cols), lambda i: (jnp.clip(i - near, 0, near - 1), 0, 0))
    return call(
        body,
        "weigh",
        4 * (tokens + block) * width * heads + 6 * block * width * heads,
        (turned, cotangent_turned, dq, dk, dv, attended, x_full, dq, dk, dv, weights),
        (max(groups, tiles),),
        [
            whole(turned.shape),
            whole(cotangent_turned.shape),
            pl.BlockSpec((block, part), column),
            pl.BlockSpec((tokens, part), column),
            pl.BlockSpec((tokens, part), column),
            pl.BlockSpec((block, part), column),
            pl.BlockSpec((TILE, width), row),
            pl.BlockSpec((TILE, heads), row),
            pl.BlockSpec((TILE, heads), row),
            pl.BlockSpec((TILE, heads), row),
            inward_spec(weights),
        ],
        [near_spec, near_spec, far_spec, far_spec, pl.BlockSpec((TILE, width), row), pl.BlockSpec((1, width), lambda i: (0, 0))],
        [out(shape)] * 4 + [out((block, width)), out((1, width), F32)],
        [pltpu.VMEM((3, width, heads), BF16)],
        after=after,
    )


def fold(kept, received, step, after=()):
    axis = None if step is None else 2 if step[0] == "seq" else 1
    shapes = [kept.shape]
    if axis is not None:
        half = kept.shape[axis] // 2
        shapes = [tuple(half if at == axis else n for at, n in enumerate(kept.shape))] * 2

    def body(kept_ref, received_ref, *refs):
        total = (kept_ref[...].astype(F32) + received_ref[...].astype(F32)).astype(BF16)
        if axis is None:
            refs[0][...] = total
        elif axis == 1:
            refs[0][...], refs[1][...] = total[:, :half], total[:, half:]
        else:
            refs[0][...], refs[1][...] = total[:, :, :half], total[:, :, half:]

    groups = kept.shape[0]
    run = next(n for n in range(groups, 0, -1) if groups % n == 0 and n * kept[0].size <= FOLD)
    spec = lambda shape: pl.BlockSpec((run, *shape[1:]), lambda g: (g, 0, 0, 0, 0))
    return call(
        body,
        "fold",
        kept.size,
        (kept, received),
        (groups // run,),
        [spec(kept.shape)] * 2,
        [spec(shape) for shape in shapes],
        [out(shape) for shape in shapes],
        after=after,
    )


def deliver(array, kind, after=()):
    rows, width = array.shape

    def body(x_ref, y_ref):
        y_ref[...] = x_ref[...].astype(kind)

    spec = pl.BlockSpec((2 * TILE, width), lambda i: (i, 0))
    return call(
        body, "deliver", rows * width, (array,), (rows // (2 * TILE),), [spec], [spec], [out(array.shape, kind)], after=after
    )[0]


def finish(x_full, hidden_grad, gain, parts, first, count, after=()):
    width = hidden_grad.shape[1]

    def body(x_ref, dh_ref, g_ref, *refs):
        grad = sum([ref[...].astype(F32) for ref in refs[1:-1]], refs[0][...].astype(F32))
        values = x_ref[...].astype(F32)
        rate = norm_rate(values)
        scaled = grad * g_ref[...]
        dot = jnp.mean(values * scaled, axis=-1, keepdims=True)
        refs[-1][...] = (dh_ref[...] + rate * scaled - values * (rate * rate * rate * dot)).astype(BF16)

    wide = pl.BlockSpec((TILE, width), lambda i: (first // TILE + i, 0))
    return call(
        body,
        "finish",
        16 * count * width,
        (x_full, hidden_grad, gain, *parts),
        (count // TILE,),
        [wide, wide, whole((1, width))] + [wide] * len(parts),
        [pl.BlockSpec((TILE, width), lambda i: (i, 0))],
        [out((count, width))],
        after=after,
    )[0]


def widen(target, fitting, first, block, right, left, before, after=()):
    count, width = right.shape
    rows = fitting * block
    step = min(2 * TILE, count)

    def body(target, right_ref, left_ref, y_ref):
        @pl.when(target[1] == 0)
        def _():
            y_ref[...] = left_ref[...].astype(F32)

        @pl.when(target[1] != 0)
        def _():
            y_ref[...] = right_ref[...].astype(F32)

    spec = pl.BlockSpec((step, width), lambda i, t: (i, 0))
    place = pl.BlockSpec((step, width), lambda i, t: (t[0] * (block // step) + first // step + i, 0))
    before = [] if before is None else [before]
    return call(
        body,
        "widen",
        count * width,
        (target, right, left),
        (count // step,),
        [spec, spec],
        [place],
        [out((rows, width), F32)],
        prefetch=1,
        after=[*before, *after],
        aliases={3: 0} if before else {},
    )[0]


def on_device(
    residual_in,
    grad_out,
    segment_lengths,
    attention_in,
    attention_out,
    expand,
    contract,
    gains,
    mean_attention_in,
    mean_attention_out,
    mean_expand,
    mean_contract,
    mean_gains,
    square_attention_in,
    square_attention_out,
    square_expand,
    square_contract,
    square_gains,
):
    span, copies = lax.axis_size("seq"), lax.axis_size("tensor")
    place, lane = lax.axis_index("seq"), lax.axis_index("tensor")
    rows, block, width = residual_in.shape
    tokens = span * block
    repeats = copies // rows
    row = lane // repeats
    piece = attention_in.shape[1]
    part = attention_in.shape[2]
    masks = owner_masks()
    index = lax.axis_index("dp") * span + place
    own = index.astype(jnp.int32)[None]
    near = copies // 2

    attention_piece = jnp.concatenate(
        [attention_in[0], attention_in[1], attention_in[2], attention_out.T], axis=1
    ).astype(BF16)
    feed_piece = jnp.stack([expand[0], expand[1], contract.T]).astype(BF16)
    x_own = lax.dynamic_index_in_dim(residual_in, row, 0, keepdims=False)
    cotangent = lax.dynamic_index_in_dim(grad_out, row, 0, keepdims=False)
    full_gains = gather_small(gains.astype(BF16).astype(F32))
    full_gains, x_own = lax.optimization_barrier((full_gains, x_own))
    x_parts = [x_own] + [exchange(x_own, ("seq", k)) for k in range(1, span)]
    everywhere = ("tensor", "dp", "seq")
    gain_one, gain_two = full_gains[:1], full_gains[1:]
    weights = gather_owners(attention_piece, everywhere)
    x_full = jnp.concatenate(x_parts, axis=0)
    lens = lax.dynamic_index_in_dim(segment_lengths, row, 0, keepdims=False)
    ends = jnp.cumsum(lens)
    starts = ends - lens
    blocks = place ^ jnp.arange(span, dtype=jnp.int32)
    places = (blocks[:, None] * block + jnp.arange(block, dtype=jnp.int32)[None, :]).reshape(tokens)
    segment = jnp.sum((places[:, None] >= ends[None, :]).astype(jnp.int32), axis=-1)
    picked = segment[:, None] == jnp.arange(lens.shape[0], dtype=jnp.int32)[None, :]
    begin = jnp.sum(jnp.where(picked, starts[None, :], 0), axis=-1)
    finish_at = jnp.sum(jnp.where(picked, ends[None, :], 0), axis=-1)
    freq = jnp.exp(jnp.arange(HD // 2, dtype=F32) * (-2.0 * jnp.log(10000.0) / HD))
    angle = (places - begin).astype(F32)[:, None] * freq
    cosine = jnp.tile(jnp.cos(angle), (1, PAIR // (HD // 2)))
    sine = jnp.tile(jnp.sin(angle), (1, PAIR // (HD // 2)))
    count = block // TILE
    firsts = begin[:block].reshape(count, TILE)[:, 0] // TILE
    lasts = (finish_at[:block].reshape(count, TILE)[:, -1] + TILE - 1) // TILE
    reach = jnp.concatenate(
        [jnp.stack([firsts, lasts], axis=1).reshape(-1), (place * (block // TILE))[None]]
    ).astype(jnp.int32)
    lanes = jnp.arange(PAIR, dtype=jnp.int32)[None, :]
    key_marks = jnp.where(segment[:, None] == lanes, NEG, 0.0).astype(BF16)
    query_marks = ((segment[:block, None] != lanes) & (lanes < lens.shape[0])).astype(BF16)

    chunks = 2
    cut = feed_piece.shape[2] // chunks
    feed_pieces = [feed_piece[:, :, at * cut : (at + 1) * cut] for at in range(chunks)]
    tables = (cosine, sine, reach, query_marks, key_marks)
    weights, feed_pieces, x_full, cotangent, tables, gain_one, gain_two = lax.optimization_barrier(
        (weights, feed_pieces, x_full, cotangent, tables, gain_one, gain_two)
    )
    cosine, sine, reach, query_marks, key_marks = tables
    feeds = [gather_owners(chunk, everywhere) for chunk in feed_pieces]

    turned_one, query, keys, values = project(own, masks, x_full, gain_one, cosine, sine, weights, block)
    attended, lse = attend(reach, query, keys, values, query_marks, key_marks)
    hidden, normed_two, turned_two, rounded, rounded_turned = lift(
        own, masks, attended, x_full, cotangent, gain_two, weights
    )

    def spread(array):
        half, columns = array.shape[-2:]
        return array.reshape(-1, half // (span * piece), span, piece, columns)

    last_step = axis_steps()[2]
    orders = [scatter_order(bool(at % 2)) for at in range(chunks)]
    flights, places, branches, grads = [], [0] * chunks, [], []

    def tie(anchor, *which):
        *tied, anchor = lax.optimization_barrier((*[flights[at] for at in which], anchor))
        for at, flight in zip(which, tied):
            flights[at] = tuple(flight) if isinstance(flight, (tuple, list)) else flight

    def move_on(*which):
        for at in which:
            if places[at] < len(orders[at]):
                step = orders[at][places[at]]
                kept, sent = fold(*flights[at], step)
                flights[at] = (kept, exchange(sent, step))
                places[at] += 1
            elif isinstance(flights[at], tuple):
                flights[at] = fold(*flights[at], None)[0]
        return [flights[at][0] if isinstance(flights[at], tuple) else flights[at] for at in which]

    for at in range(chunks):
        branch, grad, kept, sent = feed(normed_two, turned_two, rounded, rounded_turned, feeds[at], 0, cut, after=branches)
        flights.append((spread(kept), spread(exchange(sent, last_step))))
        branches.append(branch)
        grads.append(grad)
    result, hidden_grad, hidden_grad_turned, output_grad, grad_gain_two = back(
        own, masks, hidden, branches, grads, cotangent, gain_two, weights
    )
    tie(output_grad, 0, 1)
    residual_out = lax.all_gather(result, "tensor", axis=0)
    common = (reach, query, output_grad, attended, keys, values, lse, query_marks, key_marks, cosine, sine)
    sets = query.shape[1] // (2 * PAIR)
    found = unattend(0, sets - 1, *common, None, after=move_on(0, 1))
    tie(found[0], 0, 1)
    after = []
    for _ in orders[0][1:]:
        after = move_on(0, 1)
    dq, dk, dv = unattend(sets - 1, 1, *common, found, after=after)
    tie(dq, 0, 1)
    move_on(0, 1)
    feed_sums = jnp.concatenate([flight.reshape(copies, -1, piece, cut) for flight in flights], axis=-1)
    distances = list(range(1, copies))

    parts, gain_parts = [], []
    for k in range(1, span):
        grad, gain_part = unproject([dk, dv], x_full, k, block, weights, after=[feed_sums])
        parts.append(exchange(grad, ("seq", k)))
        gain_parts.append(gain_part)
    received = tensor_sends(feed_sums, distances)
    places = [0, 0]
    *found, own_grad, gain_part = weigh(
        turned_one, hidden_grad_turned, dq, dk, dv, attended, x_full, weights, after=gain_parts
    )
    gain_parts.append(gain_part)
    steady = [*received, residual_out]
    shares = 1
    size = block // shares
    lines = []
    for at in range(shares):
        own_rows = finish(x_full, hidden_grad, gain_one, [own_grad] + parts, at * size, size, after=steady)
        lines.append([(own_rows, own_rows)])
    up = [(i, i + 1) for i in range(copies - 1)]
    down = [(i + 1, i) for i in range(copies - 1)]

    def hop(count):
        for _ in range(count):
            for line in lines:
                from_low, from_high = line[-1]
                line.append((lax.ppermute(from_low, "tensor", up), lax.ppermute(from_high, "tensor", down)))

    hop(1)
    found, _ = lax.optimization_barrier((found, lines[0][0][0]))
    flights = [(spread(found[at]), spread(exchange(found[at + 1], last_step))) for at in (0, 2)]
    while isinstance(flights[1], tuple):
        move_on(0, 1)
    attention_sums = jnp.concatenate(flights).reshape(copies, piece, 4 * part)
    gain_grads = sum_over(jnp.concatenate([sum(gain_parts), grad_gain_two]), ("dp", "seq"))
    attention_sums, lines[0][1], gain_grads = lax.optimization_barrier((attention_sums, lines[0][1], gain_grads))
    hop(1)
    attention_shard = tensor_sum(attention_sums, tensor_sends(attention_sums, distances))
    feed_shard = tensor_sum(feed_sums, received)

    share = 1.0 / repeats
    attention_shard, feed_shard = attention_shard * share, feed_shard * share
    gain_grads = sum_over(gain_grads * share, ("tensor",))
    gain_shard = lax.dynamic_slice_in_dim(gain_grads, index * piece, piece, 1)

    local = jnp.sum(attention_shard * attention_shard) + jnp.sum(feed_shard * feed_shard)
    squares = sum_over(jnp.full((8, 128), local), ("tensor",))
    squares, gain_grads, lines[0][2] = lax.optimization_barrier((squares, gain_grads, lines[0][2]))
    hop(copies - 3)
    squares = sum_over(squares, ("dp", "seq"))
    norm = jnp.sqrt(squares[0, 0] + jnp.sum(gain_grads * gain_grads))
    grad_in = None
    for distance in range(copies):
        source = lax.rem(lane - distance + copies, copies)
        target = jnp.stack([source // repeats, (source > lane).astype(jnp.int32)]).astype(jnp.int32)
        for at, line in enumerate(lines):
            from_low, from_high = line[distance][0], line[(copies - distance) % copies][1]
            grad_in = widen(target, rows, at * size, block, from_high, from_low, grad_in)
    residual_out = residual_out[::repeats] if repeats > 1 else residual_out
    residual_out = deliver(residual_out.reshape(-1, width), BF16, after=[lines[-1][0][0]])
    residual_out, grad_in = residual_out.reshape(rows, block, width), grad_in.reshape(rows, block, width)

    factor = jnp.minimum(1.0, CLIP / norm)
    shards = (
        jnp.stack([attention_shard[:, k * part : (k + 1) * part] for k in range(3)]),
        attention_shard[:, 3 * part :].T,
        feed_shard[:2],
        feed_shard[2].T,
        gain_shard,
    )
    masters = (attention_in, attention_out, expand, contract, gains)
    firsts = (mean_attention_in, mean_attention_out, mean_expand, mean_contract, mean_gains)
    seconds = (
        square_attention_in,
        square_attention_out,
        square_expand,
        square_contract,
        square_gains,
    )
    new_means = []
    new_squares = []
    new_weights = []
    for member in range(5):
        clipped = shards[member] * factor
        moment = BETA_ONE * firsts[member] + (1.0 - BETA_ONE) * clipped
        square = BETA_TWO * seconds[member] + (1.0 - BETA_TWO) * clipped * clipped
        update = (
            moment / (1.0 - BETA_ONE**STEP) / (jnp.sqrt(square / (1.0 - BETA_TWO**STEP)) + ADAM_EPS)
        )
        shrink = DECAY if member < 4 else 0.0
        speed = RATE if member < 4 else GAIN_RATE
        new_means.append(moment)
        new_squares.append(square)
        new_weights.append(masters[member] - speed * (update + shrink * masters[member]))
    return (residual_out, grad_in, norm, *new_means, *new_squares, *new_weights)


def solution(mesh):
    tokens = P("dp", "seq", None)
    weights = (
        P(None, ("dp", "seq"), "tensor"),
        P("tensor", ("dp", "seq")),
        P(None, ("dp", "seq"), "tensor"),
        P("tensor", ("dp", "seq")),
        P(None, ("dp", "seq")),
    )
    return jax.shard_map(
        on_device,
        mesh=mesh,
        in_specs=(tokens, tokens, P("dp", None)) + weights * 3,
        out_specs=(tokens, tokens, P()) + weights * 3,
        check_vma=False,
    )
```

```python
import jax
import jax.numpy as jnp
from jax import lax
from jax.experimental import pallas as pl
from jax.experimental.pallas import tpu as pltpu
from jax.sharding import PartitionSpec as P

HD = 64
STEP = 10

NORM_EPS = 1e-05
NEG = -1e30
CLIP = 1.0
RATE = 0.04
GAIN_RATE = 1.0
BETA_ONE = 0.9
BETA_TWO = 0.999
ADAM_EPS = 1e-08
DECAY = 0.1

SCALE = HD ** (-0.5)
PAIR = 2 * HD
TILE = 256
VMEM = 60 * 1024 * 1024
FOLD = 1024 * 1024
F32 = jnp.float32
BF16 = jnp.bfloat16

NN = (((1,), (0,)), ((), ()))
NT = (((1,), (1,)), ((), ()))
TN = (((0,), (0,)), ((), ()))


def mm(left, right, dims=NN):
    return lax.dot_general(left, right, dims, preferred_element_type=F32)


def call(body, name, flops, args, grid, in_specs, out_specs, out_shape, scratch=(), prefetch=0, after=(), aliases={}):
    count, extra = len(args), len(after)
    moved = sum(a.size * a.dtype.itemsize for a in args) + sum(o.size * o.dtype.itemsize for o in out_shape)
    return pl.pallas_call(
        lambda *refs: body(*refs[:count], *refs[count + extra :]),
        name=name,
        grid_spec=pltpu.PrefetchScalarGridSpec(
            num_scalar_prefetch=prefetch,
            grid=grid,
            in_specs=list(in_specs) + [pl.BlockSpec(memory_space=pl.ANY)] * extra,
            out_specs=out_specs,
            scratch_shapes=list(scratch),
        ),
        out_shape=out_shape,
        input_output_aliases=dict(aliases),
        compiler_params=pltpu.CompilerParams(vmem_limit_bytes=VMEM),
        cost_estimate=pl.CostEstimate(flops=int(flops) >> 24, bytes_accessed=int(moved) >> 20, transcendentals=0),
    )(*args, *after)


def whole(shape):
    return pl.BlockSpec(shape, lambda *at: (0,) * len(shape), pipeline_mode=pl.Buffered(1))


def scalar():
    return pl.BlockSpec(memory_space=pltpu.SMEM)


def out(shape, kind=BF16):
    return jax.ShapeDtypeStruct(shape, kind)


def exchange(block, step):
    axis, bit = step
    return lax.ppermute(block, axis, [(i ^ bit, i) for i in range(lax.axis_size(axis))])


def axis_steps():
    bits = lambda axis: [(axis, 1 << k) for k in range(lax.axis_size(axis).bit_length() - 1)]
    across = bits("dp")
    return bits("seq"), across[1:], across[0]


def owner_masks():
    span = lax.axis_size("seq")
    along, across, last = axis_steps()
    masks = [0]
    for axis, bit in along + across + [last]:
        masks += [m ^ (bit if axis == "seq" else bit * span) for m in masks]
    return masks


def gather_owners(array, axes):
    whole_array = lax.all_gather(array, axes, axis=0)
    return whole_array.reshape(lax.axis_size(axes[0]), -1, *array.shape)


def gather_pieces(pieces, along_first):
    along, across, last = axis_steps()
    groups, rows, columns = pieces.shape
    held = pieces[:, None, None]
    for step in along + across if along_first else across + along:
        held = jnp.concatenate([held, exchange(held, step)], axis=2 if step[0] == "seq" else 1)
    held = held.reshape(groups, -1, columns)
    return held, exchange(held, last)


def from_tensor(array):
    size = lax.axis_size("tensor")
    others = [lax.ppermute(array, "tensor", [(i, (i + k) % size) for i in range(size)]) for k in range(1, size)]
    return [array] + others


def to_tensor(held):
    size = lax.axis_size("tensor")
    total = held[0].astype(F32)
    for k in range(1, size):
        total += lax.ppermute(held[k], "tensor", [((i + k) % size, i) for i in range(size)]).astype(F32)
    return total


def gather_small(array):
    along, across, last = axis_steps()
    for step in along + [last] + across:
        other = exchange(array, step)
        pair, swapped = jnp.concatenate([array, other], axis=1), jnp.concatenate([other, array], axis=1)
        array = jnp.where(lax.axis_index(step[0]) & step[1], swapped, pair)
    return array


def sum_over(array, axes):
    for axis in axes:
        for k in range(lax.axis_size(axis).bit_length() - 1):
            array = array + exchange(array, (axis, 1 << k))
    return array


def scatter_order(along_first):
    along, across, _ = axis_steps()
    ordered = [list(reversed(along)), list(reversed(across))]
    return ordered[0] + ordered[1] if along_first else ordered[1] + ordered[0]


def tensor_sends(held, distances):
    size, here = lax.axis_size("tensor"), lax.axis_index("tensor")
    return [
        lax.ppermute(
            lax.dynamic_index_in_dim(held, lax.rem(here + k, size), 0, keepdims=False),
            "tensor",
            [(i, (i + k) % size) for i in range(size)],
        )
        for k in distances
    ]


def tensor_sum(held, received):
    own = lax.dynamic_index_in_dim(held, lax.axis_index("tensor"), 0, keepdims=False).astype(F32)
    return sum([array.astype(F32) for array in received], own)


def row_block(own, mask, piece):
    return pl.ds(pl.multiple_of((own ^ mask) * piece, piece), piece)


def store_turned(own, masks, ref, values, scratch):
    scratch[...] = values.T.astype(BF16)
    piece = scratch.shape[0] // len(masks)
    for j, mask in enumerate(masks):
        ref[j * piece : (j + 1) * piece, :] = scratch[row_block(own, mask, piece), :]


def swap_halves(values):
    lane = lax.broadcasted_iota(jnp.int32, values.shape, 1)
    size = values.shape[1]
    ahead = pltpu.roll(values, size - HD // 2, 1)
    behind = pltpu.roll(values, HD // 2, 1)
    return jnp.where(lane % HD < HD // 2, ahead, behind)


def half_sign(shape):
    lane = lax.broadcasted_iota(jnp.int32, shape, 1)
    return jnp.where(lane % HD < HD // 2, -1.0, 1.0)


def turn(values, cosine, sine):
    return values * cosine + swap_halves(values) * (sine * half_sign(values.shape))


def unturn(values, cosine, sine):
    return values * cosine - swap_halves(values * sine) * half_sign(values.shape)


def pair_lanes(values, head):
    lane = lax.broadcasted_iota(jnp.int32, values.shape, 1)
    return jnp.where((lane < HD) == (head == 0), values, 0.0)


def stack_pair(values):
    return jnp.concatenate([pair_lanes(values, 0), pair_lanes(values, 1)], axis=0).astype(BF16)


def norm_rate(values):
    return lax.rsqrt(jnp.mean(values * values, axis=-1, keepdims=True) + NORM_EPS)


def weight_specs(weights, first, count):
    groups, half, cols = weights[0].shape
    block = (groups, half, count * (cols // 4))
    spec = pl.BlockSpec(block, lambda *at: (0, 0, first // count), pipeline_mode=pl.Buffered(1))
    return [spec] * len(weights)


def lay(own, masks, w_all, w_refs):
    kinds = w_all.shape[0]
    groups, half, cols = w_refs[0].shape
    part = cols // kinds
    piece = 2 * half // len(masks)
    for z in range(len(w_refs) // 2 * groups):
        for j, mask in enumerate(masks):
            ref = w_refs[2 * (z // groups) + j // (len(masks) // 2)]
            at = j % (len(masks) // 2) * piece
            for m in range(kinds):
                w_all[m, row_block(own, mask, piece), z * part : (z + 1) * part] = ref[
                    z % groups, at : at + piece, m * part : (m + 1) * part
                ]


def project(own, masks, x_full, gain, cosine, sine, weights, block):
    tokens, width = x_full.shape
    heads = len(weights) // 2 * weights[0].shape[0] * weights[0].shape[2] // 4
    count = len(weights)
    mine = block // TILE

    def body(own_ref, x_ref, g_ref, cos_ref, sin_ref, *refs):
        w_refs, (at_ref, q_ref, k_ref, v_ref, w_all, a_one, turned) = refs[:count], refs[count:]
        own = own_ref[0]

        @pl.when(pl.program_id(0) == 0)
        def _():
            lay(own, masks, w_all, w_refs)

        values = x_ref[...].astype(F32)
        normed = values * norm_rate(values) * g_ref[...]
        a_one[...] = normed.astype(BF16)
        store_turned(own, masks, at_ref, normed, turned)
        cosine, sine = cos_ref[...], sin_ref[...]

        def rotated(ref, m):
            for at in range(0, heads, 2 * PAIR):
                mixed = mm(a_one[...], w_all[m, :, at : at + 2 * PAIR])
                for lane in (0, PAIR):
                    ref[:, at + lane : at + lane + PAIR] = turn(mixed[:, lane : lane + PAIR], cosine, sine).astype(BF16)

        rotated(k_ref, 1)
        v_ref[...] = mm(a_one[...], w_all[2]).astype(BF16)

        @pl.when(pl.program_id(0) < mine)
        def _():
            rotated(q_ref, 0)

    rows = lambda i: (i, 0)
    return call(
        body,
        "project",
        2 * (2 * tokens + block) * width * heads,
        (own, x_full, gain, cosine, sine, *weights),
        (tokens // TILE,),
        [
            scalar(),
            pl.BlockSpec((TILE, width), rows),
            whole((1, width)),
            pl.BlockSpec((TILE, PAIR), rows),
            pl.BlockSpec((TILE, PAIR), rows),
            *weight_specs(weights, 0, 3),
        ],
        [
            pl.BlockSpec((width, TILE), lambda i: (0, i)),
            pl.BlockSpec((TILE, heads), lambda i: (jnp.minimum(i, mine - 1), 0)),
            pl.BlockSpec((TILE, heads), rows),
            pl.BlockSpec((TILE, heads), rows),
        ],
        [out((width, tokens)), out((block, heads)), out((tokens, heads)), out((tokens, heads))],
        [pltpu.VMEM((3, width, heads), BF16), pltpu.VMEM((TILE, width), BF16), pltpu.VMEM((width, TILE), BF16)],
    )


def attend(reach, query, keys, values, query_marks, key_marks):
    block, heads = query.shape
    tokens = keys.shape[0]
    wide = 2 * PAIR
    count = block // TILE

    def body(reach, q_ref, k_ref, v_ref, qm_ref, km_ref, o_ref, lse_ref, turned, acc, top, total, kept):
        at = pl.program_id(1)
        first, last, shift = reach[2 * at], reach[2 * at + 1], reach[2 * count]

        @pl.when(at == 0)
        def _():
            for tile in range(tokens // TILE):
                rows = slice(tile * TILE, (tile + 1) * TILE)
                turned[:, rows] = v_ref[rows, :].astype(F32).T.astype(BF16)

        marks = jnp.concatenate([qm_ref[...], qm_ref[...]], axis=0)
        stacked = [
            jnp.concatenate([stack_pair(q_ref[:, p * PAIR : (p + 1) * PAIR].astype(F32) * SCALE), marks], axis=1)
            for p in range(2)
        ]
        top[...] = jnp.full_like(top, NEG)
        acc[...] = jnp.zeros_like(acc)
        total[...] = jnp.zeros_like(total)

        def by_eight(values):
            return values.reshape(values.shape[0] // 8, 8, values.shape[1])

        def score(tile, carry):
            rows = pl.ds(pl.multiple_of((tile ^ shift) * TILE, TILE), TILE)
            for p in range(2):
                lanes = slice(p * PAIR, (p + 1) * PAIR)
                scores = mm(jnp.concatenate([k_ref[rows, lanes], km_ref[rows, :]], axis=1), stacked[p], NT)
                kept[p, rows, :] = scores
                top[p] = jnp.maximum(top[p], jnp.max(by_eight(scores), axis=0))
            return carry

        lax.fori_loop(first, last, score, 0)
        tops = [jnp.max(top[p], axis=0, keepdims=True) for p in range(2)]

        def step(tile, carry):
            rows = pl.ds(pl.multiple_of((tile ^ shift) * TILE, TILE), TILE)
            for p in range(2):
                probs = jnp.exp(kept[p, rows, :] - tops[p])
                total[p] += jnp.sum(by_eight(probs), axis=0)
                probs = probs.astype(BF16)
                for h in range(2):
                    part = slice(p * PAIR + h * HD, p * PAIR + (h + 1) * HD)
                    acc[part, :] += mm(turned[part, rows], probs[:, h * TILE : (h + 1) * TILE])
            return carry

        lax.fori_loop(first, last, step, 0)
        for p in range(2):
            sums = jnp.sum(total[p], axis=0, keepdims=True)
            rate = 1.0 / sums
            for h in range(2):
                part = slice(p * PAIR + h * HD, p * PAIR + (h + 1) * HD)
                acc[part, :] = acc[part, :] * rate[:, h * TILE : (h + 1) * TILE]
            lse_ref[0, 0, p : p + 1, :] = tops[p] + jnp.log(sums)
        o_ref[...] = acc[...].T.astype(BF16)

    return call(
        body,
        "attend",
        4 * block * tokens * heads,
        (reach, query, keys, values, query_marks, key_marks),
        (heads // wide, count),
        [
            pl.BlockSpec((TILE, wide), lambda h, i, r: (i, h)),
            pl.BlockSpec((tokens, wide), lambda h, i, r: (0, h)),
            pl.BlockSpec((tokens, wide), lambda h, i, r: (0, h)),
            pl.BlockSpec((TILE, PAIR), lambda h, i, r: (i, 0)),
            pl.BlockSpec((tokens, PAIR), lambda h, i, r: (0, 0)),
        ],
        [
            pl.BlockSpec((TILE, wide), lambda h, i, r: (i, h)),
            pl.BlockSpec((1, 1, 2, 2 * TILE), lambda h, i, r: (h, i, 0, 0)),
        ],
        [out((block, heads)), out((heads // wide, count, 2, 2 * TILE), F32)],
        [
            pltpu.VMEM((wide, tokens), BF16),
            pltpu.VMEM((wide, TILE), F32),
            pltpu.VMEM((2, 8, 2 * TILE), F32),
            pltpu.VMEM((2, 8, 2 * TILE), F32),
            pltpu.VMEM((2, tokens, 2 * TILE), F32),
        ],
        prefetch=1,
    )


def lift(own, masks, attended, x_full, cotangent, gain, weights):
    block, heads = attended.shape
    width = x_full.shape[1]
    count = len(weights)

    def body(own_ref, o_ref, x_ref, c_ref, g_ref, *refs):
        w_refs, (h_ref, a_ref, at_ref, e_ref, et_ref, w_all, turned) = refs[:count], refs[count:]
        own = own_ref[0]

        @pl.when(pl.program_id(0) == 0)
        def _():
            lay(own, masks, w_all, w_refs)

        values = x_ref[...].astype(F32) + mm(o_ref[...], w_all[0], NT)
        h_ref[...] = values
        normed = values * norm_rate(values) * g_ref[...]
        a_ref[...] = normed.astype(BF16)
        store_turned(own, masks, at_ref, normed, turned)
        cotangent = c_ref[...]
        e_ref[...] = cotangent.astype(BF16)
        store_turned(own, masks, et_ref, cotangent, turned)

    rows = lambda i: (i, 0)
    wide = pl.BlockSpec((TILE, width), rows)
    tall = pl.BlockSpec((width, TILE), lambda i: (0, i))
    return call(
        body,
        "lift",
        2 * block * width * heads,
        (own, attended, x_full, cotangent, gain, *weights),
        (block // TILE,),
        [scalar(), pl.BlockSpec((TILE, heads), rows), wide, wide, whole((1, width)), *weight_specs(weights, 3, 1)],
        [wide, wide, tall, wide, tall],
        [out((block, width), F32), out((block, width)), out((width, block)), out((block, width)), out((width, block))],
        [pltpu.VMEM((1, width, heads), BF16), pltpu.VMEM((width, TILE), BF16)],
    )


def feed(normed, turned, cotangent, cotangent_turned, weights, chunk, hidden, after=()):
    block, width = normed.shape
    groups, owners, kinds, piece, _ = weights.shape
    half = width // 2
    cut = min(512, hidden)
    tile = min(512, block)

    def body(a_ref, at_ref, e_ref, et_ref, w_ref, b_out, d_out, ga_ref, gb_ref, b_ref, d_ref, mid, dgate, dup):
        @pl.when((pl.program_id(0) == 0) & (pl.program_id(1) == 0))
        def _():
            b_ref[...] = jnp.zeros_like(b_ref)
            d_ref[...] = jnp.zeros_like(d_ref)

        def weight(m):
            return w_ref[0, :, m].reshape(width, cut)

        def tokens(i, carry):
            rows = pl.ds(pl.multiple_of(i * tile, tile), tile)
            gate = mm(a_ref[rows, :], weight(0))
            upper = mm(a_ref[rows, :], weight(1))
            grad = mm(e_ref[rows, :], weight(2))
            sigma = jax.nn.sigmoid(gate)
            active = gate * sigma
            mid[rows, :] = (active * upper).astype(BF16)
            dgate[rows, :] = (grad * upper * (sigma * (1.0 + gate * (1.0 - sigma)))).astype(BF16)
            dup[rows, :] = (grad * active).astype(BF16)
            b_ref[rows, :] += mm(mid[rows, :], weight(2), NT)
            d_ref[rows, :] += mm(dgate[rows, :], weight(0), NT) + mm(dup[rows, :], weight(1), NT)
            return carry

        lax.fori_loop(0, block // tile, tokens, 0)
        for ref, rows in ((ga_ref, slice(0, half)), (gb_ref, slice(half, width))):
            ref[0, 0] = mm(at_ref[rows, :], dgate[...]).astype(BF16)
            ref[0, 1] = mm(at_ref[rows, :], dup[...]).astype(BF16)
            ref[0, 2] = mm(et_ref[rows, :], mid[...]).astype(BF16)

        @pl.when((pl.program_id(0) == groups - 1) & (pl.program_id(1) == hidden // cut - 1))
        def _():
            b_out[...] = b_ref[...].astype(BF16)
            d_out[...] = d_ref[...].astype(BF16)

    place = lambda z, j: (z, 0, 0, j)
    shape = (groups, kinds, half, hidden)
    return call(
        body,
        "feed",
        18 * block * width * hidden * groups,
        (normed, turned, cotangent, cotangent_turned, weights),
        (groups, hidden // cut),
        [
            whole((block, width)),
            whole((width, block)),
            whole((block, width)),
            whole((width, block)),
            pl.BlockSpec((1, owners, kinds, piece, cut), lambda z, j: (z, 0, 0, 0, chunk * (hidden // cut) + j)),
        ],
        [
            whole((block, width)),
            whole((block, width)),
            pl.BlockSpec((1, kinds, half, cut), place),
            pl.BlockSpec((1, kinds, half, cut), place),
        ],
        [out((block, width)), out((block, width)), out(shape), out(shape)],
        [pltpu.VMEM((block, width), F32)] * 2 + [pltpu.VMEM((block, cut), BF16)] * 3,
        after=after,
    )


def back(own, masks, hidden, branches, grads, cotangent, gain, weights, after=()):
    block, width = hidden.shape
    heads = len(weights) // 2 * weights[0].shape[0] * weights[0].shape[2] // 4
    many = len(weights)

    count = len(branches)

    def body(own_ref, h_ref, c_ref, g_ref, *refs):
        w_refs, refs = refs[:many], refs[many:]
        b_refs, d_refs, refs = refs[:count], refs[count : 2 * count], refs[2 * count :]
        y_ref, dh_ref, ct_ref, do_ref, gg_ref, w_all, turned = refs
        own = own_ref[0]

        @pl.when(pl.program_id(0) == 0)
        def _():
            lay(own, masks, w_all, w_refs)
            gg_ref[...] = jnp.zeros_like(gg_ref)

        hidden = h_ref[...]
        grad = sum([ref[...].astype(F32) for ref in d_refs[1:]], d_refs[0][...].astype(F32))
        y_ref[...] = sum([ref[...].astype(F32) for ref in b_refs], hidden).astype(BF16)
        rate = norm_rate(hidden)
        scaled = grad * g_ref[...]
        dot = jnp.mean(hidden * scaled, axis=-1, keepdims=True)
        result = c_ref[...] + rate * scaled - hidden * (rate * rate * rate * dot)
        dh_ref[...] = result
        store_turned(own, masks, ct_ref, result, turned)
        do_ref[...] = mm(result.astype(BF16), w_all[0]).astype(BF16)
        gg_ref[...] += jnp.sum(grad * hidden * rate, axis=0, keepdims=True)

    rows = lambda i: (i, 0)
    wide = pl.BlockSpec((TILE, width), rows)
    return call(
        body,
        "back",
        2 * block * width * heads,
        (own, hidden, cotangent, gain, *weights, *branches, *grads),
        (block // TILE,),
        [scalar(), wide, wide, whole((1, width)), *weight_specs(weights, 3, 1)] + [wide] * (2 * count),
        [
            wide,
            wide,
            pl.BlockSpec((width, TILE), lambda i: (0, i)),
            pl.BlockSpec((TILE, heads), rows),
            pl.BlockSpec((1, width), lambda i: (0, 0)),
        ],
        [
            out((block, width)),
            out((block, width), F32),
            out((width, block)),
            out((block, heads)),
            out((1, width), F32),
        ],
        [pltpu.VMEM((1, width, heads), BF16), pltpu.VMEM((width, TILE), BF16)],
        after=after,
    )


def unattend(base, sets, reach, query, grads, attended, keys, values, lse, query_marks, key_marks, cosine, sine, before, after=()):
    block, heads = query.shape
    tokens = keys.shape[0]
    wide = 2 * PAIR
    count = block // TILE

    def body(
        reach, q_ref, g_ref, o_ref, k_ref, v_ref, lse_ref, qm_ref, km_ref, cq_ref, sq_ref, ck_ref, sk_ref,
        dq_ref, dk_ref, dv_ref, keys_turned, dq_acc, dk_acc, dv_acc,
    ):
        at = pl.program_id(1)
        first, last, shift = reach[2 * at], reach[2 * at + 1], reach[2 * count]
        marks = jnp.concatenate([qm_ref[...], qm_ref[...]], axis=0)
        queries = q_ref[...].astype(F32) * SCALE
        grads = g_ref[...].astype(F32)
        product = (grads * o_ref[...].astype(F32)).T
        stacked, marked, stacked_grads, deltas = [], [], [], []
        for p in range(2):
            lanes = slice(p * PAIR, (p + 1) * PAIR)
            stacked.append(stack_pair(queries[:, lanes]))
            marked.append(jnp.concatenate([stacked[p], marks], axis=1))
            stacked_grads.append(stack_pair(grads[:, lanes]))
            sums = [
                jnp.sum(product[p * PAIR + h * HD : p * PAIR + (h + 1) * HD], axis=0, keepdims=True) for h in range(2)
            ]
            deltas.append(jnp.concatenate(sums, axis=1))
        dq_acc[...] = jnp.zeros_like(dq_acc)

        @pl.when(at == 0)
        def _():
            dk_acc[...] = jnp.zeros_like(dk_acc)
            dv_acc[...] = jnp.zeros_like(dv_acc)
            for tile in range(tokens // TILE):
                rows = slice(tile * TILE, (tile + 1) * TILE)
                keys_turned[:, rows] = k_ref[rows, :].astype(F32).T.astype(BF16)

        def step(tile, carry):
            rows = pl.ds(pl.multiple_of((tile ^ shift) * TILE, TILE), TILE)
            for p in range(2):
                lanes = slice(p * PAIR, (p + 1) * PAIR)
                scores = mm(jnp.concatenate([k_ref[rows, lanes], km_ref[rows, :]], axis=1), marked[p], NT)
                probs = jnp.exp(scores - lse_ref[0, 0, p : p + 1, :])
                prob_grads = mm(v_ref[rows, lanes], stacked_grads[p], NT)
                score_grads = (probs * (prob_grads - deltas[p])).astype(BF16)
                dv_acc[rows, lanes] += mm(probs.astype(BF16), stacked_grads[p])
                dk_acc[rows, lanes] += mm(score_grads, stacked[p])
                for h in range(2):
                    part = slice(p * PAIR + h * HD, p * PAIR + (h + 1) * HD)
                    dq_acc[part, :] += mm(keys_turned[part, rows], score_grads[:, h * TILE : (h + 1) * TILE])
            return carry

        lax.fori_loop(first, last, step, 0)
        grad = dq_acc[...].T * SCALE
        for lane in (0, PAIR):
            dq_ref[:, lane : lane + PAIR] = unturn(grad[:, lane : lane + PAIR], cq_ref[...], sq_ref[...]).astype(BF16)

        @pl.when(at == count - 1)
        def _():
            dv_ref[...] = dv_acc[...].astype(BF16)
            for lane in (0, PAIR):
                dk_ref[:, lane : lane + PAIR] = unturn(
                    dk_acc[:, lane : lane + PAIR], ck_ref[...], sk_ref[...]
                ).astype(BF16)

    tile = pl.BlockSpec((TILE, wide), lambda h, i, r: (i, base + h))
    full = pl.BlockSpec((tokens, wide), lambda h, i, r: (0, base + h))
    table = pl.BlockSpec((TILE, PAIR), lambda h, i, r: (i, 0))
    tables = pl.BlockSpec((tokens, PAIR), lambda h, i, r: (0, 0))
    return call(
        body,
        "unattend",
        10 * block * tokens * wide * sets,
        (reach, query, grads, attended, keys, values, lse, query_marks, key_marks, cosine, sine, cosine, sine),
        (sets, count),
        [
            tile,
            tile,
            tile,
            full,
            full,
            pl.BlockSpec((1, 1, 2, 2 * TILE), lambda h, i, r: (base + h, i, 0, 0)),
            table,
            tables,
            table,
            table,
            tables,
            tables,
        ],
        [
            tile,
            full,
            full,
        ],
        [out((block, heads)), out((tokens, heads)), out((tokens, heads))],
        [
            pltpu.VMEM((wide, tokens), BF16),
            pltpu.VMEM((wide, TILE), F32),
            pltpu.VMEM((tokens, wide), F32),
            pltpu.VMEM((tokens, wide), F32),
        ],
        prefetch=1,
        after=[*(before or ()), *after],
        aliases={13: 0, 14: 1, 15: 2} if before else {},
    )


def unproject(own, masks, grads, x_full, k, block, weights, after=()):
    width = x_full.shape[1]
    heads = grads[0].shape[1]
    kinds = len(grads)
    count = len(weights)
    base = k * block // TILE

    def body(own_ref, x_ref, *refs):
        g_refs, refs = refs[:kinds], refs[kinds:]
        w_refs, (da_ref, gg_ref, w_all) = refs[:count], refs[count:]

        @pl.when(pl.program_id(0) == 0)
        def _():
            gg_ref[...] = jnp.zeros_like(gg_ref)
            lay(own_ref[0], masks, w_all, w_refs)

        grad = mm(g_refs[0][...], w_all[3 - kinds], NT)
        for at in range(1, kinds):
            grad += mm(g_refs[at][...], w_all[3 - kinds + at], NT)
        da_ref[...] = grad.astype(BF16)
        values = x_ref[...].astype(F32)
        gg_ref[...] += jnp.sum(grad * values * norm_rate(values), axis=0, keepdims=True)

    def place(array):
        return (lambda i: (i, 0)) if array.shape[0] == block else (lambda i: (base + i, 0))

    return call(
        body,
        "unproject",
        2 * kinds * block * width * heads,
        (own, x_full, *grads, *weights),
        (block // TILE,),
        [scalar(), pl.BlockSpec((TILE, width), lambda i: (base + i, 0))]
        + [pl.BlockSpec((TILE, heads), place(array)) for array in grads]
        + weight_specs(weights, 0, 3),
        [pl.BlockSpec((TILE, width), lambda i: (i, 0)), pl.BlockSpec((1, width), lambda i: (0, 0))],
        [out((block, width)), out((1, width), F32)],
        [pltpu.VMEM((3, width, heads), BF16)],
        after=after,
    )


def weigh(own, masks, turned, cotangent_turned, dq, dk, dv, attended, x_full, weights, after=()):
    width, tokens = turned.shape
    block, heads = dq.shape
    groups, _, cols = weights[0].shape
    many = len(weights)
    groups *= many // 2
    part = cols // 4
    half, near = width // 2, groups // 2
    tiles = block // TILE

    def body(
        own_ref, at_ref, ct_ref, dq_ref, dk_ref, dv_ref, o_ref, x_ref, dq_row, dk_row, dv_row, *refs
    ):
        w_refs, (ga_near, gb_near, ga_far, gb_far, da_ref, gg_ref, w_all) = refs[:many], refs[many:]
        at = pl.program_id(0)

        def write(targets):
            for ref, rows in zip(targets, (slice(0, half), slice(half, width))):
                ref[0, :, :part] = mm(at_ref[rows, :block], dq_ref[...]).astype(BF16)
                ref[0, :, part : 2 * part] = mm(at_ref[rows, :], dk_ref[...]).astype(BF16)
                ref[0, :, 2 * part : 3 * part] = mm(at_ref[rows, :], dv_ref[...]).astype(BF16)
                ref[0, :, 3 * part :] = mm(ct_ref[rows, :], o_ref[...]).astype(BF16)

        @pl.when(at < near)
        def _():
            write((ga_near, gb_near))

        @pl.when((at >= near) & (at < groups))
        def _():
            write((ga_far, gb_far))

        @pl.when(at == 0)
        def _():
            gg_ref[...] = jnp.zeros_like(gg_ref)
            lay(own_ref[0], masks, w_all, w_refs)

        @pl.when(at < tiles)
        def _():
            grad = mm(dq_row[...], w_all[0], NT)
            grad += mm(dk_row[...], w_all[1], NT)
            grad += mm(dv_row[...], w_all[2], NT)
            da_ref[...] = grad.astype(BF16)
            values = x_ref[...].astype(F32)
            gg_ref[...] += jnp.sum(grad * values * norm_rate(values), axis=0, keepdims=True)

    column = lambda i: (0, jnp.minimum(i, groups - 1))
    row = lambda i: (jnp.minimum(i, tiles - 1), 0)
    shape = (near, half, cols)
    near_spec = pl.BlockSpec((1, half, cols), lambda i: (jnp.minimum(i, near - 1), 0, 0))
    far_spec = pl.BlockSpec((1, half, cols), lambda i: (jnp.clip(i - near, 0, near - 1), 0, 0))
    return call(
        body,
        "weigh",
        4 * (tokens + block) * width * heads + 6 * block * width * heads,
        (own, turned, cotangent_turned, dq, dk, dv, attended, x_full, dq, dk, dv, *weights),
        (max(groups, tiles),),
        [
            scalar(),
            whole(turned.shape),
            whole(cotangent_turned.shape),
            pl.BlockSpec((block, part), column),
            pl.BlockSpec((tokens, part), column),
            pl.BlockSpec((tokens, part), column),
            pl.BlockSpec((block, part), column),
            pl.BlockSpec((TILE, width), row),
            pl.BlockSpec((TILE, heads), row),
            pl.BlockSpec((TILE, heads), row),
            pl.BlockSpec((TILE, heads), row),
            *weight_specs(weights, 0, 3),
        ],
        [near_spec, near_spec, far_spec, far_spec, pl.BlockSpec((TILE, width), row), pl.BlockSpec((1, width), lambda i: (0, 0))],
        [out(shape)] * 4 + [out((block, width)), out((1, width), F32)],
        [pltpu.VMEM((3, width, heads), BF16)],
        after=after,
    )


def fold(kept, received, step, after=()):
    axis = None if step is None else 2 if step[0] == "seq" else 1
    shapes = [kept.shape]
    if axis is not None:
        half = kept.shape[axis] // 2
        shapes = [tuple(half if at == axis else n for at, n in enumerate(kept.shape))] * 2

    def body(kept_ref, received_ref, *refs):
        total = (kept_ref[...].astype(F32) + received_ref[...].astype(F32)).astype(BF16)
        if axis is None:
            refs[0][...] = total
        elif axis == 1:
            refs[0][...], refs[1][...] = total[:, :half], total[:, half:]
        else:
            refs[0][...], refs[1][...] = total[:, :, :half], total[:, :, half:]

    groups = kept.shape[0]
    run = next(n for n in range(groups, 0, -1) if groups % n == 0 and n * kept[0].size <= FOLD)
    spec = lambda shape: pl.BlockSpec((run, *shape[1:]), lambda g: (g, 0, 0, 0, 0))
    return call(
        body,
        "fold",
        kept.size,
        (kept, received),
        (groups // run,),
        [spec(kept.shape)] * 2,
        [spec(shape) for shape in shapes],
        [out(shape) for shape in shapes],
        after=after,
    )


def deliver(array, kind, after=()):
    rows, width = array.shape

    def body(x_ref, y_ref):
        y_ref[...] = x_ref[...].astype(kind)

    spec = pl.BlockSpec((2 * TILE, width), lambda i: (i, 0))
    return call(
        body, "deliver", rows * width, (array,), (rows // (2 * TILE),), [spec], [spec], [out(array.shape, kind)], after=after
    )[0]


def finish(x_full, hidden_grad, gain, parts, first, count, after=()):
    width = hidden_grad.shape[1]

    def body(x_ref, dh_ref, g_ref, *refs):
        grad = sum([ref[...].astype(F32) for ref in refs[1:-1]], refs[0][...].astype(F32))
        values = x_ref[...].astype(F32)
        rate = norm_rate(values)
        scaled = grad * g_ref[...]
        dot = jnp.mean(values * scaled, axis=-1, keepdims=True)
        refs[-1][...] = (dh_ref[...] + rate * scaled - values * (rate * rate * rate * dot)).astype(BF16)

    wide = pl.BlockSpec((TILE, width), lambda i: (first // TILE + i, 0))
    return call(
        body,
        "finish",
        16 * count * width,
        (x_full, hidden_grad, gain, *parts),
        (count // TILE,),
        [wide, wide, whole((1, width))] + [wide] * len(parts),
        [pl.BlockSpec((TILE, width), lambda i: (i, 0))],
        [out((count, width))],
        after=after,
    )[0]


def widen(target, repeated, own_rows, low, high, before):
    count, width = own_rows.shape
    step = min(2 * TILE, count)
    tiles = count // step

    def body(target, own_ref, low_ref, high_ref, y_ref):
        for side, ref in ((0, low_ref), (1, high_ref)):
            real = target[2 * side + 1] != 0

            @pl.when((pl.program_id(0) == side) & real)
            def _():
                y_ref[...] = ref[...].astype(F32)

            @pl.when((pl.program_id(0) == side) & jnp.logical_not(real))
            def _():
                y_ref[...] = own_ref[...].astype(F32)

    spec = pl.BlockSpec((step, width), lambda d, i, t: (i, 0))
    low_spec = pl.BlockSpec((step, width), lambda d, i, t: (jnp.where(d == 0, i, tiles - 1), 0))
    high_spec = pl.BlockSpec((step, width), lambda d, i, t: (jnp.where(d == 1, i, 0), 0))
    place = pl.BlockSpec((step, width), lambda d, i, t: (t[2 * d] * tiles + i, 0))
    before = [] if before is None else [before]
    return call(
        body,
        "widen",
        count * width,
        (target, own_rows, low, high),
        (2, tiles),
        [spec, low_spec, high_spec],
        [place],
        [out((repeated * count, width), F32)],
        prefetch=1,
        after=before,
        aliases={4: 0} if before else {},
    )[0]


def on_device(
    residual_in,
    grad_out,
    segment_lengths,
    attention_in,
    attention_out,
    expand,
    contract,
    gains,
    mean_attention_in,
    mean_attention_out,
    mean_expand,
    mean_contract,
    mean_gains,
    square_attention_in,
    square_attention_out,
    square_expand,
    square_contract,
    square_gains,
):
    span, copies = lax.axis_size("seq"), lax.axis_size("tensor")
    place, lane = lax.axis_index("seq"), lax.axis_index("tensor")
    rows, block, width = residual_in.shape
    tokens = span * block
    repeats = copies // rows
    row = lane // repeats
    piece = attention_in.shape[1]
    part = attention_in.shape[2]
    masks = owner_masks()
    index = lax.axis_index("dp") * span + place
    own = index.astype(jnp.int32)[None]
    near = copies // 2

    attention_piece = jnp.concatenate(
        [attention_in[0], attention_in[1], attention_in[2], attention_out.T], axis=1
    ).astype(BF16)
    feed_piece = jnp.stack([expand[0], expand[1], contract.T]).astype(BF16)
    feed_all = gather_owners(feed_piece, ("tensor", "dp", "seq"))
    pieces = jnp.stack(from_tensor(attention_piece))
    weights = (*gather_pieces(pieces[:near], True), *gather_pieces(pieces[near:], False))
    x_own = lax.dynamic_index_in_dim(residual_in, row, 0, keepdims=False)
    cotangent = lax.dynamic_index_in_dim(grad_out, row, 0, keepdims=False)
    full_gains = gather_small(gains.astype(BF16).astype(F32))
    full_gains, x_own = lax.optimization_barrier((full_gains, x_own))
    x_parts = [x_own] + [exchange(x_own, ("seq", k)) for k in range(1, span)]
    gain_one, gain_two = full_gains[:1], full_gains[1:]
    x_full = jnp.concatenate(x_parts, axis=0)
    lens = lax.dynamic_index_in_dim(segment_lengths, row, 0, keepdims=False)
    ends = jnp.cumsum(lens)
    starts = ends - lens
    blocks = place ^ jnp.arange(span, dtype=jnp.int32)
    places = (blocks[:, None] * block + jnp.arange(block, dtype=jnp.int32)[None, :]).reshape(tokens)
    segment = jnp.sum((places[:, None] >= ends[None, :]).astype(jnp.int32), axis=-1)
    picked = segment[:, None] == jnp.arange(lens.shape[0], dtype=jnp.int32)[None, :]
    begin = jnp.sum(jnp.where(picked, starts[None, :], 0), axis=-1)
    finish_at = jnp.sum(jnp.where(picked, ends[None, :], 0), axis=-1)
    freq = jnp.exp(jnp.arange(HD // 2, dtype=F32) * (-2.0 * jnp.log(10000.0) / HD))
    angle = (places - begin).astype(F32)[:, None] * freq
    cosine = jnp.tile(jnp.cos(angle), (1, PAIR // (HD // 2)))
    sine = jnp.tile(jnp.sin(angle), (1, PAIR // (HD // 2)))
    count = block // TILE
    firsts = begin[:block].reshape(count, TILE)[:, 0] // TILE
    lasts = (finish_at[:block].reshape(count, TILE)[:, -1] + TILE - 1) // TILE
    reach = jnp.concatenate(
        [jnp.stack([firsts, lasts], axis=1).reshape(-1), (place * (block // TILE))[None]]
    ).astype(jnp.int32)
    lanes = jnp.arange(PAIR, dtype=jnp.int32)[None, :]
    key_marks = jnp.where(segment[:, None] == lanes, NEG, 0.0).astype(BF16)
    query_marks = ((segment[:block, None] != lanes) & (lanes < lens.shape[0])).astype(BF16)

    chunks = 2
    cut = feed_piece.shape[2] // chunks

    turned_one, query, keys, values = project(own, masks, x_full, gain_one, cosine, sine, weights, block)
    attended, lse = attend(reach, query, keys, values, query_marks, key_marks)
    hidden, normed_two, turned_two, rounded, rounded_turned = lift(
        own, masks, attended, x_full, cotangent, gain_two, weights
    )

    def spread(array):
        half, columns = array.shape[-2:]
        return array.reshape(-1, half // (span * piece), span, piece, columns)

    last_step = axis_steps()[2]
    orders = [scatter_order(bool(at % 2)) for at in range(chunks)]
    flights, places, branches, grads = [], [0] * chunks, [], []

    def tie(anchor, *which):
        *tied, anchor = lax.optimization_barrier((*[flights[at] for at in which], anchor))
        for at, flight in zip(which, tied):
            flights[at] = tuple(flight) if isinstance(flight, (tuple, list)) else flight

    def move_on(*which):
        for at in which:
            if places[at] < len(orders[at]):
                step = orders[at][places[at]]
                kept, sent = fold(*flights[at], step)
                flights[at] = (kept, exchange(sent, step))
                places[at] += 1
            elif isinstance(flights[at], tuple):
                flights[at] = fold(*flights[at], None)[0]
        return [flights[at][0] if isinstance(flights[at], tuple) else flights[at] for at in which]

    for at in range(chunks):
        branch, grad, kept, sent = feed(normed_two, turned_two, rounded, rounded_turned, feed_all, at, cut, after=branches)
        flights.append((spread(kept), spread(exchange(sent, last_step))))
        branches.append(branch)
        grads.append(grad)
    result, hidden_grad, hidden_grad_turned, output_grad, grad_gain_two = back(
        own, masks, hidden, branches, grads, cotangent, gain_two, weights
    )
    tie(output_grad, 0, 1)
    residual_out = lax.all_gather(result, "tensor", axis=0)
    common = (reach, query, output_grad, attended, keys, values, lse, query_marks, key_marks, cosine, sine)
    sets = query.shape[1] // (2 * PAIR)
    found = unattend(0, sets - 1, *common, None, after=move_on(0, 1))
    tie(found[0], 0, 1)
    after = []
    for _ in orders[0][1:]:
        after = move_on(0, 1)
    dq, dk, dv = unattend(sets - 1, 1, *common, found, after=after)
    tie(dq, 0, 1)
    move_on(0, 1)
    feed_sums = jnp.concatenate([flight.reshape(copies, -1, piece, cut) for flight in flights], axis=-1)
    distances = list(range(1, copies))

    parts, gain_parts = [], []
    for k in range(1, span):
        grad, gain_part = unproject(own, masks, [dk, dv], x_full, k, block, weights, after=[feed_sums])
        parts.append(exchange(grad, ("seq", k)))
        gain_parts.append(gain_part)
    received = tensor_sends(feed_sums, distances)
    places = [0, 0]
    *found, own_grad, gain_part = weigh(
        own, masks, turned_one, hidden_grad_turned, dq, dk, dv, attended, x_full, weights, after=gain_parts
    )
    gain_parts.append(gain_part)
    steady = [*received, residual_out]
    shares = 1
    size = block // shares
    lines = []
    for at in range(shares):
        own_rows = finish(x_full, hidden_grad, gain_one, [own_grad] + parts, at * size, size, after=steady)
        lines.append([(own_rows, own_rows)])
    up = [(i, i + 1) for i in range(copies - 1)]
    down = [(i + 1, i) for i in range(copies - 1)]

    def hop(count):
        for _ in range(count):
            for line in lines:
                from_low, from_high = line[-1]
                line.append((lax.ppermute(from_low, "tensor", up), lax.ppermute(from_high, "tensor", down)))

    hop(1)
    found, _ = lax.optimization_barrier((found, lines[0][0][0]))
    flights = [(spread(found[at]), spread(exchange(found[at + 1], last_step))) for at in (0, 2)]
    while isinstance(flights[1], tuple):
        move_on(0, 1)
    attention_sums = [flights[z // near].reshape(near, piece, 4 * part)[z % near] for z in range(copies)]
    gain_grads = sum_over(jnp.concatenate([sum(gain_parts), grad_gain_two]), ("dp", "seq"))
    attention_sums, lines[0][1], gain_grads = lax.optimization_barrier((attention_sums, lines[0][1], gain_grads))
    hop(1)
    attention_shard = to_tensor(attention_sums)
    feed_shard = tensor_sum(feed_sums, received)

    share = 1.0 / repeats
    attention_shard, feed_shard = attention_shard * share, feed_shard * share
    gain_grads = sum_over(gain_grads * share, ("tensor",))
    gain_shard = lax.dynamic_slice_in_dim(gain_grads, index * piece, piece, 1)

    local = jnp.sum(attention_shard * attention_shard) + jnp.sum(feed_shard * feed_shard)
    squares = sum_over(jnp.full((8, 128), local), ("tensor",))
    squares, gain_grads, lines[0][2] = lax.optimization_barrier((squares, gain_grads, lines[0][2]))
    hop(copies - 3)
    squares = sum_over(squares, ("dp", "seq"))
    norm = jnp.sqrt(squares[0, 0] + jnp.sum(gain_grads * gain_grads))
    grad_in = None
    for distance in range(1, copies):
        low, high = lane - distance, lane + distance
        target = [jnp.where(low >= 0, low, lane) // repeats, low >= 0, jnp.where(high < copies, high, lane) // repeats, high < copies]
        target = jnp.stack([jnp.asarray(entry).astype(jnp.int32) for entry in target])
        grad_in = widen(target, rows, lines[0][0][0], *lines[0][distance], grad_in)
    residual_out = residual_out[::repeats] if repeats > 1 else residual_out
    residual_out = deliver(residual_out.reshape(-1, width), BF16, after=[lines[-1][0][0]])
    residual_out, grad_in = residual_out.reshape(rows, block, width), grad_in.reshape(rows, block, width)

    factor = jnp.minimum(1.0, CLIP / norm)
    shards = (
        jnp.stack([attention_shard[:, k * part : (k + 1) * part] for k in range(3)]),
        attention_shard[:, 3 * part :].T,
        feed_shard[:2],
        feed_shard[2].T,
        gain_shard,
    )
    masters = (attention_in, attention_out, expand, contract, gains)
    firsts = (mean_attention_in, mean_attention_out, mean_expand, mean_contract, mean_gains)
    seconds = (
        square_attention_in,
        square_attention_out,
        square_expand,
        square_contract,
        square_gains,
    )
    new_means = []
    new_squares = []
    new_weights = []
    for member in range(5):
        clipped = shards[member] * factor
        moment = BETA_ONE * firsts[member] + (1.0 - BETA_ONE) * clipped
        square = BETA_TWO * seconds[member] + (1.0 - BETA_TWO) * clipped * clipped
        update = (
            moment / (1.0 - BETA_ONE**STEP) / (jnp.sqrt(square / (1.0 - BETA_TWO**STEP)) + ADAM_EPS)
        )
        shrink = DECAY if member < 4 else 0.0
        speed = RATE if member < 4 else GAIN_RATE
        new_means.append(moment)
        new_squares.append(square)
        new_weights.append(masters[member] - speed * (update + shrink * masters[member]))
    return (residual_out, grad_in, norm, *new_means, *new_squares, *new_weights)


def solution(mesh):
    tokens = P("dp", "seq", None)
    weights = (
        P(None, ("dp", "seq"), "tensor"),
        P("tensor", ("dp", "seq")),
        P(None, ("dp", "seq"), "tensor"),
        P("tensor", ("dp", "seq")),
        P(None, ("dp", "seq")),
    )
    return jax.shard_map(
        on_device,
        mesh=mesh,
        in_specs=(tokens, tokens, P("dp", None)) + weights * 3,
        out_specs=(tokens, tokens, P()) + weights * 3,
        check_vma=False,
    )
```

```python
import jax
import jax.numpy as jnp
from jax import lax
from jax.experimental import pallas as pl
from jax.experimental.pallas import tpu as pltpu
from jax.sharding import PartitionSpec as P

HD = 64
STEP = 10

NORM_EPS = 1e-05
NEG = -1e30
CLIP = 1.0
RATE = 0.04
GAIN_RATE = 1.0
BETA_ONE = 0.9
BETA_TWO = 0.999
ADAM_EPS = 1e-08
DECAY = 0.1

SCALE = HD ** (-0.5)
PAIR = 2 * HD
TILE = 256
VMEM = 60 * 1024 * 1024
FOLD = 1024 * 1024
F32 = jnp.float32
BF16 = jnp.bfloat16

NN = (((1,), (0,)), ((), ()))
NT = (((1,), (1,)), ((), ()))
TN = (((0,), (0,)), ((), ()))


def mm(left, right, dims=NN):
    return lax.dot_general(left, right, dims, preferred_element_type=F32)


def call(body, name, flops, args, grid, in_specs, out_specs, out_shape, scratch=(), prefetch=0, after=(), aliases={}):
    count, extra = len(args), len(after)
    moved = sum(a.size * a.dtype.itemsize for a in args) + sum(o.size * o.dtype.itemsize for o in out_shape)
    return pl.pallas_call(
        lambda *refs: body(*refs[:count], *refs[count + extra :]),
        name=name,
        grid_spec=pltpu.PrefetchScalarGridSpec(
            num_scalar_prefetch=prefetch,
            grid=grid,
            in_specs=list(in_specs) + [pl.BlockSpec(memory_space=pl.ANY)] * extra,
            out_specs=out_specs,
            scratch_shapes=list(scratch),
        ),
        out_shape=out_shape,
        input_output_aliases=dict(aliases),
        compiler_params=pltpu.CompilerParams(vmem_limit_bytes=VMEM),
        cost_estimate=pl.CostEstimate(flops=int(flops) >> 24, bytes_accessed=int(moved) >> 20, transcendentals=0),
    )(*args, *after)


def whole(shape):
    return pl.BlockSpec(shape, lambda *at: (0,) * len(shape), pipeline_mode=pl.Buffered(1))


def scalar():
    return pl.BlockSpec(memory_space=pltpu.SMEM)


def out(shape, kind=BF16):
    return jax.ShapeDtypeStruct(shape, kind)


def exchange(block, step):
    axis, bit = step
    return lax.ppermute(block, axis, [(i ^ bit, i) for i in range(lax.axis_size(axis))])


def axis_steps():
    bits = lambda axis: [(axis, 1 << k) for k in range(lax.axis_size(axis).bit_length() - 1)]
    across = bits("dp")
    return bits("seq"), across[1:], across[0]


def owner_masks():
    span = lax.axis_size("seq")
    along, across, last = axis_steps()
    masks = [0]
    for axis, bit in along + across + [last]:
        masks += [m ^ (bit if axis == "seq" else bit * span) for m in masks]
    return masks


def gather_owners(array, axes):
    whole_array = lax.all_gather(array, axes, axis=0)
    return whole_array.reshape(lax.axis_size(axes[0]), -1, *array.shape)


def gather_pieces(pieces, along_first):
    along, across, last = axis_steps()
    groups, rows, columns = pieces.shape
    held = pieces[:, None, None]
    for step in along + across if along_first else across + along:
        held = jnp.concatenate([held, exchange(held, step)], axis=2 if step[0] == "seq" else 1)
    held = held.reshape(groups, -1, columns)
    return held, exchange(held, last)


def from_tensor(array):
    size = lax.axis_size("tensor")
    others = [lax.ppermute(array, "tensor", [(i, (i + k) % size) for i in range(size)]) for k in range(1, size)]
    return [array] + others


def to_tensor(held):
    size = lax.axis_size("tensor")
    total = held[0].astype(F32)
    for k in range(1, size):
        total += lax.ppermute(held[k], "tensor", [((i + k) % size, i) for i in range(size)]).astype(F32)
    return total


def gather_small(array):
    along, across, last = axis_steps()
    array = array[:, None, None]
    for step in [last] + across + along:
        other = exchange(array, step)
        axis = 2 if step[0] == "seq" else 1
        pair, swapped = jnp.concatenate([array, other], axis=axis), jnp.concatenate([other, array], axis=axis)
        array = jnp.where(lax.axis_index(step[0]) & step[1], swapped, pair)
    return array.reshape(array.shape[0], -1)


def sum_over(array, axes):
    for axis in axes:
        for k in range(lax.axis_size(axis).bit_length() - 1):
            array = array + exchange(array, (axis, 1 << k))
    return array


def scatter_order(along_first):
    along, across, _ = axis_steps()
    ordered = [list(reversed(along)), list(reversed(across))]
    return ordered[0] + ordered[1] if along_first else ordered[1] + ordered[0]


def tensor_sends(held, distances):
    size, here = lax.axis_size("tensor"), lax.axis_index("tensor")
    return [
        lax.ppermute(
            lax.dynamic_index_in_dim(held, lax.rem(here + k, size), 0, keepdims=False),
            "tensor",
            [(i, (i + k) % size) for i in range(size)],
        )
        for k in distances
    ]


def tensor_sum(held, received):
    own = lax.dynamic_index_in_dim(held, lax.axis_index("tensor"), 0, keepdims=False).astype(F32)
    return sum([array.astype(F32) for array in received], own)


def row_block(own, mask, piece):
    return pl.ds(pl.multiple_of((own ^ mask) * piece, piece), piece)


def store_turned(own, masks, ref, values, scratch):
    scratch[...] = values.T.astype(BF16)
    piece = scratch.shape[0] // len(masks)
    for j, mask in enumerate(masks):
        ref[j * piece : (j + 1) * piece, :] = scratch[row_block(own, mask, piece), :]


def swap_halves(values):
    lane = lax.broadcasted_iota(jnp.int32, values.shape, 1)
    size = values.shape[1]
    ahead = pltpu.roll(values, size - HD // 2, 1)
    behind = pltpu.roll(values, HD // 2, 1)
    return jnp.where(lane % HD < HD // 2, ahead, behind)


def half_sign(shape):
    lane = lax.broadcasted_iota(jnp.int32, shape, 1)
    return jnp.where(lane % HD < HD // 2, -1.0, 1.0)


def turn(values, cosine, sine):
    return values * cosine + swap_halves(values) * (sine * half_sign(values.shape))


def unturn(values, cosine, sine):
    return values * cosine - swap_halves(values * sine) * half_sign(values.shape)


def pair_lanes(values, head):
    lane = lax.broadcasted_iota(jnp.int32, values.shape, 1)
    return jnp.where((lane < HD) == (head == 0), values, 0.0)


def stack_pair(values):
    return jnp.concatenate([pair_lanes(values, 0), pair_lanes(values, 1)], axis=0).astype(BF16)


def norm_rate(values):
    return lax.rsqrt(jnp.mean(values * values, axis=-1, keepdims=True) + NORM_EPS)


def weight_specs(weights, first, count):
    groups, half, cols = weights[0].shape
    block = (groups, half, count * (cols // 4))
    spec = pl.BlockSpec(block, lambda *at: (0, 0, first // count), pipeline_mode=pl.Buffered(1))
    return [spec] * len(weights)


def lay(own, masks, w_all, w_refs):
    kinds = w_all.shape[0]
    groups, half, cols = w_refs[0].shape
    part = cols // kinds
    piece = 2 * half // len(masks)
    for z in range(len(w_refs) // 2 * groups):
        for j, mask in enumerate(masks):
            ref = w_refs[2 * (z // groups) + j // (len(masks) // 2)]
            at = j % (len(masks) // 2) * piece
            for m in range(kinds):
                w_all[m, row_block(own, mask, piece), z * part : (z + 1) * part] = ref[
                    z % groups, at : at + piece, m * part : (m + 1) * part
                ]


def project(own, masks, x_full, gain, cosine, sine, weights, block):
    tokens, width = x_full.shape
    heads = len(weights) // 2 * weights[0].shape[0] * weights[0].shape[2] // 4
    count = len(weights)
    mine = block // TILE

    def body(own_ref, x_ref, g_ref, cos_ref, sin_ref, *refs):
        w_refs, (at_ref, q_ref, k_ref, v_ref, w_all, a_one, turned) = refs[:count], refs[count:]
        own = own_ref[0]

        @pl.when(pl.program_id(0) == 0)
        def _():
            lay(own, masks, w_all, w_refs)

        values = x_ref[...].astype(F32)
        normed = values * norm_rate(values) * g_ref[...]
        a_one[...] = normed.astype(BF16)
        store_turned(own, masks, at_ref, normed, turned)
        cosine, sine = cos_ref[...], sin_ref[...]

        def rotated(ref, m):
            for at in range(0, heads, 2 * PAIR):
                mixed = mm(a_one[...], w_all[m, :, at : at + 2 * PAIR])
                for lane in (0, PAIR):
                    ref[:, at + lane : at + lane + PAIR] = turn(mixed[:, lane : lane + PAIR], cosine, sine).astype(BF16)

        rotated(k_ref, 1)
        v_ref[...] = mm(a_one[...], w_all[2]).astype(BF16)

        @pl.when(pl.program_id(0) < mine)
        def _():
            rotated(q_ref, 0)

    rows = lambda i: (i, 0)
    return call(
        body,
        "project",
        2 * (2 * tokens + block) * width * heads,
        (own, x_full, gain, cosine, sine, *weights),
        (tokens // TILE,),
        [
            scalar(),
            pl.BlockSpec((TILE, width), rows),
            whole((1, width)),
            pl.BlockSpec((TILE, PAIR), rows),
            pl.BlockSpec((TILE, PAIR), rows),
            *weight_specs(weights, 0, 3),
        ],
        [
            pl.BlockSpec((width, TILE), lambda i: (0, i)),
            pl.BlockSpec((TILE, heads), lambda i: (jnp.minimum(i, mine - 1), 0)),
            pl.BlockSpec((TILE, heads), rows),
            pl.BlockSpec((TILE, heads), rows),
        ],
        [out((width, tokens)), out((block, heads)), out((tokens, heads)), out((tokens, heads))],
        [pltpu.VMEM((3, width, heads), BF16), pltpu.VMEM((TILE, width), BF16), pltpu.VMEM((width, TILE), BF16)],
    )


def attend(reach, query, keys, values, query_marks, key_marks):
    block, heads = query.shape
    tokens = keys.shape[0]
    wide = 2 * PAIR
    count = block // TILE

    def body(reach, q_ref, k_ref, v_ref, qm_ref, km_ref, o_ref, lse_ref, turned, acc, top, total, kept):
        at = pl.program_id(1)
        first, last, shift = reach[2 * at], reach[2 * at + 1], reach[2 * count]

        @pl.when(at == 0)
        def _():
            for tile in range(tokens // TILE):
                rows = slice(tile * TILE, (tile + 1) * TILE)
                turned[:, rows] = v_ref[rows, :].astype(F32).T.astype(BF16)

        marks = jnp.concatenate([qm_ref[...], qm_ref[...]], axis=0)
        stacked = [
            jnp.concatenate([stack_pair(q_ref[:, p * PAIR : (p + 1) * PAIR].astype(F32) * SCALE), marks], axis=1)
            for p in range(2)
        ]
        top[...] = jnp.full_like(top, NEG)
        acc[...] = jnp.zeros_like(acc)
        total[...] = jnp.zeros_like(total)

        def by_eight(values):
            return values.reshape(values.shape[0] // 8, 8, values.shape[1])

        def score(tile, carry):
            rows = pl.ds(pl.multiple_of((tile ^ shift) * TILE, TILE), TILE)
            for p in range(2):
                lanes = slice(p * PAIR, (p + 1) * PAIR)
                scores = mm(jnp.concatenate([k_ref[rows, lanes], km_ref[rows, :]], axis=1), stacked[p], NT)
                kept[p, rows, :] = scores
                top[p] = jnp.maximum(top[p], jnp.max(by_eight(scores), axis=0))
            return carry

        lax.fori_loop(first, last, score, 0)
        tops = [jnp.max(top[p], axis=0, keepdims=True) for p in range(2)]

        def step(tile, carry):
            rows = pl.ds(pl.multiple_of((tile ^ shift) * TILE, TILE), TILE)
            for p in range(2):
                probs = jnp.exp(kept[p, rows, :] - tops[p])
                total[p] += jnp.sum(by_eight(probs), axis=0)
                probs = probs.astype(BF16)
                for h in range(2):
                    part = slice(p * PAIR + h * HD, p * PAIR + (h + 1) * HD)
                    acc[part, :] += mm(turned[part, rows], probs[:, h * TILE : (h + 1) * TILE])
            return carry

        lax.fori_loop(first, last, step, 0)
        for p in range(2):
            sums = jnp.sum(total[p], axis=0, keepdims=True)
            rate = 1.0 / sums
            for h in range(2):
                part = slice(p * PAIR + h * HD, p * PAIR + (h + 1) * HD)
                acc[part, :] = acc[part, :] * rate[:, h * TILE : (h + 1) * TILE]
            lse_ref[0, 0, p : p + 1, :] = tops[p] + jnp.log(sums)
        o_ref[...] = acc[...].T.astype(BF16)

    return call(
        body,
        "attend",
        4 * block * tokens * heads,
        (reach, query, keys, values, query_marks, key_marks),
        (heads // wide, count),
        [
            pl.BlockSpec((TILE, wide), lambda h, i, r: (i, h)),
            pl.BlockSpec((tokens, wide), lambda h, i, r: (0, h)),
            pl.BlockSpec((tokens, wide), lambda h, i, r: (0, h)),
            pl.BlockSpec((TILE, PAIR), lambda h, i, r: (i, 0)),
            pl.BlockSpec((tokens, PAIR), lambda h, i, r: (0, 0)),
        ],
        [
            pl.BlockSpec((TILE, wide), lambda h, i, r: (i, h)),
            pl.BlockSpec((1, 1, 2, 2 * TILE), lambda h, i, r: (h, i, 0, 0)),
        ],
        [out((block, heads)), out((heads // wide, count, 2, 2 * TILE), F32)],
        [
            pltpu.VMEM((wide, tokens), BF16),
            pltpu.VMEM((wide, TILE), F32),
            pltpu.VMEM((2, 8, 2 * TILE), F32),
            pltpu.VMEM((2, 8, 2 * TILE), F32),
            pltpu.VMEM((2, tokens, 2 * TILE), F32),
        ],
        prefetch=1,
    )


def lift(own, masks, attended, x_full, cotangent, gain, weights):
    block, heads = attended.shape
    width = x_full.shape[1]
    count = len(weights)

    def body(own_ref, o_ref, x_ref, c_ref, g_ref, *refs):
        w_refs, (h_ref, a_ref, at_ref, e_ref, et_ref, w_all, turned) = refs[:count], refs[count:]
        own = own_ref[0]

        @pl.when(pl.program_id(0) == 0)
        def _():
            lay(own, masks, w_all, w_refs)

        values = x_ref[...].astype(F32) + mm(o_ref[...], w_all[0], NT)
        h_ref[...] = values
        normed = values * norm_rate(values) * g_ref[...]
        a_ref[...] = normed.astype(BF16)
        store_turned(own, masks, at_ref, normed, turned)
        cotangent = c_ref[...]
        e_ref[...] = cotangent.astype(BF16)
        store_turned(own, masks, et_ref, cotangent, turned)

    rows = lambda i: (i, 0)
    wide = pl.BlockSpec((TILE, width), rows)
    tall = pl.BlockSpec((width, TILE), lambda i: (0, i))
    return call(
        body,
        "lift",
        2 * block * width * heads,
        (own, attended, x_full, cotangent, gain, *weights),
        (block // TILE,),
        [scalar(), pl.BlockSpec((TILE, heads), rows), wide, wide, whole((1, width)), *weight_specs(weights, 3, 1)],
        [wide, wide, tall, wide, tall],
        [out((block, width), F32), out((block, width)), out((width, block)), out((block, width)), out((width, block))],
        [pltpu.VMEM((1, width, heads), BF16), pltpu.VMEM((width, TILE), BF16)],
    )


def feed(normed, turned, cotangent, cotangent_turned, weights, chunk, hidden, after=()):
    block, width = normed.shape
    groups, owners, kinds, piece, _ = weights.shape
    half = width // 2
    cut = min(512, hidden)
    tile = min(512, block)

    def body(a_ref, at_ref, e_ref, et_ref, w_ref, b_out, d_out, ga_ref, gb_ref, b_ref, d_ref, mid, dgate, dup):
        @pl.when((pl.program_id(0) == 0) & (pl.program_id(1) == 0))
        def _():
            b_ref[...] = jnp.zeros_like(b_ref)
            d_ref[...] = jnp.zeros_like(d_ref)

        def weight(m):
            return w_ref[0, :, m].reshape(width, cut)

        def tokens(i, carry):
            rows = pl.ds(pl.multiple_of(i * tile, tile), tile)
            gate = mm(a_ref[rows, :], weight(0))
            upper = mm(a_ref[rows, :], weight(1))
            grad = mm(e_ref[rows, :], weight(2))
            sigma = jax.nn.sigmoid(gate)
            active = gate * sigma
            mid[rows, :] = (active * upper).astype(BF16)
            dgate[rows, :] = (grad * upper * (sigma * (1.0 + gate * (1.0 - sigma)))).astype(BF16)
            dup[rows, :] = (grad * active).astype(BF16)
            b_ref[rows, :] += mm(mid[rows, :], weight(2), NT)
            d_ref[rows, :] += mm(dgate[rows, :], weight(0), NT) + mm(dup[rows, :], weight(1), NT)
            return carry

        lax.fori_loop(0, block // tile, tokens, 0)
        for ref, rows in ((ga_ref, slice(0, half)), (gb_ref, slice(half, width))):
            ref[0, 0] = mm(at_ref[rows, :], dgate[...]).astype(BF16)
            ref[0, 1] = mm(at_ref[rows, :], dup[...]).astype(BF16)
            ref[0, 2] = mm(et_ref[rows, :], mid[...]).astype(BF16)

        @pl.when((pl.program_id(0) == groups - 1) & (pl.program_id(1) == hidden // cut - 1))
        def _():
            b_out[...] = b_ref[...].astype(BF16)
            d_out[...] = d_ref[...].astype(BF16)

    place = lambda z, j: (z, 0, 0, j)
    shape = (groups, kinds, half, hidden)
    return call(
        body,
        "feed",
        18 * block * width * hidden * groups,
        (normed, turned, cotangent, cotangent_turned, weights),
        (groups, hidden // cut),
        [
            whole((block, width)),
            whole((width, block)),
            whole((block, width)),
            whole((width, block)),
            pl.BlockSpec((1, owners, kinds, piece, cut), lambda z, j: (z, 0, 0, 0, chunk * (hidden // cut) + j)),
        ],
        [
            whole((block, width)),
            whole((block, width)),
            pl.BlockSpec((1, kinds, half, cut), place),
            pl.BlockSpec((1, kinds, half, cut), place),
        ],
        [out((block, width)), out((block, width)), out(shape), out(shape)],
        [pltpu.VMEM((block, width), F32)] * 2 + [pltpu.VMEM((block, cut), BF16)] * 3,
        after=after,
    )


def back(own, masks, hidden, branches, grads, cotangent, gain, weights, after=()):
    block, width = hidden.shape
    heads = len(weights) // 2 * weights[0].shape[0] * weights[0].shape[2] // 4
    many = len(weights)

    count = len(branches)

    def body(own_ref, h_ref, c_ref, g_ref, *refs):
        w_refs, refs = refs[:many], refs[many:]
        b_refs, d_refs, refs = refs[:count], refs[count : 2 * count], refs[2 * count :]
        y_ref, dh_ref, ct_ref, do_ref, gg_ref, w_all, turned = refs
        own = own_ref[0]

        @pl.when(pl.program_id(0) == 0)
        def _():
            lay(own, masks, w_all, w_refs)
            gg_ref[...] = jnp.zeros_like(gg_ref)

        hidden = h_ref[...]
        grad = sum([ref[...].astype(F32) for ref in d_refs[1:]], d_refs[0][...].astype(F32))
        y_ref[...] = sum([ref[...].astype(F32) for ref in b_refs], hidden).astype(BF16)
        rate = norm_rate(hidden)
        scaled = grad * g_ref[...]
        dot = jnp.mean(hidden * scaled, axis=-1, keepdims=True)
        result = c_ref[...] + rate * scaled - hidden * (rate * rate * rate * dot)
        dh_ref[...] = result
        store_turned(own, masks, ct_ref, result, turned)
        do_ref[...] = mm(result.astype(BF16), w_all[0]).astype(BF16)
        gg_ref[...] += jnp.sum(grad * hidden * rate, axis=0, keepdims=True)

    rows = lambda i: (i, 0)
    wide = pl.BlockSpec((TILE, width), rows)
    return call(
        body,
        "back",
        2 * block * width * heads,
        (own, hidden, cotangent, gain, *weights, *branches, *grads),
        (block // TILE,),
        [scalar(), wide, wide, whole((1, width)), *weight_specs(weights, 3, 1)] + [wide] * (2 * count),
        [
            wide,
            wide,
            pl.BlockSpec((width, TILE), lambda i: (0, i)),
            pl.BlockSpec((TILE, heads), rows),
            pl.BlockSpec((1, width), lambda i: (0, 0)),
        ],
        [
            out((block, width)),
            out((block, width), F32),
            out((width, block)),
            out((block, heads)),
            out((1, width), F32),
        ],
        [pltpu.VMEM((1, width, heads), BF16), pltpu.VMEM((width, TILE), BF16)],
        after=after,
    )


def unattend(base, sets, reach, query, grads, attended, keys, values, lse, query_marks, key_marks, cosine, sine, before, after=()):
    block, heads = query.shape
    tokens = keys.shape[0]
    wide = 2 * PAIR
    count = block // TILE

    def body(
        reach, q_ref, g_ref, o_ref, k_ref, v_ref, lse_ref, qm_ref, km_ref, cq_ref, sq_ref, ck_ref, sk_ref,
        dq_ref, dk_ref, dv_ref, keys_turned, dq_acc, dk_acc, dv_acc,
    ):
        at = pl.program_id(1)
        first, last, shift = reach[2 * at], reach[2 * at + 1], reach[2 * count]
        marks = jnp.concatenate([qm_ref[...], qm_ref[...]], axis=0)
        queries = q_ref[...].astype(F32) * SCALE
        grads = g_ref[...].astype(F32)
        product = (grads * o_ref[...].astype(F32)).T
        stacked, marked, stacked_grads, deltas = [], [], [], []
        for p in range(2):
            lanes = slice(p * PAIR, (p + 1) * PAIR)
            stacked.append(stack_pair(queries[:, lanes]))
            marked.append(jnp.concatenate([stacked[p], marks], axis=1))
            stacked_grads.append(stack_pair(grads[:, lanes]))
            sums = [
                jnp.sum(product[p * PAIR + h * HD : p * PAIR + (h + 1) * HD], axis=0, keepdims=True) for h in range(2)
            ]
            deltas.append(jnp.concatenate(sums, axis=1))
        dq_acc[...] = jnp.zeros_like(dq_acc)

        @pl.when(at == 0)
        def _():
            dk_acc[...] = jnp.zeros_like(dk_acc)
            dv_acc[...] = jnp.zeros_like(dv_acc)
            for tile in range(tokens // TILE):
                rows = slice(tile * TILE, (tile + 1) * TILE)
                keys_turned[:, rows] = k_ref[rows, :].astype(F32).T.astype(BF16)

        def step(tile, carry):
            rows = pl.ds(pl.multiple_of((tile ^ shift) * TILE, TILE), TILE)
            for p in range(2):
                lanes = slice(p * PAIR, (p + 1) * PAIR)
                scores = mm(jnp.concatenate([k_ref[rows, lanes], km_ref[rows, :]], axis=1), marked[p], NT)
                probs = jnp.exp(scores - lse_ref[0, 0, p : p + 1, :])
                prob_grads = mm(v_ref[rows, lanes], stacked_grads[p], NT)
                score_grads = (probs * (prob_grads - deltas[p])).astype(BF16)
                dv_acc[rows, lanes] += mm(probs.astype(BF16), stacked_grads[p])
                dk_acc[rows, lanes] += mm(score_grads, stacked[p])
                for h in range(2):
                    part = slice(p * PAIR + h * HD, p * PAIR + (h + 1) * HD)
                    dq_acc[part, :] += mm(keys_turned[part, rows], score_grads[:, h * TILE : (h + 1) * TILE])
            return carry

        lax.fori_loop(first, last, step, 0)
        grad = dq_acc[...].T * SCALE
        for lane in (0, PAIR):
            dq_ref[:, lane : lane + PAIR] = unturn(grad[:, lane : lane + PAIR], cq_ref[...], sq_ref[...]).astype(BF16)

        @pl.when(at == count - 1)
        def _():
            dv_ref[...] = dv_acc[...].astype(BF16)
            for lane in (0, PAIR):
                dk_ref[:, lane : lane + PAIR] = unturn(
                    dk_acc[:, lane : lane + PAIR], ck_ref[...], sk_ref[...]
                ).astype(BF16)

    tile = pl.BlockSpec((TILE, wide), lambda h, i, r: (i, base + h))
    full = pl.BlockSpec((tokens, wide), lambda h, i, r: (0, base + h))
    table = pl.BlockSpec((TILE, PAIR), lambda h, i, r: (i, 0))
    tables = pl.BlockSpec((tokens, PAIR), lambda h, i, r: (0, 0))
    return call(
        body,
        "unattend",
        10 * block * tokens * wide * sets,
        (reach, query, grads, attended, keys, values, lse, query_marks, key_marks, cosine, sine, cosine, sine),
        (sets, count),
        [
            tile,
            tile,
            tile,
            full,
            full,
            pl.BlockSpec((1, 1, 2, 2 * TILE), lambda h, i, r: (base + h, i, 0, 0)),
            table,
            tables,
            table,
            table,
            tables,
            tables,
        ],
        [
            tile,
            full,
            full,
        ],
        [out((block, heads)), out((tokens, heads)), out((tokens, heads))],
        [
            pltpu.VMEM((wide, tokens), BF16),
            pltpu.VMEM((wide, TILE), F32),
            pltpu.VMEM((tokens, wide), F32),
            pltpu.VMEM((tokens, wide), F32),
        ],
        prefetch=1,
        after=[*(before or ()), *after],
        aliases={13: 0, 14: 1, 15: 2} if before else {},
    )


def unproject(own, masks, grads, x_full, k, block, weights, after=()):
    width = x_full.shape[1]
    heads = grads[0].shape[1]
    kinds = len(grads)
    count = len(weights)
    base = k * block // TILE

    def body(own_ref, x_ref, *refs):
        g_refs, refs = refs[:kinds], refs[kinds:]
        w_refs, (da_ref, gg_ref, w_all) = refs[:count], refs[count:]

        @pl.when(pl.program_id(0) == 0)
        def _():
            gg_ref[...] = jnp.zeros_like(gg_ref)
            lay(own_ref[0], masks, w_all, w_refs)

        grad = mm(g_refs[0][...], w_all[3 - kinds], NT)
        for at in range(1, kinds):
            grad += mm(g_refs[at][...], w_all[3 - kinds + at], NT)
        da_ref[...] = grad.astype(BF16)
        values = x_ref[...].astype(F32)
        gg_ref[...] += jnp.sum(grad * values * norm_rate(values), axis=0, keepdims=True)

    def place(array):
        return (lambda i: (i, 0)) if array.shape[0] == block else (lambda i: (base + i, 0))

    return call(
        body,
        "unproject",
        2 * kinds * block * width * heads,
        (own, x_full, *grads, *weights),
        (block // TILE,),
        [scalar(), pl.BlockSpec((TILE, width), lambda i: (base + i, 0))]
        + [pl.BlockSpec((TILE, heads), place(array)) for array in grads]
        + weight_specs(weights, 0, 3),
        [pl.BlockSpec((TILE, width), lambda i: (i, 0)), pl.BlockSpec((1, width), lambda i: (0, 0))],
        [out((block, width)), out((1, width), F32)],
        [pltpu.VMEM((3, width, heads), BF16)],
        after=after,
    )


def weigh(own, masks, turned, cotangent_turned, dq, dk, dv, attended, x_full, weights, after=()):
    width, tokens = turned.shape
    block, heads = dq.shape
    groups, _, cols = weights[0].shape
    many = len(weights)
    groups *= many // 2
    part = cols // 4
    half, near = width // 2, groups // 2
    tiles = block // TILE

    def body(
        own_ref, at_ref, ct_ref, dq_ref, dk_ref, dv_ref, o_ref, x_ref, dq_row, dk_row, dv_row, *refs
    ):
        w_refs, (ga_near, gb_near, ga_far, gb_far, da_ref, gg_ref, w_all) = refs[:many], refs[many:]
        at = pl.program_id(0)

        def write(targets):
            for ref, rows in zip(targets, (slice(0, half), slice(half, width))):
                ref[0, :, :part] = mm(at_ref[rows, :block], dq_ref[...]).astype(BF16)
                ref[0, :, part : 2 * part] = mm(at_ref[rows, :], dk_ref[...]).astype(BF16)
                ref[0, :, 2 * part : 3 * part] = mm(at_ref[rows, :], dv_ref[...]).astype(BF16)
                ref[0, :, 3 * part :] = mm(ct_ref[rows, :], o_ref[...]).astype(BF16)

        @pl.when(at < near)
        def _():
            write((ga_near, gb_near))

        @pl.when((at >= near) & (at < groups))
        def _():
            write((ga_far, gb_far))

        @pl.when(at == 0)
        def _():
            gg_ref[...] = jnp.zeros_like(gg_ref)
            lay(own_ref[0], masks, w_all, w_refs)

        @pl.when(at < tiles)
        def _():
            grad = mm(dq_row[...], w_all[0], NT)
            grad += mm(dk_row[...], w_all[1], NT)
            grad += mm(dv_row[...], w_all[2], NT)
            da_ref[...] = grad.astype(BF16)
            values = x_ref[...].astype(F32)
            gg_ref[...] += jnp.sum(grad * values * norm_rate(values), axis=0, keepdims=True)

    column = lambda i: (0, jnp.minimum(i, groups - 1))
    row = lambda i: (jnp.minimum(i, tiles - 1), 0)
    shape = (near, half, cols)
    near_spec = pl.BlockSpec((1, half, cols), lambda i: (jnp.minimum(i, near - 1), 0, 0))
    far_spec = pl.BlockSpec((1, half, cols), lambda i: (jnp.clip(i - near, 0, near - 1), 0, 0))
    return call(
        body,
        "weigh",
        4 * (tokens + block) * width * heads + 6 * block * width * heads,
        (own, turned, cotangent_turned, dq, dk, dv, attended, x_full, dq, dk, dv, *weights),
        (max(groups, tiles),),
        [
            scalar(),
            whole(turned.shape),
            whole(cotangent_turned.shape),
            pl.BlockSpec((block, part), column),
            pl.BlockSpec((tokens, part), column),
            pl.BlockSpec((tokens, part), column),
            pl.BlockSpec((block, part), column),
            pl.BlockSpec((TILE, width), row),
            pl.BlockSpec((TILE, heads), row),
            pl.BlockSpec((TILE, heads), row),
            pl.BlockSpec((TILE, heads), row),
            *weight_specs(weights, 0, 3),
        ],
        [near_spec, near_spec, far_spec, far_spec, pl.BlockSpec((TILE, width), row), pl.BlockSpec((1, width), lambda i: (0, 0))],
        [out(shape)] * 4 + [out((block, width)), out((1, width), F32)],
        [pltpu.VMEM((3, width, heads), BF16)],
        after=after,
    )


def fold(kept, received, step, after=()):
    axis = None if step is None else 2 if step[0] == "seq" else 1
    shapes = [kept.shape]
    if axis is not None:
        half = kept.shape[axis] // 2
        shapes = [tuple(half if at == axis else n for at, n in enumerate(kept.shape))] * 2

    def body(kept_ref, received_ref, *refs):
        total = (kept_ref[...].astype(F32) + received_ref[...].astype(F32)).astype(BF16)
        if axis is None:
            refs[0][...] = total
        elif axis == 1:
            refs[0][...], refs[1][...] = total[:, :half], total[:, half:]
        else:
            refs[0][...], refs[1][...] = total[:, :, :half], total[:, :, half:]

    groups = kept.shape[0]
    run = next(n for n in range(groups, 0, -1) if groups % n == 0 and n * kept[0].size <= FOLD)
    spec = lambda shape: pl.BlockSpec((run, *shape[1:]), lambda g: (g, 0, 0, 0, 0))
    return call(
        body,
        "fold",
        kept.size,
        (kept, received),
        (groups // run,),
        [spec(kept.shape)] * 2,
        [spec(shape) for shape in shapes],
        [out(shape) for shape in shapes],
        after=after,
    )


def deliver(array, kind, after=()):
    rows, width = array.shape

    def body(x_ref, y_ref):
        y_ref[...] = x_ref[...].astype(kind)

    spec = pl.BlockSpec((2 * TILE, width), lambda i: (i, 0))
    return call(
        body, "deliver", rows * width, (array,), (rows // (2 * TILE),), [spec], [spec], [out(array.shape, kind)], after=after
    )[0]


def finish(x_full, hidden_grad, gain, parts, first, count, after=()):
    width = hidden_grad.shape[1]

    def body(x_ref, dh_ref, g_ref, *refs):
        grad = sum([ref[...].astype(F32) for ref in refs[1:-1]], refs[0][...].astype(F32))
        values = x_ref[...].astype(F32)
        rate = norm_rate(values)
        scaled = grad * g_ref[...]
        dot = jnp.mean(values * scaled, axis=-1, keepdims=True)
        refs[-1][...] = (dh_ref[...] + rate * scaled - values * (rate * rate * rate * dot)).astype(BF16)

    wide = pl.BlockSpec((TILE, width), lambda i: (first // TILE + i, 0))
    return call(
        body,
        "finish",
        16 * count * width,
        (x_full, hidden_grad, gain, *parts),
        (count // TILE,),
        [wide, wide, whole((1, width))] + [wide] * len(parts),
        [pl.BlockSpec((TILE, width), lambda i: (i, 0))],
        [out((count, width))],
        after=after,
    )[0]


def widen(target, repeated, own_rows, low, high, before):
    count, width = own_rows.shape
    step = min(2 * TILE, count)
    tiles = count // step

    def body(target, own_ref, low_ref, high_ref, y_ref):
        for side, ref in ((0, low_ref), (1, high_ref)):
            real = target[2 * side + 1] != 0

            @pl.when((pl.program_id(0) == side) & real)
            def _():
                y_ref[...] = ref[...].astype(F32)

            @pl.when((pl.program_id(0) == side) & jnp.logical_not(real))
            def _():
                y_ref[...] = own_ref[...].astype(F32)

    spec = pl.BlockSpec((step, width), lambda d, i, t: (i, 0))
    low_spec = pl.BlockSpec((step, width), lambda d, i, t: (jnp.where(d == 0, i, tiles - 1), 0))
    high_spec = pl.BlockSpec((step, width), lambda d, i, t: (jnp.where(d == 1, i, 0), 0))
    place = pl.BlockSpec((step, width), lambda d, i, t: (t[2 * d] * tiles + i, 0))
    before = [] if before is None else [before]
    return call(
        body,
        "widen",
        count * width,
        (target, own_rows, low, high),
        (2, tiles),
        [spec, low_spec, high_spec],
        [place],
        [out((repeated * count, width), F32)],
        prefetch=1,
        after=before,
        aliases={4: 0} if before else {},
    )[0]


def on_device(
    residual_in,
    grad_out,
    segment_lengths,
    attention_in,
    attention_out,
    expand,
    contract,
    gains,
    mean_attention_in,
    mean_attention_out,
    mean_expand,
    mean_contract,
    mean_gains,
    square_attention_in,
    square_attention_out,
    square_expand,
    square_contract,
    square_gains,
):
    span, copies = lax.axis_size("seq"), lax.axis_size("tensor")
    place, lane = lax.axis_index("seq"), lax.axis_index("tensor")
    rows, block, width = residual_in.shape
    tokens = span * block
    repeats = copies // rows
    row = lane // repeats
    piece = attention_in.shape[1]
    part = attention_in.shape[2]
    masks = owner_masks()
    index = lax.axis_index("dp") * span + place
    own = index.astype(jnp.int32)[None]
    near = copies // 2

    attention_piece = jnp.concatenate(
        [attention_in[0], attention_in[1], attention_in[2], attention_out.T], axis=1
    ).astype(BF16)
    feed_piece = jnp.stack([expand[0], expand[1], contract.T]).astype(BF16)
    feed_all = gather_owners(feed_piece, ("tensor", "dp", "seq"))
    x_own = lax.dynamic_index_in_dim(residual_in, row, 0, keepdims=False)
    cotangent = lax.dynamic_index_in_dim(grad_out, row, 0, keepdims=False)
    x_parts = [x_own] + [exchange(x_own, ("seq", k)) for k in range(1, span)]
    pieces = from_tensor(attention_piece)
    first, second = jnp.stack(pieces[:near]), jnp.stack(pieces[near:])
    x_parts, second = lax.optimization_barrier((x_parts, second))
    weights = (*gather_pieces(first, True), *gather_pieces(second, False))
    x_parts, small = lax.optimization_barrier((x_parts, gains.astype(BF16).astype(F32)))
    full_gains = gather_small(small)
    gain_one, gain_two = full_gains[:1], full_gains[1:]
    x_full = jnp.concatenate(x_parts, axis=0)
    lens = lax.dynamic_index_in_dim(segment_lengths, row, 0, keepdims=False)
    ends = jnp.cumsum(lens)
    starts = ends - lens
    blocks = place ^ jnp.arange(span, dtype=jnp.int32)
    places = (blocks[:, None] * block + jnp.arange(block, dtype=jnp.int32)[None, :]).reshape(tokens)
    segment = jnp.sum((places[:, None] >= ends[None, :]).astype(jnp.int32), axis=-1)
    picked = segment[:, None] == jnp.arange(lens.shape[0], dtype=jnp.int32)[None, :]
    begin = jnp.sum(jnp.where(picked, starts[None, :], 0), axis=-1)
    finish_at = jnp.sum(jnp.where(picked, ends[None, :], 0), axis=-1)
    freq = jnp.exp(jnp.arange(HD // 2, dtype=F32) * (-2.0 * jnp.log(10000.0) / HD))
    angle = (places - begin).astype(F32)[:, None] * freq
    cosine = jnp.tile(jnp.cos(angle), (1, PAIR // (HD // 2)))
    sine = jnp.tile(jnp.sin(angle), (1, PAIR // (HD // 2)))
    count = block // TILE
    firsts = begin[:block].reshape(count, TILE)[:, 0] // TILE
    lasts = (finish_at[:block].reshape(count, TILE)[:, -1] + TILE - 1) // TILE
    reach = jnp.concatenate(
        [jnp.stack([firsts, lasts], axis=1).reshape(-1), (place * (block // TILE))[None]]
    ).astype(jnp.int32)
    lanes = jnp.arange(PAIR, dtype=jnp.int32)[None, :]
    key_marks = jnp.where(segment[:, None] == lanes, NEG, 0.0).astype(BF16)
    query_marks = ((segment[:block, None] != lanes) & (lanes < lens.shape[0])).astype(BF16)

    chunks = 2
    cut = feed_piece.shape[2] // chunks

    turned_one, query, keys, values = project(own, masks, x_full, gain_one, cosine, sine, weights, block)
    attended, lse = attend(reach, query, keys, values, query_marks, key_marks)
    hidden, normed_two, turned_two, rounded, rounded_turned = lift(
        own, masks, attended, x_full, cotangent, gain_two, weights
    )

    def spread(array):
        half, columns = array.shape[-2:]
        return array.reshape(-1, half // (span * piece), span, piece, columns)

    last_step = axis_steps()[2]
    orders = [scatter_order(bool(at % 2)) for at in range(chunks)]
    flights, places, branches, grads = [], [0] * chunks, [], []

    def tie(anchor, *which):
        *tied, anchor = lax.optimization_barrier((*[flights[at] for at in which], anchor))
        for at, flight in zip(which, tied):
            flights[at] = tuple(flight) if isinstance(flight, (tuple, list)) else flight

    def move_on(*which):
        for at in which:
            if places[at] < len(orders[at]):
                step = orders[at][places[at]]
                kept, sent = fold(*flights[at], step)
                flights[at] = (kept, exchange(sent, step))
                places[at] += 1
            elif isinstance(flights[at], tuple):
                flights[at] = fold(*flights[at], None)[0]
        return [flights[at][0] if isinstance(flights[at], tuple) else flights[at] for at in which]

    for at in range(chunks):
        branch, grad, kept, sent = feed(normed_two, turned_two, rounded, rounded_turned, feed_all, at, cut, after=branches)
        flights.append((spread(kept), spread(exchange(sent, last_step))))
        branches.append(branch)
        grads.append(grad)
    result, hidden_grad, hidden_grad_turned, output_grad, grad_gain_two = back(
        own, masks, hidden, branches, grads, cotangent, gain_two, weights
    )
    tie(output_grad, 0, 1)
    residual_out = lax.all_gather(result, "tensor", axis=0)
    common = (reach, query, output_grad, attended, keys, values, lse, query_marks, key_marks, cosine, sine)
    sets = query.shape[1] // (2 * PAIR)
    found = unattend(0, sets - 1, *common, None, after=move_on(0, 1))
    tie(found[0], 0, 1)
    after = []
    for _ in orders[0][1:]:
        after = move_on(0, 1)
    dq, dk, dv = unattend(sets - 1, 1, *common, found, after=after)
    tie(dq, 0, 1)
    move_on(0, 1)
    feed_sums = jnp.concatenate([flight.reshape(copies, -1, piece, cut) for flight in flights], axis=-1)
    distances = list(range(1, copies))

    parts, gain_parts = [], []
    for k in range(1, span):
        grad, gain_part = unproject(own, masks, [dk, dv], x_full, k, block, weights, after=[feed_sums])
        parts.append(exchange(grad, ("seq", k)))
        gain_parts.append(gain_part)
    received = tensor_sends(feed_sums, distances)
    places = [0, 0]
    *found, own_grad, gain_part = weigh(
        own, masks, turned_one, hidden_grad_turned, dq, dk, dv, attended, x_full, weights, after=gain_parts
    )
    gain_parts.append(gain_part)
    steady = [*received, residual_out]
    shares = 1
    size = block // shares
    lines = []
    for at in range(shares):
        own_rows = finish(x_full, hidden_grad, gain_one, [own_grad] + parts, at * size, size, after=steady)
        lines.append([(own_rows, own_rows)])
    up = [(i, i + 1) for i in range(copies - 1)]
    down = [(i + 1, i) for i in range(copies - 1)]

    def hop(count):
        for _ in range(count):
            for line in lines:
                from_low, from_high = line[-1]
                line.append((lax.ppermute(from_low, "tensor", up), lax.ppermute(from_high, "tensor", down)))

    hop(1)
    found, _ = lax.optimization_barrier((found, lines[0][0][0]))
    flights = [(spread(found[at]), spread(exchange(found[at + 1], last_step))) for at in (0, 2)]
    while isinstance(flights[1], tuple):
        move_on(0, 1)
    attention_sums = [flights[z // near].reshape(near, piece, 4 * part)[z % near] for z in range(copies)]
    gain_grads = sum_over(jnp.concatenate([sum(gain_parts), grad_gain_two]), ("dp", "seq"))
    residual_out = residual_out[::repeats] if repeats > 1 else residual_out
    residual_out = deliver(residual_out.reshape(-1, width), BF16, after=[lines[0][0][0]])
    attention_sums, lines[0][1], gain_grads, residual_out = lax.optimization_barrier(
        (attention_sums, lines[0][1], gain_grads, residual_out)
    )
    hop(1)
    attention_shard = to_tensor(attention_sums)
    feed_shard = tensor_sum(feed_sums, received)

    share = 1.0 / repeats
    attention_shard, feed_shard = attention_shard * share, feed_shard * share
    gain_grads = sum_over(gain_grads * share, ("tensor",))
    gain_shard = lax.dynamic_slice_in_dim(gain_grads, index * piece, piece, 1)

    local = jnp.sum(attention_shard * attention_shard) + jnp.sum(feed_shard * feed_shard)
    def widened(distance, before):
        low, high = lane - distance, lane + distance
        target = [jnp.where(low >= 0, low, lane) // repeats, low >= 0, jnp.where(high < copies, high, lane) // repeats, high < copies]
        target = jnp.stack([jnp.asarray(entry).astype(jnp.int32) for entry in target])
        return widen(target, rows, lines[0][0][0], *lines[0][distance], before)

    grad_in = widened(1, None)
    local, grad_in = lax.optimization_barrier((local, grad_in))
    squares = sum_over(jnp.full((8, 128), local), ("tensor",))
    squares, gain_grads, lines[0][2] = lax.optimization_barrier((squares, gain_grads, lines[0][2]))
    hop(copies - 3)
    squares = sum_over(squares, ("dp", "seq"))
    norm = jnp.sqrt(squares[0, 0] + jnp.sum(gain_grads * gain_grads))
    for distance in range(2, copies):
        grad_in = widened(distance, grad_in)
    residual_out, grad_in = residual_out.reshape(rows, block, width), grad_in.reshape(rows, block, width)

    factor = jnp.minimum(1.0, CLIP / norm)
    shards = (
        jnp.stack([attention_shard[:, k * part : (k + 1) * part] for k in range(3)]),
        attention_shard[:, 3 * part :].T,
        feed_shard[:2],
        feed_shard[2].T,
        gain_shard,
    )
    masters = (attention_in, attention_out, expand, contract, gains)
    firsts = (mean_attention_in, mean_attention_out, mean_expand, mean_contract, mean_gains)
    seconds = (
        square_attention_in,
        square_attention_out,
        square_expand,
        square_contract,
        square_gains,
    )
    new_means = []
    new_squares = []
    new_weights = []
    for member in range(5):
        clipped = shards[member] * factor
        moment = BETA_ONE * firsts[member] + (1.0 - BETA_ONE) * clipped
        square = BETA_TWO * seconds[member] + (1.0 - BETA_TWO) * clipped * clipped
        update = (
            moment / (1.0 - BETA_ONE**STEP) / (jnp.sqrt(square / (1.0 - BETA_TWO**STEP)) + ADAM_EPS)
        )
        shrink = DECAY if member < 4 else 0.0
        speed = RATE if member < 4 else GAIN_RATE
        new_means.append(moment)
        new_squares.append(square)
        new_weights.append(masters[member] - speed * (update + shrink * masters[member]))
    return (residual_out, grad_in, norm, *new_means, *new_squares, *new_weights)


def solution(mesh):
    tokens = P("dp", "seq", None)
    weights = (
        P(None, ("dp", "seq"), "tensor"),
        P("tensor", ("dp", "seq")),
        P(None, ("dp", "seq"), "tensor"),
        P("tensor", ("dp", "seq")),
        P(None, ("dp", "seq")),
    )
    return jax.shard_map(
        on_device,
        mesh=mesh,
        in_specs=(tokens, tokens, P("dp", None)) + weights * 3,
        out_specs=(tokens, tokens, P()) + weights * 3,
        check_vma=False,
    )
```

```python
import jax
import jax.numpy as jnp
from jax import lax
from jax.experimental import pallas as pl
from jax.experimental.pallas import tpu as pltpu
from jax.sharding import PartitionSpec as P

HD = 64
STEP = 10

NORM_EPS = 1e-05
NEG = -1e30
CLIP = 1.0
RATE = 0.04
GAIN_RATE = 1.0
BETA_ONE = 0.9
BETA_TWO = 0.999
ADAM_EPS = 1e-08
DECAY = 0.1

SCALE = HD ** (-0.5)
PAIR = 2 * HD
TILE = 256
VMEM = 60 * 1024 * 1024
FOLD = 1024 * 1024
F32 = jnp.float32
BF16 = jnp.bfloat16

NN = (((1,), (0,)), ((), ()))
NT = (((1,), (1,)), ((), ()))
TN = (((0,), (0,)), ((), ()))


def mm(left, right, dims=NN):
    return lax.dot_general(left, right, dims, preferred_element_type=F32)


def call(body, name, flops, args, grid, in_specs, out_specs, out_shape, scratch=(), prefetch=0, after=(), aliases={}):
    count, extra = len(args), len(after)
    moved = sum(a.size * a.dtype.itemsize for a in args) + sum(o.size * o.dtype.itemsize for o in out_shape)
    return pl.pallas_call(
        lambda *refs: body(*refs[:count], *refs[count + extra :]),
        name=name,
        grid_spec=pltpu.PrefetchScalarGridSpec(
            num_scalar_prefetch=prefetch,
            grid=grid,
            in_specs=list(in_specs) + [pl.BlockSpec(memory_space=pl.ANY)] * extra,
            out_specs=out_specs,
            scratch_shapes=list(scratch),
        ),
        out_shape=out_shape,
        input_output_aliases=dict(aliases),
        compiler_params=pltpu.CompilerParams(vmem_limit_bytes=VMEM),
        cost_estimate=pl.CostEstimate(flops=int(flops) >> 24, bytes_accessed=int(moved) >> 20, transcendentals=0),
    )(*args, *after)


def whole(shape):
    return pl.BlockSpec(shape, lambda *at: (0,) * len(shape), pipeline_mode=pl.Buffered(1))


def scalar():
    return pl.BlockSpec(memory_space=pltpu.SMEM)


def out(shape, kind=BF16):
    return jax.ShapeDtypeStruct(shape, kind)


def exchange(block, step):
    axis, bit = step
    return lax.ppermute(block, axis, [(i ^ bit, i) for i in range(lax.axis_size(axis))])


def axis_steps():
    bits = lambda axis: [(axis, 1 << k) for k in range(lax.axis_size(axis).bit_length() - 1)]
    across = bits("dp")
    return bits("seq"), across[1:], across[0]


def owner_masks():
    span = lax.axis_size("seq")
    along, across, last = axis_steps()
    masks = [0]
    for axis, bit in along + across + [last]:
        masks += [m ^ (bit if axis == "seq" else bit * span) for m in masks]
    return masks


def gather_owners(array, axes):
    whole_array = lax.all_gather(array, axes, axis=0)
    return whole_array.reshape(lax.axis_size(axes[0]), -1, *array.shape)


def gather_pieces(pieces, along_first, gate):
    along, across, last = axis_steps()
    groups, rows, columns = pieces.shape
    held = pieces[:, None, None]
    for at, step in enumerate(along + across if along_first else across + along):
        if at == 1:
            held, gate = lax.optimization_barrier((held, gate))
        held = jnp.concatenate([held, exchange(held, step)], axis=2 if step[0] == "seq" else 1)
    held = held.reshape(groups, -1, columns)
    return (held, exchange(held, last)), gate


def from_tensor(array):
    size = lax.axis_size("tensor")
    others = [lax.ppermute(array, "tensor", [(i, (i + k) % size) for i in range(size)]) for k in range(1, size)]
    return [array] + others


def to_tensor(held):
    size = lax.axis_size("tensor")
    total = held[0].astype(F32)
    for k in range(1, size):
        total += lax.ppermute(held[k], "tensor", [((i + k) % size, i) for i in range(size)]).astype(F32)
    return total


def gather_small(array):
    along, across, last = axis_steps()
    array = array[:, None, None]
    for step in [last] + across + along:
        other = exchange(array, step)
        axis = 2 if step[0] == "seq" else 1
        pair, swapped = jnp.concatenate([array, other], axis=axis), jnp.concatenate([other, array], axis=axis)
        array = jnp.where(lax.axis_index(step[0]) & step[1], swapped, pair)
    return array.reshape(array.shape[0], -1)


def sum_over(array, axes):
    for axis in axes:
        for k in range(lax.axis_size(axis).bit_length() - 1):
            array = array + exchange(array, (axis, 1 << k))
    return array


def scatter_order(along_first):
    along, across, _ = axis_steps()
    ordered = [list(reversed(along)), list(reversed(across))]
    return ordered[0] + ordered[1] if along_first else ordered[1] + ordered[0]


def tensor_sends(held, distances):
    size, here = lax.axis_size("tensor"), lax.axis_index("tensor")
    return [
        lax.ppermute(
            lax.dynamic_index_in_dim(held, lax.rem(here + k, size), 0, keepdims=False),
            "tensor",
            [(i, (i + k) % size) for i in range(size)],
        )
        for k in distances
    ]


def tensor_sum(held, received):
    own = lax.dynamic_index_in_dim(held, lax.axis_index("tensor"), 0, keepdims=False).astype(F32)
    return sum([array.astype(F32) for array in received], own)


def row_block(own, mask, piece):
    return pl.ds(pl.multiple_of((own ^ mask) * piece, piece), piece)


def store_turned(own, masks, ref, values, scratch):
    scratch[...] = values.T.astype(BF16)
    piece = scratch.shape[0] // len(masks)
    for j, mask in enumerate(masks):
        ref[j * piece : (j + 1) * piece, :] = scratch[row_block(own, mask, piece), :]


def swap_halves(values):
    lane = lax.broadcasted_iota(jnp.int32, values.shape, 1)
    size = values.shape[1]
    ahead = pltpu.roll(values, size - HD // 2, 1)
    behind = pltpu.roll(values, HD // 2, 1)
    return jnp.where(lane % HD < HD // 2, ahead, behind)


def half_sign(shape):
    lane = lax.broadcasted_iota(jnp.int32, shape, 1)
    return jnp.where(lane % HD < HD // 2, -1.0, 1.0)


def turn(values, cosine, sine):
    return values * cosine + swap_halves(values) * (sine * half_sign(values.shape))


def unturn(values, cosine, sine):
    return values * cosine - swap_halves(values * sine) * half_sign(values.shape)


def pair_lanes(values, head):
    lane = lax.broadcasted_iota(jnp.int32, values.shape, 1)
    return jnp.where((lane < HD) == (head == 0), values, 0.0)


def stack_pair(values):
    return jnp.concatenate([pair_lanes(values, 0), pair_lanes(values, 1)], axis=0).astype(BF16)


def norm_rate(values):
    return lax.rsqrt(jnp.mean(values * values, axis=-1, keepdims=True) + NORM_EPS)


def weight_specs(weights, first, count):
    groups, half, cols = weights[0].shape
    block = (groups, half, count * (cols // 4))
    spec = pl.BlockSpec(block, lambda *at: (0, 0, first // count), pipeline_mode=pl.Buffered(1))
    return [spec] * len(weights)


def lay(own, masks, w_all, w_refs):
    kinds = w_all.shape[0]
    groups, half, cols = w_refs[0].shape
    part = cols // kinds
    piece = 2 * half // len(masks)
    for z in range(len(w_refs) // 2 * groups):
        for j, mask in enumerate(masks):
            ref = w_refs[2 * (z // groups) + j // (len(masks) // 2)]
            at = j % (len(masks) // 2) * piece
            for m in range(kinds):
                w_all[m, row_block(own, mask, piece), z * part : (z + 1) * part] = ref[
                    z % groups, at : at + piece, m * part : (m + 1) * part
                ]


def project(own, masks, x_full, gain, cosine, sine, weights, block):
    tokens, width = x_full.shape
    heads = len(weights) // 2 * weights[0].shape[0] * weights[0].shape[2] // 4
    count = len(weights)
    mine = block // TILE

    def body(own_ref, x_ref, g_ref, cos_ref, sin_ref, *refs):
        w_refs, (at_ref, q_ref, k_ref, v_ref, w_all, a_one, turned) = refs[:count], refs[count:]
        own = own_ref[0]

        @pl.when(pl.program_id(0) == 0)
        def _():
            lay(own, masks, w_all, w_refs)

        values = x_ref[...].astype(F32)
        normed = values * norm_rate(values) * g_ref[...]
        a_one[...] = normed.astype(BF16)
        store_turned(own, masks, at_ref, normed, turned)
        cosine, sine = cos_ref[...], sin_ref[...]

        def rotated(ref, m):
            for at in range(0, heads, 2 * PAIR):
                mixed = mm(a_one[...], w_all[m, :, at : at + 2 * PAIR])
                for lane in (0, PAIR):
                    ref[:, at + lane : at + lane + PAIR] = turn(mixed[:, lane : lane + PAIR], cosine, sine).astype(BF16)

        rotated(k_ref, 1)
        v_ref[...] = mm(a_one[...], w_all[2]).astype(BF16)

        @pl.when(pl.program_id(0) < mine)
        def _():
            rotated(q_ref, 0)

    rows = lambda i: (i, 0)
    return call(
        body,
        "project",
        2 * (2 * tokens + block) * width * heads,
        (own, x_full, gain, cosine, sine, *weights),
        (tokens // TILE,),
        [
            scalar(),
            pl.BlockSpec((TILE, width), rows),
            whole((1, width)),
            pl.BlockSpec((TILE, PAIR), rows),
            pl.BlockSpec((TILE, PAIR), rows),
            *weight_specs(weights, 0, 3),
        ],
        [
            pl.BlockSpec((width, TILE), lambda i: (0, i)),
            pl.BlockSpec((TILE, heads), lambda i: (jnp.minimum(i, mine - 1), 0)),
            pl.BlockSpec((TILE, heads), rows),
            pl.BlockSpec((TILE, heads), rows),
        ],
        [out((width, tokens)), out((block, heads)), out((tokens, heads)), out((tokens, heads))],
        [pltpu.VMEM((3, width, heads), BF16), pltpu.VMEM((TILE, width), BF16), pltpu.VMEM((width, TILE), BF16)],
    )


def attend(reach, query, keys, values, query_marks, key_marks):
    block, heads = query.shape
    tokens = keys.shape[0]
    wide = 2 * PAIR
    count = block // TILE

    def body(reach, q_ref, k_ref, v_ref, qm_ref, km_ref, o_ref, lse_ref, turned, acc, top, total, kept):
        at = pl.program_id(1)
        first, last, shift = reach[2 * at], reach[2 * at + 1], reach[2 * count]

        @pl.when(at == 0)
        def _():
            for tile in range(tokens // TILE):
                rows = slice(tile * TILE, (tile + 1) * TILE)
                turned[:, rows] = v_ref[rows, :].astype(F32).T.astype(BF16)

        marks = jnp.concatenate([qm_ref[...], qm_ref[...]], axis=0)
        stacked = [
            jnp.concatenate([stack_pair(q_ref[:, p * PAIR : (p + 1) * PAIR].astype(F32) * SCALE), marks], axis=1)
            for p in range(2)
        ]
        top[...] = jnp.full_like(top, NEG)
        acc[...] = jnp.zeros_like(acc)
        total[...] = jnp.zeros_like(total)

        def by_eight(values):
            return values.reshape(values.shape[0] // 8, 8, values.shape[1])

        def score(tile, carry):
            rows = pl.ds(pl.multiple_of((tile ^ shift) * TILE, TILE), TILE)
            for p in range(2):
                lanes = slice(p * PAIR, (p + 1) * PAIR)
                scores = mm(jnp.concatenate([k_ref[rows, lanes], km_ref[rows, :]], axis=1), stacked[p], NT)
                kept[p, rows, :] = scores
                top[p] = jnp.maximum(top[p], jnp.max(by_eight(scores), axis=0))
            return carry

        lax.fori_loop(first, last, score, 0)
        tops = [jnp.max(top[p], axis=0, keepdims=True) for p in range(2)]

        def step(tile, carry):
            rows = pl.ds(pl.multiple_of((tile ^ shift) * TILE, TILE), TILE)
            for p in range(2):
                probs = jnp.exp(kept[p, rows, :] - tops[p])
                total[p] += jnp.sum(by_eight(probs), axis=0)
                probs = probs.astype(BF16)
                for h in range(2):
                    part = slice(p * PAIR + h * HD, p * PAIR + (h + 1) * HD)
                    acc[part, :] += mm(turned[part, rows], probs[:, h * TILE : (h + 1) * TILE])
            return carry

        lax.fori_loop(first, last, step, 0)
        for p in range(2):
            sums = jnp.sum(total[p], axis=0, keepdims=True)
            rate = 1.0 / sums
            for h in range(2):
                part = slice(p * PAIR + h * HD, p * PAIR + (h + 1) * HD)
                acc[part, :] = acc[part, :] * rate[:, h * TILE : (h + 1) * TILE]
            lse_ref[0, 0, p : p + 1, :] = tops[p] + jnp.log(sums)
        o_ref[...] = acc[...].T.astype(BF16)

    return call(
        body,
        "attend",
        4 * block * tokens * heads,
        (reach, query, keys, values, query_marks, key_marks),
        (heads // wide, count),
        [
            pl.BlockSpec((TILE, wide), lambda h, i, r: (i, h)),
            pl.BlockSpec((tokens, wide), lambda h, i, r: (0, h)),
            pl.BlockSpec((tokens, wide), lambda h, i, r: (0, h)),
            pl.BlockSpec((TILE, PAIR), lambda h, i, r: (i, 0)),
            pl.BlockSpec((tokens, PAIR), lambda h, i, r: (0, 0)),
        ],
        [
            pl.BlockSpec((TILE, wide), lambda h, i, r: (i, h)),
            pl.BlockSpec((1, 1, 2, 2 * TILE), lambda h, i, r: (h, i, 0, 0)),
        ],
        [out((block, heads)), out((heads // wide, count, 2, 2 * TILE), F32)],
        [
            pltpu.VMEM((wide, tokens), BF16),
            pltpu.VMEM((wide, TILE), F32),
            pltpu.VMEM((2, 8, 2 * TILE), F32),
            pltpu.VMEM((2, 8, 2 * TILE), F32),
            pltpu.VMEM((2, tokens, 2 * TILE), F32),
        ],
        prefetch=1,
    )


def lift(own, masks, attended, x_full, cotangent, gain, weights):
    block, heads = attended.shape
    width = x_full.shape[1]
    count = len(weights)

    def body(own_ref, o_ref, x_ref, c_ref, g_ref, *refs):
        w_refs, (h_ref, a_ref, at_ref, e_ref, et_ref, w_all, turned) = refs[:count], refs[count:]
        own = own_ref[0]

        @pl.when(pl.program_id(0) == 0)
        def _():
            lay(own, masks, w_all, w_refs)

        values = x_ref[...].astype(F32) + mm(o_ref[...], w_all[0], NT)
        h_ref[...] = values
        normed = values * norm_rate(values) * g_ref[...]
        a_ref[...] = normed.astype(BF16)
        store_turned(own, masks, at_ref, normed, turned)
        cotangent = c_ref[...]
        e_ref[...] = cotangent.astype(BF16)
        store_turned(own, masks, et_ref, cotangent, turned)

    rows = lambda i: (i, 0)
    wide = pl.BlockSpec((TILE, width), rows)
    tall = pl.BlockSpec((width, TILE), lambda i: (0, i))
    return call(
        body,
        "lift",
        2 * block * width * heads,
        (own, attended, x_full, cotangent, gain, *weights),
        (block // TILE,),
        [scalar(), pl.BlockSpec((TILE, heads), rows), wide, wide, whole((1, width)), *weight_specs(weights, 3, 1)],
        [wide, wide, tall, wide, tall],
        [out((block, width), F32), out((block, width)), out((width, block)), out((block, width)), out((width, block))],
        [pltpu.VMEM((1, width, heads), BF16), pltpu.VMEM((width, TILE), BF16)],
    )


def feed(normed, turned, cotangent, cotangent_turned, weights, chunk, hidden, after=()):
    block, width = normed.shape
    groups, owners, kinds, piece, _ = weights.shape
    half = width // 2
    cut = min(512, hidden)
    tile = min(512, block)

    def body(a_ref, at_ref, e_ref, et_ref, w_ref, b_out, d_out, ga_ref, gb_ref, b_ref, d_ref, mid, dgate, dup):
        @pl.when((pl.program_id(0) == 0) & (pl.program_id(1) == 0))
        def _():
            b_ref[...] = jnp.zeros_like(b_ref)
            d_ref[...] = jnp.zeros_like(d_ref)

        def weight(m):
            return w_ref[0, :, m].reshape(width, cut)

        def tokens(i, carry):
            rows = pl.ds(pl.multiple_of(i * tile, tile), tile)
            gate = mm(a_ref[rows, :], weight(0))
            upper = mm(a_ref[rows, :], weight(1))
            grad = mm(e_ref[rows, :], weight(2))
            sigma = jax.nn.sigmoid(gate)
            active = gate * sigma
            mid[rows, :] = (active * upper).astype(BF16)
            dgate[rows, :] = (grad * upper * (sigma * (1.0 + gate * (1.0 - sigma)))).astype(BF16)
            dup[rows, :] = (grad * active).astype(BF16)
            b_ref[rows, :] += mm(mid[rows, :], weight(2), NT)
            d_ref[rows, :] += mm(dgate[rows, :], weight(0), NT) + mm(dup[rows, :], weight(1), NT)
            return carry

        lax.fori_loop(0, block // tile, tokens, 0)
        for ref, rows in ((ga_ref, slice(0, half)), (gb_ref, slice(half, width))):
            ref[0, 0] = mm(at_ref[rows, :], dgate[...]).astype(BF16)
            ref[0, 1] = mm(at_ref[rows, :], dup[...]).astype(BF16)
            ref[0, 2] = mm(et_ref[rows, :], mid[...]).astype(BF16)

        @pl.when((pl.program_id(0) == groups - 1) & (pl.program_id(1) == hidden // cut - 1))
        def _():
            b_out[...] = b_ref[...].astype(BF16)
            d_out[...] = d_ref[...].astype(BF16)

    place = lambda z, j: (z, 0, 0, j)
    shape = (groups, kinds, half, hidden)
    return call(
        body,
        "feed",
        18 * block * width * hidden * groups,
        (normed, turned, cotangent, cotangent_turned, weights),
        (groups, hidden // cut),
        [
            whole((block, width)),
            whole((width, block)),
            whole((block, width)),
            whole((width, block)),
            pl.BlockSpec((1, owners, kinds, piece, cut), lambda z, j: (z, 0, 0, 0, chunk * (hidden // cut) + j)),
        ],
        [
            whole((block, width)),
            whole((block, width)),
            pl.BlockSpec((1, kinds, half, cut), place),
            pl.BlockSpec((1, kinds, half, cut), place),
        ],
        [out((block, width)), out((block, width)), out(shape), out(shape)],
        [pltpu.VMEM((block, width), F32)] * 2 + [pltpu.VMEM((block, cut), BF16)] * 3,
        after=after,
    )


def back(own, masks, hidden, branches, grads, cotangent, gain, weights, after=()):
    block, width = hidden.shape
    heads = len(weights) // 2 * weights[0].shape[0] * weights[0].shape[2] // 4
    many = len(weights)

    count = len(branches)

    def body(own_ref, h_ref, c_ref, g_ref, *refs):
        w_refs, refs = refs[:many], refs[many:]
        b_refs, d_refs, refs = refs[:count], refs[count : 2 * count], refs[2 * count :]
        y_ref, dh_ref, ct_ref, do_ref, gg_ref, w_all, turned = refs
        own = own_ref[0]

        @pl.when(pl.program_id(0) == 0)
        def _():
            lay(own, masks, w_all, w_refs)
            gg_ref[...] = jnp.zeros_like(gg_ref)

        hidden = h_ref[...]
        grad = sum([ref[...].astype(F32) for ref in d_refs[1:]], d_refs[0][...].astype(F32))
        y_ref[...] = sum([ref[...].astype(F32) for ref in b_refs], hidden).astype(BF16)
        rate = norm_rate(hidden)
        scaled = grad * g_ref[...]
        dot = jnp.mean(hidden * scaled, axis=-1, keepdims=True)
        result = c_ref[...] + rate * scaled - hidden * (rate * rate * rate * dot)
        dh_ref[...] = result
        store_turned(own, masks, ct_ref, result, turned)
        do_ref[...] = mm(result.astype(BF16), w_all[0]).astype(BF16)
        gg_ref[...] += jnp.sum(grad * hidden * rate, axis=0, keepdims=True)

    rows = lambda i: (i, 0)
    wide = pl.BlockSpec((TILE, width), rows)
    return call(
        body,
        "back",
        2 * block * width * heads,
        (own, hidden, cotangent, gain, *weights, *branches, *grads),
        (block // TILE,),
        [scalar(), wide, wide, whole((1, width)), *weight_specs(weights, 3, 1)] + [wide] * (2 * count),
        [
            wide,
            wide,
            pl.BlockSpec((width, TILE), lambda i: (0, i)),
            pl.BlockSpec((TILE, heads), rows),
            pl.BlockSpec((1, width), lambda i: (0, 0)),
        ],
        [
            out((block, width)),
            out((block, width), F32),
            out((width, block)),
            out((block, heads)),
            out((1, width), F32),
        ],
        [pltpu.VMEM((1, width, heads), BF16), pltpu.VMEM((width, TILE), BF16)],
        after=after,
    )


def unattend(base, sets, reach, query, grads, attended, keys, values, lse, query_marks, key_marks, cosine, sine, before, after=()):
    block, heads = query.shape
    tokens = keys.shape[0]
    wide = 2 * PAIR
    count = block // TILE

    def body(
        reach, q_ref, g_ref, o_ref, k_ref, v_ref, lse_ref, qm_ref, km_ref, cq_ref, sq_ref, ck_ref, sk_ref,
        dq_ref, dk_ref, dv_ref, keys_turned, dq_acc, dk_acc, dv_acc,
    ):
        at = pl.program_id(1)
        first, last, shift = reach[2 * at], reach[2 * at + 1], reach[2 * count]
        marks = jnp.concatenate([qm_ref[...], qm_ref[...]], axis=0)
        queries = q_ref[...].astype(F32) * SCALE
        grads = g_ref[...].astype(F32)
        product = (grads * o_ref[...].astype(F32)).T
        stacked, marked, stacked_grads, deltas = [], [], [], []
        for p in range(2):
            lanes = slice(p * PAIR, (p + 1) * PAIR)
            stacked.append(stack_pair(queries[:, lanes]))
            marked.append(jnp.concatenate([stacked[p], marks], axis=1))
            stacked_grads.append(stack_pair(grads[:, lanes]))
            sums = [
                jnp.sum(product[p * PAIR + h * HD : p * PAIR + (h + 1) * HD], axis=0, keepdims=True) for h in range(2)
            ]
            deltas.append(jnp.concatenate(sums, axis=1))
        dq_acc[...] = jnp.zeros_like(dq_acc)

        @pl.when(at == 0)
        def _():
            dk_acc[...] = jnp.zeros_like(dk_acc)
            dv_acc[...] = jnp.zeros_like(dv_acc)
            for tile in range(tokens // TILE):
                rows = slice(tile * TILE, (tile + 1) * TILE)
                keys_turned[:, rows] = k_ref[rows, :].astype(F32).T.astype(BF16)

        def step(tile, carry):
            rows = pl.ds(pl.multiple_of((tile ^ shift) * TILE, TILE), TILE)
            for p in range(2):
                lanes = slice(p * PAIR, (p + 1) * PAIR)
                scores = mm(jnp.concatenate([k_ref[rows, lanes], km_ref[rows, :]], axis=1), marked[p], NT)
                probs = jnp.exp(scores - lse_ref[0, 0, p : p + 1, :])
                prob_grads = mm(v_ref[rows, lanes], stacked_grads[p], NT)
                score_grads = (probs * (prob_grads - deltas[p])).astype(BF16)
                dv_acc[rows, lanes] += mm(probs.astype(BF16), stacked_grads[p])
                dk_acc[rows, lanes] += mm(score_grads, stacked[p])
                for h in range(2):
                    part = slice(p * PAIR + h * HD, p * PAIR + (h + 1) * HD)
                    dq_acc[part, :] += mm(keys_turned[part, rows], score_grads[:, h * TILE : (h + 1) * TILE])
            return carry

        lax.fori_loop(first, last, step, 0)
        grad = dq_acc[...].T * SCALE
        for lane in (0, PAIR):
            dq_ref[:, lane : lane + PAIR] = unturn(grad[:, lane : lane + PAIR], cq_ref[...], sq_ref[...]).astype(BF16)

        @pl.when(at == count - 1)
        def _():
            dv_ref[...] = dv_acc[...].astype(BF16)
            for lane in (0, PAIR):
                dk_ref[:, lane : lane + PAIR] = unturn(
                    dk_acc[:, lane : lane + PAIR], ck_ref[...], sk_ref[...]
                ).astype(BF16)

    tile = pl.BlockSpec((TILE, wide), lambda h, i, r: (i, base + h))
    full = pl.BlockSpec((tokens, wide), lambda h, i, r: (0, base + h))
    table = pl.BlockSpec((TILE, PAIR), lambda h, i, r: (i, 0))
    tables = pl.BlockSpec((tokens, PAIR), lambda h, i, r: (0, 0))
    return call(
        body,
        "unattend",
        10 * block * tokens * wide * sets,
        (reach, query, grads, attended, keys, values, lse, query_marks, key_marks, cosine, sine, cosine, sine),
        (sets, count),
        [
            tile,
            tile,
            tile,
            full,
            full,
            pl.BlockSpec((1, 1, 2, 2 * TILE), lambda h, i, r: (base + h, i, 0, 0)),
            table,
            tables,
            table,
            table,
            tables,
            tables,
        ],
        [
            tile,
            full,
            full,
        ],
        [out((block, heads)), out((tokens, heads)), out((tokens, heads))],
        [
            pltpu.VMEM((wide, tokens), BF16),
            pltpu.VMEM((wide, TILE), F32),
            pltpu.VMEM((tokens, wide), F32),
            pltpu.VMEM((tokens, wide), F32),
        ],
        prefetch=1,
        after=[*(before or ()), *after],
        aliases={13: 0, 14: 1, 15: 2} if before else {},
    )


def unproject(own, masks, grads, x_full, k, block, weights, after=()):
    width = x_full.shape[1]
    heads = grads[0].shape[1]
    kinds = len(grads)
    count = len(weights)
    base = k * block // TILE

    def body(own_ref, x_ref, *refs):
        g_refs, refs = refs[:kinds], refs[kinds:]
        w_refs, (da_ref, gg_ref, w_all) = refs[:count], refs[count:]

        @pl.when(pl.program_id(0) == 0)
        def _():
            gg_ref[...] = jnp.zeros_like(gg_ref)
            lay(own_ref[0], masks, w_all, w_refs)

        grad = mm(g_refs[0][...], w_all[3 - kinds], NT)
        for at in range(1, kinds):
            grad += mm(g_refs[at][...], w_all[3 - kinds + at], NT)
        da_ref[...] = grad.astype(BF16)
        values = x_ref[...].astype(F32)
        gg_ref[...] += jnp.sum(grad * values * norm_rate(values), axis=0, keepdims=True)

    def place(array):
        return (lambda i: (i, 0)) if array.shape[0] == block else (lambda i: (base + i, 0))

    return call(
        body,
        "unproject",
        2 * kinds * block * width * heads,
        (own, x_full, *grads, *weights),
        (block // TILE,),
        [scalar(), pl.BlockSpec((TILE, width), lambda i: (base + i, 0))]
        + [pl.BlockSpec((TILE, heads), place(array)) for array in grads]
        + weight_specs(weights, 0, 3),
        [pl.BlockSpec((TILE, width), lambda i: (i, 0)), pl.BlockSpec((1, width), lambda i: (0, 0))],
        [out((block, width)), out((1, width), F32)],
        [pltpu.VMEM((3, width, heads), BF16)],
        after=after,
    )


def weigh(own, masks, turned, cotangent_turned, dq, dk, dv, attended, x_full, weights, after=()):
    width, tokens = turned.shape
    block, heads = dq.shape
    groups, _, cols = weights[0].shape
    many = len(weights)
    groups *= many // 2
    part = cols // 4
    half, near = width // 2, groups // 2
    tiles = block // TILE

    def body(
        own_ref, at_ref, ct_ref, dq_ref, dk_ref, dv_ref, o_ref, x_ref, dq_row, dk_row, dv_row, *refs
    ):
        w_refs, (ga_near, gb_near, ga_far, gb_far, da_ref, gg_ref, w_all) = refs[:many], refs[many:]
        at = pl.program_id(0)

        def write(targets):
            for ref, rows in zip(targets, (slice(0, half), slice(half, width))):
                ref[0, :, :part] = mm(at_ref[rows, :block], dq_ref[...]).astype(BF16)
                ref[0, :, part : 2 * part] = mm(at_ref[rows, :], dk_ref[...]).astype(BF16)
                ref[0, :, 2 * part : 3 * part] = mm(at_ref[rows, :], dv_ref[...]).astype(BF16)
                ref[0, :, 3 * part :] = mm(ct_ref[rows, :], o_ref[...]).astype(BF16)

        @pl.when(at < near)
        def _():
            write((ga_near, gb_near))

        @pl.when((at >= near) & (at < groups))
        def _():
            write((ga_far, gb_far))

        @pl.when(at == 0)
        def _():
            gg_ref[...] = jnp.zeros_like(gg_ref)
            lay(own_ref[0], masks, w_all, w_refs)

        @pl.when(at < tiles)
        def _():
            grad = mm(dq_row[...], w_all[0], NT)
            grad += mm(dk_row[...], w_all[1], NT)
            grad += mm(dv_row[...], w_all[2], NT)
            da_ref[...] = grad.astype(BF16)
            values = x_ref[...].astype(F32)
            gg_ref[...] += jnp.sum(grad * values * norm_rate(values), axis=0, keepdims=True)

    column = lambda i: (0, jnp.minimum(i, groups - 1))
    row = lambda i: (jnp.minimum(i, tiles - 1), 0)
    shape = (near, half, cols)
    near_spec = pl.BlockSpec((1, half, cols), lambda i: (jnp.minimum(i, near - 1), 0, 0))
    far_spec = pl.BlockSpec((1, half, cols), lambda i: (jnp.clip(i - near, 0, near - 1), 0, 0))
    return call(
        body,
        "weigh",
        4 * (tokens + block) * width * heads + 6 * block * width * heads,
        (own, turned, cotangent_turned, dq, dk, dv, attended, x_full, dq, dk, dv, *weights),
        (max(groups, tiles),),
        [
            scalar(),
            whole(turned.shape),
            whole(cotangent_turned.shape),
            pl.BlockSpec((block, part), column),
            pl.BlockSpec((tokens, part), column),
            pl.BlockSpec((tokens, part), column),
            pl.BlockSpec((block, part), column),
            pl.BlockSpec((TILE, width), row),
            pl.BlockSpec((TILE, heads), row),
            pl.BlockSpec((TILE, heads), row),
            pl.BlockSpec((TILE, heads), row),
            *weight_specs(weights, 0, 3),
        ],
        [near_spec, near_spec, far_spec, far_spec, pl.BlockSpec((TILE, width), row), pl.BlockSpec((1, width), lambda i: (0, 0))],
        [out(shape)] * 4 + [out((block, width)), out((1, width), F32)],
        [pltpu.VMEM((3, width, heads), BF16)],
        after=after,
    )


def fold(kept, received, step, after=()):
    axis = None if step is None else 2 if step[0] == "seq" else 1
    shapes = [kept.shape]
    if axis is not None:
        half = kept.shape[axis] // 2
        shapes = [tuple(half if at == axis else n for at, n in enumerate(kept.shape))] * 2

    def body(kept_ref, received_ref, *refs):
        total = (kept_ref[...].astype(F32) + received_ref[...].astype(F32)).astype(BF16)
        if axis is None:
            refs[0][...] = total
        elif axis == 1:
            refs[0][...], refs[1][...] = total[:, :half], total[:, half:]
        else:
            refs[0][...], refs[1][...] = total[:, :, :half], total[:, :, half:]

    groups = kept.shape[0]
    run = next(n for n in range(groups, 0, -1) if groups % n == 0 and n * kept[0].size <= FOLD)
    spec = lambda shape: pl.BlockSpec((run, *shape[1:]), lambda g: (g, 0, 0, 0, 0))
    return call(
        body,
        "fold",
        kept.size,
        (kept, received),
        (groups // run,),
        [spec(kept.shape)] * 2,
        [spec(shape) for shape in shapes],
        [out(shape) for shape in shapes],
        after=after,
    )


def deliver(array, kind, after=()):
    rows, width = array.shape

    def body(x_ref, y_ref):
        y_ref[...] = x_ref[...].astype(kind)

    spec = pl.BlockSpec((2 * TILE, width), lambda i: (i, 0))
    return call(
        body, "deliver", rows * width, (array,), (rows // (2 * TILE),), [spec], [spec], [out(array.shape, kind)], after=after
    )[0]


def finish(x_full, hidden_grad, gain, parts, first, count, after=()):
    width = hidden_grad.shape[1]

    def body(x_ref, dh_ref, g_ref, *refs):
        grad = sum([ref[...].astype(F32) for ref in refs[1:-1]], refs[0][...].astype(F32))
        values = x_ref[...].astype(F32)
        rate = norm_rate(values)
        scaled = grad * g_ref[...]
        dot = jnp.mean(values * scaled, axis=-1, keepdims=True)
        refs[-1][...] = (dh_ref[...] + rate * scaled - values * (rate * rate * rate * dot)).astype(BF16)

    wide = pl.BlockSpec((TILE, width), lambda i: (first // TILE + i, 0))
    return call(
        body,
        "finish",
        16 * count * width,
        (x_full, hidden_grad, gain, *parts),
        (count // TILE,),
        [wide, wide, whole((1, width))] + [wide] * len(parts),
        [pl.BlockSpec((TILE, width), lambda i: (i, 0))],
        [out((count, width))],
        after=after,
    )[0]


def widen(target, repeated, own_rows, low, high, before):
    count, width = own_rows.shape
    step = min(2 * TILE, count)
    tiles = count // step

    def body(target, own_ref, low_ref, high_ref, y_ref):
        for side, ref in ((0, low_ref), (1, high_ref)):
            real = target[2 * side + 1] != 0

            @pl.when((pl.program_id(0) == side) & real)
            def _():
                y_ref[...] = ref[...].astype(F32)

            @pl.when((pl.program_id(0) == side) & jnp.logical_not(real))
            def _():
                y_ref[...] = own_ref[...].astype(F32)

    spec = pl.BlockSpec((step, width), lambda d, i, t: (i, 0))
    low_spec = pl.BlockSpec((step, width), lambda d, i, t: (jnp.where(d == 0, i, tiles - 1), 0))
    high_spec = pl.BlockSpec((step, width), lambda d, i, t: (jnp.where(d == 1, i, 0), 0))
    place = pl.BlockSpec((step, width), lambda d, i, t: (t[2 * d] * tiles + i, 0))
    before = [] if before is None else [before]
    return call(
        body,
        "widen",
        count * width,
        (target, own_rows, low, high),
        (2, tiles),
        [spec, low_spec, high_spec],
        [place],
        [out((repeated * count, width), F32)],
        prefetch=1,
        after=before,
        aliases={4: 0} if before else {},
    )[0]


def on_device(
    residual_in,
    grad_out,
    segment_lengths,
    attention_in,
    attention_out,
    expand,
    contract,
    gains,
    mean_attention_in,
    mean_attention_out,
    mean_expand,
    mean_contract,
    mean_gains,
    square_attention_in,
    square_attention_out,
    square_expand,
    square_contract,
    square_gains,
):
    span, copies = lax.axis_size("seq"), lax.axis_size("tensor")
    place, lane = lax.axis_index("seq"), lax.axis_index("tensor")
    rows, block, width = residual_in.shape
    tokens = span * block
    repeats = copies // rows
    row = lane // repeats
    piece = attention_in.shape[1]
    part = attention_in.shape[2]
    masks = owner_masks()
    index = lax.axis_index("dp") * span + place
    own = index.astype(jnp.int32)[None]
    near = copies // 2

    attention_piece = jnp.concatenate(
        [attention_in[0], attention_in[1], attention_in[2], attention_out.T], axis=1
    ).astype(BF16)
    feed_piece = jnp.stack([expand[0], expand[1], contract.T]).astype(BF16)
    feed_all = gather_owners(feed_piece, ("tensor", "dp", "seq"))
    x_own = lax.dynamic_index_in_dim(residual_in, row, 0, keepdims=False)
    cotangent = lax.dynamic_index_in_dim(grad_out, row, 0, keepdims=False)
    x_parts = [x_own] + [exchange(x_own, ("seq", k)) for k in range(1, span)]
    pieces = from_tensor(attention_piece)
    first, second = jnp.stack(pieces[:near]), jnp.stack(pieces[near:])
    x_parts, second = lax.optimization_barrier((x_parts, second))
    x_parts, small = lax.optimization_barrier((x_parts, gains.astype(BF16).astype(F32)))
    full_gains = gather_small(small)
    weights_one, full_gains = gather_pieces(first, True, full_gains)
    weights_two, x_parts = gather_pieces(second, False, x_parts)
    weights = (*weights_one, *weights_two)
    gain_one, gain_two = full_gains[:1], full_gains[1:]
    x_full = jnp.concatenate(x_parts, axis=0)
    lens = lax.dynamic_index_in_dim(segment_lengths, row, 0, keepdims=False)
    ends = jnp.cumsum(lens)
    starts = ends - lens
    blocks = place ^ jnp.arange(span, dtype=jnp.int32)
    places = (blocks[:, None] * block + jnp.arange(block, dtype=jnp.int32)[None, :]).reshape(tokens)
    segment = jnp.sum((places[:, None] >= ends[None, :]).astype(jnp.int32), axis=-1)
    picked = segment[:, None] == jnp.arange(lens.shape[0], dtype=jnp.int32)[None, :]
    begin = jnp.sum(jnp.where(picked, starts[None, :], 0), axis=-1)
    finish_at = jnp.sum(jnp.where(picked, ends[None, :], 0), axis=-1)
    freq = jnp.exp(jnp.arange(HD // 2, dtype=F32) * (-2.0 * jnp.log(10000.0) / HD))
    angle = (places - begin).astype(F32)[:, None] * freq
    cosine = jnp.tile(jnp.cos(angle), (1, PAIR // (HD // 2)))
    sine = jnp.tile(jnp.sin(angle), (1, PAIR // (HD // 2)))
    count = block // TILE
    firsts = begin[:block].reshape(count, TILE)[:, 0] // TILE
    lasts = (finish_at[:block].reshape(count, TILE)[:, -1] + TILE - 1) // TILE
    reach = jnp.concatenate(
        [jnp.stack([firsts, lasts], axis=1).reshape(-1), (place * (block // TILE))[None]]
    ).astype(jnp.int32)
    lanes = jnp.arange(PAIR, dtype=jnp.int32)[None, :]
    key_marks = jnp.where(segment[:, None] == lanes, NEG, 0.0).astype(BF16)
    query_marks = ((segment[:block, None] != lanes) & (lanes < lens.shape[0])).astype(BF16)

    chunks = 2
    cut = feed_piece.shape[2] // chunks

    turned_one, query, keys, values = project(own, masks, x_full, gain_one, cosine, sine, weights, block)
    attended, lse = attend(reach, query, keys, values, query_marks, key_marks)
    hidden, normed_two, turned_two, rounded, rounded_turned = lift(
        own, masks, attended, x_full, cotangent, gain_two, weights
    )

    def spread(array):
        half, columns = array.shape[-2:]
        return array.reshape(-1, half // (span * piece), span, piece, columns)

    last_step = axis_steps()[2]
    orders = [scatter_order(bool(at % 2)) for at in range(chunks)]
    flights, places, branches, grads = [], [0] * chunks, [], []

    def tie(anchor, *which):
        *tied, anchor = lax.optimization_barrier((*[flights[at] for at in which], anchor))
        for at, flight in zip(which, tied):
            flights[at] = tuple(flight) if isinstance(flight, (tuple, list)) else flight

    def move_on(*which):
        for at in which:
            if places[at] < len(orders[at]):
                step = orders[at][places[at]]
                kept, sent = fold(*flights[at], step)
                flights[at] = (kept, exchange(sent, step))
                places[at] += 1
            elif isinstance(flights[at], tuple):
                flights[at] = fold(*flights[at], None)[0]
        return [flights[at][0] if isinstance(flights[at], tuple) else flights[at] for at in which]

    for at in range(chunks):
        branch, grad, kept, sent = feed(normed_two, turned_two, rounded, rounded_turned, feed_all, at, cut, after=branches)
        flights.append((spread(kept), spread(exchange(sent, last_step))))
        branches.append(branch)
        grads.append(grad)
    result, hidden_grad, hidden_grad_turned, output_grad, grad_gain_two = back(
        own, masks, hidden, branches, grads, cotangent, gain_two, weights
    )
    tie(output_grad, 0, 1)
    residual_out = lax.all_gather(result, "tensor", axis=0)
    common = (reach, query, output_grad, attended, keys, values, lse, query_marks, key_marks, cosine, sine)
    sets = query.shape[1] // (2 * PAIR)
    found = unattend(0, sets - 1, *common, None, after=move_on(0, 1))
    tie(found[0], 0, 1)
    after = []
    for _ in orders[0][1:]:
        after = move_on(0, 1)
    dq, dk, dv = unattend(sets - 1, 1, *common, found, after=after)
    tie(dq, 0, 1)
    move_on(0, 1)
    feed_sums = jnp.concatenate([flight.reshape(copies, -1, piece, cut) for flight in flights], axis=-1)
    distances = list(range(1, copies))

    parts, gain_parts = [], []
    for k in range(1, span):
        grad, gain_part = unproject(own, masks, [dk, dv], x_full, k, block, weights, after=[feed_sums])
        parts.append(exchange(grad, ("seq", k)))
        gain_parts.append(gain_part)
    received = tensor_sends(feed_sums, distances)
    places = [0, 0]
    *found, own_grad, gain_part = weigh(
        own, masks, turned_one, hidden_grad_turned, dq, dk, dv, attended, x_full, weights, after=gain_parts
    )
    gain_parts.append(gain_part)
    steady = [*received, residual_out]
    shares = 1
    size = block // shares
    lines = []
    for at in range(shares):
        own_rows = finish(x_full, hidden_grad, gain_one, [own_grad] + parts, at * size, size, after=steady)
        lines.append([(own_rows, own_rows)])
    up = [(i, i + 1) for i in range(copies - 1)]
    down = [(i + 1, i) for i in range(copies - 1)]

    def hop(count):
        for _ in range(count):
            for line in lines:
                from_low, from_high = line[-1]
                line.append((lax.ppermute(from_low, "tensor", up), lax.ppermute(from_high, "tensor", down)))

    hop(1)
    found, _ = lax.optimization_barrier((found, lines[0][0][0]))
    flights = [(spread(found[at]), spread(exchange(found[at + 1], last_step))) for at in (0, 2)]
    while isinstance(flights[1], tuple):
        move_on(0, 1)
    attention_sums = [flights[z // near].reshape(near, piece, 4 * part)[z % near] for z in range(copies)]
    gain_grads = sum_over(jnp.concatenate([sum(gain_parts), grad_gain_two]), ("dp", "seq"))
    residual_out = residual_out[::repeats] if repeats > 1 else residual_out
    residual_out = deliver(residual_out.reshape(-1, width), BF16, after=[lines[0][0][0]])
    attention_shard = to_tensor(attention_sums)
    attention_shard, lines[0][1], gain_grads, residual_out = lax.optimization_barrier(
        (attention_shard, lines[0][1], gain_grads, residual_out)
    )
    hop(1)
    feed_shard = tensor_sum(feed_sums, received)

    share = 1.0 / repeats
    attention_shard, feed_shard = attention_shard * share, feed_shard * share
    gain_grads = sum_over(gain_grads * share, ("tensor",))
    gain_shard = lax.dynamic_slice_in_dim(gain_grads, index * piece, piece, 1)

    local = jnp.sum(attention_shard * attention_shard) + jnp.sum(feed_shard * feed_shard)
    def widened(distance, before):
        low, high = lane - distance, lane + distance
        target = [jnp.where(low >= 0, low, lane) // repeats, low >= 0, jnp.where(high < copies, high, lane) // repeats, high < copies]
        target = jnp.stack([jnp.asarray(entry).astype(jnp.int32) for entry in target])
        return widen(target, rows, lines[0][0][0], *lines[0][distance], before)

    grad_in = widened(1, None)
    local, grad_in = lax.optimization_barrier((local, grad_in))
    squares = sum_over(jnp.full((8, 128), local), ("tensor",))
    squares, gain_grads, lines[0][2] = lax.optimization_barrier((squares, gain_grads, lines[0][2]))
    hop(copies - 3)
    squares = sum_over(squares, ("dp", "seq"))
    norm = jnp.sqrt(squares[0, 0] + jnp.sum(gain_grads * gain_grads))
    for distance in range(2, copies):
        grad_in = widened(distance, grad_in)
    residual_out, grad_in = residual_out.reshape(rows, block, width), grad_in.reshape(rows, block, width)

    factor = jnp.minimum(1.0, CLIP / norm)
    shards = (
        jnp.stack([attention_shard[:, k * part : (k + 1) * part] for k in range(3)]),
        attention_shard[:, 3 * part :].T,
        feed_shard[:2],
        feed_shard[2].T,
        gain_shard,
    )
    masters = (attention_in, attention_out, expand, contract, gains)
    firsts = (mean_attention_in, mean_attention_out, mean_expand, mean_contract, mean_gains)
    seconds = (
        square_attention_in,
        square_attention_out,
        square_expand,
        square_contract,
        square_gains,
    )
    new_means = []
    new_squares = []
    new_weights = []
    for member in range(5):
        clipped = shards[member] * factor
        moment = BETA_ONE * firsts[member] + (1.0 - BETA_ONE) * clipped
        square = BETA_TWO * seconds[member] + (1.0 - BETA_TWO) * clipped * clipped
        update = (
            moment / (1.0 - BETA_ONE**STEP) / (jnp.sqrt(square / (1.0 - BETA_TWO**STEP)) + ADAM_EPS)
        )
        shrink = DECAY if member < 4 else 0.0
        speed = RATE if member < 4 else GAIN_RATE
        new_means.append(moment)
        new_squares.append(square)
        new_weights.append(masters[member] - speed * (update + shrink * masters[member]))
    return (residual_out, grad_in, norm, *new_means, *new_squares, *new_weights)


def solution(mesh):
    tokens = P("dp", "seq", None)
    weights = (
        P(None, ("dp", "seq"), "tensor"),
        P("tensor", ("dp", "seq")),
        P(None, ("dp", "seq"), "tensor"),
        P("tensor", ("dp", "seq")),
        P(None, ("dp", "seq")),
    )
    return jax.shard_map(
        on_device,
        mesh=mesh,
        in_specs=(tokens, tokens, P("dp", None)) + weights * 3,
        out_specs=(tokens, tokens, P()) + weights * 3,
        check_vma=False,
    )
```

```python
import jax
import jax.numpy as jnp
from jax import lax
from jax.experimental import pallas as pl
from jax.experimental.pallas import tpu as pltpu
from jax.sharding import PartitionSpec as P

HD = 64
STEP = 10

NORM_EPS = 1e-05
NEG = -1e30
CLIP = 1.0
RATE = 0.04
GAIN_RATE = 1.0
BETA_ONE = 0.9
BETA_TWO = 0.999
ADAM_EPS = 1e-08
DECAY = 0.1

SCALE = HD ** (-0.5)
PAIR = 2 * HD
TILE = 256
VMEM = 60 * 1024 * 1024
FOLD = 1024 * 1024
F32 = jnp.float32
BF16 = jnp.bfloat16

NN = (((1,), (0,)), ((), ()))
NT = (((1,), (1,)), ((), ()))
TN = (((0,), (0,)), ((), ()))


def mm(left, right, dims=NN):
    return lax.dot_general(left, right, dims, preferred_element_type=F32)


def call(body, name, flops, args, grid, in_specs, out_specs, out_shape, scratch=(), prefetch=0, after=(), aliases={}):
    count, extra = len(args), len(after)
    moved = sum(a.size * a.dtype.itemsize for a in args) + sum(o.size * o.dtype.itemsize for o in out_shape)
    return pl.pallas_call(
        lambda *refs: body(*refs[:count], *refs[count + extra :]),
        name=name,
        grid_spec=pltpu.PrefetchScalarGridSpec(
            num_scalar_prefetch=prefetch,
            grid=grid,
            in_specs=list(in_specs) + [pl.BlockSpec(memory_space=pl.ANY)] * extra,
            out_specs=out_specs,
            scratch_shapes=list(scratch),
        ),
        out_shape=out_shape,
        input_output_aliases=dict(aliases),
        compiler_params=pltpu.CompilerParams(vmem_limit_bytes=VMEM),
        cost_estimate=pl.CostEstimate(flops=int(flops) >> 24, bytes_accessed=int(moved) >> 20, transcendentals=0),
    )(*args, *after)


def whole(shape):
    return pl.BlockSpec(shape, lambda *at: (0,) * len(shape), pipeline_mode=pl.Buffered(1))


def scalar():
    return pl.BlockSpec(memory_space=pltpu.SMEM)


def out(shape, kind=BF16):
    return jax.ShapeDtypeStruct(shape, kind)


def exchange(block, step):
    axis, bit = step
    return lax.ppermute(block, axis, [(i ^ bit, i) for i in range(lax.axis_size(axis))])


def axis_steps():
    bits = lambda axis: [(axis, 1 << k) for k in range(lax.axis_size(axis).bit_length() - 1)]
    across = bits("dp")
    return bits("seq"), across[1:], across[0]


def owner_masks():
    span = lax.axis_size("seq")
    along, across, last = axis_steps()
    masks = [0]
    for axis, bit in along + across + [last]:
        masks += [m ^ (bit if axis == "seq" else bit * span) for m in masks]
    return masks


def gather_owners(array, axes):
    whole_array = lax.all_gather(array, axes, axis=0)
    return whole_array.reshape(lax.axis_size(axes[0]), -1, *array.shape)


def gather_pieces(pieces, along_first, gate):
    along, across, last = axis_steps()
    groups, rows, columns = pieces.shape
    held = pieces[:, None, None]
    for at, step in enumerate(along + across if along_first else across + along):
        if at == 1:
            held, gate = lax.optimization_barrier((held, gate))
        held = jnp.concatenate([held, exchange(held, step)], axis=2 if step[0] == "seq" else 1)
    held = held.reshape(groups, -1, columns)
    return (held, exchange(held, last)), gate


def from_tensor(array):
    size = lax.axis_size("tensor")
    others = [lax.ppermute(array, "tensor", [(i, (i + k) % size) for i in range(size)]) for k in range(1, size)]
    return [array] + others


def to_tensor(held):
    size = lax.axis_size("tensor")
    total = held[0].astype(F32)
    for k in range(1, size):
        total += lax.ppermute(held[k], "tensor", [((i + k) % size, i) for i in range(size)]).astype(F32)
    return total


def gather_small(array):
    along, across, last = axis_steps()
    array = array[:, None, None]
    for step in [last] + across + along:
        other = exchange(array, step)
        axis = 2 if step[0] == "seq" else 1
        pair, swapped = jnp.concatenate([array, other], axis=axis), jnp.concatenate([other, array], axis=axis)
        array = jnp.where(lax.axis_index(step[0]) & step[1], swapped, pair)
    return array.reshape(array.shape[0], -1)


def sum_over(array, axes):
    for axis in axes:
        for k in range(lax.axis_size(axis).bit_length() - 1):
            array = array + exchange(array, (axis, 1 << k))
    return array


def scatter_order(along_first):
    along, across, _ = axis_steps()
    ordered = [list(reversed(along)), list(reversed(across))]
    return ordered[0] + ordered[1] if along_first else ordered[1] + ordered[0]


def tensor_sends(held, distances):
    size, here = lax.axis_size("tensor"), lax.axis_index("tensor")
    return [
        lax.ppermute(
            lax.dynamic_index_in_dim(held, lax.rem(here + k, size), 0, keepdims=False),
            "tensor",
            [(i, (i + k) % size) for i in range(size)],
        )
        for k in distances
    ]


def tensor_sum(held, received):
    own = lax.dynamic_index_in_dim(held, lax.axis_index("tensor"), 0, keepdims=False).astype(F32)
    return sum([array.astype(F32) for array in received], own)


def row_block(own, mask, piece):
    return pl.ds(pl.multiple_of((own ^ mask) * piece, piece), piece)


def store_turned(own, masks, ref, values, scratch):
    scratch[...] = values.T.astype(BF16)
    piece = scratch.shape[0] // len(masks)
    for j, mask in enumerate(masks):
        ref[j * piece : (j + 1) * piece, :] = scratch[row_block(own, mask, piece), :]


def swap_halves(values):
    lane = lax.broadcasted_iota(jnp.int32, values.shape, 1)
    size = values.shape[1]
    ahead = pltpu.roll(values, size - HD // 2, 1)
    behind = pltpu.roll(values, HD // 2, 1)
    return jnp.where(lane % HD < HD // 2, ahead, behind)


def half_sign(shape):
    lane = lax.broadcasted_iota(jnp.int32, shape, 1)
    return jnp.where(lane % HD < HD // 2, -1.0, 1.0)


def turn(values, cosine, sine):
    return values * cosine + swap_halves(values) * (sine * half_sign(values.shape))


def unturn(values, cosine, sine):
    return values * cosine - swap_halves(values * sine) * half_sign(values.shape)


def pair_lanes(values, head):
    lane = lax.broadcasted_iota(jnp.int32, values.shape, 1)
    return jnp.where((lane < HD) == (head == 0), values, 0.0)


def stack_pair(values):
    return jnp.concatenate([pair_lanes(values, 0), pair_lanes(values, 1)], axis=0).astype(BF16)


def norm_rate(values):
    return lax.rsqrt(jnp.mean(values * values, axis=-1, keepdims=True) + NORM_EPS)


def weight_specs(weights, first, count):
    groups, half, cols = weights[0].shape
    block = (groups, half, count * (cols // 4))
    spec = pl.BlockSpec(block, lambda *at: (0, 0, first // count), pipeline_mode=pl.Buffered(1))
    return [spec] * len(weights)


def lay(own, masks, w_all, w_refs):
    kinds = w_all.shape[0]
    groups, half, cols = w_refs[0].shape
    part = cols // kinds
    piece = 2 * half // len(masks)
    for z in range(len(w_refs) // 2 * groups):
        for j, mask in enumerate(masks):
            ref = w_refs[2 * (z // groups) + j // (len(masks) // 2)]
            at = j % (len(masks) // 2) * piece
            for m in range(kinds):
                w_all[m, row_block(own, mask, piece), z * part : (z + 1) * part] = ref[
                    z % groups, at : at + piece, m * part : (m + 1) * part
                ]


def project(own, masks, x_full, gain, cosine, sine, weights, block):
    tokens, width = x_full.shape
    heads = len(weights) // 2 * weights[0].shape[0] * weights[0].shape[2] // 4
    count = len(weights)
    mine = block // TILE

    def body(own_ref, x_ref, g_ref, cos_ref, sin_ref, *refs):
        w_refs, (at_ref, q_ref, k_ref, v_ref, w_all, a_one, turned) = refs[:count], refs[count:]
        own = own_ref[0]

        @pl.when(pl.program_id(0) == 0)
        def _():
            lay(own, masks, w_all, w_refs)

        values = x_ref[...].astype(F32)
        normed = values * norm_rate(values) * g_ref[...]
        a_one[...] = normed.astype(BF16)
        store_turned(own, masks, at_ref, normed, turned)
        cosine, sine = cos_ref[...], sin_ref[...]

        def rotated(ref, m):
            for at in range(0, heads, 2 * PAIR):
                mixed = mm(a_one[...], w_all[m, :, at : at + 2 * PAIR])
                for lane in (0, PAIR):
                    ref[:, at + lane : at + lane + PAIR] = turn(mixed[:, lane : lane + PAIR], cosine, sine).astype(BF16)

        rotated(k_ref, 1)
        v_ref[...] = mm(a_one[...], w_all[2]).astype(BF16)

        @pl.when(pl.program_id(0) < mine)
        def _():
            rotated(q_ref, 0)

    rows = lambda i: (i, 0)
    return call(
        body,
        "project",
        2 * (2 * tokens + block) * width * heads,
        (own, x_full, gain, cosine, sine, *weights),
        (tokens // TILE,),
        [
            scalar(),
            pl.BlockSpec((TILE, width), rows),
            whole((1, width)),
            pl.BlockSpec((TILE, PAIR), rows),
            pl.BlockSpec((TILE, PAIR), rows),
            *weight_specs(weights, 0, 3),
        ],
        [
            pl.BlockSpec((width, TILE), lambda i: (0, i)),
            pl.BlockSpec((TILE, heads), lambda i: (jnp.minimum(i, mine - 1), 0)),
            pl.BlockSpec((TILE, heads), rows),
            pl.BlockSpec((TILE, heads), rows),
        ],
        [out((width, tokens)), out((block, heads)), out((tokens, heads)), out((tokens, heads))],
        [pltpu.VMEM((3, width, heads), BF16), pltpu.VMEM((TILE, width), BF16), pltpu.VMEM((width, TILE), BF16)],
    )


def attend(reach, query, keys, values, query_marks, key_marks):
    block, heads = query.shape
    tokens = keys.shape[0]
    wide = 2 * PAIR
    count = block // TILE

    def body(reach, q_ref, k_ref, v_ref, qm_ref, km_ref, o_ref, lse_ref, turned, acc, top, total, kept):
        at = pl.program_id(1)
        first, last, shift = reach[2 * at], reach[2 * at + 1], reach[2 * count]

        @pl.when(at == 0)
        def _():
            for tile in range(tokens // TILE):
                rows = slice(tile * TILE, (tile + 1) * TILE)
                turned[:, rows] = v_ref[rows, :].astype(F32).T.astype(BF16)

        marks = jnp.concatenate([qm_ref[...], qm_ref[...]], axis=0)
        stacked = [
            jnp.concatenate([stack_pair(q_ref[:, p * PAIR : (p + 1) * PAIR].astype(F32) * SCALE), marks], axis=1)
            for p in range(2)
        ]
        top[...] = jnp.full_like(top, NEG)
        acc[...] = jnp.zeros_like(acc)
        total[...] = jnp.zeros_like(total)

        def by_eight(values):
            return values.reshape(values.shape[0] // 8, 8, values.shape[1])

        def score(tile, carry):
            rows = pl.ds(pl.multiple_of((tile ^ shift) * TILE, TILE), TILE)
            for p in range(2):
                lanes = slice(p * PAIR, (p + 1) * PAIR)
                scores = mm(jnp.concatenate([k_ref[rows, lanes], km_ref[rows, :]], axis=1), stacked[p], NT)
                kept[p, rows, :] = scores
                top[p] = jnp.maximum(top[p], jnp.max(by_eight(scores), axis=0))
            return carry

        lax.fori_loop(first, last, score, 0)
        tops = [jnp.max(top[p], axis=0, keepdims=True) for p in range(2)]

        def step(tile, carry):
            rows = pl.ds(pl.multiple_of((tile ^ shift) * TILE, TILE), TILE)
            for p in range(2):
                probs = jnp.exp(kept[p, rows, :] - tops[p])
                total[p] += jnp.sum(by_eight(probs), axis=0)
                probs = probs.astype(BF16)
                for h in range(2):
                    part = slice(p * PAIR + h * HD, p * PAIR + (h + 1) * HD)
                    acc[part, :] += mm(turned[part, rows], probs[:, h * TILE : (h + 1) * TILE])
            return carry

        lax.fori_loop(first, last, step, 0)
        for p in range(2):
            sums = jnp.sum(total[p], axis=0, keepdims=True)
            rate = 1.0 / sums
            for h in range(2):
                part = slice(p * PAIR + h * HD, p * PAIR + (h + 1) * HD)
                acc[part, :] = acc[part, :] * rate[:, h * TILE : (h + 1) * TILE]
            lse_ref[0, 0, p : p + 1, :] = tops[p] + jnp.log(sums)
        o_ref[...] = acc[...].T.astype(BF16)

    return call(
        body,
        "attend",
        4 * block * tokens * heads,
        (reach, query, keys, values, query_marks, key_marks),
        (heads // wide, count),
        [
            pl.BlockSpec((TILE, wide), lambda h, i, r: (i, h)),
            pl.BlockSpec((tokens, wide), lambda h, i, r: (0, h)),
            pl.BlockSpec((tokens, wide), lambda h, i, r: (0, h)),
            pl.BlockSpec((TILE, PAIR), lambda h, i, r: (i, 0)),
            pl.BlockSpec((tokens, PAIR), lambda h, i, r: (0, 0)),
        ],
        [
            pl.BlockSpec((TILE, wide), lambda h, i, r: (i, h)),
            pl.BlockSpec((1, 1, 2, 2 * TILE), lambda h, i, r: (h, i, 0, 0)),
        ],
        [out((block, heads)), out((heads // wide, count, 2, 2 * TILE), F32)],
        [
            pltpu.VMEM((wide, tokens), BF16),
            pltpu.VMEM((wide, TILE), F32),
            pltpu.VMEM((2, 8, 2 * TILE), F32),
            pltpu.VMEM((2, 8, 2 * TILE), F32),
            pltpu.VMEM((2, tokens, 2 * TILE), F32),
        ],
        prefetch=1,
    )


def lift(own, masks, attended, x_full, cotangent, gain, weights):
    block, heads = attended.shape
    width = x_full.shape[1]
    count = len(weights)

    def body(own_ref, o_ref, x_ref, c_ref, g_ref, *refs):
        w_refs, (h_ref, a_ref, at_ref, e_ref, et_ref, w_all, turned) = refs[:count], refs[count:]
        own = own_ref[0]

        @pl.when(pl.program_id(0) == 0)
        def _():
            lay(own, masks, w_all, w_refs)

        values = x_ref[...].astype(F32) + mm(o_ref[...], w_all[0], NT)
        h_ref[...] = values
        normed = values * norm_rate(values) * g_ref[...]
        a_ref[...] = normed.astype(BF16)
        store_turned(own, masks, at_ref, normed, turned)
        cotangent = c_ref[...]
        e_ref[...] = cotangent.astype(BF16)
        store_turned(own, masks, et_ref, cotangent, turned)

    rows = lambda i: (i, 0)
    wide = pl.BlockSpec((TILE, width), rows)
    tall = pl.BlockSpec((width, TILE), lambda i: (0, i))
    return call(
        body,
        "lift",
        2 * block * width * heads,
        (own, attended, x_full, cotangent, gain, *weights),
        (block // TILE,),
        [scalar(), pl.BlockSpec((TILE, heads), rows), wide, wide, whole((1, width)), *weight_specs(weights, 3, 1)],
        [wide, wide, tall, wide, tall],
        [out((block, width), F32), out((block, width)), out((width, block)), out((block, width)), out((width, block))],
        [pltpu.VMEM((1, width, heads), BF16), pltpu.VMEM((width, TILE), BF16)],
    )


def feed(normed, turned, cotangent, cotangent_turned, weights, chunk, hidden, after=()):
    block, width = normed.shape
    groups, owners, kinds, piece, _ = weights.shape
    half = width // 2
    cut = min(512, hidden)
    tile = min(512, block)

    def body(a_ref, at_ref, e_ref, et_ref, w_ref, b_out, d_out, ga_ref, gb_ref, b_ref, d_ref, mid, dgate, dup):
        @pl.when((pl.program_id(0) == 0) & (pl.program_id(1) == 0))
        def _():
            b_ref[...] = jnp.zeros_like(b_ref)
            d_ref[...] = jnp.zeros_like(d_ref)

        def weight(m):
            return w_ref[0, :, m].reshape(width, cut)

        def tokens(i, carry):
            rows = pl.ds(pl.multiple_of(i * tile, tile), tile)
            gate = mm(a_ref[rows, :], weight(0))
            upper = mm(a_ref[rows, :], weight(1))
            grad = mm(e_ref[rows, :], weight(2))
            sigma = jax.nn.sigmoid(gate)
            active = gate * sigma
            mid[rows, :] = (active * upper).astype(BF16)
            dgate[rows, :] = (grad * upper * (sigma * (1.0 + gate * (1.0 - sigma)))).astype(BF16)
            dup[rows, :] = (grad * active).astype(BF16)
            b_ref[rows, :] += mm(mid[rows, :], weight(2), NT)
            d_ref[rows, :] += mm(dgate[rows, :], weight(0), NT) + mm(dup[rows, :], weight(1), NT)
            return carry

        lax.fori_loop(0, block // tile, tokens, 0)
        for ref, rows in ((ga_ref, slice(0, half)), (gb_ref, slice(half, width))):
            ref[0, 0] = mm(at_ref[rows, :], dgate[...]).astype(BF16)
            ref[0, 1] = mm(at_ref[rows, :], dup[...]).astype(BF16)
            ref[0, 2] = mm(et_ref[rows, :], mid[...]).astype(BF16)

        @pl.when((pl.program_id(0) == groups - 1) & (pl.program_id(1) == hidden // cut - 1))
        def _():
            b_out[...] = b_ref[...].astype(BF16)
            d_out[...] = d_ref[...].astype(BF16)

    place = lambda z, j: (z, 0, 0, j)
    shape = (groups, kinds, half, hidden)
    return call(
        body,
        "feed",
        18 * block * width * hidden * groups,
        (normed, turned, cotangent, cotangent_turned, weights),
        (groups, hidden // cut),
        [
            whole((block, width)),
            whole((width, block)),
            whole((block, width)),
            whole((width, block)),
            pl.BlockSpec((1, owners, kinds, piece, cut), lambda z, j: (z, 0, 0, 0, chunk * (hidden // cut) + j)),
        ],
        [
            whole((block, width)),
            whole((block, width)),
            pl.BlockSpec((1, kinds, half, cut), place),
            pl.BlockSpec((1, kinds, half, cut), place),
        ],
        [out((block, width)), out((block, width)), out(shape), out(shape)],
        [pltpu.VMEM((block, width), F32)] * 2 + [pltpu.VMEM((block, cut), BF16)] * 3,
        after=after,
    )


def back(own, masks, hidden, branches, grads, cotangent, gain, weights, after=()):
    block, width = hidden.shape
    heads = len(weights) // 2 * weights[0].shape[0] * weights[0].shape[2] // 4
    many = len(weights)

    count = len(branches)

    def body(own_ref, h_ref, c_ref, g_ref, *refs):
        w_refs, refs = refs[:many], refs[many:]
        b_refs, d_refs, refs = refs[:count], refs[count : 2 * count], refs[2 * count :]
        y_ref, dh_ref, ct_ref, do_ref, gg_ref, w_all, turned = refs
        own = own_ref[0]

        @pl.when(pl.program_id(0) == 0)
        def _():
            lay(own, masks, w_all, w_refs)
            gg_ref[...] = jnp.zeros_like(gg_ref)

        hidden = h_ref[...]
        grad = sum([ref[...].astype(F32) for ref in d_refs[1:]], d_refs[0][...].astype(F32))
        y_ref[...] = sum([ref[...].astype(F32) for ref in b_refs], hidden).astype(BF16)
        rate = norm_rate(hidden)
        scaled = grad * g_ref[...]
        dot = jnp.mean(hidden * scaled, axis=-1, keepdims=True)
        result = c_ref[...] + rate * scaled - hidden * (rate * rate * rate * dot)
        dh_ref[...] = result
        store_turned(own, masks, ct_ref, result, turned)
        do_ref[...] = mm(result.astype(BF16), w_all[0]).astype(BF16)
        gg_ref[...] += jnp.sum(grad * hidden * rate, axis=0, keepdims=True)

    rows = lambda i: (i, 0)
    wide = pl.BlockSpec((TILE, width), rows)
    return call(
        body,
        "back",
        2 * block * width * heads,
        (own, hidden, cotangent, gain, *weights, *branches, *grads),
        (block // TILE,),
        [scalar(), wide, wide, whole((1, width)), *weight_specs(weights, 3, 1)] + [wide] * (2 * count),
        [
            wide,
            wide,
            pl.BlockSpec((width, TILE), lambda i: (0, i)),
            pl.BlockSpec((TILE, heads), rows),
            pl.BlockSpec((1, width), lambda i: (0, 0)),
        ],
        [
            out((block, width)),
            out((block, width), F32),
            out((width, block)),
            out((block, heads)),
            out((1, width), F32),
        ],
        [pltpu.VMEM((1, width, heads), BF16), pltpu.VMEM((width, TILE), BF16)],
        after=after,
    )


def unattend(base, sets, reach, query, grads, attended, keys, values, lse, query_marks, key_marks, cosine, sine, before, after=()):
    block, heads = query.shape
    tokens = keys.shape[0]
    wide = 2 * PAIR
    count = block // TILE

    def body(
        reach, q_ref, g_ref, o_ref, k_ref, v_ref, lse_ref, qm_ref, km_ref, cq_ref, sq_ref, ck_ref, sk_ref,
        dq_ref, dk_ref, dv_ref, keys_turned, dq_acc, dk_acc, dv_acc,
    ):
        at = pl.program_id(1)
        first, last, shift = reach[2 * at], reach[2 * at + 1], reach[2 * count]
        marks = jnp.concatenate([qm_ref[...], qm_ref[...]], axis=0)
        queries = q_ref[...].astype(F32) * SCALE
        grads = g_ref[...].astype(F32)
        product = (grads * o_ref[...].astype(F32)).T
        stacked, marked, stacked_grads, deltas = [], [], [], []
        for p in range(2):
            lanes = slice(p * PAIR, (p + 1) * PAIR)
            stacked.append(stack_pair(queries[:, lanes]))
            marked.append(jnp.concatenate([stacked[p], marks], axis=1))
            stacked_grads.append(stack_pair(grads[:, lanes]))
            sums = [
                jnp.sum(product[p * PAIR + h * HD : p * PAIR + (h + 1) * HD], axis=0, keepdims=True) for h in range(2)
            ]
            deltas.append(jnp.concatenate(sums, axis=1))
        dq_acc[...] = jnp.zeros_like(dq_acc)

        @pl.when(at == 0)
        def _():
            dk_acc[...] = jnp.zeros_like(dk_acc)
            dv_acc[...] = jnp.zeros_like(dv_acc)
            for tile in range(tokens // TILE):
                rows = slice(tile * TILE, (tile + 1) * TILE)
                keys_turned[:, rows] = k_ref[rows, :].astype(F32).T.astype(BF16)

        def step(tile, carry):
            rows = pl.ds(pl.multiple_of((tile ^ shift) * TILE, TILE), TILE)
            for p in range(2):
                lanes = slice(p * PAIR, (p + 1) * PAIR)
                scores = mm(jnp.concatenate([k_ref[rows, lanes], km_ref[rows, :]], axis=1), marked[p], NT)
                probs = jnp.exp(scores - lse_ref[0, 0, p : p + 1, :])
                prob_grads = mm(v_ref[rows, lanes], stacked_grads[p], NT)
                score_grads = (probs * (prob_grads - deltas[p])).astype(BF16)
                dv_acc[rows, lanes] += mm(probs.astype(BF16), stacked_grads[p])
                dk_acc[rows, lanes] += mm(score_grads, stacked[p])
                for h in range(2):
                    part = slice(p * PAIR + h * HD, p * PAIR + (h + 1) * HD)
                    dq_acc[part, :] += mm(keys_turned[part, rows], score_grads[:, h * TILE : (h + 1) * TILE])
            return carry

        lax.fori_loop(first, last, step, 0)
        grad = dq_acc[...].T * SCALE
        for lane in (0, PAIR):
            dq_ref[:, lane : lane + PAIR] = unturn(grad[:, lane : lane + PAIR], cq_ref[...], sq_ref[...]).astype(BF16)

        @pl.when(at == count - 1)
        def _():
            dv_ref[...] = dv_acc[...].astype(BF16)
            for lane in (0, PAIR):
                dk_ref[:, lane : lane + PAIR] = unturn(
                    dk_acc[:, lane : lane + PAIR], ck_ref[...], sk_ref[...]
                ).astype(BF16)

    tile = pl.BlockSpec((TILE, wide), lambda h, i, r: (i, base + h))
    full = pl.BlockSpec((tokens, wide), lambda h, i, r: (0, base + h))
    table = pl.BlockSpec((TILE, PAIR), lambda h, i, r: (i, 0))
    tables = pl.BlockSpec((tokens, PAIR), lambda h, i, r: (0, 0))
    return call(
        body,
        "unattend",
        10 * block * tokens * wide * sets,
        (reach, query, grads, attended, keys, values, lse, query_marks, key_marks, cosine, sine, cosine, sine),
        (sets, count),
        [
            tile,
            tile,
            tile,
            full,
            full,
            pl.BlockSpec((1, 1, 2, 2 * TILE), lambda h, i, r: (base + h, i, 0, 0)),
            table,
            tables,
            table,
            table,
            tables,
            tables,
        ],
        [
            tile,
            full,
            full,
        ],
        [out((block, heads)), out((tokens, heads)), out((tokens, heads))],
        [
            pltpu.VMEM((wide, tokens), BF16),
            pltpu.VMEM((wide, TILE), F32),
            pltpu.VMEM((tokens, wide), F32),
            pltpu.VMEM((tokens, wide), F32),
        ],
        prefetch=1,
        after=[*(before or ()), *after],
        aliases={13: 0, 14: 1, 15: 2} if before else {},
    )


def unproject(own, masks, grads, x_full, k, block, weights, after=()):
    width = x_full.shape[1]
    heads = grads[0].shape[1]
    kinds = len(grads)
    count = len(weights)
    base = k * block // TILE

    def body(own_ref, x_ref, *refs):
        g_refs, refs = refs[:kinds], refs[kinds:]
        w_refs, (da_ref, gg_ref, w_all) = refs[:count], refs[count:]

        @pl.when(pl.program_id(0) == 0)
        def _():
            gg_ref[...] = jnp.zeros_like(gg_ref)
            lay(own_ref[0], masks, w_all, w_refs)

        grad = mm(g_refs[0][...], w_all[3 - kinds], NT)
        for at in range(1, kinds):
            grad += mm(g_refs[at][...], w_all[3 - kinds + at], NT)
        da_ref[...] = grad.astype(BF16)
        values = x_ref[...].astype(F32)
        gg_ref[...] += jnp.sum(grad * values * norm_rate(values), axis=0, keepdims=True)

    def place(array):
        return (lambda i: (i, 0)) if array.shape[0] == block else (lambda i: (base + i, 0))

    return call(
        body,
        "unproject",
        2 * kinds * block * width * heads,
        (own, x_full, *grads, *weights),
        (block // TILE,),
        [scalar(), pl.BlockSpec((TILE, width), lambda i: (base + i, 0))]
        + [pl.BlockSpec((TILE, heads), place(array)) for array in grads]
        + weight_specs(weights, 0, 3),
        [pl.BlockSpec((TILE, width), lambda i: (i, 0)), pl.BlockSpec((1, width), lambda i: (0, 0))],
        [out((block, width)), out((1, width), F32)],
        [pltpu.VMEM((3, width, heads), BF16)],
        after=after,
    )


def weigh(own, masks, turned, cotangent_turned, dq, dk, dv, attended, x_full, weights, after=()):
    width, tokens = turned.shape
    block, heads = dq.shape
    groups, _, cols = weights[0].shape
    many = len(weights)
    groups *= many // 2
    part = cols // 4
    half, near = width // 2, groups // 2
    tiles = block // TILE

    def body(
        own_ref, at_ref, ct_ref, dq_ref, dk_ref, dv_ref, o_ref, x_ref, dq_row, dk_row, dv_row, *refs
    ):
        w_refs, (ga_near, gb_near, ga_far, gb_far, da_ref, gg_ref, w_all) = refs[:many], refs[many:]
        at = pl.program_id(0)

        def write(targets):
            for ref, rows in zip(targets, (slice(0, half), slice(half, width))):
                ref[0, :, :part] = mm(at_ref[rows, :block], dq_ref[...]).astype(BF16)
                ref[0, :, part : 2 * part] = mm(at_ref[rows, :], dk_ref[...]).astype(BF16)
                ref[0, :, 2 * part : 3 * part] = mm(at_ref[rows, :], dv_ref[...]).astype(BF16)
                ref[0, :, 3 * part :] = mm(ct_ref[rows, :], o_ref[...]).astype(BF16)

        @pl.when(at < near)
        def _():
            write((ga_near, gb_near))

        @pl.when((at >= near) & (at < groups))
        def _():
            write((ga_far, gb_far))

        @pl.when(at == 0)
        def _():
            gg_ref[...] = jnp.zeros_like(gg_ref)
            lay(own_ref[0], masks, w_all, w_refs)

        @pl.when(at < tiles)
        def _():
            grad = mm(dq_row[...], w_all[0], NT)
            grad += mm(dk_row[...], w_all[1], NT)
            grad += mm(dv_row[...], w_all[2], NT)
            da_ref[...] = grad.astype(BF16)
            values = x_ref[...].astype(F32)
            gg_ref[...] += jnp.sum(grad * values * norm_rate(values), axis=0, keepdims=True)

    column = lambda i: (0, jnp.minimum(i, groups - 1))
    row = lambda i: (jnp.minimum(i, tiles - 1), 0)
    shape = (near, half, cols)
    near_spec = pl.BlockSpec((1, half, cols), lambda i: (jnp.minimum(i, near - 1), 0, 0))
    far_spec = pl.BlockSpec((1, half, cols), lambda i: (jnp.clip(i - near, 0, near - 1), 0, 0))
    return call(
        body,
        "weigh",
        4 * (tokens + block) * width * heads + 6 * block * width * heads,
        (own, turned, cotangent_turned, dq, dk, dv, attended, x_full, dq, dk, dv, *weights),
        (max(groups, tiles),),
        [
            scalar(),
            whole(turned.shape),
            whole(cotangent_turned.shape),
            pl.BlockSpec((block, part), column),
            pl.BlockSpec((tokens, part), column),
            pl.BlockSpec((tokens, part), column),
            pl.BlockSpec((block, part), column),
            pl.BlockSpec((TILE, width), row),
            pl.BlockSpec((TILE, heads), row),
            pl.BlockSpec((TILE, heads), row),
            pl.BlockSpec((TILE, heads), row),
            *weight_specs(weights, 0, 3),
        ],
        [near_spec, near_spec, far_spec, far_spec, pl.BlockSpec((TILE, width), row), pl.BlockSpec((1, width), lambda i: (0, 0))],
        [out(shape)] * 4 + [out((block, width)), out((1, width), F32)],
        [pltpu.VMEM((3, width, heads), BF16)],
        after=after,
    )


def fold(kept, received, step, after=()):
    axis = None if step is None else 2 if step[0] == "seq" else 1
    shapes = [kept.shape]
    if axis is not None:
        half = kept.shape[axis] // 2
        shapes = [tuple(half if at == axis else n for at, n in enumerate(kept.shape))] * 2

    def body(kept_ref, received_ref, *refs):
        total = (kept_ref[...].astype(F32) + received_ref[...].astype(F32)).astype(BF16)
        if axis is None:
            refs[0][...] = total
        elif axis == 1:
            refs[0][...], refs[1][...] = total[:, :half], total[:, half:]
        else:
            refs[0][...], refs[1][...] = total[:, :, :half], total[:, :, half:]

    groups = kept.shape[0]
    run = next(n for n in range(groups, 0, -1) if groups % n == 0 and n * kept[0].size <= FOLD)
    spec = lambda shape: pl.BlockSpec((run, *shape[1:]), lambda g: (g, 0, 0, 0, 0))
    return call(
        body,
        "fold",
        kept.size,
        (kept, received),
        (groups // run,),
        [spec(kept.shape)] * 2,
        [spec(shape) for shape in shapes],
        [out(shape) for shape in shapes],
        after=after,
    )


def deliver(array, kind, after=()):
    rows, width = array.shape

    def body(x_ref, y_ref):
        y_ref[...] = x_ref[...].astype(kind)

    spec = pl.BlockSpec((2 * TILE, width), lambda i: (i, 0))
    return call(
        body, "deliver", rows * width, (array,), (rows // (2 * TILE),), [spec], [spec], [out(array.shape, kind)], after=after
    )[0]


def finish(x_full, hidden_grad, gain, parts, first, count, after=()):
    width = hidden_grad.shape[1]

    def body(x_ref, dh_ref, g_ref, *refs):
        grad = sum([ref[...].astype(F32) for ref in refs[1:-1]], refs[0][...].astype(F32))
        values = x_ref[...].astype(F32)
        rate = norm_rate(values)
        scaled = grad * g_ref[...]
        dot = jnp.mean(values * scaled, axis=-1, keepdims=True)
        refs[-1][...] = (dh_ref[...] + rate * scaled - values * (rate * rate * rate * dot)).astype(BF16)

    wide = pl.BlockSpec((TILE, width), lambda i: (first // TILE + i, 0))
    return call(
        body,
        "finish",
        16 * count * width,
        (x_full, hidden_grad, gain, *parts),
        (count // TILE,),
        [wide, wide, whole((1, width))] + [wide] * len(parts),
        [pl.BlockSpec((TILE, width), lambda i: (i, 0))],
        [out((count, width))],
        after=after,
    )[0]


def widen(target, repeated, own_rows, low, high, sides, before):
    count, width = own_rows.shape
    step = min(2 * TILE, count)
    tiles = count // step

    def body(target, own_ref, low_ref, high_ref, y_ref):
        low_real, high_real = target[1] != 0, target[3] != 0
        if sides == 2:
            first = pl.program_id(0) == 0
            low_real, high_real = low_real & first, high_real & jnp.logical_not(first)

        @pl.when(low_real)
        def _():
            y_ref[...] = low_ref[...].astype(F32)

        @pl.when(high_real)
        def _():
            y_ref[...] = high_ref[...].astype(F32)

        @pl.when(jnp.logical_not(low_real | high_real))
        def _():
            y_ref[...] = own_ref[...].astype(F32)

    spec = pl.BlockSpec((step, width), lambda d, i, t: (i, 0))
    low_spec = pl.BlockSpec((step, width), lambda d, i, t: (jnp.where(d == 0, i, tiles - 1), 0))
    high_spec = pl.BlockSpec((step, width), lambda d, i, t: (jnp.where(d == sides - 1, i, 0), 0))
    if sides == 2:
        row = lambda d, t: t[2 * d]
    else:
        row = lambda d, t: jnp.where(t[3] != 0, t[2], t[0])
    place = pl.BlockSpec((step, width), lambda d, i, t: (row(d, t) * tiles + i, 0))
    before = [] if before is None else [before]
    return call(
        body,
        "widen",
        count * width,
        (target, own_rows, low, high),
        (sides, tiles),
        [spec, low_spec, high_spec],
        [place],
        [out((repeated * count, width), F32)],
        prefetch=1,
        after=before,
        aliases={4: 0} if before else {},
    )[0]


def on_device(
    residual_in,
    grad_out,
    segment_lengths,
    attention_in,
    attention_out,
    expand,
    contract,
    gains,
    mean_attention_in,
    mean_attention_out,
    mean_expand,
    mean_contract,
    mean_gains,
    square_attention_in,
    square_attention_out,
    square_expand,
    square_contract,
    square_gains,
):
    span, copies = lax.axis_size("seq"), lax.axis_size("tensor")
    place, lane = lax.axis_index("seq"), lax.axis_index("tensor")
    rows, block, width = residual_in.shape
    tokens = span * block
    repeats = copies // rows
    row = lane // repeats
    piece = attention_in.shape[1]
    part = attention_in.shape[2]
    masks = owner_masks()
    index = lax.axis_index("dp") * span + place
    own = index.astype(jnp.int32)[None]
    near = copies // 2

    attention_piece = jnp.concatenate(
        [attention_in[0], attention_in[1], attention_in[2], attention_out.T], axis=1
    ).astype(BF16)
    feed_piece = jnp.stack([expand[0], expand[1], contract.T]).astype(BF16)
    feed_all = gather_owners(feed_piece, ("tensor", "dp", "seq"))
    x_own = lax.dynamic_index_in_dim(residual_in, row, 0, keepdims=False)
    cotangent = lax.dynamic_index_in_dim(grad_out, row, 0, keepdims=False)
    x_parts = [x_own] + [exchange(x_own, ("seq", k)) for k in range(1, span)]
    pieces = from_tensor(attention_piece)
    first, second = jnp.stack(pieces[:near]), jnp.stack(pieces[near:])
    x_parts, second = lax.optimization_barrier((x_parts, second))
    x_parts, small = lax.optimization_barrier((x_parts, gains.astype(BF16).astype(F32)))
    full_gains = gather_small(small)
    weights_one, full_gains = gather_pieces(first, True, full_gains)
    gain_one, gain_two = full_gains[:1], full_gains[1:]
    x_full = jnp.concatenate(x_parts, axis=0)
    lens = lax.dynamic_index_in_dim(segment_lengths, row, 0, keepdims=False)
    ends = jnp.cumsum(lens)
    starts = ends - lens
    blocks = place ^ jnp.arange(span, dtype=jnp.int32)
    places = (blocks[:, None] * block + jnp.arange(block, dtype=jnp.int32)[None, :]).reshape(tokens)
    segment = jnp.sum((places[:, None] >= ends[None, :]).astype(jnp.int32), axis=-1)
    picked = segment[:, None] == jnp.arange(lens.shape[0], dtype=jnp.int32)[None, :]
    begin = jnp.sum(jnp.where(picked, starts[None, :], 0), axis=-1)
    finish_at = jnp.sum(jnp.where(picked, ends[None, :], 0), axis=-1)
    freq = jnp.exp(jnp.arange(HD // 2, dtype=F32) * (-2.0 * jnp.log(10000.0) / HD))
    angle = (places - begin).astype(F32)[:, None] * freq
    cosine = jnp.tile(jnp.cos(angle), (1, PAIR // (HD // 2)))
    sine = jnp.tile(jnp.sin(angle), (1, PAIR // (HD // 2)))
    count = block // TILE
    firsts = begin[:block].reshape(count, TILE)[:, 0] // TILE
    lasts = (finish_at[:block].reshape(count, TILE)[:, -1] + TILE - 1) // TILE
    reach = jnp.concatenate(
        [jnp.stack([firsts, lasts], axis=1).reshape(-1), (place * (block // TILE))[None]]
    ).astype(jnp.int32)
    lanes = jnp.arange(PAIR, dtype=jnp.int32)[None, :]
    key_marks = jnp.where(segment[:, None] == lanes, NEG, 0.0).astype(BF16)
    query_marks = ((segment[:block, None] != lanes) & (lanes < lens.shape[0])).astype(BF16)

    chunks = 2
    cut = feed_piece.shape[2] // chunks

    ready = (x_full, cotangent, cosine, sine, reach, query_marks, key_marks)
    weights_two, ready = gather_pieces(second, False, ready)
    x_full, cotangent, cosine, sine, reach, query_marks, key_marks = ready
    weights = (*weights_one, *weights_two)
    turned_one, query, keys, values = project(own, masks, x_full, gain_one, cosine, sine, weights, block)
    attended, lse = attend(reach, query, keys, values, query_marks, key_marks)
    hidden, normed_two, turned_two, rounded, rounded_turned = lift(
        own, masks, attended, x_full, cotangent, gain_two, weights
    )

    def spread(array):
        half, columns = array.shape[-2:]
        return array.reshape(-1, half // (span * piece), span, piece, columns)

    last_step = axis_steps()[2]
    orders = [scatter_order(bool(at % 2)) for at in range(chunks)]
    flights, places, branches, grads = [], [0] * chunks, [], []

    def tie(anchor, *which):
        *tied, anchor = lax.optimization_barrier((*[flights[at] for at in which], anchor))
        for at, flight in zip(which, tied):
            flights[at] = tuple(flight) if isinstance(flight, (tuple, list)) else flight

    def move_on(*which):
        for at in which:
            if places[at] < len(orders[at]):
                step = orders[at][places[at]]
                kept, sent = fold(*flights[at], step)
                flights[at] = (kept, exchange(sent, step))
                places[at] += 1
            elif isinstance(flights[at], tuple):
                flights[at] = fold(*flights[at], None)[0]
        return [flights[at][0] if isinstance(flights[at], tuple) else flights[at] for at in which]

    for at in range(chunks):
        branch, grad, kept, sent = feed(normed_two, turned_two, rounded, rounded_turned, feed_all, at, cut, after=branches)
        flights.append((spread(kept), spread(exchange(sent, last_step))))
        branches.append(branch)
        grads.append(grad)
    result, hidden_grad, hidden_grad_turned, output_grad, grad_gain_two = back(
        own, masks, hidden, branches, grads, cotangent, gain_two, weights
    )
    tie(output_grad, 0, 1)
    residual_out = lax.all_gather(result, "tensor", axis=0)
    common = (reach, query, output_grad, attended, keys, values, lse, query_marks, key_marks, cosine, sine)
    sets = query.shape[1] // (2 * PAIR)
    found = unattend(0, sets - 1, *common, None, after=move_on(0, 1))
    tie(found[0], 0, 1)
    after = []
    for _ in orders[0][1:]:
        after = move_on(0, 1)
    dq, dk, dv = unattend(sets - 1, 1, *common, found, after=after)
    tie(dq, 0, 1)
    move_on(0, 1)
    feed_sums = jnp.concatenate([flight.reshape(copies, -1, piece, cut) for flight in flights], axis=-1)
    distances = list(range(1, copies))

    parts, gain_parts = [], []
    for k in range(1, span):
        grad, gain_part = unproject(own, masks, [dk, dv], x_full, k, block, weights, after=[feed_sums])
        parts.append(exchange(grad, ("seq", k)))
        gain_parts.append(gain_part)
    received = tensor_sends(feed_sums, distances)
    places = [0, 0]
    *found, own_grad, gain_part = weigh(
        own, masks, turned_one, hidden_grad_turned, dq, dk, dv, attended, x_full, weights, after=gain_parts
    )
    gain_parts.append(gain_part)
    steady = [*received, residual_out]
    shares = 1
    size = block // shares
    lines = []
    for at in range(shares):
        own_rows = finish(x_full, hidden_grad, gain_one, [own_grad] + parts, at * size, size, after=steady)
        lines.append([(own_rows, own_rows)])
    up = [(i, i + 1) for i in range(copies - 1)]
    down = [(i + 1, i) for i in range(copies - 1)]

    def hop(count):
        for _ in range(count):
            for line in lines:
                from_low, from_high = line[-1]
                line.append((lax.ppermute(from_low, "tensor", up), lax.ppermute(from_high, "tensor", down)))

    hop(1)
    found, _ = lax.optimization_barrier((found, lines[0][0][0]))
    flights = [(spread(found[at]), spread(exchange(found[at + 1], last_step))) for at in (0, 2)]
    while isinstance(flights[1], tuple):
        move_on(0, 1)
    attention_sums = [flights[z // near].reshape(near, piece, 4 * part)[z % near] for z in range(copies)]
    gain_grads = sum_over(jnp.concatenate([sum(gain_parts), grad_gain_two]), ("dp", "seq"))
    residual_out = residual_out[::repeats] if repeats > 1 else residual_out
    residual_out = deliver(residual_out.reshape(-1, width), BF16, after=[lines[0][0][0]])
    attention_shard = to_tensor(attention_sums)
    attention_shard, lines[0][1], gain_grads, residual_out = lax.optimization_barrier(
        (attention_shard, lines[0][1], gain_grads, residual_out)
    )
    hop(1)
    feed_shard = tensor_sum(feed_sums, received)

    share = 1.0 / repeats
    attention_shard, feed_shard = attention_shard * share, feed_shard * share
    gain_grads = sum_over(gain_grads * share, ("tensor",))
    gain_shard = lax.dynamic_slice_in_dim(gain_grads, index * piece, piece, 1)

    local = jnp.sum(attention_shard * attention_shard) + jnp.sum(feed_shard * feed_shard)
    def widened(distance, before):
        low, high = lane - distance, lane + distance
        target = [jnp.where(low >= 0, low, lane) // repeats, low >= 0, jnp.where(high < copies, high, lane) // repeats, high < copies]
        target = jnp.stack([jnp.asarray(entry).astype(jnp.int32) for entry in target])
        sides = 2 if 2 * distance < copies else 1
        return widen(target, rows, lines[0][0][0], *lines[0][distance], sides, before)

    grad_in = widened(1, None)
    local, grad_in = lax.optimization_barrier((local, grad_in))
    squares = sum_over(jnp.full((8, 128), local), ("tensor",))
    squares, gain_grads, lines[0][2] = lax.optimization_barrier((squares, gain_grads, lines[0][2]))
    hop(copies - 3)
    squares = sum_over(squares, ("dp", "seq"))
    norm = jnp.sqrt(squares[0, 0] + jnp.sum(gain_grads * gain_grads))
    for distance in range(2, copies):
        grad_in = widened(distance, grad_in)
    residual_out, grad_in = residual_out.reshape(rows, block, width), grad_in.reshape(rows, block, width)

    factor = jnp.minimum(1.0, CLIP / norm)
    shards = (
        jnp.stack([attention_shard[:, k * part : (k + 1) * part] for k in range(3)]),
        attention_shard[:, 3 * part :].T,
        feed_shard[:2],
        feed_shard[2].T,
        gain_shard,
    )
    masters = (attention_in, attention_out, expand, contract, gains)
    firsts = (mean_attention_in, mean_attention_out, mean_expand, mean_contract, mean_gains)
    seconds = (
        square_attention_in,
        square_attention_out,
        square_expand,
        square_contract,
        square_gains,
    )
    new_means = []
    new_squares = []
    new_weights = []
    for member in range(5):
        clipped = shards[member] * factor
        moment = BETA_ONE * firsts[member] + (1.0 - BETA_ONE) * clipped
        square = BETA_TWO * seconds[member] + (1.0 - BETA_TWO) * clipped * clipped
        update = (
            moment / (1.0 - BETA_ONE**STEP) / (jnp.sqrt(square / (1.0 - BETA_TWO**STEP)) + ADAM_EPS)
        )
        shrink = DECAY if member < 4 else 0.0
        speed = RATE if member < 4 else GAIN_RATE
        new_means.append(moment)
        new_squares.append(square)
        new_weights.append(masters[member] - speed * (update + shrink * masters[member]))
    return (residual_out, grad_in, norm, *new_means, *new_squares, *new_weights)


def solution(mesh):
    tokens = P("dp", "seq", None)
    weights = (
        P(None, ("dp", "seq"), "tensor"),
        P("tensor", ("dp", "seq")),
        P(None, ("dp", "seq"), "tensor"),
        P("tensor", ("dp", "seq")),
        P(None, ("dp", "seq")),
    )
    return jax.shard_map(
        on_device,
        mesh=mesh,
        in_specs=(tokens, tokens, P("dp", None)) + weights * 3,
        out_specs=(tokens, tokens, P()) + weights * 3,
        check_vma=False,
    )
```
